32 devices in a mesh: dp: 32 (over z, y, x, core), mp: 1.
Axes of the slice: x: 2, y: 2, z: 4, core: 2. Of those that a mesh axis runs over, the one named last changes fastest.
Arguments:
- tokens: bfloat16 [4096, 4096], P('dp')
- key_cot: bfloat16 [4096, 1024], P('dp', 'mp'), may hold values from -6 to 6
- routes: int32 [4096, 1], P('dp'), may hold values from 0 to 31; in each aligned block of 128 rows (0 to 127, 128 to 255, ...) at most 8 rows name the same one
- counts: int32 [32, 4], P('dp'), may hold values from 1 to 64, 128 in all within a row
- widths: int32 [4], replicated, may hold values from 2 to 8, as said below
- key_weight: bfloat16 [4096, 1024], P('dp', 'mp')
Outputs:
- row_grads: bfloat16 [8192, 4096], P('dp', 'mp')
- key_grad: float32 [4096, 1024], P('dp', 'mp')
The draws below stay inside these ranges and needn't reach their ends.
Inputs may be any that keep to these rules, and one draw needn't show every extreme that they name: `routes`: within the rows of one index of dp no destination is named more than 8 times, a bound that some block reaches. Each index of dp has 4 counts that sum to 128. widths[0] = 8 (the full net), widths[1] = 8 // 4 (the smallest), the other two lie strictly between.
All inputs are finite; a program needn't handle non-finite values.
Results may differ from the reference program's by a relative error of at most 0.0058.
Values may be sent and summed in bfloat16 or wider, within the bound.
No kernel may reach another device: no remote copies, remote signals or barrier semaphores. Data moves between devices by JAX's collectives and lax.ppermute only.
A program may use at most 64 MiB of HBM per device.

```python
import math
import jax
import jax.numpy as jnp
import numpy as np
from jax import lax

D = 4096
KV_HEADS = 8
HEAD_DIM = 128
NSUB = 4
ROWS = 128
MOST = 8
RECV = 256
TOKENS = 4096
N_DP = 32
N_MP = 1


def log_scales(key, shape, low, high):
    return jnp.exp(jax.random.uniform(key, shape, jnp.float32, jnp.log(low), jnp.log(high)))


def draw_tokens(key, part):
    first_key, second_key, third_key = jax.random.split(key, 3)
    row_scale = log_scales(second_key, (TOKENS, 1), 0.3, 3.0)
    col_scale = log_scales(third_key, (1, D), 0.3, 3.0)
    base = jax.random.normal(first_key, (TOKENS, D), jnp.float32)
    return (base * row_scale * col_scale).astype(jnp.bfloat16)


def draw_key_weight(key, part):
    first_key, second_key, third_key = jax.random.split(key, 3)
    row_scale = log_scales(second_key, (D, 1), 0.3, 3.0)
    col_scale = log_scales(third_key, (1, KV_HEADS * HEAD_DIM), 0.3, 3.0)
    base = jax.random.normal(first_key, (D, KV_HEADS * HEAD_DIM), jnp.float32)
    return (base * row_scale * col_scale / jnp.sqrt(jnp.float32(D))).astype(jnp.bfloat16)


def draw_widths(key, part):
    middle = jax.random.randint(jax.random.fold_in(key, 7), (2,), KV_HEADS // 4 + 1, KV_HEADS).astype(jnp.int32)
    ends = jnp.array([KV_HEADS, KV_HEADS // 4], jnp.int32)
    return jnp.concatenate([ends, middle])


def levels(key, extent, shards, least, largest):
    loudness = 1.0
    for axis_at, blocks in shards:
        draws = jax.random.uniform(jax.random.fold_in(jax.random.fold_in(key, 6), axis_at), (blocks,), jnp.float32, least / len(shards), largest / len(shards))
        loudness = loudness * jnp.repeat(jnp.exp(draws), extent[axis_at] // blocks).reshape((-1,) + (1,) * (len(extent) - 1 - axis_at))
    return loudness


def length_profile(count, total, limit, lean):
    portions = [(1 << 20) // math.isqrt(standing ** lean) + 1 for standing in range(2, count + 1)]
    rest, holding = total - limit - (count - 1), [1] * (count - 1)
    while rest > 0:
        movable = [i for i in range(count - 1) if holding[i] < limit]
        pool, budget = sum([portions[i] for i in movable]), rest
        for i in movable:
            extra = min(limit - holding[i], max(1, budget * portions[i] // pool), rest)
            holding[i] = holding[i] + extra
            rest = rest - extra
    return np.array([limit] + holding)


def ragged_sizes(own_key, number_of, total, bound, lean):
    if number_of == 2:
        one = jax.random.randint(own_key, (), max(1, total - bound), min(bound, total - 1) + 1)
        return jnp.stack([one, total - one])
    tallies = jnp.asarray(length_profile(number_of, total, bound, lean), jnp.int32)
    pairs = (number_of - 1) // 2
    giver, taker = tallies[1:1 + 2 * pairs:2], tallies[2:2 + 2 * pairs:2]
    room = jnp.minimum(giver - 1, bound - taker)
    moved = jax.random.randint(jax.random.fold_in(own_key, 1), (pairs,), 0, 1 << 20) % (room + 1)
    tallies = tallies.at[1:1 + 2 * pairs:2].set(giver - moved).at[2:2 + 2 * pairs:2].set(taker + moved)
    return tallies[jax.random.permutation(jax.random.fold_in(own_key, 2), number_of)]


def deal_out(stream_key, own, number, rows, count, top, most, slope):
    order = jax.random.permutation(stream_key, count)
    packed, ordinary = load_shares(count, rows * top, most, slope, True), load_shares(count, rows * top, most, slope, False)
    places = jnp.arange(count)

    def named(sizes, turn):
        used = int((sizes > 0).sum())
        fixed = max(1, used // 4)
        shifted = fixed + (places - fixed + turn * (used - fixed)) % max(1, count - fixed)
        return jnp.zeros((count,), jnp.int32).at[order[jnp.where(places < fixed, places, shifted)]].set(jnp.asarray(sizes, jnp.int32))

    sizes = jnp.where(number % 4 == 0, named(packed, number // 4), named(ordinary, number - number // 4 - 1))
    mixed = jax.random.permutation(jax.random.fold_in(own, 3), count)
    giver, receiver = mixed[0:count // 2 * 2:2], mixed[1:count // 2 * 2:2]
    margin = jnp.minimum(sizes[giver] - 1, most - sizes[receiver]) // 2
    margin = jnp.where((giver == order[0]) | (receiver == order[0]) | (sizes[receiver] == 0), 0, jnp.maximum(margin, 0))
    shifted = jax.random.randint(jax.random.fold_in(own, 4), (count // 2,), 0, 1 << 20) % (margin + 1)
    sizes = sizes.at[giver].add(-shifted).at[receiver].add(shifted)
    members = jnp.searchsorted(jnp.cumsum(sizes), jnp.arange(rows * top), side="right").astype(jnp.int32)
    listing = members.reshape(top, rows).T
    listing = listing[jax.random.permutation(jax.random.fold_in(own, 1), rows)]
    turn = jax.random.randint(jax.random.fold_in(own, 2), (rows, 1), 0, top)
    return jnp.take_along_axis(listing, (jnp.arange(top)[None, :] + turn) % top, axis=1)


def load_shares(amount, total, limit, skew, full):
    weights = [(1 << 20) // math.isqrt(rank ** skew) + 1 for rank in range(1, amount + 1)]
    largest = limit if full else min(limit, max(-(-total // amount), total * weights[0] // sum(weights)))
    least = 1 if total - largest >= amount - 1 else 0
    holding, spare = [largest] + [least] * (amount - 1), total - largest - least * (amount - 1)
    while spare > 0:
        candidates = [i for i in range(1, amount) if holding[i] < largest] or [i for i in range(1, amount) if holding[i] < limit]
        pool, left = sum([weights[i] for i in candidates]), spare
        for i in candidates:
            more = min(limit - holding[i], max(1, left * weights[i] // pool), spare)
            holding[i] = holding[i] + more
            spare = spare - more
    return np.array(holding)


def gaussian(stream_key, extent, scale, limit, shards=(), held_as=jnp.bfloat16):
    gain = levels(stream_key, extent, shards, -0.22, 0.18) if shards else 1.0
    result = jax.random.normal(stream_key, extent, jnp.float32) * scale * gain
    return jnp.minimum(jnp.maximum(result, -limit), limit).astype(held_as)


def setup_inputs(seed: int = 0) -> dict:
    seeds = jax.random.split(jax.random.key(seed), 7)
    tokens = draw_tokens(jax.random.fold_in(seeds[6], 71), 0)
    key_cot = gaussian(seeds[1], (TOKENS, KV_HEADS * HEAD_DIM), 1.0, 6.0, ((0, 32),))
    routes_keys = jax.random.split(jax.random.fold_in(seeds[2], 1), TOKENS // ROWS)
    routes_turns = jax.random.permutation(jax.random.fold_in(seeds[2], 3), TOKENS // ROWS)
    routes = jax.vmap(lambda own, number: deal_out(jax.random.fold_in(seeds[2], 2), own, number, ROWS, N_DP, 1, MOST, 2))(routes_keys, routes_turns).reshape((TOKENS, 1))
    counts = jax.vmap(lambda own: ragged_sizes(own, NSUB, ROWS, ROWS // 2, 2))(jax.random.split(seeds[3], N_DP)).reshape((N_DP, NSUB)).astype(jnp.int32)
    widths = draw_widths(jax.random.fold_in(seeds[6], 71), 0)
    key_weight = draw_key_weight(jax.random.fold_in(seeds[6], 71), 0)
    return {"tokens": tokens, "key_cot": key_cot, "routes": routes, "counts": counts, "widths": widths, "key_weight": key_weight}


epsilon = 1e-06

def subnet_of_rows(counts):
    bounds = jnp.cumsum(counts, axis=1)
    positions = jnp.arange(ROWS, dtype=jnp.int32)
    above = positions[None, :, None] >= bounds[:, None, :NSUB - 1]
    return lax.optimization_barrier(jnp.sum(above.astype(jnp.int32), axis=2))

def block_grads(block_tokens, block_cot, head_mask, key_weight):
    hidden = block_tokens
    key_proj = jnp.dot(hidden, key_weight, preferred_element_type=jnp.float32)
    row_count = key_proj.shape[0]
    per_head = key_proj.reshape(row_count, KV_HEADS, HEAD_DIM)
    head_scale = jnp.sqrt(lax.optimization_barrier(jnp.mean(per_head * per_head, axis=2, keepdims=True)) + epsilon)
    outputs = per_head / head_scale
    upstream = block_cot.astype(jnp.float32).reshape(row_count, KV_HEADS, HEAD_DIM) * head_mask[:, :, None]
    key_delta = (upstream - outputs * lax.optimization_barrier(jnp.mean(upstream * outputs, axis=2, keepdims=True))) / head_scale
    delta_low = key_delta.reshape(row_count, KV_HEADS * HEAD_DIM).astype(jnp.bfloat16)
    group_cols = KV_HEADS * HEAD_DIM // N_MP
    feature_delta = jnp.zeros((row_count, D), jnp.float32)
    for group_index in range(N_MP):
        first_col = group_index * group_cols
        part_delta = lax.dot_general(delta_low[:, first_col:first_col + group_cols], key_weight[:, first_col:first_col + group_cols], (((1,), (1,)), ((), ())), preferred_element_type=jnp.float32)
        rounded = lax.optimization_barrier(part_delta.astype(jnp.bfloat16))
        feature_delta = feature_delta + rounded.astype(jnp.float32)
    weight_term = lax.dot_general(hidden, delta_low, (((0,), (0,)), ((), ())), preferred_element_type=jnp.float32)
    return (feature_delta.astype(jnp.bfloat16), weight_term)

def reference(tokens, key_cot, routes, counts, widths, key_weight):
    subnet = subnet_of_rows(counts)
    row_width = widths[subnet]
    head_mask = (jnp.arange(KV_HEADS, dtype=jnp.int32)[None, None, :] < row_width[:, :, None]).astype(jnp.float32)
    token_blocks = tokens.reshape(N_DP, ROWS, D)
    cot_blocks = key_cot.reshape(N_DP, ROWS, KV_HEADS * HEAD_DIM)

    def step_block(total, inputs):
        input_grad, weight_term = block_grads(inputs[0], inputs[1], inputs[2], key_weight)
        return (total + weight_term, input_grad)
    start_total = jnp.zeros((D, KV_HEADS * HEAD_DIM), jnp.float32)
    total, input_grads = lax.scan(step_block, start_total, (token_blocks, cot_blocks, head_mask))
    key_grad = total / jnp.sqrt(jnp.float32(TOKENS))
    destination = routes[:, 0].reshape(N_DP, ROWS)
    one_hot = (destination[:, :, None] == jnp.arange(N_DP, dtype=jnp.int32)[None, None, :]).astype(jnp.int32)
    earlier = lax.optimization_barrier(jnp.sum(jnp.cumsum(one_hot, axis=1) * one_hot, axis=2)) - 1
    sources = jnp.arange(N_DP, dtype=jnp.int32)[:, None]
    target = (destination * RECV + sources * MOST + earlier).reshape(TOKENS).astype(jnp.int32)
    row_grads = jnp.zeros((N_DP * RECV, D), jnp.bfloat16).at[target].set(input_grads.reshape(TOKENS, D))
    return (row_grads, key_grad)
```

```python
import functools
import math

import jax
import jax.numpy as jnp
from jax import lax
from jax.experimental import pallas as pl
from jax.experimental.pallas import tpu as pltpu
from jax.sharding import PartitionSpec as P

HEAD_DIM = 128
NSUB = 4
VMEM_LIMIT = 48 * 1024 * 1024
epsilon = 1e-06


def per_device_general(tokens, key_cot, routes, counts, widths, key_weight):
    row_count = tokens.shape[0]
    width_model = tokens.shape[1]
    local_cols = key_cot.shape[1]
    local_heads = local_cols // HEAD_DIM
    dp_size = lax.axis_size("dp")
    per_peer = 2 * row_count // dp_size
    receive = dp_size * per_peer
    destination = routes[:, 0]
    one_hot = (destination[:, None] == jnp.arange(dp_size, dtype=jnp.int32)[None, :]).astype(
        jnp.int32
    )
    earlier = jnp.sum(jnp.cumsum(one_hot, axis=0) * one_hot, axis=1) - 1
    send_slot = destination * per_peer + earlier
    bounds = jnp.cumsum(counts[0])
    positions = jnp.arange(row_count, dtype=jnp.int32)
    subnet = jnp.sum((positions[:, None] >= bounds[None, : NSUB - 1]).astype(jnp.int32), axis=1)
    send_subnet = (
        jnp.full((receive,), -1, jnp.int32).at[send_slot].set(subnet).reshape(dp_size, per_peer)
    )
    send_cot = jnp.zeros((receive, local_cols), jnp.bfloat16).at[send_slot].set(key_cot)
    send_cot = send_cot.reshape(dp_size, per_peer, local_cols)
    send_tokens = jnp.zeros((receive, width_model), jnp.bfloat16).at[send_slot].set(tokens)
    send_tokens = send_tokens.reshape(dp_size, per_peer, width_model)
    got_tokens, got_cot, got_subnet = (
        lax.all_to_all(send_tokens, "dp", split_axis=0, concat_axis=0, tiled=True),
        lax.all_to_all(send_cot, "dp", split_axis=0, concat_axis=0, tiled=True),
        lax.all_to_all(send_subnet, "dp", split_axis=0, concat_axis=0, tiled=True),
    )
    hidden = got_tokens.reshape(receive, width_model)
    got_cot = got_cot.reshape(receive, local_cols)
    got_subnet = got_subnet.reshape(receive)
    full_weight = lax.all_gather(key_weight, "dp", axis=0, tiled=True)
    key_proj = jnp.dot(hidden, full_weight, preferred_element_type=jnp.float32)
    per_head = key_proj.reshape(receive, local_heads, HEAD_DIM)
    head_scale = jnp.sqrt(jnp.mean(per_head * per_head, axis=2, keepdims=True) + epsilon)
    outputs = per_head / head_scale
    subnet_match = got_subnet[:, None] == jnp.arange(NSUB, dtype=jnp.int32)[None, :]
    row_width = jnp.sum(jnp.where(subnet_match, widths[None, :], 0), axis=1)
    head_index = lax.axis_index("mp") * local_heads + jnp.arange(local_heads, dtype=jnp.int32)
    head_mask = (head_index[None, :] < row_width[:, None]).astype(jnp.float32)
    upstream = (
        got_cot.astype(jnp.float32).reshape(receive, local_heads, HEAD_DIM) * head_mask[:, :, None]
    )
    key_delta = (
        upstream - outputs * jnp.mean(upstream * outputs, axis=2, keepdims=True)
    ) / head_scale
    delta_low = key_delta.reshape(receive, local_cols).astype(jnp.bfloat16)
    part_delta = lax.dot_general(
        delta_low, full_weight, (((1,), (1,)), ((), ())), preferred_element_type=jnp.float32
    )
    rounded = lax.optimization_barrier(part_delta.astype(jnp.bfloat16)).astype(jnp.float32)
    feature_delta = lax.psum_scatter(
        rounded.astype(jnp.bfloat16), "mp", scatter_dimension=1, tiled=True
    )
    weight_sum = lax.psum_scatter(
        lax.dot_general(
            hidden, delta_low, (((0,), (0,)), ((), ())), preferred_element_type=jnp.float32
        ),
        "dp",
        scatter_dimension=0,
        tiled=True,
    )
    key_grad = weight_sum / math.sqrt(row_count * dp_size)
    return (feature_delta, key_grad)


CORE, X, Y = 1, 2, 4


def swap(value, mask):
    size = lax.axis_size("dp")
    return lax.ppermute(value, "dp", [(i, i ^ mask) for i in range(size)])


def gather_chips(piece):
    size = lax.axis_size("dp")
    half = piece.shape[0] // 2
    column = {0: piece}
    bits = []
    bit = 8
    while bit < size:
        bits.append(bit)
        bit *= 2
    for bit in reversed(bits):
        for mask in list(column):
            column[mask | bit] = swap(column[mask], bit)
    out = []
    for mask, own in column.items():
        by_x, by_y = swap(own, X), swap(own, Y)
        out += [
            (mask, 0, own),
            (mask | X, 0, by_x),
            (mask | Y, 0, by_y),
            (mask | X | Y, 0, swap(by_y[:half], X)),
            (mask | X | Y, half, swap(by_x[half:], Y)),
        ]
    return out


def dot(a, b, dims):
    return lax.dot_general(a, b, (dims, ((), ())), preferred_element_type=jnp.float32)


def delta_kernel(places, me_ref, own_ref, mate_ref, own_cot_ref, mate_cot_ref, *refs):
    pieces = refs[: len(places)]
    delta_ref, weight_ref, acc = refs[len(places) :]
    me = me_ref[0]
    core = me & 1
    rows = own_ref.shape[0]
    chip_rows = 2 * pieces[0].shape[0] // 2
    for n, (mask, first, _) in enumerate(places):
        piece = pieces[n][...]
        depth = piece.shape[0]
        at = pl.multiple_of(((me ^ mask) >> 1) * chip_rows + first, 128)
        weight_ref[pl.ds(at, depth), :] = piece
        for side, ref in enumerate((own_ref, mate_ref)):
            part = dot(ref[:, pl.ds(at, depth)], piece, ((1,), (0,)))
            if n == 0:
                acc[side] = part
            else:
                acc[side] += part
    for side, cot_ref in enumerate((own_cot_ref, mate_cot_ref)):
        at = pl.multiple_of((core ^ side) * rows, rows)
        for head in range(own_cot_ref.shape[1] // HEAD_DIM):
            cols = slice(head * HEAD_DIM, (head + 1) * HEAD_DIM)
            proj = acc[side, :, cols]
            scale = jnp.sqrt(jnp.mean(proj * proj, axis=1, keepdims=True) + epsilon)
            normed = proj / scale
            upstream = cot_ref[:, cols].astype(jnp.float32)
            delta = (upstream - normed * jnp.mean(upstream * normed, axis=1, keepdims=True)) / scale
            delta_ref[pl.ds(at, rows), cols] = delta.astype(jnp.bfloat16)


def select_kernel(places, per_peer, me_ref, target_ref, *refs):
    pieces, sel_ref = refs[: len(places)], refs[len(places)]
    me = me_ref[0]
    receive = sel_ref.shape[0] // 2
    sel_ref[...] = jnp.zeros_like(sel_ref)
    rows = target_ref.shape[2]
    for n, (mask, first, _) in enumerate(places):
        chip = (me ^ mask) >> 1
        depth = pieces[n].shape[0]
        for block in range(first // rows, (first + depth) // rows):
            index = chip * 2 + block
            want = target_ref[index]
            delta = pieces[n][block * rows - first : (block + 1) * rows - first, :]
            for side in range(2):
                slots = lax.broadcasted_iota(jnp.int32, (2 * per_peer, rows), 0)
                slots = slots + ((me & -2) + side) * receive + chip * 2 * per_peer
                hot = (slots == want).astype(jnp.bfloat16)
                at = pl.multiple_of(side * receive + chip * 2 * per_peer, 2 * per_peer)
                sel_ref[pl.ds(at, 2 * per_peer), :] += dot(hot, delta, ((1,), (0,))).astype(
                    jnp.bfloat16
                )


def weight_grad_kernel(places, norm, me_ref, own_ref, mate_ref, *refs):
    pieces, grad_ref = refs[: len(places)], refs[len(places)]
    me = me_ref[0]
    core = me & 1
    rows = own_ref.shape[1]
    total = None
    for n, (mask, first, _) in enumerate(places):
        chip = (me ^ mask) >> 1
        depth = pieces[n].shape[0]
        for block in range(first // rows, (first + depth) // rows):
            delta = pieces[n][block * rows - first : (block + 1) * rows - first, :]
            hidden = jnp.where(core == block, own_ref[chip], mate_ref[chip])
            part = dot(hidden, delta, ((0,), (0,)))
            if n == 0 and block == 0:
                grad_ref[...] = part
            else:
                grad_ref[...] += part
    grad_ref[...] = grad_ref[...] / norm


def row_grad_kernel(sel_a_ref, sel_b_ref, weight_a_ref, weight_b_ref, out_ref):
    total = dot(sel_a_ref[...], weight_a_ref[...], ((1,), (1,)))
    total += dot(sel_b_ref[...], weight_b_ref[...], ((1,), (1,)))
    out_ref[...] = total.astype(jnp.bfloat16)


def whole(count):
    return [pl.BlockSpec(memory_space=pltpu.VMEM)] * count


SCALAR = pl.BlockSpec(memory_space=pltpu.SMEM)
PARAMS = pltpu.CompilerParams(vmem_limit_bytes=VMEM_LIMIT)


def per_device_paired(tokens, key_cot, routes, counts, widths, key_weight):
    rows, width_model = tokens.shape
    cols = key_cot.shape[1]
    half_cols = cols // 2
    size = lax.axis_size("dp")
    chips = size // 2
    per_peer = 2 * rows // size
    receive = size * per_peer
    me = lax.axis_index("dp")
    core = me % 2
    me_scalar = me.astype(jnp.int32).reshape(1)

    def mine(value):
        return lax.dynamic_slice_in_dim(value, core * half_cols, half_cols, 1)

    def theirs(value):
        return lax.dynamic_slice_in_dim(value, (1 - core) * half_cols, half_cols, 1)

    own_weight, mate_weight = mine(key_weight), swap(theirs(key_weight), CORE)
    piece = jnp.where(
        core == 0,
        jnp.concatenate([own_weight, mate_weight], axis=0),
        jnp.concatenate([mate_weight, own_weight], axis=0),
    )
    weights = gather_chips(piece)

    mate_tokens = swap(tokens, CORE)
    groups = [[c + 2 * i for i in range(chips)] for c in range(2)]
    by_chip = tokens.reshape(rows, chips, width_model // chips).transpose(1, 0, 2)
    own_features = lax.all_to_all(
        by_chip, "dp", split_axis=0, concat_axis=0, axis_index_groups=groups, tiled=True
    )
    mate_features = swap(own_features, CORE)

    bounds = jnp.cumsum(counts[0])
    positions = jnp.arange(rows, dtype=jnp.int32)
    subnet = jnp.sum((positions[:, None] >= bounds[None, : NSUB - 1]).astype(jnp.int32), axis=1)
    subnet_match = subnet[:, None] == jnp.arange(NSUB, dtype=jnp.int32)[None, :]
    row_width = jnp.sum(jnp.where(subnet_match, widths[None, :], 0), axis=1)
    head_of_col = jnp.arange(cols, dtype=jnp.int32) // HEAD_DIM
    upstream = jnp.where(
        head_of_col[None, :] < row_width[:, None], key_cot, jnp.zeros_like(key_cot)
    )
    own_cot, mate_cot = mine(upstream), swap(theirs(upstream), CORE)

    destination = routes[:, 0]
    same = (destination[:, None] == destination[None, :]) & (
        positions[:, None] < positions[None, :]
    )
    earlier = jnp.sum(same.astype(jnp.int32), axis=0)
    target = destination * receive + me * per_peer + earlier
    targets = lax.all_gather(target.reshape(1, 1, rows), "dp", axis=0, tiled=True)

    places = [(mask, first, None) for mask, first, _ in weights]
    arrays = [array for _, _, array in weights]
    delta, weight_half = pl.pallas_call(
        functools.partial(delta_kernel, places),
        out_shape=(
            jax.ShapeDtypeStruct((2 * rows, half_cols), jnp.bfloat16),
            jax.ShapeDtypeStruct((width_model, half_cols), jnp.bfloat16),
        ),
        in_specs=[SCALAR] + whole(4 + len(arrays)),
        out_specs=tuple(whole(2)),
        scratch_shapes=[pltpu.VMEM((2, rows, half_cols), jnp.float32)],
        compiler_params=PARAMS,
        name="delta",
    )(me_scalar, tokens, mate_tokens, own_cot, mate_cot, *arrays)

    mate_half = swap(weight_half, CORE)
    deltas = gather_chips(delta)
    arrays = [array for _, _, array in deltas]
    selected = pl.pallas_call(
        functools.partial(select_kernel, places, per_peer),
        out_shape=jax.ShapeDtypeStruct((2 * receive, half_cols), jnp.bfloat16),
        in_specs=[SCALAR] + whole(1 + len(arrays)),
        out_specs=whole(1)[0],
        compiler_params=PARAMS,
        name="select",
    )(me_scalar, targets, *arrays)
    own_selected = lax.dynamic_slice_in_dim(selected, core * receive, receive, 0)
    mate_selected = swap(
        lax.dynamic_slice_in_dim(selected, (1 - core) * receive, receive, 0), CORE
    )
    chip_grad = pl.pallas_call(
        functools.partial(weight_grad_kernel, places, math.sqrt(rows * size)),
        out_shape=jax.ShapeDtypeStruct((2 * rows, half_cols), jnp.float32),
        in_specs=[SCALAR] + whole(2 + len(arrays)),
        out_specs=whole(1)[0],
        compiler_params=PARAMS,
        name="weight_grad",
    )(me_scalar, own_features, mate_features, *arrays)
    shard = width_model // size
    own_grad = lax.dynamic_slice_in_dim(chip_grad, core * shard, shard, 0)
    mate_grad = swap(lax.dynamic_slice_in_dim(chip_grad, (1 - core) * shard, shard, 0), CORE)
    key_grad = jnp.where(
        core == 0,
        jnp.concatenate([own_grad, mate_grad], axis=1),
        jnp.concatenate([mate_grad, own_grad], axis=1),
    )

    tile = 1024
    row_grads = pl.pallas_call(
        row_grad_kernel,
        out_shape=jax.ShapeDtypeStruct((receive, width_model), jnp.bfloat16),
        grid=(width_model // tile,),
        in_specs=[pl.BlockSpec((receive, half_cols), lambda i: (0, 0))] * 2
        + [pl.BlockSpec((tile, half_cols), lambda i: (i, 0))] * 2,
        out_specs=pl.BlockSpec((receive, tile), lambda i: (0, i)),
        compiler_params=PARAMS,
        name="row_grad",
    )(own_selected, mate_selected, weight_half, mate_half)
    return (row_grads, key_grad)


def solution(mesh):
    size, split = mesh.shape["dp"], mesh.shape["mp"]
    paired = split == 1 and size == 32
    return jax.shard_map(
        per_device_paired if paired else per_device_general,
        mesh=mesh,
        in_specs=(P("dp", None), P("dp", "mp"), P("dp", None), P("dp", None), P(), P("dp", "mp")),
        out_specs=(P("dp", "mp"), P("dp", "mp")),
        check_vma=False,
    )
```

```python
import functools
import math

import jax
import jax.numpy as jnp
from jax import lax
from jax.experimental import pallas as pl
from jax.experimental.pallas import tpu as pltpu
from jax.sharding import PartitionSpec as P

HEAD_DIM = 128
NSUB = 4
VMEM_LIMIT = 48 * 1024 * 1024
epsilon = 1e-06


def per_device_general(tokens, key_cot, routes, counts, widths, key_weight):
    row_count = tokens.shape[0]
    width_model = tokens.shape[1]
    local_cols = key_cot.shape[1]
    local_heads = local_cols // HEAD_DIM
    dp_size = lax.axis_size("dp")
    per_peer = 2 * row_count // dp_size
    receive = dp_size * per_peer
    destination = routes[:, 0]
    one_hot = (destination[:, None] == jnp.arange(dp_size, dtype=jnp.int32)[None, :]).astype(
        jnp.int32
    )
    earlier = jnp.sum(jnp.cumsum(one_hot, axis=0) * one_hot, axis=1) - 1
    send_slot = destination * per_peer + earlier
    bounds = jnp.cumsum(counts[0])
    positions = jnp.arange(row_count, dtype=jnp.int32)
    subnet = jnp.sum((positions[:, None] >= bounds[None, : NSUB - 1]).astype(jnp.int32), axis=1)
    send_subnet = (
        jnp.full((receive,), -1, jnp.int32).at[send_slot].set(subnet).reshape(dp_size, per_peer)
    )
    send_cot = jnp.zeros((receive, local_cols), jnp.bfloat16).at[send_slot].set(key_cot)
    send_cot = send_cot.reshape(dp_size, per_peer, local_cols)
    send_tokens = jnp.zeros((receive, width_model), jnp.bfloat16).at[send_slot].set(tokens)
    send_tokens = send_tokens.reshape(dp_size, per_peer, width_model)
    got_tokens, got_cot, got_subnet = (
        lax.all_to_all(send_tokens, "dp", split_axis=0, concat_axis=0, tiled=True),
        lax.all_to_all(send_cot, "dp", split_axis=0, concat_axis=0, tiled=True),
        lax.all_to_all(send_subnet, "dp", split_axis=0, concat_axis=0, tiled=True),
    )
    hidden = got_tokens.reshape(receive, width_model)
    got_cot = got_cot.reshape(receive, local_cols)
    got_subnet = got_subnet.reshape(receive)
    full_weight = lax.all_gather(key_weight, "dp", axis=0, tiled=True)
    key_proj = jnp.dot(hidden, full_weight, preferred_element_type=jnp.float32)
    per_head = key_proj.reshape(receive, local_heads, HEAD_DIM)
    head_scale = jnp.sqrt(jnp.mean(per_head * per_head, axis=2, keepdims=True) + epsilon)
    outputs = per_head / head_scale
    subnet_match = got_subnet[:, None] == jnp.arange(NSUB, dtype=jnp.int32)[None, :]
    row_width = jnp.sum(jnp.where(subnet_match, widths[None, :], 0), axis=1)
    head_index = lax.axis_index("mp") * local_heads + jnp.arange(local_heads, dtype=jnp.int32)
    head_mask = (head_index[None, :] < row_width[:, None]).astype(jnp.float32)
    upstream = (
        got_cot.astype(jnp.float32).reshape(receive, local_heads, HEAD_DIM) * head_mask[:, :, None]
    )
    key_delta = (
        upstream - outputs * jnp.mean(upstream * outputs, axis=2, keepdims=True)
    ) / head_scale
    delta_low = key_delta.reshape(receive, local_cols).astype(jnp.bfloat16)
    part_delta = lax.dot_general(
        delta_low, full_weight, (((1,), (1,)), ((), ())), preferred_element_type=jnp.float32
    )
    rounded = lax.optimization_barrier(part_delta.astype(jnp.bfloat16)).astype(jnp.float32)
    feature_delta = lax.psum_scatter(
        rounded.astype(jnp.bfloat16), "mp", scatter_dimension=1, tiled=True
    )
    weight_sum = lax.psum_scatter(
        lax.dot_general(
            hidden, delta_low, (((0,), (0,)), ((), ())), preferred_element_type=jnp.float32
        ),
        "dp",
        scatter_dimension=0,
        tiled=True,
    )
    key_grad = weight_sum / math.sqrt(row_count * dp_size)
    return (feature_delta, key_grad)


CORE, X, Y = 1, 2, 4


def swap(value, mask):
    size = lax.axis_size("dp")
    return lax.ppermute(value, "dp", [(i, i ^ mask) for i in range(size)])


def gather_chips(piece):
    size = lax.axis_size("dp")
    half = piece.shape[0] // 2
    column = {0: piece}
    bits = []
    bit = 8
    while bit < size:
        bits.append(bit)
        bit *= 2
    for bit in reversed(bits):
        for mask in list(column):
            column[mask | bit] = swap(column[mask], bit)
    out = []
    for mask, own in column.items():
        by_x, by_y = swap(own, X), swap(own, Y)
        out += [
            (mask, 0, own),
            (mask | X, 0, by_x),
            (mask | Y, 0, by_y),
            (mask | X | Y, 0, swap(by_y[:half], X)),
            (mask | X | Y, half, swap(by_x[half:], Y)),
        ]
    return out


def dot(a, b, dims):
    return lax.dot_general(a, b, (dims, ((), ())), preferred_element_type=jnp.float32)


def delta_kernel(
    places, me_ref, own_slot_ref, mate_slot_ref, own_ref, mate_ref, own_cot_ref, mate_cot_ref, *refs
):
    pieces = refs[: len(places)]
    delta_ref, send_ref, weight_ref, acc = refs[len(places) :]
    me = me_ref[0]
    core = me & 1
    rows = own_ref.shape[0]
    chip_rows = pieces[0].shape[0]
    for n, (mask, first) in enumerate(places):
        piece = pieces[n][...]
        depth = piece.shape[0]
        at = pl.multiple_of(((me ^ mask) >> 1) * chip_rows + first, 128)
        weight_ref[pl.ds(at, depth), :] = piece
        for side, ref in enumerate((own_ref, mate_ref)):
            part = dot(ref[:, pl.ds(at, depth)], piece, ((1,), (0,)))
            if n == 0:
                acc[side] = part
            else:
                acc[side] += part
    for side, cot_ref in enumerate((own_cot_ref, mate_cot_ref)):
        at = pl.multiple_of((core ^ side) * rows, rows)
        for head in range(own_cot_ref.shape[1] // HEAD_DIM):
            cols = slice(head * HEAD_DIM, (head + 1) * HEAD_DIM)
            proj = acc[side, :, cols]
            scale = jnp.sqrt(jnp.mean(proj * proj, axis=1, keepdims=True) + epsilon)
            normed = proj / scale
            upstream = cot_ref[:, cols].astype(jnp.float32)
            delta = (upstream - normed * jnp.mean(upstream * normed, axis=1, keepdims=True)) / scale
            delta_ref[pl.ds(at, rows), cols] = delta.astype(jnp.bfloat16)
    slots = lax.broadcasted_iota(jnp.int32, (send_ref.shape[0], rows), 0)
    sent = None
    for side, slot_ref in enumerate((own_slot_ref, mate_slot_ref)):
        at = pl.multiple_of((core ^ side) * rows, rows)
        hot = (slots == slot_ref[...]).astype(jnp.bfloat16)
        part = dot(hot, delta_ref[pl.ds(at, rows), :], ((1,), (0,)))
        sent = part if sent is None else sent + part
    send_ref[...] = sent.astype(jnp.bfloat16)


def weight_grad_kernel(masks, me_ref, own_ref, mate_ref, *refs):
    pieces, part_ref, acc = refs[: len(masks)], refs[len(masks)], refs[len(masks) + 1]
    me = me_ref[0]
    core = me & 1
    rows = own_ref.shape[1]
    for n, mask in enumerate(masks):
        level = (me ^ mask) >> 3
        for side, ref in enumerate((own_ref, mate_ref)):
            at = pl.multiple_of((core ^ side) * rows, rows)
            part = dot(ref[level], pieces[n][pl.ds(at, rows), :], ((0,), (0,)))
            if n == 0 and side == 0:
                acc[...] = part
            else:
                acc[...] += part
    part_ref[...] = acc[...].astype(jnp.bfloat16)


def sum_kernel(norm, parts_ref, grad_ref):
    half = parts_ref.shape[3]
    for side in range(2):
        total = parts_ref[0, side].astype(jnp.float32)
        for chip in range(1, parts_ref.shape[0]):
            total += parts_ref[chip, side].astype(jnp.float32)
        grad_ref[:, side * half : (side + 1) * half] = total / norm


def row_grad_kernel(me_ref, got_ref, own_weight_ref, mate_weight_ref, out_ref):
    core = me_ref[0] & 1
    receive = out_ref.shape[0]
    half = got_ref.shape[3]
    low, high = got_ref[:, 0].reshape(receive, half), got_ref[:, 1].reshape(receive, half)
    own, mate = jnp.where(core == 0, low, high), jnp.where(core == 0, high, low)
    total = dot(own, own_weight_ref[...], ((1,), (1,)))
    total += dot(mate, mate_weight_ref[...], ((1,), (1,)))
    out_ref[...] = total.astype(jnp.bfloat16)


def vmem(count):
    return [pl.BlockSpec(memory_space=pltpu.VMEM)] * count


SCALAR = pl.BlockSpec(memory_space=pltpu.SMEM)
PARAMS = pltpu.CompilerParams(vmem_limit_bytes=VMEM_LIMIT)


def per_device_paired(tokens, key_cot, routes, counts, widths, key_weight):
    rows, width_model = tokens.shape
    cols = key_cot.shape[1]
    half_cols = cols // 2
    size = lax.axis_size("dp")
    chips = size // 2
    plane = 8
    levels = size // plane
    per_peer = 2 * rows // size
    receive = size * per_peer
    me = lax.axis_index("dp")
    core = me % 2
    me_scalar = me.astype(jnp.int32).reshape(1)

    def mine(value):
        return lax.dynamic_slice_in_dim(value, core * half_cols, half_cols, 1)

    def theirs(value):
        return lax.dynamic_slice_in_dim(value, (1 - core) * half_cols, half_cols, 1)

    own_weight, mate_weight = mine(key_weight), swap(theirs(key_weight), CORE)
    piece = jnp.where(
        core == 0,
        jnp.concatenate([own_weight, mate_weight], axis=0),
        jnp.concatenate([mate_weight, own_weight], axis=0),
    )
    weights = gather_chips(piece)
    places = [(mask, first) for mask, first, _ in weights]
    arrays = [array for _, _, array in weights]

    mate_tokens = swap(tokens, CORE)
    columns = [[p + plane * z for z in range(levels)] for p in range(plane)]
    by_level = tokens.reshape(rows, levels, width_model // levels).transpose(1, 0, 2)
    own_features = lax.all_to_all(
        by_level, "dp", split_axis=0, concat_axis=0, axis_index_groups=columns, tiled=True
    )
    mate_features = swap(own_features, CORE)

    bounds = jnp.cumsum(counts[0])
    positions = jnp.arange(rows, dtype=jnp.int32)
    subnet = jnp.sum((positions[:, None] >= bounds[None, : NSUB - 1]).astype(jnp.int32), axis=1)
    subnet_match = subnet[:, None] == jnp.arange(NSUB, dtype=jnp.int32)[None, :]
    row_width = jnp.sum(jnp.where(subnet_match, widths[None, :], 0), axis=1)
    head_of_col = jnp.arange(cols, dtype=jnp.int32) // HEAD_DIM
    upstream = jnp.where(
        head_of_col[None, :] < row_width[:, None], key_cot, jnp.zeros_like(key_cot)
    )
    own_cot, mate_cot = mine(upstream), swap(theirs(upstream), CORE)

    destination = routes[:, 0]
    same = (destination[:, None] == destination[None, :]) & (
        positions[:, None] < positions[None, :]
    )
    earlier = jnp.sum(same.astype(jnp.int32), axis=0)
    own_slot = ((destination * 2 + core) * per_peer + earlier).reshape(1, rows)
    mate_slot = swap(own_slot, CORE)

    delta, send, weight_half = pl.pallas_call(
        functools.partial(delta_kernel, places),
        out_shape=(
            jax.ShapeDtypeStruct((2 * rows, half_cols), jnp.bfloat16),
            jax.ShapeDtypeStruct((2 * receive, half_cols), jnp.bfloat16),
            jax.ShapeDtypeStruct((width_model, half_cols), jnp.bfloat16),
        ),
        in_specs=[SCALAR] + vmem(6 + len(arrays)),
        out_specs=tuple(vmem(3)),
        scratch_shapes=[pltpu.VMEM((2, rows, half_cols), jnp.float32)],
        compiler_params=PARAMS,
        name="delta",
    )(me_scalar, own_slot, mate_slot, tokens, mate_tokens, own_cot, mate_cot, *arrays)

    masks = [plane * z for z in range(levels)]
    deltas = [delta if mask == 0 else swap(delta, mask) for mask in masks]
    part = pl.pallas_call(
        functools.partial(weight_grad_kernel, masks),
        out_shape=jax.ShapeDtypeStruct((width_model // levels, half_cols), jnp.bfloat16),
        in_specs=[SCALAR] + vmem(2 + len(deltas)),
        out_specs=vmem(1)[0],
        scratch_shapes=[pltpu.VMEM((width_model // levels, half_cols), jnp.float32)],
        compiler_params=PARAMS,
        name="weight_grad",
    )(me_scalar, own_features, mate_features, *deltas)
    shard = width_model // size
    planes = [[z * plane + p for p in range(plane)] for z in range(levels)]
    parts = lax.all_to_all(
        part.reshape(plane, shard, half_cols),
        "dp",
        split_axis=0,
        concat_axis=0,
        axis_index_groups=planes,
        tiled=True,
    )
    key_grad = pl.pallas_call(
        functools.partial(sum_kernel, math.sqrt(rows * size)),
        out_shape=jax.ShapeDtypeStruct((shard, cols), jnp.float32),
        in_specs=vmem(1),
        out_specs=vmem(1)[0],
        compiler_params=PARAMS,
        name="sum",
    )(parts.reshape(plane // 2, 2, shard, half_cols))

    mate_half = swap(weight_half, CORE)
    got = lax.all_to_all(
        send.reshape(size, 2 * per_peer, half_cols), "dp", split_axis=0, concat_axis=0, tiled=True
    )
    tile = 1024
    row_grads = pl.pallas_call(
        row_grad_kernel,
        out_shape=jax.ShapeDtypeStruct((receive, width_model), jnp.bfloat16),
        grid=(width_model // tile,),
        in_specs=[
            SCALAR,
            pl.BlockSpec((chips, 2, 2 * per_peer, half_cols), lambda i: (0, 0, 0, 0)),
            pl.BlockSpec((tile, half_cols), lambda i: (i, 0)),
            pl.BlockSpec((tile, half_cols), lambda i: (i, 0)),
        ],
        out_specs=pl.BlockSpec((receive, tile), lambda i: (0, i)),
        compiler_params=PARAMS,
        name="row_grad",
    )(me_scalar, got.reshape(chips, 2, 2 * per_peer, half_cols), weight_half, mate_half)
    return (row_grads, key_grad)


def solution(mesh):
    size, split = mesh.shape["dp"], mesh.shape["mp"]
    paired = split == 1 and size == 32
    return jax.shard_map(
        per_device_paired if paired else per_device_general,
        mesh=mesh,
        in_specs=(P("dp", None), P("dp", "mp"), P("dp", None), P("dp", None), P(), P("dp", "mp")),
        out_specs=(P("dp", "mp"), P("dp", "mp")),
        check_vma=False,
    )
```

```python
import functools
import math

import jax
import jax.numpy as jnp
from jax import lax
from jax.experimental import pallas as pl
from jax.experimental.pallas import tpu as pltpu
from jax.sharding import PartitionSpec as P

HEAD_DIM = 128
NSUB = 4
VMEM_LIMIT = 48 * 1024 * 1024
epsilon = 1e-06


def per_device_general(tokens, key_cot, routes, counts, widths, key_weight):
    row_count = tokens.shape[0]
    width_model = tokens.shape[1]
    local_cols = key_cot.shape[1]
    local_heads = local_cols // HEAD_DIM
    dp_size = lax.axis_size("dp")
    per_peer = 2 * row_count // dp_size
    receive = dp_size * per_peer
    destination = routes[:, 0]
    one_hot = (destination[:, None] == jnp.arange(dp_size, dtype=jnp.int32)[None, :]).astype(
        jnp.int32
    )
    earlier = jnp.sum(jnp.cumsum(one_hot, axis=0) * one_hot, axis=1) - 1
    send_slot = destination * per_peer + earlier
    bounds = jnp.cumsum(counts[0])
    positions = jnp.arange(row_count, dtype=jnp.int32)
    subnet = jnp.sum((positions[:, None] >= bounds[None, : NSUB - 1]).astype(jnp.int32), axis=1)
    send_subnet = (
        jnp.full((receive,), -1, jnp.int32).at[send_slot].set(subnet).reshape(dp_size, per_peer)
    )
    send_cot = jnp.zeros((receive, local_cols), jnp.bfloat16).at[send_slot].set(key_cot)
    send_cot = send_cot.reshape(dp_size, per_peer, local_cols)
    send_tokens = jnp.zeros((receive, width_model), jnp.bfloat16).at[send_slot].set(tokens)
    send_tokens = send_tokens.reshape(dp_size, per_peer, width_model)
    got_tokens, got_cot, got_subnet = (
        lax.all_to_all(send_tokens, "dp", split_axis=0, concat_axis=0, tiled=True),
        lax.all_to_all(send_cot, "dp", split_axis=0, concat_axis=0, tiled=True),
        lax.all_to_all(send_subnet, "dp", split_axis=0, concat_axis=0, tiled=True),
    )
    hidden = got_tokens.reshape(receive, width_model)
    got_cot = got_cot.reshape(receive, local_cols)
    got_subnet = got_subnet.reshape(receive)
    full_weight = lax.all_gather(key_weight, "dp", axis=0, tiled=True)
    key_proj = jnp.dot(hidden, full_weight, preferred_element_type=jnp.float32)
    per_head = key_proj.reshape(receive, local_heads, HEAD_DIM)
    head_scale = jnp.sqrt(jnp.mean(per_head * per_head, axis=2, keepdims=True) + epsilon)
    outputs = per_head / head_scale
    subnet_match = got_subnet[:, None] == jnp.arange(NSUB, dtype=jnp.int32)[None, :]
    row_width = jnp.sum(jnp.where(subnet_match, widths[None, :], 0), axis=1)
    head_index = lax.axis_index("mp") * local_heads + jnp.arange(local_heads, dtype=jnp.int32)
    head_mask = (head_index[None, :] < row_width[:, None]).astype(jnp.float32)
    upstream = (
        got_cot.astype(jnp.float32).reshape(receive, local_heads, HEAD_DIM) * head_mask[:, :, None]
    )
    key_delta = (
        upstream - outputs * jnp.mean(upstream * outputs, axis=2, keepdims=True)
    ) / head_scale
    delta_low = key_delta.reshape(receive, local_cols).astype(jnp.bfloat16)
    part_delta = lax.dot_general(
        delta_low, full_weight, (((1,), (1,)), ((), ())), preferred_element_type=jnp.float32
    )
    rounded = lax.optimization_barrier(part_delta.astype(jnp.bfloat16)).astype(jnp.float32)
    feature_delta = lax.psum_scatter(
        rounded.astype(jnp.bfloat16), "mp", scatter_dimension=1, tiled=True
    )
    weight_sum = lax.psum_scatter(
        lax.dot_general(
            hidden, delta_low, (((0,), (0,)), ((), ())), preferred_element_type=jnp.float32
        ),
        "dp",
        scatter_dimension=0,
        tiled=True,
    )
    key_grad = weight_sum / math.sqrt(row_count * dp_size)
    return (feature_delta, key_grad)


CORE, X, Y = 1, 2, 4
PLANE = 8


def swap(value, mask):
    size = lax.axis_size("dp")
    return lax.ppermute(value, "dp", [(i, i ^ mask) for i in range(size)])


def after(value, *others):
    return lax.optimization_barrier((value, *others))[0]


def gather_column(piece):
    size = lax.axis_size("dp")
    column = {0: piece}
    bit = PLANE
    bits = []
    while bit < size:
        bits.append(bit)
        bit *= 2
    for bit in reversed(bits):
        for mask in list(column):
            column[mask | bit] = swap(column[mask], bit)
    return column


def gather_planes(column, masks):
    arrays, places = [], []
    depth = column[masks[0]].shape[0]
    half = depth // 2
    to_x, to_y = [], []
    for mask in masks:
        by_x, by_y = swap(column[mask], X), swap(column[mask], Y)
        for bits, array in ((0, column[mask]), (X, by_x), (Y, by_y)):
            places.append((mask | bits, 0, len(arrays), 0, depth))
            arrays.append(array)
        to_x.append(by_y[:half])
        to_y.append(by_x[half:])
    for first, bits, halves in ((0, X, to_x), (half, Y, to_y)):
        for n, mask in enumerate(masks):
            places.append((mask | X | Y, first, len(arrays), n * half, half))
        arrays.append(swap(jnp.concatenate(halves, axis=0), bits))
    return arrays, places


def dot(a, b, dims):
    return lax.dot_general(a, b, (dims, ((), ())), preferred_element_type=jnp.float32)


def add_products(places, me, own_ref, mate_ref, pieces, weight_ref, acc, fresh):
    masks = sorted({mask for mask, *_ in places})
    chip_rows = weight_ref.shape[0] // len(masks)
    for mask, first, array, begin, depth in places:
        piece = pieces[array][begin : begin + depth, :]
        at = pl.multiple_of(((me ^ mask) >> 1) * chip_rows + first, 128)
        kept = masks.index(mask) * chip_rows + first
        weight_ref[kept : kept + depth, :] = piece
        for side, ref in enumerate((own_ref, mate_ref)):
            part = dot(ref[:, pl.ds(at, depth)], piece, ((1,), (0,)))
            if fresh:
                acc[side] = part
            else:
                acc[side] += part
        fresh = False


def project_kernel(places, count, me_ref, own_ref, mate_ref, *refs):
    weight_ref, acc_ref = refs[count:]
    add_products(places, me_ref[0], own_ref, mate_ref, refs[:count], weight_ref, acc_ref, True)


def delta_kernel(
    places,
    count,
    me_ref,
    own_slot_ref,
    mate_slot_ref,
    own_ref,
    mate_ref,
    own_cot_ref,
    mate_cot_ref,
    begun_ref,
    *refs,
):
    delta_ref, send_ref, weight_ref, acc = refs[count:]
    me = me_ref[0]
    core = me & 1
    rows = own_ref.shape[0]
    acc[...] = begun_ref[...]
    add_products(places, me, own_ref, mate_ref, refs[:count], weight_ref, acc, False)
    for side, cot_ref in enumerate((own_cot_ref, mate_cot_ref)):
        at = pl.multiple_of((core ^ side) * rows, rows)
        for head in range(own_cot_ref.shape[1] // HEAD_DIM):
            cols = slice(head * HEAD_DIM, (head + 1) * HEAD_DIM)
            proj = acc[side, :, cols]
            scale = jnp.sqrt(jnp.mean(proj * proj, axis=1, keepdims=True) + epsilon)
            normed = proj / scale
            upstream = cot_ref[:, cols].astype(jnp.float32)
            delta = (upstream - normed * jnp.mean(upstream * normed, axis=1, keepdims=True)) / scale
            delta_ref[pl.ds(at, rows), cols] = delta.astype(jnp.bfloat16)
    slots = lax.broadcasted_iota(jnp.int32, (send_ref.shape[0], rows), 0)
    sent = None
    for side, slot_ref in enumerate((own_slot_ref, mate_slot_ref)):
        at = pl.multiple_of((core ^ side) * rows, rows)
        hot = (slots == slot_ref[...]).astype(jnp.bfloat16)
        part = dot(hot, delta_ref[pl.ds(at, rows), :], ((1,), (0,)))
        sent = part if sent is None else sent + part
    send_ref[...] = sent.astype(jnp.bfloat16)


def weight_grad_kernel(count, me_ref, own_ref, mate_ref, *refs):
    own, mate, deltas = refs[: count - 1], refs[count - 1 : 2 * count - 2], refs[2 * count - 2 : -2]
    part_ref, acc = refs[-2:]
    me = me_ref[0]
    core = me & 1
    rows = own_ref.shape[0]
    wide = part_ref.shape[0]
    here = pl.ds(pl.multiple_of((me // PLANE) * wide, wide), wide)
    for n in range(count):
        for side, (whole, parts) in enumerate(((own_ref, own), (mate_ref, mate))):
            at = pl.multiple_of((core ^ side) * rows, rows)
            hidden = whole[:, here] if n == 0 else parts[n - 1][...]
            part = dot(hidden, deltas[n][pl.ds(at, rows), :], ((0,), (0,)))
            if n == 0 and side == 0:
                acc[...] = part
            else:
                acc[...] += part
    part_ref[...] = acc[...].astype(jnp.bfloat16)


def sum_kernel(norm, parts_ref, grad_ref):
    half = parts_ref.shape[3]
    for side in range(2):
        total = parts_ref[0, side].astype(jnp.float32)
        for chip in range(1, parts_ref.shape[0]):
            total += parts_ref[chip, side].astype(jnp.float32)
        grad_ref[:, side * half : (side + 1) * half] = total / norm


def row_grad_kernel(first_masks, me_ref, got_ref, *refs):
    out_ref = refs[-1]
    me = me_ref[0]
    receive = out_ref.shape[0]
    half = got_ref.shape[3]
    depth = refs[0].shape[0]
    low, high = got_ref[:, 0].reshape(receive, half), got_ref[:, 1].reshape(receive, half)
    own = jnp.where(me & 1 == 0, low, high)
    mate = jnp.where(me & 1 == 0, high, low)
    for n, first in enumerate(first_masks):
        total = dot(own, refs[2 * n][...], ((1,), (1,)))
        total += dot(mate, refs[2 * n + 1][...], ((1,), (1,)))
        chip = (me ^ (first + 2 * pl.program_id(0))) >> 1
        out_ref[:, pl.ds(pl.multiple_of(chip * depth, depth), depth)] = total.astype(jnp.bfloat16)


def vmem(count):
    return [pl.BlockSpec(memory_space=pltpu.VMEM)] * count


SCALAR = pl.BlockSpec(memory_space=pltpu.SMEM)
PARAMS = pltpu.CompilerParams(vmem_limit_bytes=VMEM_LIMIT)


def cost(products, moved):
    return pl.CostEstimate(flops=2 * products, bytes_accessed=moved, transcendentals=0)


def per_device_paired(tokens, key_cot, routes, counts, widths, key_weight):
    rows, width_model = tokens.shape
    cols = key_cot.shape[1]
    half_cols = cols // 2
    size = lax.axis_size("dp")
    chips = size // 2
    levels = size // PLANE
    per_peer = 2 * rows // size
    receive = size * per_peer
    wide = width_model // levels
    me = lax.axis_index("dp")
    core = me % 2
    me_scalar = me.astype(jnp.int32).reshape(1)

    def mine(value):
        return lax.dynamic_slice_in_dim(value, core * half_cols, half_cols, 1)

    def theirs(value):
        return lax.dynamic_slice_in_dim(value, (1 - core) * half_cols, half_cols, 1)

    own_weight, mate_weight = mine(key_weight), swap(theirs(key_weight), CORE)
    piece = jnp.where(
        core == 0,
        jnp.concatenate([own_weight, mate_weight], axis=0),
        jnp.concatenate([mate_weight, own_weight], axis=0),
    )
    column = gather_column(piece)
    masks = sorted(column)
    parts_of = [masks[: levels // 2], masks[levels // 2 :]]
    sets = [gather_planes(column, part) for part in parts_of]

    mate_tokens = swap(tokens, CORE)
    late_tokens = after(tokens, column[masks[-1]])
    own_features = []
    for mask in masks[1:]:
        there = lax.shift_right_logical(me ^ mask, 3)
        own_features.append(
            swap(lax.dynamic_slice_in_dim(late_tokens, there * wide, wide, 1), mask)
        )
    mate_features = [swap(value, CORE) for value in own_features]

    key_cot, routes, counts = lax.optimization_barrier((key_cot, routes, counts, column[PLANE]))[:3]
    bounds = jnp.cumsum(counts[0])
    positions = jnp.arange(rows, dtype=jnp.int32)
    subnet = jnp.sum((positions[:, None] >= bounds[None, : NSUB - 1]).astype(jnp.int32), axis=1)
    subnet_match = subnet[:, None] == jnp.arange(NSUB, dtype=jnp.int32)[None, :]
    row_width = jnp.sum(jnp.where(subnet_match, widths[None, :], 0), axis=1)
    head_of_col = jnp.arange(cols, dtype=jnp.int32) // HEAD_DIM
    upstream = jnp.where(
        head_of_col[None, :] < row_width[:, None], key_cot, jnp.zeros_like(key_cot)
    )
    own_cot, mate_cot = mine(upstream), swap(theirs(upstream), CORE)

    destination = routes[:, 0]
    same = (destination[:, None] == destination[None, :]) & (
        positions[:, None] < positions[None, :]
    )
    earlier = jnp.sum(same.astype(jnp.int32), axis=0)
    own_slot = ((destination * 2 + core) * per_peer + earlier).reshape(1, rows)
    mate_slot = swap(own_slot, CORE)

    kept = jax.ShapeDtypeStruct((width_model // 2, half_cols), jnp.bfloat16)
    sums = jax.ShapeDtypeStruct((2, rows, half_cols), jnp.float32)
    arrays, places = sets[0]
    first_weight, begun = pl.pallas_call(
        functools.partial(project_kernel, places, len(arrays)),
        out_shape=(kept, sums),
        in_specs=[SCALAR] + vmem(2 + len(arrays)),
        out_specs=tuple(vmem(2)),
        compiler_params=PARAMS,
        cost_estimate=cost(2 * rows * width_model // 2 * half_cols, 6 << 20),
        name="project",
    )(me_scalar, tokens, mate_tokens, *arrays)
    arrays, places = sets[1]
    delta, send, last_weight = pl.pallas_call(
        functools.partial(delta_kernel, places, len(arrays)),
        out_shape=(
            jax.ShapeDtypeStruct((2 * rows, half_cols), jnp.bfloat16),
            jax.ShapeDtypeStruct((2 * receive, half_cols), jnp.bfloat16),
            kept,
        ),
        in_specs=[SCALAR] + vmem(7 + len(arrays)),
        out_specs=tuple(vmem(3)),
        scratch_shapes=[pltpu.VMEM(sums.shape, sums.dtype)],
        compiler_params=PARAMS,
        cost_estimate=cost(2 * rows * width_model // 2 * half_cols, 6 << 20),
        name="delta",
    )(me_scalar, own_slot, mate_slot, tokens, mate_tokens, own_cot, mate_cot, begun, *arrays)

    deltas = gather_column(delta)
    part = pl.pallas_call(
        functools.partial(weight_grad_kernel, levels),
        out_shape=jax.ShapeDtypeStruct((wide, half_cols), jnp.bfloat16),
        in_specs=[SCALAR] + vmem(2 + 2 * (levels - 1) + levels),
        out_specs=vmem(1)[0],
        scratch_shapes=[pltpu.VMEM((wide, half_cols), jnp.float32)],
        compiler_params=PARAMS,
        cost_estimate=cost(2 * rows * levels * wide * half_cols, 4 << 20),
        name="weight_grad",
    )(
        me_scalar,
        tokens,
        mate_tokens,
        *own_features,
        *mate_features,
        *[deltas[mask] for mask in masks],
    )
    got = lax.all_to_all(
        send.reshape(size, 2 * per_peer, half_cols), "dp", split_axis=0, concat_axis=0, tiled=True
    )
    part = after(part, got)
    shard = width_model // size
    planes = [[z * PLANE + p for p in range(PLANE)] for z in range(levels)]
    parts = lax.all_to_all(
        part.reshape(PLANE, shard, half_cols),
        "dp",
        split_axis=0,
        concat_axis=0,
        axis_index_groups=planes,
        tiled=True,
    )
    key_grad = pl.pallas_call(
        functools.partial(sum_kernel, math.sqrt(rows * size)),
        out_shape=jax.ShapeDtypeStruct((shard, cols), jnp.float32),
        in_specs=vmem(1),
        out_specs=vmem(1)[0],
        compiler_params=PARAMS,
        cost_estimate=cost(PLANE * shard * half_cols, 2 << 20),
        name="sum",
    )(parts.reshape(PLANE // 2, 2, shard, half_cols))

    depth = width_model // chips
    kept_weights = [first_weight, swap(first_weight, CORE), last_weight, swap(last_weight, CORE)]
    row_grads = pl.pallas_call(
        functools.partial(row_grad_kernel, [part[0] for part in parts_of]),
        out_shape=jax.ShapeDtypeStruct((receive, width_model), jnp.bfloat16),
        grid=(chips // 2,),
        in_specs=[
            SCALAR,
            pl.BlockSpec((chips, 2, 2 * per_peer, half_cols), lambda i: (0, 0, 0, 0)),
        ]
        + [pl.BlockSpec((depth, half_cols), lambda i: (i, 0))] * len(kept_weights),
        out_specs=pl.BlockSpec((receive, width_model), lambda i: (0, 0)),
        compiler_params=PARAMS,
        cost_estimate=cost(receive * width_model * cols, 12 << 20),
        name="row_grad",
    )(me_scalar, got.reshape(chips, 2, 2 * per_peer, half_cols), *kept_weights)
    return (row_grads, key_grad)


def solution(mesh):
    size, split = mesh.shape["dp"], mesh.shape["mp"]
    paired = split == 1 and size == 32
    return jax.shard_map(
        per_device_paired if paired else per_device_general,
        mesh=mesh,
        in_specs=(P("dp", None), P("dp", "mp"), P("dp", None), P("dp", None), P(), P("dp", "mp")),
        out_specs=(P("dp", "mp"), P("dp", "mp")),
        check_vma=False,
    )
```

```python
import functools
import math

import jax
import jax.numpy as jnp
from jax import lax
from jax.experimental import pallas as pl
from jax.experimental.pallas import tpu as pltpu
from jax.sharding import PartitionSpec as P

HEAD_DIM = 128
NSUB = 4
VMEM_LIMIT = 48 * 1024 * 1024
epsilon = 1e-06


def per_device_general(tokens, key_cot, routes, counts, widths, key_weight):
    row_count = tokens.shape[0]
    width_model = tokens.shape[1]
    local_cols = key_cot.shape[1]
    local_heads = local_cols // HEAD_DIM
    dp_size = lax.axis_size("dp")
    per_peer = 2 * row_count // dp_size
    receive = dp_size * per_peer
    destination = routes[:, 0]
    one_hot = (destination[:, None] == jnp.arange(dp_size, dtype=jnp.int32)[None, :]).astype(
        jnp.int32
    )
    earlier = jnp.sum(jnp.cumsum(one_hot, axis=0) * one_hot, axis=1) - 1
    send_slot = destination * per_peer + earlier
    bounds = jnp.cumsum(counts[0])
    positions = jnp.arange(row_count, dtype=jnp.int32)
    subnet = jnp.sum((positions[:, None] >= bounds[None, : NSUB - 1]).astype(jnp.int32), axis=1)
    send_subnet = (
        jnp.full((receive,), -1, jnp.int32).at[send_slot].set(subnet).reshape(dp_size, per_peer)
    )
    send_cot = jnp.zeros((receive, local_cols), jnp.bfloat16).at[send_slot].set(key_cot)
    send_cot = send_cot.reshape(dp_size, per_peer, local_cols)
    send_tokens = jnp.zeros((receive, width_model), jnp.bfloat16).at[send_slot].set(tokens)
    send_tokens = send_tokens.reshape(dp_size, per_peer, width_model)
    got_tokens, got_cot, got_subnet = (
        lax.all_to_all(send_tokens, "dp", split_axis=0, concat_axis=0, tiled=True),
        lax.all_to_all(send_cot, "dp", split_axis=0, concat_axis=0, tiled=True),
        lax.all_to_all(send_subnet, "dp", split_axis=0, concat_axis=0, tiled=True),
    )
    hidden = got_tokens.reshape(receive, width_model)
    got_cot = got_cot.reshape(receive, local_cols)
    got_subnet = got_subnet.reshape(receive)
    full_weight = lax.all_gather(key_weight, "dp", axis=0, tiled=True)
    key_proj = jnp.dot(hidden, full_weight, preferred_element_type=jnp.float32)
    per_head = key_proj.reshape(receive, local_heads, HEAD_DIM)
    head_scale = jnp.sqrt(jnp.mean(per_head * per_head, axis=2, keepdims=True) + epsilon)
    outputs = per_head / head_scale
    subnet_match = got_subnet[:, None] == jnp.arange(NSUB, dtype=jnp.int32)[None, :]
    row_width = jnp.sum(jnp.where(subnet_match, widths[None, :], 0), axis=1)
    head_index = lax.axis_index("mp") * local_heads + jnp.arange(local_heads, dtype=jnp.int32)
    head_mask = (head_index[None, :] < row_width[:, None]).astype(jnp.float32)
    upstream = (
        got_cot.astype(jnp.float32).reshape(receive, local_heads, HEAD_DIM) * head_mask[:, :, None]
    )
    key_delta = (
        upstream - outputs * jnp.mean(upstream * outputs, axis=2, keepdims=True)
    ) / head_scale
    delta_low = key_delta.reshape(receive, local_cols).astype(jnp.bfloat16)
    part_delta = lax.dot_general(
        delta_low, full_weight, (((1,), (1,)), ((), ())), preferred_element_type=jnp.float32
    )
    rounded = lax.optimization_barrier(part_delta.astype(jnp.bfloat16)).astype(jnp.float32)
    feature_delta = lax.psum_scatter(
        rounded.astype(jnp.bfloat16), "mp", scatter_dimension=1, tiled=True
    )
    weight_sum = lax.psum_scatter(
        lax.dot_general(
            hidden, delta_low, (((0,), (0,)), ((), ())), preferred_element_type=jnp.float32
        ),
        "dp",
        scatter_dimension=0,
        tiled=True,
    )
    key_grad = weight_sum / math.sqrt(row_count * dp_size)
    return (feature_delta, key_grad)


CORE, X, Y = 1, 2, 4
PLANE = 8


def swap(value, mask):
    size = lax.axis_size("dp")
    return lax.ppermute(value, "dp", [(i, i ^ mask) for i in range(size)])


def after(value, *others):
    return lax.optimization_barrier((value, *others))[0]


def gather_column(piece):
    size = lax.axis_size("dp")
    column = {0: piece}
    bit = PLANE
    bits = []
    while bit < size:
        bits.append(bit)
        bit *= 2
    for bit in reversed(bits):
        for mask in list(column):
            column[mask | bit] = swap(column[mask], bit)
    return column


def gather_planes(column, masks):
    arrays, places = [], []

    def add(mask, first, array):
        places.append((mask, first, len(arrays), 0, array.shape[0]))
        arrays.append(array)

    half = column[masks[0]].shape[0] // 2
    for mask in masks:
        by_x, by_y = swap(column[mask], X), swap(column[mask], Y)
        add(mask, 0, column[mask])
        add(mask | X, 0, by_x)
        add(mask | Y, 0, by_y)
        add(mask | X | Y, 0, swap(by_y[:half], X))
        add(mask | X | Y, half, swap(by_x[half:], Y))
    return arrays, places


def dot(a, b, dims):
    return lax.dot_general(a, b, (dims, ((), ())), preferred_element_type=jnp.float32)


def add_products(places, me, own_ref, mate_ref, pieces, weight_ref, acc, fresh):
    masks = sorted({mask for mask, *_ in places})
    chip_rows = weight_ref.shape[0] // len(masks)
    for mask, first, array, begin, depth in places:
        piece = pieces[array][begin : begin + depth, :]
        at = pl.multiple_of(((me ^ mask) >> 1) * chip_rows + first, 128)
        kept = masks.index(mask) * chip_rows + first
        weight_ref[kept : kept + depth, :] = piece
        for side, ref in enumerate((own_ref, mate_ref)):
            part = dot(ref[:, pl.ds(at, depth)], piece, ((1,), (0,)))
            if fresh:
                acc[side] = part
            else:
                acc[side] += part
        fresh = False


def project_kernel(places, count, me_ref, own_ref, mate_ref, *refs):
    weight_ref, acc_ref = refs[count:]
    add_products(places, me_ref[0], own_ref, mate_ref, refs[:count], weight_ref, acc_ref, True)


def delta_kernel(
    places,
    count,
    me_ref,
    own_ref,
    mate_ref,
    own_cot_ref,
    mate_cot_ref,
    begun_ref,
    *refs,
):
    delta_ref, weight_ref, acc = refs[count:]
    me = me_ref[0]
    core = me & 1
    rows = own_ref.shape[0]
    acc[...] = begun_ref[...]
    add_products(places, me, own_ref, mate_ref, refs[:count], weight_ref, acc, False)
    for side, cot_ref in enumerate((own_cot_ref, mate_cot_ref)):
        at = pl.multiple_of((core ^ side) * rows, rows)
        for head in range(own_cot_ref.shape[1] // HEAD_DIM):
            cols = slice(head * HEAD_DIM, (head + 1) * HEAD_DIM)
            proj = acc[side, :, cols]
            scale = jnp.sqrt(jnp.mean(proj * proj, axis=1, keepdims=True) + epsilon)
            normed = proj / scale
            upstream = cot_ref[:, cols].astype(jnp.float32)
            delta = (upstream - normed * jnp.mean(upstream * normed, axis=1, keepdims=True)) / scale
            delta_ref[pl.ds(at, rows), cols] = delta.astype(jnp.bfloat16)


def select_kernel(count, me_ref, code_ref, *refs):
    sent_ref = refs[count]
    slot_count, half_cols = sent_ref.shape
    rows = code_ref.shape[1]
    level = lax.shift_right_logical(me_ref[0], 3)
    slots = lax.broadcasted_iota(jnp.int32, (slot_count, rows), 0) + level * slot_count
    total = None
    for n in range(count):
        for side in range(2):
            hot = (slots == code_ref[2 * n + side : 2 * n + side + 1, :]).astype(jnp.bfloat16)
            part = dot(hot, refs[n][side * rows : (side + 1) * rows, :], ((1,), (0,)))
            total = part if total is None else total + part
    sent_ref[...] = total.astype(jnp.bfloat16)


def weight_grad_kernel(count, me_ref, own_ref, mate_ref, *refs):
    own, mate, deltas = refs[: count - 1], refs[count - 1 : 2 * count - 2], refs[2 * count - 2 : -2]
    part_ref, acc = refs[-2:]
    me = me_ref[0]
    core = me & 1
    rows = own_ref.shape[0]
    wide = part_ref.shape[0]
    here = pl.ds(pl.multiple_of((me // PLANE) * wide, wide), wide)
    for n in range(count):
        for side, (whole, parts) in enumerate(((own_ref, own), (mate_ref, mate))):
            at = pl.multiple_of((core ^ side) * rows, rows)
            hidden = whole[:, here] if n == 0 else parts[n - 1][...]
            part = dot(hidden, deltas[n][pl.ds(at, rows), :], ((0,), (0,)))
            if n == 0 and side == 0:
                acc[...] = part
            else:
                acc[...] += part
    part_ref[...] = acc[...].astype(jnp.bfloat16)


def sum_kernel(norm, parts_ref, grad_ref):
    half = parts_ref.shape[3]
    for side in range(2):
        total = parts_ref[0, side].astype(jnp.float32)
        for chip in range(1, parts_ref.shape[0]):
            total += parts_ref[chip, side].astype(jnp.float32)
        grad_ref[:, side * half : (side + 1) * half] = total / norm


def row_grad_kernel(first_masks, me_ref, got_ref, *refs):
    out_ref, rows_ref = refs[-2:]
    me = me_ref[0]
    chips, _, count, _ = got_ref.shape
    depth = refs[0].shape[0]
    block = 16

    @pl.when(pl.program_id(0) == 0)
    def _():
        for level in range(count // block):
            for chip in range(chips):
                at = (level * chips + chip) * block
                for side in range(2):
                    rows_ref[side, at : at + block, :] = got_ref[
                        chip, side, level * block : (level + 1) * block, :
                    ]

    own, mate = rows_ref[me & 1], rows_ref[1 - (me & 1)]
    for n, first in enumerate(first_masks):
        total = dot(own, refs[2 * n][...], ((1,), (1,)))
        total += dot(mate, refs[2 * n + 1][...], ((1,), (1,)))
        chip = (me ^ (first + 2 * pl.program_id(0))) >> 1
        out_ref[:, pl.ds(pl.multiple_of(chip * depth, depth), depth)] = total.astype(jnp.bfloat16)


def vmem(count):
    return [pl.BlockSpec(memory_space=pltpu.VMEM)] * count


SCALAR = pl.BlockSpec(memory_space=pltpu.SMEM)
PARAMS = pltpu.CompilerParams(vmem_limit_bytes=VMEM_LIMIT)


def cost(products, moved):
    return pl.CostEstimate(flops=2 * products, bytes_accessed=moved, transcendentals=0)


def per_device_paired(tokens, key_cot, routes, counts, widths, key_weight):
    rows, width_model = tokens.shape
    cols = key_cot.shape[1]
    half_cols = cols // 2
    size = lax.axis_size("dp")
    chips = size // 2
    levels = size // PLANE
    per_peer = 2 * rows // size
    receive = size * per_peer
    wide = width_model // levels
    me = lax.axis_index("dp")
    core = me % 2
    me_scalar = me.astype(jnp.int32).reshape(1)

    def mine(value):
        return lax.dynamic_slice_in_dim(value, core * half_cols, half_cols, 1)

    def theirs(value):
        return lax.dynamic_slice_in_dim(value, (1 - core) * half_cols, half_cols, 1)

    own_weight, mate_weight = mine(key_weight), swap(theirs(key_weight), CORE)
    piece = jnp.where(
        core == 0,
        jnp.concatenate([own_weight, mate_weight], axis=0),
        jnp.concatenate([mate_weight, own_weight], axis=0),
    )
    column = gather_column(piece)
    masks = sorted(column)
    parts_of = [masks[: levels // 2], masks[levels // 2 :]]
    sets = [gather_planes(column, part) for part in parts_of]

    mate_tokens = swap(tokens, CORE)
    far_tokens = after(tokens, sets[0][0][3], sets[0][0][4])
    near_tokens = after(tokens, column[masks[-1]])
    own_features = []
    for mask in masks[1:]:
        there = lax.shift_right_logical(me ^ mask, 3)
        source = near_tokens if mask == PLANE else far_tokens
        own_features.append(swap(lax.dynamic_slice_in_dim(source, there * wide, wide, 1), mask))
    mate_features = [swap(value, CORE) for value in own_features]

    key_cot, routes, counts = lax.optimization_barrier((key_cot, routes, counts, column[PLANE]))[:3]
    bounds = jnp.cumsum(counts[0])
    positions = jnp.arange(rows, dtype=jnp.int32)
    subnet = jnp.sum((positions[:, None] >= bounds[None, : NSUB - 1]).astype(jnp.int32), axis=1)
    subnet_match = subnet[:, None] == jnp.arange(NSUB, dtype=jnp.int32)[None, :]
    row_width = jnp.sum(jnp.where(subnet_match, widths[None, :], 0), axis=1)
    head_of_col = jnp.arange(cols, dtype=jnp.int32) // HEAD_DIM
    upstream = jnp.where(
        head_of_col[None, :] < row_width[:, None], key_cot, jnp.zeros_like(key_cot)
    )
    own_cot, mate_cot = mine(upstream), swap(theirs(upstream), CORE)

    destination = routes[:, 0]
    same = (destination[:, None] == destination[None, :]) & (
        positions[:, None] < positions[None, :]
    )
    earlier = jnp.sum(same.astype(jnp.int32), axis=0)
    source = 2 * lax.shift_right_logical(me, 3) + core
    code = ((destination * 2 * levels + source) * per_peer + earlier).reshape(1, rows)
    mate_code = swap(code, CORE)
    codes = jnp.where(
        core == 0,
        jnp.concatenate([code, mate_code], axis=0),
        jnp.concatenate([mate_code, code], axis=0),
    )
    order = [0]
    for bit in reversed([PLANE << n for n in range(levels.bit_length() - 1)]):
        codes = jnp.concatenate([codes, swap(codes, bit)], axis=0)
        order += [mask | bit for mask in order]

    kept = jax.ShapeDtypeStruct((width_model // 2, half_cols), jnp.bfloat16)
    sums = jax.ShapeDtypeStruct((2, rows, half_cols), jnp.float32)
    arrays, places = sets[0]
    first_weight, begun = pl.pallas_call(
        functools.partial(project_kernel, places, len(arrays)),
        out_shape=(kept, sums),
        in_specs=[SCALAR] + vmem(2 + len(arrays)),
        out_specs=tuple(vmem(2)),
        compiler_params=PARAMS,
        cost_estimate=cost(2 * rows * width_model // 2 * half_cols, 6 << 20),
        name="project",
    )(me_scalar, tokens, mate_tokens, *arrays)
    arrays, places = sets[1]
    begun = after(begun, codes, *own_features)
    delta, last_weight = pl.pallas_call(
        functools.partial(delta_kernel, places, len(arrays)),
        out_shape=(jax.ShapeDtypeStruct((2 * rows, half_cols), jnp.bfloat16), kept),
        in_specs=[SCALAR] + vmem(5 + len(arrays)),
        out_specs=tuple(vmem(2)),
        scratch_shapes=[pltpu.VMEM(sums.shape, sums.dtype)],
        compiler_params=PARAMS,
        cost_estimate=cost(2 * rows * width_model // 2 * half_cols, 6 << 20),
        name="delta",
    )(me_scalar, tokens, mate_tokens, own_cot, mate_cot, begun, *arrays)

    deltas = gather_column(delta)
    selected = pl.pallas_call(
        functools.partial(select_kernel, levels),
        out_shape=jax.ShapeDtypeStruct((PLANE * 2 * levels * per_peer, half_cols), jnp.bfloat16),
        in_specs=[SCALAR] + vmem(1 + levels),
        out_specs=vmem(1)[0],
        compiler_params=PARAMS,
        cost_estimate=cost(receive * 2 * levels * 2 * rows * half_cols, 2 << 20),
        name="select",
    )(me_scalar, codes, *[deltas[mask] for mask in order])
    planes = [[z * PLANE + p for p in range(PLANE)] for z in range(levels)]

    def to_plane(value):
        return lax.all_to_all(
            value.reshape(PLANE, -1, half_cols),
            "dp",
            split_axis=0,
            concat_axis=0,
            axis_index_groups=planes,
            tiled=True,
        )

    got = to_plane(selected)

    ready = after(deltas[0], selected)
    part = pl.pallas_call(
        functools.partial(weight_grad_kernel, levels),
        out_shape=jax.ShapeDtypeStruct((wide, half_cols), jnp.bfloat16),
        in_specs=[SCALAR] + vmem(2 + 2 * (levels - 1) + levels),
        out_specs=vmem(1)[0],
        scratch_shapes=[pltpu.VMEM((wide, half_cols), jnp.float32)],
        compiler_params=PARAMS,
        cost_estimate=cost(2 * rows * levels * wide * half_cols, 4 << 20),
        name="weight_grad",
    )(
        me_scalar,
        tokens,
        mate_tokens,
        *own_features,
        *mate_features,
        *[ready if mask == 0 else deltas[mask] for mask in masks],
    )
    shard = width_model // size
    parts = to_plane(part)

    depth = width_model // chips
    kept_weights = [first_weight, swap(first_weight, CORE), last_weight, swap(last_weight, CORE)]
    row_grads = pl.pallas_call(
        functools.partial(row_grad_kernel, [part[0] for part in parts_of]),
        out_shape=jax.ShapeDtypeStruct((receive, width_model), jnp.bfloat16),
        grid=(chips // 2,),
        in_specs=[
            SCALAR,
            pl.BlockSpec((PLANE // 2, 2, 2 * levels * per_peer, half_cols), lambda i: (0, 0, 0, 0)),
        ]
        + [pl.BlockSpec((depth, half_cols), lambda i: (i, 0))] * len(kept_weights),
        out_specs=pl.BlockSpec((receive, width_model), lambda i: (0, 0)),
        scratch_shapes=[pltpu.VMEM((2, receive, half_cols), jnp.bfloat16)],
        compiler_params=PARAMS,
        cost_estimate=cost(receive * width_model * cols, 12 << 20),
        name="row_grad",
    )(me_scalar, got.reshape(PLANE // 2, 2, 2 * levels * per_peer, half_cols), *kept_weights)

    parts = after(parts, row_grads)
    key_grad = pl.pallas_call(
        functools.partial(sum_kernel, math.sqrt(rows * size)),
        out_shape=jax.ShapeDtypeStruct((shard, cols), jnp.float32),
        in_specs=vmem(1),
        out_specs=vmem(1)[0],
        compiler_params=PARAMS,
        cost_estimate=cost(PLANE * shard * half_cols, 2 << 20),
        name="sum",
    )(parts.reshape(PLANE // 2, 2, shard, half_cols))
    return (row_grads, key_grad)


def solution(mesh):
    size, split = mesh.shape["dp"], mesh.shape["mp"]
    paired = split == 1 and size == 32
    return jax.shard_map(
        per_device_paired if paired else per_device_general,
        mesh=mesh,
        in_specs=(P("dp", None), P("dp", "mp"), P("dp", None), P("dp", None), P(), P("dp", "mp")),
        out_specs=(P("dp", "mp"), P("dp", "mp")),
        check_vma=False,
    )
```

```python
import functools
import math

import jax
import jax.numpy as jnp
from jax import lax
from jax.experimental import pallas as pl
from jax.experimental.pallas import tpu as pltpu
from jax.sharding import PartitionSpec as P

HEAD_DIM = 128
NSUB = 4
VMEM_LIMIT = 48 * 1024 * 1024
epsilon = 1e-06


def per_device_general(tokens, key_cot, routes, counts, widths, key_weight):
    row_count = tokens.shape[0]
    width_model = tokens.shape[1]
    local_cols = key_cot.shape[1]
    local_heads = local_cols // HEAD_DIM
    dp_size = lax.axis_size("dp")
    per_peer = 2 * row_count // dp_size
    receive = dp_size * per_peer
    destination = routes[:, 0]
    one_hot = (destination[:, None] == jnp.arange(dp_size, dtype=jnp.int32)[None, :]).astype(
        jnp.int32
    )
    earlier = jnp.sum(jnp.cumsum(one_hot, axis=0) * one_hot, axis=1) - 1
    send_slot = destination * per_peer + earlier
    bounds = jnp.cumsum(counts[0])
    positions = jnp.arange(row_count, dtype=jnp.int32)
    subnet = jnp.sum((positions[:, None] >= bounds[None, : NSUB - 1]).astype(jnp.int32), axis=1)
    send_subnet = (
        jnp.full((receive,), -1, jnp.int32).at[send_slot].set(subnet).reshape(dp_size, per_peer)
    )
    send_cot = jnp.zeros((receive, local_cols), jnp.bfloat16).at[send_slot].set(key_cot)
    send_cot = send_cot.reshape(dp_size, per_peer, local_cols)
    send_tokens = jnp.zeros((receive, width_model), jnp.bfloat16).at[send_slot].set(tokens)
    send_tokens = send_tokens.reshape(dp_size, per_peer, width_model)
    got_tokens, got_cot, got_subnet = (
        lax.all_to_all(send_tokens, "dp", split_axis=0, concat_axis=0, tiled=True),
        lax.all_to_all(send_cot, "dp", split_axis=0, concat_axis=0, tiled=True),
        lax.all_to_all(send_subnet, "dp", split_axis=0, concat_axis=0, tiled=True),
    )
    hidden = got_tokens.reshape(receive, width_model)
    got_cot = got_cot.reshape(receive, local_cols)
    got_subnet = got_subnet.reshape(receive)
    full_weight = lax.all_gather(key_weight, "dp", axis=0, tiled=True)
    key_proj = jnp.dot(hidden, full_weight, preferred_element_type=jnp.float32)
    per_head = key_proj.reshape(receive, local_heads, HEAD_DIM)
    head_scale = jnp.sqrt(jnp.mean(per_head * per_head, axis=2, keepdims=True) + epsilon)
    outputs = per_head / head_scale
    subnet_match = got_subnet[:, None] == jnp.arange(NSUB, dtype=jnp.int32)[None, :]
    row_width = jnp.sum(jnp.where(subnet_match, widths[None, :], 0), axis=1)
    head_index = lax.axis_index("mp") * local_heads + jnp.arange(local_heads, dtype=jnp.int32)
    head_mask = (head_index[None, :] < row_width[:, None]).astype(jnp.float32)
    upstream = (
        got_cot.astype(jnp.float32).reshape(receive, local_heads, HEAD_DIM) * head_mask[:, :, None]
    )
    key_delta = (
        upstream - outputs * jnp.mean(upstream * outputs, axis=2, keepdims=True)
    ) / head_scale
    delta_low = key_delta.reshape(receive, local_cols).astype(jnp.bfloat16)
    part_delta = lax.dot_general(
        delta_low, full_weight, (((1,), (1,)), ((), ())), preferred_element_type=jnp.float32
    )
    rounded = lax.optimization_barrier(part_delta.astype(jnp.bfloat16)).astype(jnp.float32)
    feature_delta = lax.psum_scatter(
        rounded.astype(jnp.bfloat16), "mp", scatter_dimension=1, tiled=True
    )
    weight_sum = lax.psum_scatter(
        lax.dot_general(
            hidden, delta_low, (((0,), (0,)), ((), ())), preferred_element_type=jnp.float32
        ),
        "dp",
        scatter_dimension=0,
        tiled=True,
    )
    key_grad = weight_sum / math.sqrt(row_count * dp_size)
    return (feature_delta, key_grad)


CORE, X, Y = 1, 2, 4
PLANE = 8


def swap(value, mask):
    size = lax.axis_size("dp")
    return lax.ppermute(value, "dp", [(i, i ^ mask) for i in range(size)])


def after(value, *others):
    return lax.optimization_barrier((value, *others))[0]


def gather_column(piece):
    size = lax.axis_size("dp")
    column = {0: piece}
    bit = PLANE
    bits = []
    while bit < size:
        bits.append(bit)
        bit *= 2
    for bit in reversed(bits):
        for mask in list(column):
            column[mask | bit] = swap(column[mask], bit)
    return column


class Places:
    def __init__(self):
        self.arrays, self.places = [], []

    def add(self, mask, first, array):
        self.places.append((mask, first, len(self.arrays), 0, array.shape[0]))
        self.arrays.append(array)


def diagonal(by_x, by_y):
    half = by_x.shape[0] // 2
    return swap(by_y[:half], X), swap(by_x[half:], Y)


def dot(a, b, dims):
    return lax.dot_general(a, b, (dims, ((), ())), preferred_element_type=jnp.float32)


def add_products(places, me, own_ref, mate_ref, pieces, weight_ref, acc, fresh):
    masks = sorted({mask for mask, *_ in places})
    chip_rows = weight_ref.shape[0] // len(masks)
    for mask, first, array, begin, depth in places:
        piece = pieces[array][begin : begin + depth, :]
        at = pl.multiple_of(((me ^ mask) >> 1) * chip_rows + first, 128)
        kept = masks.index(mask) * chip_rows + first
        weight_ref[kept : kept + depth, :] = piece
        for side, ref in enumerate((own_ref, mate_ref)):
            part = dot(ref[:, pl.ds(at, depth)], piece, ((1,), (0,)))
            if fresh:
                acc[side] = part
            else:
                acc[side] += part
        fresh = False


def project_kernel(places, count, me_ref, own_ref, mate_ref, *refs):
    weight_ref, acc_ref = refs[count:]
    add_products(places, me_ref[0], own_ref, mate_ref, refs[:count], weight_ref, acc_ref, True)


def delta_kernel(
    places,
    count,
    me_ref,
    own_ref,
    mate_ref,
    own_cot_ref,
    mate_cot_ref,
    begun_ref,
    *refs,
):
    delta_ref, weight_ref, acc = refs[count:]
    me = me_ref[0]
    core = me & 1
    rows = own_ref.shape[0]
    acc[...] = begun_ref[...]
    add_products(places, me, own_ref, mate_ref, refs[:count], weight_ref, acc, False)
    for side, cot_ref in enumerate((own_cot_ref, mate_cot_ref)):
        at = pl.multiple_of((core ^ side) * rows, rows)
        for head in range(own_cot_ref.shape[1] // HEAD_DIM):
            cols = slice(head * HEAD_DIM, (head + 1) * HEAD_DIM)
            proj = acc[side, :, cols]
            scale = jnp.sqrt(jnp.mean(proj * proj, axis=1, keepdims=True) + epsilon)
            normed = proj / scale
            upstream = cot_ref[:, cols].astype(jnp.float32)
            delta = (upstream - normed * jnp.mean(upstream * normed, axis=1, keepdims=True)) / scale
            delta_ref[pl.ds(at, rows), cols] = delta.astype(jnp.bfloat16)


def select_kernel(count, me_ref, code_ref, *refs):
    sent_ref = refs[count]
    slot_count, half_cols = sent_ref.shape
    rows = code_ref.shape[1]
    level = lax.shift_right_logical(me_ref[0], 3)
    slots = lax.broadcasted_iota(jnp.int32, (slot_count, rows), 0) + level * slot_count
    total = None
    for n in range(count):
        for side in range(2):
            hot = (slots == code_ref[2 * n + side : 2 * n + side + 1, :]).astype(jnp.bfloat16)
            part = dot(hot, refs[n][side * rows : (side + 1) * rows, :], ((1,), (0,)))
            total = part if total is None else total + part
    sent_ref[...] = total.astype(jnp.bfloat16)


def weight_grad_kernel(count, me_ref, own_ref, mate_ref, *refs):
    part_ref, acc = refs[count:]
    me = me_ref[0]
    core = me & 1
    rows = own_ref.shape[1]
    for n in range(count):
        level = lax.shift_right_logical(me, 3) ^ n
        for side, ref in enumerate((own_ref, mate_ref)):
            at = pl.multiple_of((core ^ side) * rows, rows)
            part = dot(ref[level], refs[n][pl.ds(at, rows), :], ((0,), (0,)))
            if n == 0 and side == 0:
                acc[...] = part
            else:
                acc[...] += part
    part_ref[...] = acc[...].astype(jnp.bfloat16)


def sum_kernel(norm, parts_ref, grad_ref):
    half = parts_ref.shape[3]
    for side in range(2):
        total = parts_ref[0, side].astype(jnp.float32)
        for chip in range(1, parts_ref.shape[0]):
            total += parts_ref[chip, side].astype(jnp.float32)
        grad_ref[:, side * half : (side + 1) * half] = total / norm


def row_grad_kernel(first_masks, me_ref, got_ref, *refs):
    out_ref, rows_ref = refs[-2:]
    me = me_ref[0]
    chips, _, count, _ = got_ref.shape
    depth = refs[0].shape[0]
    block = 16

    @pl.when(pl.program_id(0) == 0)
    def _():
        for level in range(count // block):
            for chip in range(chips):
                at = (level * chips + chip) * block
                for side in range(2):
                    rows_ref[side, at : at + block, :] = got_ref[
                        chip, side, level * block : (level + 1) * block, :
                    ]

    own, mate = rows_ref[me & 1], rows_ref[1 - (me & 1)]
    for n, first in enumerate(first_masks):
        total = dot(own, refs[2 * n][...], ((1,), (1,)))
        total += dot(mate, refs[2 * n + 1][...], ((1,), (1,)))
        chip = (me ^ (first + 2 * pl.program_id(0))) >> 1
        out_ref[:, pl.ds(pl.multiple_of(chip * depth, depth), depth)] = total.astype(jnp.bfloat16)


def vmem(count):
    return [pl.BlockSpec(memory_space=pltpu.VMEM)] * count


SCALAR = pl.BlockSpec(memory_space=pltpu.SMEM)
PARAMS = pltpu.CompilerParams(vmem_limit_bytes=VMEM_LIMIT)


def cost(products, moved):
    return pl.CostEstimate(flops=2 * products, bytes_accessed=moved, transcendentals=0)


def per_device_paired(tokens, key_cot, routes, counts, widths, key_weight):
    rows, width_model = tokens.shape
    cols = key_cot.shape[1]
    half_cols = cols // 2
    size = lax.axis_size("dp")
    chips = size // 2
    levels = size // PLANE
    per_peer = 2 * rows // size
    receive = size * per_peer
    wide = width_model // levels
    me = lax.axis_index("dp")
    core = me % 2
    me_scalar = me.astype(jnp.int32).reshape(1)

    def mine(value):
        return lax.dynamic_slice_in_dim(value, core * half_cols, half_cols, 1)

    def theirs(value):
        return lax.dynamic_slice_in_dim(value, (1 - core) * half_cols, half_cols, 1)

    mate_shard = swap(key_weight, CORE)
    piece = jnp.where(
        core == 0,
        jnp.concatenate([key_weight[:, :half_cols], mate_shard[:, :half_cols]], axis=0),
        jnp.concatenate([mate_shard[:, half_cols:], key_weight[:, half_cols:]], axis=0),
    )
    bits = [PLANE << n for n in range(levels.bit_length() - 1)]
    column = {0: piece}
    for bit in bits:
        column[bit] = swap(piece, bit)
    by_x, by_y = swap(piece, X), swap(piece, Y)
    across = diagonal(by_x, by_y)
    planes_of = {0: (by_x, by_y, *across)}
    arrived = lax.optimization_barrier([column[bit] for bit in bits])
    column.update(zip(bits, arrived))
    waits = {bits[0]: (by_x, by_y), bits[-1]: across}
    for mask in [PLANE * n for n in range(1, levels)]:
        if mask not in column:
            low = mask & -mask
            column[mask] = swap(column[mask ^ low], low)
    order = bits + [PLANE * n for n in range(1, levels) if PLANE * n not in bits]
    for n, mask in enumerate(order):
        before = waits[mask] if mask in waits else planes_of[order[n - 2]][:2]
        own = after(column[mask], *before)
        by_x, by_y = swap(own, X), swap(own, Y)
        planes_of[mask] = (by_x, by_y, *diagonal(by_x, by_y))
    masks = sorted(column)
    parts_of = [masks[: levels // 2], masks[levels // 2 :]]
    sets = []
    for part in parts_of:
        found = Places()
        for mask in part:
            by_x, by_y, first, last = planes_of[mask]
            found.add(mask, 0, column[mask])
            found.add(mask | X, 0, by_x)
            found.add(mask | Y, 0, by_y)
            found.add(mask | X | Y, 0, first)
            found.add(mask | X | Y, first.shape[0], last)
        sets.append((found.arrays, found.places))

    mate_tokens = swap(after(tokens, *arrived), CORE)
    columns = [[p + PLANE * z for z in range(levels)] for p in range(PLANE)]
    late_tokens = after(tokens, *arrived)
    own_features = lax.all_to_all(
        jnp.stack([late_tokens[:, z * wide : (z + 1) * wide] for z in range(levels)]),
        "dp",
        split_axis=0,
        concat_axis=0,
        axis_index_groups=columns,
        tiled=True,
    )
    mate_features = swap(own_features, CORE)

    key_cot, counts = lax.optimization_barrier((key_cot, counts, *planes_of[bits[-1]][:2]))[:2]
    routes = after(routes, *planes_of[bits[0]][:2])
    bounds = jnp.cumsum(counts[0])
    positions = jnp.arange(rows, dtype=jnp.int32)
    subnet = jnp.sum((positions[:, None] >= bounds[None, : NSUB - 1]).astype(jnp.int32), axis=1)
    subnet_match = subnet[:, None] == jnp.arange(NSUB, dtype=jnp.int32)[None, :]
    row_width = jnp.sum(jnp.where(subnet_match, widths[None, :], 0), axis=1)
    head_of_col = jnp.arange(cols, dtype=jnp.int32) // HEAD_DIM
    upstream = jnp.where(
        head_of_col[None, :] < row_width[:, None], key_cot, jnp.zeros_like(key_cot)
    )
    own_cot, mate_cot = mine(upstream), swap(theirs(upstream), CORE)

    destination = routes[:, 0]
    same = (destination[:, None] == destination[None, :]) & (
        positions[:, None] < positions[None, :]
    )
    earlier = jnp.sum(same.astype(jnp.int32), axis=0)
    source = 2 * lax.shift_right_logical(me, 3) + core
    code = ((destination * 2 * levels + source) * per_peer + earlier).reshape(1, rows)
    mate_code = swap(code, CORE)
    codes = jnp.where(
        core == 0,
        jnp.concatenate([code, mate_code], axis=0),
        jnp.concatenate([mate_code, code], axis=0),
    )
    order = [0]
    for bit in reversed(bits):
        codes = jnp.concatenate([codes, swap(codes, bit)], axis=0)
        order += [mask | bit for mask in order]

    kept = jax.ShapeDtypeStruct((width_model // 2, half_cols), jnp.bfloat16)
    sums = jax.ShapeDtypeStruct((2, rows, half_cols), jnp.float32)
    arrays, places = sets[0]
    first_weight, begun = pl.pallas_call(
        functools.partial(project_kernel, places, len(arrays)),
        out_shape=(kept, sums),
        in_specs=[SCALAR] + vmem(2 + len(arrays)),
        out_specs=tuple(vmem(2)),
        compiler_params=PARAMS,
        cost_estimate=cost(2 * rows * width_model // 2 * half_cols, 6 << 20),
        name="project",
    )(me_scalar, tokens, mate_tokens, *arrays)
    arrays, places = sets[1]
    begun = after(begun, codes, own_features, mate_features)
    delta, last_weight = pl.pallas_call(
        functools.partial(delta_kernel, places, len(arrays)),
        out_shape=(jax.ShapeDtypeStruct((2 * rows, half_cols), jnp.bfloat16), kept),
        in_specs=[SCALAR] + vmem(5 + len(arrays)),
        out_specs=tuple(vmem(2)),
        scratch_shapes=[pltpu.VMEM(sums.shape, sums.dtype)],
        compiler_params=PARAMS,
        cost_estimate=cost(2 * rows * width_model // 2 * half_cols, 6 << 20),
        name="delta",
    )(me_scalar, tokens, mate_tokens, own_cot, mate_cot, begun, *arrays)

    deltas = gather_column(delta)
    selected = pl.pallas_call(
        functools.partial(select_kernel, levels),
        out_shape=jax.ShapeDtypeStruct((PLANE * 2 * levels * per_peer, half_cols), jnp.bfloat16),
        in_specs=[SCALAR] + vmem(1 + levels),
        out_specs=vmem(1)[0],
        compiler_params=PARAMS,
        cost_estimate=cost(receive * 2 * levels * 2 * rows * half_cols, 2 << 20),
        name="select",
    )(me_scalar, codes, *[deltas[mask] for mask in order])
    planes = [[z * PLANE + p for p in range(PLANE)] for z in range(levels)]

    def to_plane(value):
        return lax.all_to_all(
            value.reshape(PLANE, -1, half_cols),
            "dp",
            split_axis=0,
            concat_axis=0,
            axis_index_groups=planes,
            tiled=True,
        )

    got = to_plane(selected)

    ready = after(deltas[0], selected)
    part = pl.pallas_call(
        functools.partial(weight_grad_kernel, levels),
        out_shape=jax.ShapeDtypeStruct((wide, half_cols), jnp.bfloat16),
        in_specs=[SCALAR] + vmem(2 + levels),
        out_specs=vmem(1)[0],
        scratch_shapes=[pltpu.VMEM((wide, half_cols), jnp.float32)],
        compiler_params=PARAMS,
        cost_estimate=cost(2 * rows * levels * wide * half_cols, 4 << 20),
        name="weight_grad",
    )(
        me_scalar,
        own_features,
        mate_features,
        *[ready if mask == 0 else deltas[mask] for mask in masks],
    )
    shard = width_model // size
    parts = to_plane(part)

    depth = width_model // chips
    kept_weights = [first_weight, swap(first_weight, CORE), last_weight, swap(last_weight, CORE)]
    row_grads = pl.pallas_call(
        functools.partial(row_grad_kernel, [part[0] for part in parts_of]),
        out_shape=jax.ShapeDtypeStruct((receive, width_model), jnp.bfloat16),
        grid=(chips // 2,),
        in_specs=[
            SCALAR,
            pl.BlockSpec((PLANE // 2, 2, 2 * levels * per_peer, half_cols), lambda i: (0, 0, 0, 0)),
        ]
        + [pl.BlockSpec((depth, half_cols), lambda i: (i, 0))] * len(kept_weights),
        out_specs=pl.BlockSpec((receive, width_model), lambda i: (0, 0)),
        scratch_shapes=[pltpu.VMEM((2, receive, half_cols), jnp.bfloat16)],
        compiler_params=PARAMS,
        cost_estimate=cost(receive * width_model * cols, 12 << 20),
        name="row_grad",
    )(me_scalar, got.reshape(PLANE // 2, 2, 2 * levels * per_peer, half_cols), *kept_weights)

    parts = after(parts, row_grads)
    key_grad = pl.pallas_call(
        functools.partial(sum_kernel, math.sqrt(rows * size)),
        out_shape=jax.ShapeDtypeStruct((shard, cols), jnp.float32),
        in_specs=vmem(1),
        out_specs=vmem(1)[0],
        compiler_params=PARAMS,
        cost_estimate=cost(PLANE * shard * half_cols, 2 << 20),
        name="sum",
    )(parts.reshape(PLANE // 2, 2, shard, half_cols))
    return (row_grads, key_grad)


def solution(mesh):
    size, split = mesh.shape["dp"], mesh.shape["mp"]
    paired = split == 1 and size == 32
    return jax.shard_map(
        per_device_paired if paired else per_device_general,
        mesh=mesh,
        in_specs=(P("dp", None), P("dp", "mp"), P("dp", None), P("dp", None), P(), P("dp", "mp")),
        out_specs=(P("dp", "mp"), P("dp", "mp")),
        check_vma=False,
    )
```

```python
import functools
import math

import jax
import jax.numpy as jnp
from jax import lax
from jax.experimental import pallas as pl
from jax.experimental.pallas import tpu as pltpu
from jax.sharding import PartitionSpec as P

HEAD_DIM = 128
NSUB = 4
VMEM_LIMIT = 48 * 1024 * 1024
epsilon = 1e-06


def per_device_general(tokens, key_cot, routes, counts, widths, key_weight):
    row_count = tokens.shape[0]
    width_model = tokens.shape[1]
    local_cols = key_cot.shape[1]
    local_heads = local_cols // HEAD_DIM
    dp_size = lax.axis_size("dp")
    per_peer = 2 * row_count // dp_size
    receive = dp_size * per_peer
    destination = routes[:, 0]
    one_hot = (destination[:, None] == jnp.arange(dp_size, dtype=jnp.int32)[None, :]).astype(
        jnp.int32
    )
    earlier = jnp.sum(jnp.cumsum(one_hot, axis=0) * one_hot, axis=1) - 1
    send_slot = destination * per_peer + earlier
    bounds = jnp.cumsum(counts[0])
    positions = jnp.arange(row_count, dtype=jnp.int32)
    subnet = jnp.sum((positions[:, None] >= bounds[None, : NSUB - 1]).astype(jnp.int32), axis=1)
    send_subnet = (
        jnp.full((receive,), -1, jnp.int32).at[send_slot].set(subnet).reshape(dp_size, per_peer)
    )
    send_cot = jnp.zeros((receive, local_cols), jnp.bfloat16).at[send_slot].set(key_cot)
    send_cot = send_cot.reshape(dp_size, per_peer, local_cols)
    send_tokens = jnp.zeros((receive, width_model), jnp.bfloat16).at[send_slot].set(tokens)
    send_tokens = send_tokens.reshape(dp_size, per_peer, width_model)
    got_tokens, got_cot, got_subnet = (
        lax.all_to_all(send_tokens, "dp", split_axis=0, concat_axis=0, tiled=True),
        lax.all_to_all(send_cot, "dp", split_axis=0, concat_axis=0, tiled=True),
        lax.all_to_all(send_subnet, "dp", split_axis=0, concat_axis=0, tiled=True),
    )
    hidden = got_tokens.reshape(receive, width_model)
    got_cot = got_cot.reshape(receive, local_cols)
    got_subnet = got_subnet.reshape(receive)
    full_weight = lax.all_gather(key_weight, "dp", axis=0, tiled=True)
    key_proj = jnp.dot(hidden, full_weight, preferred_element_type=jnp.float32)
    per_head = key_proj.reshape(receive, local_heads, HEAD_DIM)
    head_scale = jnp.sqrt(jnp.mean(per_head * per_head, axis=2, keepdims=True) + epsilon)
    outputs = per_head / head_scale
    subnet_match = got_subnet[:, None] == jnp.arange(NSUB, dtype=jnp.int32)[None, :]
    row_width = jnp.sum(jnp.where(subnet_match, widths[None, :], 0), axis=1)
    head_index = lax.axis_index("mp") * local_heads + jnp.arange(local_heads, dtype=jnp.int32)
    head_mask = (head_index[None, :] < row_width[:, None]).astype(jnp.float32)
    upstream = (
        got_cot.astype(jnp.float32).reshape(receive, local_heads, HEAD_DIM) * head_mask[:, :, None]
    )
    key_delta = (
        upstream - outputs * jnp.mean(upstream * outputs, axis=2, keepdims=True)
    ) / head_scale
    delta_low = key_delta.reshape(receive, local_cols).astype(jnp.bfloat16)
    part_delta = lax.dot_general(
        delta_low, full_weight, (((1,), (1,)), ((), ())), preferred_element_type=jnp.float32
    )
    rounded = lax.optimization_barrier(part_delta.astype(jnp.bfloat16)).astype(jnp.float32)
    feature_delta = lax.psum_scatter(
        rounded.astype(jnp.bfloat16), "mp", scatter_dimension=1, tiled=True
    )
    weight_sum = lax.psum_scatter(
        lax.dot_general(
            hidden, delta_low, (((0,), (0,)), ((), ())), preferred_element_type=jnp.float32
        ),
        "dp",
        scatter_dimension=0,
        tiled=True,
    )
    key_grad = weight_sum / math.sqrt(row_count * dp_size)
    return (feature_delta, key_grad)


CORE, X, Y = 1, 2, 4
PLANE = 8


def swap(value, mask):
    size = lax.axis_size("dp")
    return lax.ppermute(value, "dp", [(i, i ^ mask) for i in range(size)])


def after(value, *others):
    return lax.optimization_barrier((value, *others))[0]


def dot(a, b, dims):
    return lax.dot_general(a, b, (dims, ((), ())), preferred_element_type=jnp.float32)


def add_products(chips_ref, begin, own_ref, mate_ref, pieces, weight_ref, acc, fresh):
    for n, piece_ref in enumerate(pieces):
        piece = piece_ref[...]
        depth = piece.shape[0]
        at = pl.multiple_of(chips_ref[begin + n] * depth, depth)
        weight_ref[n * depth : (n + 1) * depth, :] = piece
        for side, ref in enumerate((own_ref, mate_ref)):
            part = dot(ref[:, pl.ds(at, depth)], piece, ((1,), (0,)))
            if fresh and n == 0:
                acc[side] = part
            else:
                acc[side] += part


def project_kernel(count, chips_ref, own_ref, mate_ref, *refs):
    weight_ref, acc_ref = refs[count:]
    add_products(chips_ref, 0, own_ref, mate_ref, refs[:count], weight_ref, acc_ref, True)


def delta_kernel(
    count,
    begin,
    chips_ref,
    me_ref,
    own_ref,
    mate_ref,
    own_cot_ref,
    mate_cot_ref,
    begun_ref,
    *refs,
):
    delta_ref, weight_ref, acc = refs[count:]
    core = me_ref[0] & 1
    rows = own_ref.shape[0]
    acc[...] = begun_ref[...]
    add_products(chips_ref, begin, own_ref, mate_ref, refs[:count], weight_ref, acc, False)
    for side, cot_ref in enumerate((own_cot_ref, mate_cot_ref)):
        at = pl.multiple_of((core ^ side) * rows, rows)
        for head in range(own_cot_ref.shape[1] // HEAD_DIM):
            cols = slice(head * HEAD_DIM, (head + 1) * HEAD_DIM)
            proj = acc[side, :, cols]
            scale = jnp.sqrt(jnp.mean(proj * proj, axis=1, keepdims=True) + epsilon)
            normed = proj / scale
            upstream = cot_ref[:, cols].astype(jnp.float32)
            delta = (upstream - normed * jnp.mean(upstream * normed, axis=1, keepdims=True)) / scale
            delta_ref[pl.ds(at, rows), cols] = delta.astype(jnp.bfloat16)


def select_kernel(levels, me_ref, code_ref, *refs):
    deltas, sent_ref = refs[:-1], refs[-1]
    slot_count = sent_ref.shape[0]
    rows = code_ref.shape[1]
    plane = lax.shift_right_logical(me_ref[0], 3)
    per_chip = slot_count // (PLANE * len(deltas))
    iota = lax.broadcasted_iota(jnp.int32, (slot_count, rows), 0)
    destination, slot = iota // (per_chip * len(deltas)), iota % (per_chip * len(deltas))
    total = None
    for n, level in enumerate(levels):
        for side in range(2):
            want = (plane * PLANE + destination) * per_chip + slot - n * per_chip
            inside = (slot >= n * per_chip) & (slot < (n + 1) * per_chip)
            code = code_ref[2 * level + side : 2 * level + side + 1, :]
            hot = (inside & (want == code)).astype(jnp.bfloat16)
            part = dot(hot, deltas[n][side * rows : (side + 1) * rows, :], ((1,), (0,)))
            total = part if total is None else total + part
    sent_ref[...] = total.astype(jnp.bfloat16)


def weight_grad_kernel(begin, me_ref, own_ref, mate_ref, *refs):
    if begin:
        begun_ref, *deltas, part_ref, acc = refs
        acc[...] = begun_ref[...]
    else:
        *deltas, acc = refs
    core = me_ref[0] & 1
    rows = own_ref.shape[1]
    for n, delta_ref in enumerate(deltas):
        level = lax.shift_right_logical(me_ref[0], 3) ^ (begin + n)
        for side, ref in enumerate((own_ref, mate_ref)):
            at = pl.multiple_of((core ^ side) * rows, rows)
            part = dot(ref[level], delta_ref[pl.ds(at, rows), :], ((0,), (0,)))
            if begin + n + side == 0:
                acc[...] = part
            else:
                acc[...] += part
    if begin:
        part_ref[...] = acc[...].astype(jnp.bfloat16)


def sum_kernel(norm, parts_ref, grad_ref):
    half = parts_ref.shape[3]
    for side in range(2):
        total = parts_ref[0, side].astype(jnp.float32)
        for chip in range(1, parts_ref.shape[0]):
            total += parts_ref[chip, side].astype(jnp.float32)
        grad_ref[:, side * half : (side + 1) * half] = total / norm


def row_grad_kernel(me_ref, chips_ref, near_ref, far_ref, *refs):
    out_ref, rows_ref = refs[-2:]
    me = me_ref[0]
    step = pl.program_id(0)
    chips, _, count, _ = near_ref.shape
    depth = refs[0].shape[0]
    block = far_ref.shape[2]
    level = lax.shift_right_logical(me, 3)

    @pl.when(step == 0)
    def _():
        for n in range(count // block + 1):
            for chip in range(chips):
                at = pl.multiple_of(((level ^ n) * chips + chip) * block, block)
                for side in range(2):
                    if n < count // block:
                        rows = near_ref[chip, side, n * block : (n + 1) * block, :]
                    else:
                        rows = far_ref[chip, side]
                    rows_ref[side, pl.ds(at, block), :] = rows

    own, mate = rows_ref[me & 1], rows_ref[1 - (me & 1)]
    for n in range(2):
        total = dot(own, refs[2 * n][...], ((1,), (1,)))
        total += dot(mate, refs[2 * n + 1][...], ((1,), (1,)))
        at = chips_ref[n * pl.num_programs(0) + step] * depth
        out_ref[:, pl.ds(pl.multiple_of(at, depth), depth)] = total.astype(jnp.bfloat16)


def vmem(count):
    return [pl.BlockSpec(memory_space=pltpu.VMEM)] * count


SCALAR = pl.BlockSpec(memory_space=pltpu.SMEM)
PARAMS = pltpu.CompilerParams(vmem_limit_bytes=VMEM_LIMIT)


def cost(products, moved):
    return pl.CostEstimate(flops=2 * products, bytes_accessed=moved, transcendentals=0)


def per_device_paired(tokens, key_cot, routes, counts, widths, key_weight):
    rows, width_model = tokens.shape
    cols = key_cot.shape[1]
    half_cols = cols // 2
    size = lax.axis_size("dp")
    chips = size // 2
    levels = size // PLANE
    per_peer = 2 * rows // size
    receive = size * per_peer
    wide = width_model // levels
    me = lax.axis_index("dp")
    core = me % 2
    me_scalar = me.astype(jnp.int32).reshape(1)

    def mine(value):
        return lax.dynamic_slice_in_dim(value, core * half_cols, half_cols, 1)

    def theirs(value):
        return lax.dynamic_slice_in_dim(value, (1 - core) * half_cols, half_cols, 1)

    mate_shard = swap(key_weight, CORE)
    piece = jnp.where(
        core == 0,
        jnp.concatenate([key_weight[:, :half_cols], mate_shard[:, :half_cols]], axis=0),
        jnp.concatenate([mate_shard[:, half_cols:], key_weight[:, half_cols:]], axis=0),
    )
    near, far, both = PLANE, 2 * PLANE, 3 * PLANE
    z_far, z_near = swap(piece, far), swap(piece, near)
    x_own, y_own = swap(piece, X), swap(piece, Y)
    d_own = swap(y_own, X)
    z_far, z_near = lax.optimization_barrier((z_far, z_near, x_own, y_own))[:2]
    z_both = swap(z_far, near)
    x_near, y_near = swap(z_near, X), swap(z_near, Y)
    z_far = after(z_far, d_own)
    x_far, y_far = swap(z_far, X), swap(z_far, Y)
    z_both_late = after(z_both, x_near, y_near)
    x_both, y_both = swap(z_both_late, X), swap(z_both_late, Y)
    d_far = swap(x_far, Y)
    d_near = swap(after(y_near, x_both), X)
    first_pieces = {
        0: piece,
        X: x_own,
        Y: y_own,
        near: z_near,
        near | X: x_near,
        near | Y: y_near,
        far: z_far,
        far | X: x_far,
    }

    mate_tokens = swap(after(tokens, z_near), CORE)
    columns = [[p + PLANE * z for z in range(levels)] for p in range(PLANE)]
    late_tokens = after(tokens, z_both)
    own_features = lax.all_to_all(
        jnp.stack([late_tokens[:, z * wide : (z + 1) * wide] for z in range(levels)]),
        "dp",
        split_axis=0,
        concat_axis=0,
        axis_index_groups=columns,
        tiled=True,
    )
    mate_features = swap(own_features, CORE)

    key_cot, counts = lax.optimization_barrier((key_cot, counts, x_far, y_far))[:2]
    routes = after(routes, x_near, y_near)
    bounds = jnp.cumsum(counts[0])
    positions = jnp.arange(rows, dtype=jnp.int32)
    subnet = jnp.sum((positions[:, None] >= bounds[None, : NSUB - 1]).astype(jnp.int32), axis=1)
    subnet_match = subnet[:, None] == jnp.arange(NSUB, dtype=jnp.int32)[None, :]
    row_width = jnp.sum(jnp.where(subnet_match, widths[None, :], 0), axis=1)
    head_of_col = jnp.arange(cols, dtype=jnp.int32) // HEAD_DIM
    upstream = jnp.where(
        head_of_col[None, :] < row_width[:, None], key_cot, jnp.zeros_like(key_cot)
    )
    own_cot, mate_cot = mine(upstream), swap(theirs(upstream), CORE)

    destination = routes[:, 0]
    same = (destination[:, None] == destination[None, :]) & (
        positions[:, None] < positions[None, :]
    )
    earlier = jnp.sum(same.astype(jnp.int32), axis=0)
    code = ((destination * 2 + core) * per_peer + earlier).reshape(1, rows)
    mate_code = swap(code, CORE)
    codes = jnp.where(
        core == 0,
        jnp.concatenate([code, mate_code], axis=0),
        jnp.concatenate([mate_code, code], axis=0),
    )
    for bit in (near, far):
        codes = jnp.concatenate([codes, swap(codes, bit)], axis=0)

    kept = jax.ShapeDtypeStruct((width_model // 2, half_cols), jnp.bfloat16)
    sums = jax.ShapeDtypeStruct((2, rows, half_cols), jnp.float32)
    first_weight, begun = pl.pallas_call(
        functools.partial(project_kernel, len(first_pieces)),
        out_shape=(kept, sums),
        in_specs=[SCALAR] + vmem(2 + len(first_pieces)),
        out_specs=tuple(vmem(2)),
        compiler_params=PARAMS,
        cost_estimate=cost(2 * rows * width_model // 2 * half_cols, 6 << 20),
        name="project",
    )(
        jnp.stack([lax.shift_right_logical(me ^ mask, 1) for mask in first_pieces]),
        tokens,
        mate_tokens,
        *first_pieces.values(),
    )
    d_both = swap(after(x_both, begun), Y)
    last_pieces = {
        far | Y: y_far,
        X | Y: d_own,
        both: z_both,
        both | X: x_both,
        both | Y: y_both,
        near | X | Y: d_near,
        far | X | Y: d_far,
        both | X | Y: d_both,
    }
    order = jnp.stack(
        [lax.shift_right_logical(me ^ mask, 1) for mask in (*first_pieces, *last_pieces)]
    )
    begun = after(begun, codes, own_features, mate_features)
    delta, last_weight = pl.pallas_call(
        functools.partial(delta_kernel, len(last_pieces), len(first_pieces)),
        out_shape=(jax.ShapeDtypeStruct((2 * rows, half_cols), jnp.bfloat16), kept),
        in_specs=[SCALAR] * 2 + vmem(5 + len(last_pieces)),
        out_specs=tuple(vmem(2)),
        scratch_shapes=[pltpu.VMEM(sums.shape, sums.dtype)],
        compiler_params=PARAMS,
        cost_estimate=cost(2 * rows * width_model // 2 * half_cols, 6 << 20),
        name="delta",
    )(
        order,
        me_scalar,
        tokens,
        mate_tokens,
        own_cot,
        mate_cot,
        begun,
        *last_pieces.values(),
    )

    delta_far, delta_near = swap(delta, far), swap(delta, near)
    delta_both = swap(delta_far, near)
    planes = [[z * PLANE + p for p in range(PLANE)] for z in range(levels)]

    def to_plane(value):
        return lax.all_to_all(
            value.reshape(PLANE, -1, half_cols),
            "dp",
            split_axis=0,
            concat_axis=0,
            axis_index_groups=planes,
            tiled=True,
        )

    def select(codes, levels, deltas, name):
        return pl.pallas_call(
            functools.partial(select_kernel, levels),
            out_shape=jax.ShapeDtypeStruct(
                (PLANE * 2 * per_peer * len(deltas), half_cols), jnp.bfloat16
            ),
            in_specs=[SCALAR] + vmem(1 + len(deltas)),
            out_specs=vmem(1)[0],
            compiler_params=PARAMS,
            cost_estimate=cost(receive * len(deltas) * 2 * rows * half_cols, 2 << 20),
            name=name,
        )(me_scalar, codes, *deltas)

    near_deltas = [delta, delta_near, delta_far]
    selected = select(codes, (0, 1, 2), near_deltas, "select_near")
    got_near = to_plane(selected)

    ready = after(delta, selected)
    terms = jax.ShapeDtypeStruct((wide, half_cols), jnp.float32)
    begun_terms = pl.pallas_call(
        functools.partial(weight_grad_kernel, 0),
        out_shape=terms,
        in_specs=[SCALAR] + vmem(5),
        out_specs=vmem(1)[0],
        compiler_params=PARAMS,
        cost_estimate=cost(6 * rows * wide * half_cols, 4 << 20),
        name="weight_grad_near",
    )(me_scalar, own_features, mate_features, ready, delta_near, delta_far)
    delta_both = after(delta_both, begun_terms)
    part = pl.pallas_call(
        functools.partial(weight_grad_kernel, 3),
        out_shape=jax.ShapeDtypeStruct(terms.shape, jnp.bfloat16),
        in_specs=[SCALAR] + vmem(4),
        out_specs=vmem(1)[0],
        scratch_shapes=[pltpu.VMEM(terms.shape, terms.dtype)],
        compiler_params=PARAMS,
        cost_estimate=cost(2 * rows * wide * half_cols, 4 << 20),
        name="weight_grad",
    )(me_scalar, own_features, mate_features, begun_terms, delta_both)
    parts = to_plane(part)
    got_both = to_plane(select(after(codes, part), (3,), [delta_both], "select_far"))
    shard = width_model // size

    depth = width_model // chips
    kept_weights = [first_weight, swap(first_weight, CORE), last_weight, swap(last_weight, CORE)]
    row_grads = pl.pallas_call(
        row_grad_kernel,
        out_shape=jax.ShapeDtypeStruct((receive, width_model), jnp.bfloat16),
        grid=(chips // 2,),
        in_specs=[SCALAR] * 2
        + [
            pl.BlockSpec((PLANE // 2, 2, 2 * per_peer * n, half_cols), lambda i: (0, 0, 0, 0))
            for n in (levels - 1, 1)
        ]
        + [pl.BlockSpec((depth, half_cols), lambda i: (i, 0))] * len(kept_weights),
        out_specs=pl.BlockSpec((receive, width_model), lambda i: (0, 0)),
        scratch_shapes=[pltpu.VMEM((2, receive, half_cols), jnp.bfloat16)],
        compiler_params=PARAMS,
        cost_estimate=cost(receive * width_model * cols, 12 << 20),
        name="row_grad",
    )(
        me_scalar,
        order,
        got_near.reshape(PLANE // 2, 2, -1, half_cols),
        got_both.reshape(PLANE // 2, 2, -1, half_cols),
        *kept_weights,
    )

    parts = after(parts, row_grads)
    key_grad = pl.pallas_call(
        functools.partial(sum_kernel, math.sqrt(rows * size)),
        out_shape=jax.ShapeDtypeStruct((shard, cols), jnp.float32),
        in_specs=vmem(1),
        out_specs=vmem(1)[0],
        compiler_params=PARAMS,
        cost_estimate=cost(PLANE * shard * half_cols, 2 << 20),
        name="sum",
    )(parts.reshape(PLANE // 2, 2, shard, half_cols))
    return (row_grads, key_grad)


def solution(mesh):
    size, split = mesh.shape["dp"], mesh.shape["mp"]
    paired = split == 1 and size == 32
    return jax.shard_map(
        per_device_paired if paired else per_device_general,
        mesh=mesh,
        in_specs=(P("dp", None), P("dp", "mp"), P("dp", None), P("dp", None), P(), P("dp", "mp")),
        out_specs=(P("dp", "mp"), P("dp", "mp")),
        check_vma=False,
    )
```

```python
import functools
import math

import jax
import jax.numpy as jnp
from jax import lax
from jax.experimental import pallas as pl
from jax.experimental.pallas import tpu as pltpu
from jax.sharding import PartitionSpec as P

HEAD_DIM = 128
NSUB = 4
VMEM_LIMIT = 48 * 1024 * 1024
epsilon = 1e-06


def per_device_general(tokens, key_cot, routes, counts, widths, key_weight):
    row_count = tokens.shape[0]
    width_model = tokens.shape[1]
    local_cols = key_cot.shape[1]
    local_heads = local_cols // HEAD_DIM
    dp_size = lax.axis_size("dp")
    per_peer = 2 * row_count // dp_size
    receive = dp_size * per_peer
    destination = routes[:, 0]
    one_hot = (destination[:, None] == jnp.arange(dp_size, dtype=jnp.int32)[None, :]).astype(
        jnp.int32
    )
    earlier = jnp.sum(jnp.cumsum(one_hot, axis=0) * one_hot, axis=1) - 1
    send_slot = destination * per_peer + earlier
    bounds = jnp.cumsum(counts[0])
    positions = jnp.arange(row_count, dtype=jnp.int32)
    subnet = jnp.sum((positions[:, None] >= bounds[None, : NSUB - 1]).astype(jnp.int32), axis=1)
    send_subnet = (
        jnp.full((receive,), -1, jnp.int32).at[send_slot].set(subnet).reshape(dp_size, per_peer)
    )
    send_cot = jnp.zeros((receive, local_cols), jnp.bfloat16).at[send_slot].set(key_cot)
    send_cot = send_cot.reshape(dp_size, per_peer, local_cols)
    send_tokens = jnp.zeros((receive, width_model), jnp.bfloat16).at[send_slot].set(tokens)
    send_tokens = send_tokens.reshape(dp_size, per_peer, width_model)
    got_tokens, got_cot, got_subnet = (
        lax.all_to_all(send_tokens, "dp", split_axis=0, concat_axis=0, tiled=True),
        lax.all_to_all(send_cot, "dp", split_axis=0, concat_axis=0, tiled=True),
        lax.all_to_all(send_subnet, "dp", split_axis=0, concat_axis=0, tiled=True),
    )
    hidden = got_tokens.reshape(receive, width_model)
    got_cot = got_cot.reshape(receive, local_cols)
    got_subnet = got_subnet.reshape(receive)
    full_weight = lax.all_gather(key_weight, "dp", axis=0, tiled=True)
    key_proj = jnp.dot(hidden, full_weight, preferred_element_type=jnp.float32)
    per_head = key_proj.reshape(receive, local_heads, HEAD_DIM)
    head_scale = jnp.sqrt(jnp.mean(per_head * per_head, axis=2, keepdims=True) + epsilon)
    outputs = per_head / head_scale
    subnet_match = got_subnet[:, None] == jnp.arange(NSUB, dtype=jnp.int32)[None, :]
    row_width = jnp.sum(jnp.where(subnet_match, widths[None, :], 0), axis=1)
    head_index = lax.axis_index("mp") * local_heads + jnp.arange(local_heads, dtype=jnp.int32)
    head_mask = (head_index[None, :] < row_width[:, None]).astype(jnp.float32)
    upstream = (
        got_cot.astype(jnp.float32).reshape(receive, local_heads, HEAD_DIM) * head_mask[:, :, None]
    )
    key_delta = (
        upstream - outputs * jnp.mean(upstream * outputs, axis=2, keepdims=True)
    ) / head_scale
    delta_low = key_delta.reshape(receive, local_cols).astype(jnp.bfloat16)
    part_delta = lax.dot_general(
        delta_low, full_weight, (((1,), (1,)), ((), ())), preferred_element_type=jnp.float32
    )
    rounded = lax.optimization_barrier(part_delta.astype(jnp.bfloat16)).astype(jnp.float32)
    feature_delta = lax.psum_scatter(
        rounded.astype(jnp.bfloat16), "mp", scatter_dimension=1, tiled=True
    )
    weight_sum = lax.psum_scatter(
        lax.dot_general(
            hidden, delta_low, (((0,), (0,)), ((), ())), preferred_element_type=jnp.float32
        ),
        "dp",
        scatter_dimension=0,
        tiled=True,
    )
    key_grad = weight_sum / math.sqrt(row_count * dp_size)
    return (feature_delta, key_grad)


CORE, X, Y = 1, 2, 4
PLANE = 8


def swap(value, mask):
    size = lax.axis_size("dp")
    return lax.ppermute(value, "dp", [(i, i ^ mask) for i in range(size)])


def after(value, *others):
    return lax.optimization_barrier((value, *others))[0]


def dot(a, b, dims):
    return lax.dot_general(a, b, (dims, ((), ())), preferred_element_type=jnp.float32)


def fetch(pairs, sems):
    copies = [
        pltpu.make_async_copy(source, target, sems.at[n])
        for n, (source, target) in enumerate(pairs)
    ]
    for copy in copies:
        copy.start()
    return copies


def add_products(chips_ref, begin, token_refs, pieces, weight_ref, acc, held, weights, sems, fresh):
    depth = pieces[0].shape[0]

    def rows_of(ref, n):
        return ref.at[n * depth : (n + 1) * depth, :]

    pairs = [(ref, held.at[side]) for side, ref in enumerate(token_refs)]
    pairs += [(ref, rows_of(weights, n)) for n, ref in enumerate(pieces)]
    copies = fetch(pairs, sems)
    for copy in copies[:2]:
        copy.wait()
    kept = []
    for n in range(len(pieces)):
        copies[2 + n].wait()
        out = pltpu.make_async_copy(
            rows_of(weights, n), rows_of(weight_ref, n), sems.at[2 + len(pieces) + n]
        )
        out.start()
        kept.append(out)
        piece = weights[n * depth : (n + 1) * depth, :]
        at = pl.multiple_of(chips_ref[begin + n] * depth, depth)
        for side in range(2):
            part = dot(held[side, :, pl.ds(at, depth)], piece, ((1,), (0,)))
            if fresh and n == 0:
                acc[side] = part
            else:
                acc[side] += part
    return kept


def project_kernel(count, chips_ref, own_ref, mate_ref, *refs):
    pieces = refs[:count]
    weight_ref, acc_ref, held, weights, sems = refs[count:]
    kept = add_products(
        chips_ref, 0, (own_ref, mate_ref), pieces, weight_ref, acc_ref, held, weights, sems, True
    )
    for copy in kept:
        copy.wait()


def delta_kernel(
    count,
    begin,
    chips_ref,
    me_ref,
    own_ref,
    mate_ref,
    own_cot_ref,
    mate_cot_ref,
    begun_ref,
    *refs,
):
    pieces = refs[:count]
    delta_ref, weight_ref, acc, held, weights, sems = refs[count:]
    core = me_ref[0] & 1
    rows = own_ref.shape[0]
    acc[...] = begun_ref[...]
    kept = add_products(
        chips_ref, begin, (own_ref, mate_ref), pieces, weight_ref, acc, held, weights, sems, False
    )
    for side, cot_ref in enumerate((own_cot_ref, mate_cot_ref)):
        at = pl.multiple_of((core ^ side) * rows, rows)
        for head in range(own_cot_ref.shape[1] // HEAD_DIM):
            cols = slice(head * HEAD_DIM, (head + 1) * HEAD_DIM)
            proj = acc[side, :, cols]
            scale = jnp.sqrt(jnp.mean(proj * proj, axis=1, keepdims=True) + epsilon)
            normed = proj / scale
            upstream = cot_ref[:, cols].astype(jnp.float32)
            delta = (upstream - normed * jnp.mean(upstream * normed, axis=1, keepdims=True)) / scale
            delta_ref[pl.ds(at, rows), cols] = delta.astype(jnp.bfloat16)
    for copy in kept:
        copy.wait()


def selected_rows(plane, code_ref, levels, deltas, slot_count):
    rows = code_ref.shape[1]
    per_chip = slot_count // (PLANE * len(levels))
    iota = lax.broadcasted_iota(jnp.int32, (slot_count, rows), 0)
    destination, slot = iota // (per_chip * len(levels)), iota % (per_chip * len(levels))
    total = None
    for n, level in enumerate(levels):
        for side in range(2):
            want = (plane * PLANE + destination) * per_chip + slot - n * per_chip
            inside = (slot >= n * per_chip) & (slot < (n + 1) * per_chip)
            code = code_ref[2 * level + side : 2 * level + side + 1, :]
            hot = (inside & (want == code)).astype(jnp.bfloat16)
            part = dot(hot, deltas[n][side * rows : (side + 1) * rows, :], ((1,), (0,)))
            total = part if total is None else total + part
    return total.astype(jnp.bfloat16)


def select_kernel(levels, me_ref, code_ref, *refs):
    *deltas, sent_ref, held, sems = refs
    for copy in fetch([(ref, held.at[n]) for n, ref in enumerate(deltas)], sems):
        copy.wait()
    plane = lax.shift_right_logical(me_ref[0], 3)
    values = [held[n] for n in range(len(deltas))]
    sent_ref[...] = selected_rows(plane, code_ref, levels, values, sent_ref.shape[0])


def weight_grad_kernel(me_ref, code_ref, own_ref, mate_ref, *refs):
    *deltas, part_ref, hidden, held, acc, sems = refs
    plane = lax.shift_right_logical(me_ref[0], 3)
    core = me_ref[0] & 1
    rows = own_ref.shape[1]
    count = len(deltas)
    pairs = []
    for n, ref in enumerate(deltas):
        pairs += [
            (own_ref.at[plane ^ n], hidden.at[n, 0]),
            (mate_ref.at[plane ^ n], hidden.at[n, 1]),
            (ref, held.at[n]),
        ]
    copies = fetch(pairs, sems)
    for n in range(count):
        for copy in copies[3 * n : 3 * n + 3]:
            copy.wait()
        for side in range(2):
            at = pl.multiple_of((core ^ side) * rows, rows)
            part = dot(hidden[n, side], held[n, pl.ds(at, rows), :], ((0,), (0,)))
            if n + side == 0:
                acc[...] = part
            else:
                acc[...] += part
    blocks, depth, _ = part_ref.shape
    shard = acc.shape[0] // blocks
    extra = depth - shard
    far = selected_rows(plane, code_ref, (count - 1,), [held[count - 1]], blocks * extra)
    for block in range(blocks):
        part_ref[block, :shard, :] = acc[block * shard : (block + 1) * shard, :].astype(
            jnp.bfloat16
        )
        part_ref[block, shard:, :] = far[block * extra : (block + 1) * extra, :]


def sum_kernel(norm, parts_ref, grad_ref):
    shard, cols = grad_ref.shape
    half = cols // 2
    for side in range(2):
        total = parts_ref[0, side, :shard, :].astype(jnp.float32)
        for chip in range(1, parts_ref.shape[0]):
            total += parts_ref[chip, side, :shard, :].astype(jnp.float32)
        grad_ref[:, side * half : (side + 1) * half] = total / norm


def add_columns(core, step, chips_ref, rows_ref, weights, out_ref):
    own, mate = rows_ref[core], rows_ref[1 - core]
    depth = weights[0].shape[0]
    for n in range(2):
        total = dot(own, weights[2 * n][...], ((1,), (1,)))
        total += dot(mate, weights[2 * n + 1][...], ((1,), (1,)))
        at = chips_ref[n * pl.num_programs(0) + step] * depth
        out_ref[:, pl.ds(pl.multiple_of(at, depth), depth)] = total.astype(jnp.bfloat16)


def row_grad_kernel(chips_ref, me_ref, got_ref, *refs):
    *weights, out_ref, rows_ref = refs
    step = pl.program_id(0)
    chips, _, count, _ = got_ref.shape
    block = rows_ref.shape[1] // (chips * 4)
    level = lax.shift_right_logical(me_ref[0], 3)

    @pl.when(step == 0)
    def _():
        for n in range(4):
            for chip in range(chips):
                at = pl.multiple_of(((level ^ n) * chips + chip) * block, block)
                for side in range(2):
                    if n < count // block:
                        rows = got_ref[chip, side, n * block : (n + 1) * block, :]
                    else:
                        rows = jnp.zeros((block, got_ref.shape[3]), jnp.bfloat16)
                    rows_ref[side, pl.ds(at, block), :] = rows

    add_columns(me_ref[0] & 1, step, chips_ref, rows_ref, weights, out_ref)


def far_row_grad_kernel(chips_ref, me_ref, before_ref, got_ref, *refs):
    *weights, out_ref, rows_ref = refs
    step = pl.program_id(0)
    chips, _, count, _ = got_ref.shape
    block = rows_ref.shape[1] // chips

    @pl.when(step == 0)
    def _():
        for chip in range(chips):
            for side in range(2):
                rows_ref[side, chip * block : (chip + 1) * block, :] = got_ref[
                    chip, side, count - block :, :
                ]

    add_columns(me_ref[0] & 1, step, chips_ref, rows_ref, weights, out_ref)


def column_codes(destination, core, per_peer):
    positions = jnp.arange(destination.shape[0], dtype=jnp.int32)
    same = (destination[:, None] == destination[None, :]) & (
        positions[:, None] < positions[None, :]
    )
    earlier = jnp.sum(same.astype(jnp.int32), axis=0)
    code = ((destination * 2 + core) * per_peer + earlier).reshape(1, -1)
    mate_code = swap(code, CORE)
    codes = jnp.where(
        core == 0,
        jnp.concatenate([code, mate_code], axis=0),
        jnp.concatenate([mate_code, code], axis=0),
    )
    for bit in (PLANE, 2 * PLANE):
        codes = jnp.concatenate([codes, swap(codes, bit)], axis=0)
    return codes


def vmem(count):
    return [pl.BlockSpec(memory_space=pltpu.VMEM)] * count


def anywhere(count):
    return [pl.BlockSpec(memory_space=pl.ANY)] * count


SCALAR = pl.BlockSpec(memory_space=pltpu.SMEM)
PARAMS = pltpu.CompilerParams(vmem_limit_bytes=VMEM_LIMIT)


COST = pl.CostEstimate(flops=1024, bytes_accessed=1024, transcendentals=0)


def per_device_paired(tokens, key_cot, routes, counts, widths, key_weight):
    rows, width_model = tokens.shape
    cols = key_cot.shape[1]
    half_cols = cols // 2
    size = lax.axis_size("dp")
    chips = size // 2
    levels = size // PLANE
    per_peer = 2 * rows // size
    receive = size * per_peer
    wide = width_model // levels
    me = lax.axis_index("dp")
    core = me % 2
    me_scalar = me.astype(jnp.int32).reshape(1)

    def mine(value):
        return lax.dynamic_slice_in_dim(value, core * half_cols, half_cols, 1)

    def theirs(value):
        return lax.dynamic_slice_in_dim(value, (1 - core) * half_cols, half_cols, 1)

    mate_shard = swap(key_weight, CORE)
    piece = jnp.where(
        core == 0,
        jnp.concatenate([key_weight[:, :half_cols], mate_shard[:, :half_cols]], axis=0),
        jnp.concatenate([mate_shard[:, half_cols:], key_weight[:, half_cols:]], axis=0),
    )
    near, far, both = PLANE, 2 * PLANE, 3 * PLANE
    z_far, z_near = swap(piece, far), swap(piece, near)
    x_own, y_own = swap(piece, X), swap(piece, Y)
    z_far, z_near, y_own, *_ = lax.optimization_barrier((z_far, z_near, y_own, x_own))
    z_both = swap(z_far, near)
    x_near, y_near = swap(z_near, X), swap(z_near, Y)
    x_far, y_far = swap(z_far, X), swap(z_far, Y)
    codes = column_codes(routes[:, 0], core, per_peer)
    z_both_late = after(z_both, x_near, y_near, codes)
    x_both, y_both = swap(z_both_late, X), swap(z_both_late, Y)
    d_far = swap(after(x_far, y_far), Y)
    d_own = swap(after(y_own, x_far), X)
    d_near = swap(after(y_near, x_both, d_own), X)
    first_pieces = {
        0: piece,
        X: x_own,
        Y: y_own,
        near: z_near,
        near | X: x_near,
        near | Y: y_near,
        far: z_far,
        far | X: x_far,
    }

    mate_tokens = swap(after(tokens, z_near), CORE)
    columns = [[p + PLANE * z for z in range(levels)] for p in range(PLANE)]
    late_tokens = after(tokens, z_both, x_near, y_near)
    own_features = lax.all_to_all(
        jnp.stack([late_tokens[:, z * wide : (z + 1) * wide] for z in range(levels)]),
        "dp",
        split_axis=0,
        concat_axis=0,
        axis_index_groups=columns,
        tiled=True,
    )
    mate_features = swap(own_features, CORE)

    key_cot, counts = lax.optimization_barrier((key_cot, counts, x_far, y_far))[:2]
    bounds = jnp.cumsum(counts[0])
    positions = jnp.arange(rows, dtype=jnp.int32)
    subnet = jnp.sum((positions[:, None] >= bounds[None, : NSUB - 1]).astype(jnp.int32), axis=1)
    subnet_match = subnet[:, None] == jnp.arange(NSUB, dtype=jnp.int32)[None, :]
    row_width = jnp.sum(jnp.where(subnet_match, widths[None, :], 0), axis=1)
    head_of_col = jnp.arange(cols, dtype=jnp.int32) // HEAD_DIM
    upstream = jnp.where(
        head_of_col[None, :] < row_width[:, None], key_cot, jnp.zeros_like(key_cot)
    )
    own_cot, mate_cot = mine(upstream), swap(theirs(upstream), CORE)

    kept = jax.ShapeDtypeStruct((width_model // 2, half_cols), jnp.bfloat16)
    sums = jax.ShapeDtypeStruct((2, rows, half_cols), jnp.float32)
    room = [
        pltpu.VMEM((2, rows, width_model), jnp.bfloat16),
        pltpu.VMEM((width_model // 2, half_cols), jnp.bfloat16),
        pltpu.SemaphoreType.DMA((2 + chips,)),
    ]
    first_weight, begun = pl.pallas_call(
        functools.partial(project_kernel, len(first_pieces)),
        out_shape=(kept, sums),
        in_specs=[SCALAR] + anywhere(2 + len(first_pieces)),
        out_specs=(anywhere(1)[0], vmem(1)[0]),
        scratch_shapes=room,
        compiler_params=PARAMS,
        cost_estimate=COST,
        name="project",
    )(
        jnp.stack([lax.shift_right_logical(me ^ mask, 1) for mask in first_pieces]),
        tokens,
        mate_tokens,
        *first_pieces.values(),
    )
    d_both = swap(after(x_both, begun, d_far, y_both), Y)
    last_pieces = {
        far | Y: y_far,
        X | Y: d_own,
        both: z_both,
        both | X: x_both,
        both | Y: y_both,
        far | X | Y: d_far,
        near | X | Y: d_near,
        both | X | Y: d_both,
    }
    order = jnp.stack(
        [lax.shift_right_logical(me ^ mask, 1) for mask in (*first_pieces, *last_pieces)]
    )
    begun = after(begun, own_features)
    delta, last_weight = pl.pallas_call(
        functools.partial(delta_kernel, len(last_pieces), len(first_pieces)),
        out_shape=(jax.ShapeDtypeStruct((2 * rows, half_cols), jnp.bfloat16), kept),
        in_specs=[SCALAR] * 2 + anywhere(2) + vmem(3) + anywhere(len(last_pieces)),
        out_specs=(vmem(1)[0], anywhere(1)[0]),
        scratch_shapes=[pltpu.VMEM(sums.shape, sums.dtype)] + room,
        compiler_params=PARAMS,
        cost_estimate=COST,
        name="delta",
    )(
        order,
        me_scalar,
        tokens,
        mate_tokens,
        own_cot,
        mate_cot,
        begun,
        *last_pieces.values(),
    )

    delta_far, delta_near = swap(delta, far), swap(delta, near)
    delta_both = swap(delta_far, near)
    planes = [[z * PLANE + p for p in range(PLANE)] for z in range(levels)]

    def to_plane(value):
        got = lax.all_to_all(
            value, "dp", split_axis=0, concat_axis=0, axis_index_groups=planes, tiled=True
        )
        return got.reshape(PLANE // 2, 2, *value.shape[1:])

    per_chip = 2 * per_peer
    near_deltas = [delta, delta_near, delta_far]
    piece_room = (2 * rows, half_cols)
    selected = pl.pallas_call(
        functools.partial(select_kernel, (0, 1, 2)),
        out_shape=jax.ShapeDtypeStruct((PLANE * 3 * per_chip, half_cols), jnp.bfloat16),
        in_specs=[SCALAR] + vmem(1) + anywhere(3),
        out_specs=vmem(1)[0],
        scratch_shapes=[
            pltpu.VMEM((3, *piece_room), jnp.bfloat16),
            pltpu.SemaphoreType.DMA((3,)),
        ],
        compiler_params=PARAMS,
        cost_estimate=COST,
        name="select",
    )(me_scalar, codes, *near_deltas)
    got_near = to_plane(selected.reshape(PLANE, 3 * per_chip, half_cols))

    shard = width_model // size
    terms = pl.pallas_call(
        weight_grad_kernel,
        out_shape=jax.ShapeDtypeStruct((PLANE, shard + per_chip, half_cols), jnp.bfloat16),
        in_specs=[SCALAR] + vmem(1) + anywhere(2 + levels),
        out_specs=vmem(1)[0],
        scratch_shapes=[
            pltpu.VMEM((levels, 2, rows, wide), jnp.bfloat16),
            pltpu.VMEM((levels, *piece_room), jnp.bfloat16),
            pltpu.VMEM((wide, half_cols), jnp.float32),
            pltpu.SemaphoreType.DMA((3 * levels,)),
        ],
        compiler_params=PARAMS,
        cost_estimate=COST,
        name="weight_grad",
    )(me_scalar, codes, own_features, mate_features, *near_deltas, delta_both)
    got = to_plane(terms)

    depth = width_model // chips
    kept_weights = [first_weight, swap(first_weight, CORE), last_weight, swap(last_weight, CORE)]
    weight_specs = [pl.BlockSpec((depth, half_cols), lambda i, *_: (i, 0))] * len(kept_weights)
    row_shape = jax.ShapeDtypeStruct((receive, width_model), jnp.bfloat16)
    row_grads = pl.pallas_call(
        row_grad_kernel,
        out_shape=row_shape,
        grid_spec=pltpu.PrefetchScalarGridSpec(
            num_scalar_prefetch=2,
            grid=(chips // 2,),
            in_specs=[pl.BlockSpec(got_near.shape, lambda i, *_: (0, 0, 0, 0))] + weight_specs,
            out_specs=pl.BlockSpec((receive, width_model), lambda i, *_: (0, 0)),
            scratch_shapes=[pltpu.VMEM((2, receive, half_cols), jnp.bfloat16)],
        ),
        compiler_params=PARAMS,
        cost_estimate=COST,
        name="row_grad",
    )(order, me_scalar, got_near, *kept_weights)
    count = receive // levels
    row_grads = pl.pallas_call(
        far_row_grad_kernel,
        out_shape=row_shape,
        grid_spec=pltpu.PrefetchScalarGridSpec(
            num_scalar_prefetch=2,
            grid=(chips // 2,),
            in_specs=anywhere(1)
            + [pl.BlockSpec(got.shape, lambda i, *_: (0, 0, 0, 0))]
            + weight_specs,
            out_specs=pl.BlockSpec(
                (count, width_model),
                lambda i, order, me: (lax.shift_right_logical(me[0], 3) ^ (levels - 1), 0),
            ),
            scratch_shapes=[pltpu.VMEM((2, count, half_cols), jnp.bfloat16)],
        ),
        input_output_aliases={2: 0},
        compiler_params=PARAMS,
        cost_estimate=COST,
        name="far_row_grad",
    )(order, me_scalar, row_grads, got, *kept_weights)

    key_grad = pl.pallas_call(
        functools.partial(sum_kernel, math.sqrt(rows * size)),
        out_shape=jax.ShapeDtypeStruct((shard, cols), jnp.float32),
        in_specs=vmem(1),
        out_specs=vmem(1)[0],
        compiler_params=PARAMS,
        cost_estimate=COST,
        name="sum",
    )(got)
    return (row_grads, key_grad)


def solution(mesh):
    size, split = mesh.shape["dp"], mesh.shape["mp"]
    paired = split == 1 and size == 32
    return jax.shard_map(
        per_device_paired if paired else per_device_general,
        mesh=mesh,
        in_specs=(P("dp", None), P("dp", "mp"), P("dp", None), P("dp", None), P(), P("dp", "mp")),
        out_specs=(P("dp", "mp"), P("dp", "mp")),
        check_vma=False,
    )
```

```python
import functools
import math

import jax
import jax.numpy as jnp
from jax import lax
from jax.experimental import pallas as pl
from jax.experimental.pallas import tpu as pltpu
from jax.sharding import PartitionSpec as P

HEAD_DIM = 128
NSUB = 4
VMEM_LIMIT = 20 * 1024 * 1024
CODE_ROWS = 16
epsilon = 1e-06


def per_device_general(tokens, key_cot, routes, counts, widths, key_weight):
    row_count = tokens.shape[0]
    width_model = tokens.shape[1]
    local_cols = key_cot.shape[1]
    local_heads = local_cols // HEAD_DIM
    dp_size = lax.axis_size("dp")
    per_peer = 2 * row_count // dp_size
    receive = dp_size * per_peer
    destination = routes[:, 0]
    one_hot = (destination[:, None] == jnp.arange(dp_size, dtype=jnp.int32)[None, :]).astype(
        jnp.int32
    )
    earlier = jnp.sum(jnp.cumsum(one_hot, axis=0) * one_hot, axis=1) - 1
    send_slot = destination * per_peer + earlier
    bounds = jnp.cumsum(counts[0])
    positions = jnp.arange(row_count, dtype=jnp.int32)
    subnet = jnp.sum((positions[:, None] >= bounds[None, : NSUB - 1]).astype(jnp.int32), axis=1)
    send_subnet = (
        jnp.full((receive,), -1, jnp.int32).at[send_slot].set(subnet).reshape(dp_size, per_peer)
    )
    send_cot = jnp.zeros((receive, local_cols), jnp.bfloat16).at[send_slot].set(key_cot)
    send_cot = send_cot.reshape(dp_size, per_peer, local_cols)
    send_tokens = jnp.zeros((receive, width_model), jnp.bfloat16).at[send_slot].set(tokens)
    send_tokens = send_tokens.reshape(dp_size, per_peer, width_model)
    got_tokens, got_cot, got_subnet = (
        lax.all_to_all(send_tokens, "dp", split_axis=0, concat_axis=0, tiled=True),
        lax.all_to_all(send_cot, "dp", split_axis=0, concat_axis=0, tiled=True),
        lax.all_to_all(send_subnet, "dp", split_axis=0, concat_axis=0, tiled=True),
    )
    hidden = got_tokens.reshape(receive, width_model)
    got_cot = got_cot.reshape(receive, local_cols)
    got_subnet = got_subnet.reshape(receive)
    full_weight = lax.all_gather(key_weight, "dp", axis=0, tiled=True)
    key_proj = jnp.dot(hidden, full_weight, preferred_element_type=jnp.float32)
    per_head = key_proj.reshape(receive, local_heads, HEAD_DIM)
    head_scale = jnp.sqrt(jnp.mean(per_head * per_head, axis=2, keepdims=True) + epsilon)
    outputs = per_head / head_scale
    subnet_match = got_subnet[:, None] == jnp.arange(NSUB, dtype=jnp.int32)[None, :]
    row_width = jnp.sum(jnp.where(subnet_match, widths[None, :], 0), axis=1)
    head_index = lax.axis_index("mp") * local_heads + jnp.arange(local_heads, dtype=jnp.int32)
    head_mask = (head_index[None, :] < row_width[:, None]).astype(jnp.float32)
    upstream = (
        got_cot.astype(jnp.float32).reshape(receive, local_heads, HEAD_DIM) * head_mask[:, :, None]
    )
    key_delta = (
        upstream - outputs * jnp.mean(upstream * outputs, axis=2, keepdims=True)
    ) / head_scale
    delta_low = key_delta.reshape(receive, local_cols).astype(jnp.bfloat16)
    part_delta = lax.dot_general(
        delta_low, full_weight, (((1,), (1,)), ((), ())), preferred_element_type=jnp.float32
    )
    rounded = lax.optimization_barrier(part_delta.astype(jnp.bfloat16)).astype(jnp.float32)
    feature_delta = lax.psum_scatter(
        rounded.astype(jnp.bfloat16), "mp", scatter_dimension=1, tiled=True
    )
    weight_sum = lax.psum_scatter(
        lax.dot_general(
            hidden, delta_low, (((0,), (0,)), ((), ())), preferred_element_type=jnp.float32
        ),
        "dp",
        scatter_dimension=0,
        tiled=True,
    )
    key_grad = weight_sum / math.sqrt(row_count * dp_size)
    return (feature_delta, key_grad)


CORE, X, Y = 1, 2, 4
PLANE = 8


def swap(value, mask):
    size = lax.axis_size("dp")
    return lax.ppermute(value, "dp", [(i, i ^ mask) for i in range(size)])


def after(value, *others):
    return lax.optimization_barrier((value, *others))[0]


def dot(a, b, dims):
    return lax.dot_general(a, b, (dims, ((), ())), preferred_element_type=jnp.float32)


def add_products(places, chips_ref, begin, token_refs, pieces, weight_ref, acc, fresh):
    chip_rows = max(piece.shape[0] for piece in pieces)
    for (chip, first), piece_ref in zip(places, pieces):
        piece = piece_ref[...]
        depth = piece.shape[0]
        weight_ref[chip * chip_rows + first : chip * chip_rows + first + depth, :] = piece
        at = pl.multiple_of(chips_ref[begin + chip] * chip_rows + first, 128)
        for side, ref in enumerate(token_refs):
            part = dot(ref[:, pl.ds(at, depth)], piece, ((1,), (0,)))
            if fresh:
                acc[side] = part
            else:
                acc[side] += part
        fresh = False


def project_kernel(places, chips_ref, own_ref, mate_ref, *refs):
    *pieces, weight_ref, acc_ref = refs
    add_products(places, chips_ref, 0, (own_ref, mate_ref), pieces, weight_ref, acc_ref, True)


def delta_kernel(
    places,
    begin,
    chips_ref,
    me_ref,
    own_ref,
    mate_ref,
    own_cot_ref,
    mate_cot_ref,
    begun_ref,
    *refs,
):
    *pieces, delta_ref, weight_ref, acc = refs
    core = me_ref[0] & 1
    rows = own_ref.shape[0]
    acc[...] = begun_ref[...]
    add_products(places, chips_ref, begin, (own_ref, mate_ref), pieces, weight_ref, acc, False)
    delta_ref[2 * rows :, :] = jnp.zeros_like(delta_ref[2 * rows :, :])
    for side, cot_ref in enumerate((own_cot_ref, mate_cot_ref)):
        at = pl.multiple_of((core ^ side) * rows, rows)
        for head in range(own_cot_ref.shape[1] // HEAD_DIM):
            cols = slice(head * HEAD_DIM, (head + 1) * HEAD_DIM)
            proj = acc[side, :, cols]
            scale = jnp.sqrt(jnp.mean(proj * proj, axis=1, keepdims=True) + epsilon)
            normed = proj / scale
            upstream = cot_ref[:rows, cols].astype(jnp.float32)
            delta = (upstream - normed * jnp.mean(upstream * normed, axis=1, keepdims=True)) / scale
            delta_ref[pl.ds(at, rows), cols] = delta.astype(jnp.bfloat16)
        delta_ref[2 * rows :, pl.ds(at, rows)] = cot_ref[rows:, :rows]


def selected_rows(plane, deltas, slot_count):
    rows = (deltas[0].shape[0] - CODE_ROWS) // 2
    per_chip = slot_count // (PLANE * len(deltas))
    iota = lax.broadcasted_iota(jnp.int32, (slot_count, 2 * rows), 0)
    destination, slot = iota // (per_chip * len(deltas)), iota % (per_chip * len(deltas))
    destination = destination + plane * PLANE
    total = None
    for n, delta in enumerate(deltas):
        code = delta[2 * rows :, : 2 * rows].astype(jnp.float32).astype(jnp.int32)
        hot = (destination == code[0:1, :]) & (slot == code[1:2, :] + n * per_chip)
        part = dot(hot.astype(jnp.bfloat16), delta[: 2 * rows, :], ((1,), (0,)))
        total = part if total is None else total + part
    return total.astype(jnp.bfloat16)


def select_kernel(me_ref, *refs):
    *deltas, sent_ref = refs
    plane = lax.shift_right_logical(me_ref[0], 3)
    values = [ref[...] for ref in deltas]
    sent_ref[...] = selected_rows(plane, values, sent_ref.shape[0])


def weight_grad_kernel(me_ref, own_ref, mate_ref, *refs):
    *deltas, part_ref, acc = refs
    plane = lax.shift_right_logical(me_ref[0], 3)
    core = me_ref[0] & 1
    rows = own_ref.shape[1]
    for n, delta_ref in enumerate(deltas):
        for side, ref in enumerate((own_ref, mate_ref)):
            at = pl.multiple_of((core ^ side) * rows, rows)
            part = dot(ref[plane ^ n], delta_ref[pl.ds(at, rows), :], ((0,), (0,)))
            if n + side == 0:
                acc[...] = part
            else:
                acc[...] += part
    blocks, depth, _ = part_ref.shape
    shard = acc.shape[0] // blocks
    extra = depth - shard
    far = selected_rows(plane, [deltas[-1][...]], blocks * extra)
    for block in range(blocks):
        part_ref[block, :shard, :] = acc[block * shard : (block + 1) * shard, :].astype(
            jnp.bfloat16
        )
        part_ref[block, shard:, :] = far[block * extra : (block + 1) * extra, :]


def sum_kernel(norm, parts_ref, grad_ref):
    shard, cols = grad_ref.shape
    half = cols // 2
    for side in range(2):
        total = parts_ref[0, side, :shard, :].astype(jnp.float32)
        for chip in range(1, parts_ref.shape[0]):
            total += parts_ref[chip, side, :shard, :].astype(jnp.float32)
        grad_ref[:, side * half : (side + 1) * half] = total / norm


def add_columns(core, step, chips_ref, rows_ref, weights, out_ref):
    own, mate = rows_ref[core], rows_ref[1 - core]
    depth = weights[0].shape[0]
    for n in range(2):
        total = dot(own, weights[2 * n][...], ((1,), (1,)))
        total += dot(mate, weights[2 * n + 1][...], ((1,), (1,)))
        at = chips_ref[n * pl.num_programs(0) + step] * depth
        out_ref[:, pl.ds(pl.multiple_of(at, depth), depth)] = total.astype(jnp.bfloat16)


def row_grad_kernel(chips_ref, me_ref, got_ref, *refs):
    *weights, out_ref, rows_ref = refs
    step = pl.program_id(0)
    chips, _, count, _ = got_ref.shape
    block = rows_ref.shape[1] // (chips * 4)
    level = lax.shift_right_logical(me_ref[0], 3)

    @pl.when(step == 0)
    def _():
        for n in range(4):
            for chip in range(chips):
                at = pl.multiple_of(((level ^ n) * chips + chip) * block, block)
                for side in range(2):
                    if n < count // block:
                        rows = got_ref[chip, side, n * block : (n + 1) * block, :]
                    else:
                        rows = jnp.zeros((block, got_ref.shape[3]), jnp.bfloat16)
                    rows_ref[side, pl.ds(at, block), :] = rows

    add_columns(me_ref[0] & 1, step, chips_ref, rows_ref, weights, out_ref)


def far_row_grad_kernel(chips_ref, me_ref, before_ref, got_ref, *refs):
    *weights, out_ref, rows_ref = refs
    step = pl.program_id(0)
    chips, _, count, _ = got_ref.shape
    block = rows_ref.shape[1] // chips

    @pl.when(step == 0)
    def _():
        for chip in range(chips):
            for side in range(2):
                rows_ref[side, chip * block : (chip + 1) * block, :] = got_ref[
                    chip, side, count - block :, :
                ]

    add_columns(me_ref[0] & 1, step, chips_ref, rows_ref, weights, out_ref)


def code_rows(destination, core, per_peer, width):
    positions = jnp.arange(destination.shape[0], dtype=jnp.int32)
    same = (destination[:, None] == destination[None, :]) & (
        positions[:, None] < positions[None, :]
    )
    earlier = jnp.sum(same.astype(jnp.int32), axis=0)
    codes = jnp.stack([destination, core * per_peer + earlier]).astype(jnp.bfloat16)
    return jnp.pad(codes, ((0, CODE_ROWS - 2), (0, width - destination.shape[0])))


def vmem(count):
    return [pl.BlockSpec(memory_space=pltpu.VMEM)] * count


def anywhere(count):
    return [pl.BlockSpec(memory_space=pl.ANY)] * count


SCALAR = pl.BlockSpec(memory_space=pltpu.SMEM)
PARAMS = pltpu.CompilerParams(vmem_limit_bytes=VMEM_LIMIT)


COST = pl.CostEstimate(flops=1024, bytes_accessed=1024, transcendentals=0)


def per_device_paired(tokens, key_cot, routes, counts, widths, key_weight):
    rows, width_model = tokens.shape
    cols = key_cot.shape[1]
    half_cols = cols // 2
    size = lax.axis_size("dp")
    chips = size // 2
    levels = size // PLANE
    per_peer = 2 * rows // size
    receive = size * per_peer
    wide = width_model // levels
    me = lax.axis_index("dp")
    core = me % 2
    me_scalar = me.astype(jnp.int32).reshape(1)

    def mine(value):
        return lax.dynamic_slice_in_dim(value, core * half_cols, half_cols, 1)

    def theirs(value):
        return lax.dynamic_slice_in_dim(value, (1 - core) * half_cols, half_cols, 1)

    mate_shard = swap(key_weight, CORE)
    piece = jnp.where(
        core == 0,
        jnp.concatenate([key_weight[:, :half_cols], mate_shard[:, :half_cols]], axis=0),
        jnp.concatenate([mate_shard[:, half_cols:], key_weight[:, half_cols:]], axis=0),
    )
    near, far, both = PLANE, 2 * PLANE, 3 * PLANE
    column = {0: piece, far: swap(piece, far), near: swap(piece, near)}
    column[both] = swap(column[far], near)
    half = piece.shape[0] // 2
    sets, masks = [], []
    for part in ((0, near), (far, both)):
        pieces, places = [], []
        for mask in part:
            own = column[mask]
            by_x, by_y = swap(own, X), swap(own, Y)
            chip = len(masks) % (chips // 2)
            masks += [mask, mask | X, mask | Y, mask | X | Y]
            pieces += [own, by_x, by_y, swap(by_y[:half], X), swap(by_x[half:], Y)]
            places += [(chip, 0), (chip + 1, 0), (chip + 2, 0), (chip + 3, 0), (chip + 3, half)]
        sets.append((pieces, places))
    order = jnp.stack([lax.shift_right_logical(me ^ mask, 1) for mask in masks])

    mate_tokens = swap(after(tokens, column[near]), CORE)
    columns = [[p + PLANE * z for z in range(levels)] for p in range(PLANE)]
    own_features = lax.all_to_all(
        jnp.stack([tokens[:, z * wide : (z + 1) * wide] for z in range(levels)]),
        "dp",
        split_axis=0,
        concat_axis=0,
        axis_index_groups=columns,
        tiled=True,
    )
    mate_features = swap(own_features, CORE)

    key_cot, counts, routes = lax.optimization_barrier((key_cot, counts, routes, column[near]))[:3]
    bounds = jnp.cumsum(counts[0])
    positions = jnp.arange(rows, dtype=jnp.int32)
    subnet = jnp.sum((positions[:, None] >= bounds[None, : NSUB - 1]).astype(jnp.int32), axis=1)
    subnet_match = subnet[:, None] == jnp.arange(NSUB, dtype=jnp.int32)[None, :]
    row_width = jnp.sum(jnp.where(subnet_match, widths[None, :], 0), axis=1)
    head_of_col = jnp.arange(cols, dtype=jnp.int32) // HEAD_DIM
    upstream = jnp.where(
        head_of_col[None, :] < row_width[:, None], key_cot, jnp.zeros_like(key_cot)
    )
    codes = code_rows(routes[:, 0], core, per_peer, half_cols)
    own_cot = jnp.concatenate([mine(upstream), codes], axis=0)
    mate_cot = swap(jnp.concatenate([theirs(upstream), codes], axis=0), CORE)

    kept = jax.ShapeDtypeStruct((width_model // 2, half_cols), jnp.bfloat16)
    sums = jax.ShapeDtypeStruct((2, rows, half_cols), jnp.float32)
    (pieces, places), (last_pieces, last_places) = sets
    first_weight, begun = pl.pallas_call(
        functools.partial(project_kernel, places),
        out_shape=(kept, sums),
        in_specs=[SCALAR] + vmem(2 + len(pieces)),
        out_specs=tuple(vmem(2)),
        compiler_params=PARAMS,
        cost_estimate=COST,
        name="project",
    )(order, tokens, mate_tokens, *pieces)
    delta, last_weight = pl.pallas_call(
        functools.partial(delta_kernel, last_places, chips // 2),
        out_shape=(jax.ShapeDtypeStruct((2 * rows + CODE_ROWS, half_cols), jnp.bfloat16), kept),
        in_specs=[SCALAR] * 2 + vmem(5 + len(last_pieces)),
        out_specs=tuple(vmem(2)),
        scratch_shapes=[pltpu.VMEM(sums.shape, sums.dtype)],
        compiler_params=PARAMS,
        cost_estimate=COST,
        name="delta",
    )(order, me_scalar, tokens, mate_tokens, own_cot, mate_cot, begun, *last_pieces)

    delta_far, delta_near = swap(delta, far), swap(delta, near)
    delta_both = swap(delta_far, near)
    planes = [[z * PLANE + p for p in range(PLANE)] for z in range(levels)]

    def to_plane(value):
        got = lax.all_to_all(
            value, "dp", split_axis=0, concat_axis=0, axis_index_groups=planes, tiled=True
        )
        return got.reshape(PLANE // 2, 2, *value.shape[1:])

    per_chip = 2 * per_peer
    near_deltas = [delta, delta_near, delta_far]
    selected = pl.pallas_call(
        select_kernel,
        out_shape=jax.ShapeDtypeStruct((PLANE * 3 * per_chip, half_cols), jnp.bfloat16),
        in_specs=[SCALAR] + vmem(3),
        out_specs=vmem(1)[0],
        compiler_params=PARAMS,
        cost_estimate=COST,
        name="select",
    )(me_scalar, *near_deltas)
    got_near = to_plane(selected.reshape(PLANE, 3 * per_chip, half_cols))

    shard = width_model // size
    terms = pl.pallas_call(
        weight_grad_kernel,
        out_shape=jax.ShapeDtypeStruct((PLANE, shard + per_chip, half_cols), jnp.bfloat16),
        in_specs=[SCALAR] + vmem(2 + levels),
        out_specs=vmem(1)[0],
        scratch_shapes=[pltpu.VMEM((wide, half_cols), jnp.float32)],
        compiler_params=PARAMS,
        cost_estimate=COST,
        name="weight_grad",
    )(me_scalar, own_features, mate_features, *near_deltas, delta_both)
    got = to_plane(terms)

    depth = width_model // chips
    kept_weights = [first_weight, swap(first_weight, CORE), last_weight, swap(last_weight, CORE)]
    weight_specs = [pl.BlockSpec((depth, half_cols), lambda i, *_: (i, 0))] * len(kept_weights)
    row_shape = jax.ShapeDtypeStruct((receive, width_model), jnp.bfloat16)
    row_grads = pl.pallas_call(
        row_grad_kernel,
        out_shape=row_shape,
        grid_spec=pltpu.PrefetchScalarGridSpec(
            num_scalar_prefetch=2,
            grid=(chips // 2,),
            in_specs=[pl.BlockSpec(got_near.shape, lambda i, *_: (0, 0, 0, 0))] + weight_specs,
            out_specs=pl.BlockSpec((receive, width_model), lambda i, *_: (0, 0)),
            scratch_shapes=[pltpu.VMEM((2, receive, half_cols), jnp.bfloat16)],
        ),
        compiler_params=PARAMS,
        cost_estimate=COST,
        name="row_grad",
    )(order, me_scalar, got_near, *kept_weights)
    count = receive // levels
    row_grads = pl.pallas_call(
        far_row_grad_kernel,
        out_shape=row_shape,
        grid_spec=pltpu.PrefetchScalarGridSpec(
            num_scalar_prefetch=2,
            grid=(chips // 2,),
            in_specs=anywhere(1)
            + [pl.BlockSpec(got.shape, lambda i, *_: (0, 0, 0, 0))]
            + weight_specs,
            out_specs=pl.BlockSpec(
                (count, width_model),
                lambda i, order, me: (lax.shift_right_logical(me[0], 3) ^ (levels - 1), 0),
            ),
            scratch_shapes=[pltpu.VMEM((2, count, half_cols), jnp.bfloat16)],
        ),
        input_output_aliases={2: 0},
        compiler_params=PARAMS,
        cost_estimate=COST,
        name="far_row_grad",
    )(order, me_scalar, row_grads, got, *kept_weights)

    key_grad = pl.pallas_call(
        functools.partial(sum_kernel, math.sqrt(rows * size)),
        out_shape=jax.ShapeDtypeStruct((shard, cols), jnp.float32),
        in_specs=vmem(1),
        out_specs=vmem(1)[0],
        compiler_params=PARAMS,
        cost_estimate=COST,
        name="sum",
    )(got)
    return (row_grads, key_grad)


def solution(mesh):
    size, split = mesh.shape["dp"], mesh.shape["mp"]
    paired = split == 1 and size == 32
    return jax.shard_map(
        per_device_paired if paired else per_device_general,
        mesh=mesh,
        in_specs=(P("dp", None), P("dp", "mp"), P("dp", None), P("dp", None), P(), P("dp", "mp")),
        out_specs=(P("dp", "mp"), P("dp", "mp")),
        check_vma=False,
    )
```

```python
import functools
import math

import jax
import jax.numpy as jnp
from jax import lax
from jax.experimental import pallas as pl
from jax.experimental.pallas import tpu as pltpu
from jax.sharding import PartitionSpec as P

HEAD_DIM = 128
NSUB = 4
VMEM_LIMIT = 48 * 1024 * 1024
CODE_ROWS = 16
epsilon = 1e-06


def per_device_general(tokens, key_cot, routes, counts, widths, key_weight):
    row_count = tokens.shape[0]
    width_model = tokens.shape[1]
    local_cols = key_cot.shape[1]
    local_heads = local_cols // HEAD_DIM
    dp_size = lax.axis_size("dp")
    per_peer = 2 * row_count // dp_size
    receive = dp_size * per_peer
    destination = routes[:, 0]
    one_hot = (destination[:, None] == jnp.arange(dp_size, dtype=jnp.int32)[None, :]).astype(
        jnp.int32
    )
    earlier = jnp.sum(jnp.cumsum(one_hot, axis=0) * one_hot, axis=1) - 1
    send_slot = destination * per_peer + earlier
    bounds = jnp.cumsum(counts[0])
    positions = jnp.arange(row_count, dtype=jnp.int32)
    subnet = jnp.sum((positions[:, None] >= bounds[None, : NSUB - 1]).astype(jnp.int32), axis=1)
    send_subnet = (
        jnp.full((receive,), -1, jnp.int32).at[send_slot].set(subnet).reshape(dp_size, per_peer)
    )
    send_cot = jnp.zeros((receive, local_cols), jnp.bfloat16).at[send_slot].set(key_cot)
    send_cot = send_cot.reshape(dp_size, per_peer, local_cols)
    send_tokens = jnp.zeros((receive, width_model), jnp.bfloat16).at[send_slot].set(tokens)
    send_tokens = send_tokens.reshape(dp_size, per_peer, width_model)
    got_tokens, got_cot, got_subnet = (
        lax.all_to_all(send_tokens, "dp", split_axis=0, concat_axis=0, tiled=True),
        lax.all_to_all(send_cot, "dp", split_axis=0, concat_axis=0, tiled=True),
        lax.all_to_all(send_subnet, "dp", split_axis=0, concat_axis=0, tiled=True),
    )
    hidden = got_tokens.reshape(receive, width_model)
    got_cot = got_cot.reshape(receive, local_cols)
    got_subnet = got_subnet.reshape(receive)
    full_weight = lax.all_gather(key_weight, "dp", axis=0, tiled=True)
    key_proj = jnp.dot(hidden, full_weight, preferred_element_type=jnp.float32)
    per_head = key_proj.reshape(receive, local_heads, HEAD_DIM)
    head_scale = jnp.sqrt(jnp.mean(per_head * per_head, axis=2, keepdims=True) + epsilon)
    outputs = per_head / head_scale
    subnet_match = got_subnet[:, None] == jnp.arange(NSUB, dtype=jnp.int32)[None, :]
    row_width = jnp.sum(jnp.where(subnet_match, widths[None, :], 0), axis=1)
    head_index = lax.axis_index("mp") * local_heads + jnp.arange(local_heads, dtype=jnp.int32)
    head_mask = (head_index[None, :] < row_width[:, None]).astype(jnp.float32)
    upstream = (
        got_cot.astype(jnp.float32).reshape(receive, local_heads, HEAD_DIM) * head_mask[:, :, None]
    )
    key_delta = (
        upstream - outputs * jnp.mean(upstream * outputs, axis=2, keepdims=True)
    ) / head_scale
    delta_low = key_delta.reshape(receive, local_cols).astype(jnp.bfloat16)
    part_delta = lax.dot_general(
        delta_low, full_weight, (((1,), (1,)), ((), ())), preferred_element_type=jnp.float32
    )
    rounded = lax.optimization_barrier(part_delta.astype(jnp.bfloat16)).astype(jnp.float32)
    feature_delta = lax.psum_scatter(
        rounded.astype(jnp.bfloat16), "mp", scatter_dimension=1, tiled=True
    )
    weight_sum = lax.psum_scatter(
        lax.dot_general(
            hidden, delta_low, (((0,), (0,)), ((), ())), preferred_element_type=jnp.float32
        ),
        "dp",
        scatter_dimension=0,
        tiled=True,
    )
    key_grad = weight_sum / math.sqrt(row_count * dp_size)
    return (feature_delta, key_grad)


CORE, X, Y = 1, 2, 4
PLANE = 8


def swap(value, mask):
    size = lax.axis_size("dp")
    return lax.ppermute(value, "dp", [(i, i ^ mask) for i in range(size)])


def after(value, *others):
    return lax.optimization_barrier((value, *others))[0]


def dot(a, b, dims):
    return lax.dot_general(a, b, (dims, ((), ())), preferred_element_type=jnp.float32)


def fetch(pairs, sems):
    copies = [
        pltpu.make_async_copy(source, target, sems.at[n])
        for n, (source, target) in enumerate(pairs)
    ]
    for copy in copies:
        copy.start()
    return copies


def project_kernel(places, begin, last, chips_ref, me_ref, own_ref, mate_ref, *refs):
    count = len(places)
    refs = list(refs)
    cots = [refs.pop(0) for _ in range(2)] if last else []
    begun = refs.pop(0) if begin else None
    pieces, refs = refs[:count], refs[count:]
    weight_ref, out_ref, held, weights, sems = refs[:5]
    acc = refs[5] if last else out_ref
    rows = own_ref.shape[0]
    chip_rows = max(piece.shape[0] for piece in pieces)

    def at_place(ref, n):
        chip, first = places[n]
        first += chip * chip_rows
        return ref.at[first : first + pieces[n].shape[0], :]

    pairs = [(own_ref, held.at[0]), (mate_ref, held.at[1])]
    pairs += [(piece, at_place(weights, n)) for n, piece in enumerate(pieces)]
    copies = fetch(pairs, sems)
    if begin:
        acc[...] = begun[...]
    for copy in copies[:2]:
        copy.wait()
    kept = []
    for n, (chip, first) in enumerate(places):
        copies[2 + n].wait()
        out = pltpu.make_async_copy(
            at_place(weights, n), at_place(weight_ref, n), sems.at[2 + count + n]
        )
        out.start()
        kept.append(out)
        piece = at_place(weights, n)[...]
        depth = piece.shape[0]
        at = pl.multiple_of(chips_ref[begin + chip] * chip_rows + first, 128)
        for side in range(2):
            part = dot(held[side, :, pl.ds(at, depth)], piece, ((1,), (0,)))
            if begin + n == 0:
                acc[side] = part
            else:
                acc[side] += part
    if last:
        core = me_ref[0] & 1
        delta_ref = out_ref
        delta_ref[2 * rows :, :] = jnp.zeros_like(delta_ref[2 * rows :, :])
        for side, cot_ref in enumerate(cots):
            at = pl.multiple_of((core ^ side) * rows, rows)
            for head in range(cot_ref.shape[1] // HEAD_DIM):
                cols = slice(head * HEAD_DIM, (head + 1) * HEAD_DIM)
                proj = acc[side, :, cols]
                scale = jnp.sqrt(jnp.mean(proj * proj, axis=1, keepdims=True) + epsilon)
                normed = proj / scale
                upstream = cot_ref[:rows, cols].astype(jnp.float32)
                inner = jnp.mean(upstream * normed, axis=1, keepdims=True)
                delta = (upstream - normed * inner) / scale
                delta_ref[pl.ds(at, rows), cols] = delta.astype(jnp.bfloat16)
            delta_ref[2 * rows :, pl.ds(at, rows)] = cot_ref[rows:, :rows]
    for copy in kept:
        copy.wait()


def selected_rows(plane, deltas, slot_count):
    rows = (deltas[0].shape[0] - CODE_ROWS) // 2
    per_chip = slot_count // (PLANE * len(deltas))
    iota = lax.broadcasted_iota(jnp.int32, (slot_count, 2 * rows), 0)
    destination, slot = iota // (per_chip * len(deltas)), iota % (per_chip * len(deltas))
    destination = destination + plane * PLANE
    total = None
    for n, delta in enumerate(deltas):
        code = delta[2 * rows :, : 2 * rows].astype(jnp.float32).astype(jnp.int32)
        hot = (destination == code[0:1, :]) & (slot == code[1:2, :] + n * per_chip)
        part = dot(hot.astype(jnp.bfloat16), delta[: 2 * rows, :], ((1,), (0,)))
        total = part if total is None else total + part
    return total.astype(jnp.bfloat16)


def select_kernel(me_ref, *refs):
    *deltas, sent_ref, held, sems = refs
    for copy in fetch([(ref, held.at[n]) for n, ref in enumerate(deltas)], sems):
        copy.wait()
    plane = lax.shift_right_logical(me_ref[0], 3)
    values = [held[n] for n in range(len(deltas))]
    sent_ref[...] = selected_rows(plane, values, sent_ref.shape[0])


def weight_grad_kernel(me_ref, own_ref, mate_ref, *refs):
    *deltas, part_ref, hidden, held, acc, made, sems = refs
    plane = lax.shift_right_logical(me_ref[0], 3)
    core = me_ref[0] & 1
    rows = own_ref.shape[1]
    count = len(deltas)
    pairs = []
    for n, ref in enumerate(deltas):
        pairs += [
            (own_ref.at[plane ^ n], hidden.at[n, 0]),
            (mate_ref.at[plane ^ n], hidden.at[n, 1]),
            (ref, held.at[n]),
        ]
    copies = fetch(pairs, sems)
    for n in range(count):
        for copy in copies[3 * n : 3 * n + 3]:
            copy.wait()
        for side in range(2):
            at = pl.multiple_of((core ^ side) * rows, rows)
            part = dot(hidden[n, side], held[n, pl.ds(at, rows), :], ((0,), (0,)))
            if n + side == 0:
                acc[...] = part
            else:
                acc[...] += part
    blocks, depth, _ = part_ref.shape
    shard = acc.shape[0] // blocks
    extra = depth - shard
    far = selected_rows(plane, [held[count - 1]], blocks * extra)
    sent = []
    for block in range(blocks):
        made[block, :shard, :] = acc[block * shard : (block + 1) * shard, :].astype(jnp.bfloat16)
        made[block, shard:, :] = far[block * extra : (block + 1) * extra, :]
        copy = pltpu.make_async_copy(made.at[block], part_ref.at[block], sems.at[3 * count + block])
        copy.start()
        sent.append(copy)
    for copy in sent:
        copy.wait()


def sum_kernel(norm, parts_ref, grad_ref):
    shard, cols = grad_ref.shape
    half = cols // 2
    for side in range(2):
        total = parts_ref[0, side, :shard, :].astype(jnp.float32)
        for chip in range(1, parts_ref.shape[0]):
            total += parts_ref[chip, side, :shard, :].astype(jnp.float32)
        grad_ref[:, side * half : (side + 1) * half] = total / norm


def add_columns(core, step, chips_ref, rows_ref, weights, out_ref):
    own, mate = rows_ref[core], rows_ref[1 - core]
    depth = weights[0].shape[0]
    for n in range(len(weights) // 2):
        total = dot(weights[2 * n][...], own, ((1,), (0,)))
        total += dot(weights[2 * n + 1][...], mate, ((1,), (0,)))
        at = chips_ref[n * pl.num_programs(0) + step] * depth
        out_ref[:, pl.ds(pl.multiple_of(at, depth), depth)] = total.T.astype(jnp.bfloat16)


def row_grad_kernel(chips_ref, me_ref, got_ref, *refs):
    *weights, out_ref, rows_ref, held = refs
    step = pl.program_id(0)
    chips, _, count, half = got_ref.shape
    block = held.shape[0] // (chips * 4)
    level = lax.shift_right_logical(me_ref[0], 3)

    @pl.when(step == 0)
    def _():
        for side in range(2):
            for n in range(4):
                for chip in range(chips):
                    at = pl.multiple_of(((level ^ n) * chips + chip) * block, block)
                    if n < count // block:
                        rows = got_ref[chip, side, n * block : (n + 1) * block, :]
                    else:
                        rows = jnp.zeros((block, half), jnp.bfloat16)
                    held[pl.ds(at, block), :] = rows.astype(jnp.float32)
            rows_ref[side] = held[...].T.astype(jnp.bfloat16)

    add_columns(me_ref[0] & 1, step, chips_ref, rows_ref, weights, out_ref)


def far_row_grad_kernel(chips_ref, me_ref, before_ref, got_ref, *refs):
    *weights, out_ref, rows_ref, held = refs
    step = pl.program_id(0)
    chips, _, count, _ = got_ref.shape
    block = out_ref.shape[0] // chips

    @pl.when(step == 0)
    def _():
        held[...] = jnp.zeros_like(held)
        for side in range(2):
            for chip in range(chips):
                rows = got_ref[chip, side, count - block :, :]
                held[chip * block : (chip + 1) * block, :] = rows.astype(jnp.float32)
            rows_ref[side] = held[...].T.astype(jnp.bfloat16)

    own, mate = rows_ref[me_ref[0] & 1], rows_ref[1 - (me_ref[0] & 1)]
    depth = weights[0].shape[0]
    for n in range(len(weights) // 2):
        total = dot(weights[2 * n][...], own, ((1,), (0,)))
        total += dot(weights[2 * n + 1][...], mate, ((1,), (0,)))
        at = chips_ref[n * pl.num_programs(0) + step] * depth
        out_ref[:, pl.ds(pl.multiple_of(at, depth), depth)] = total.T[: chips * block].astype(
            jnp.bfloat16
        )


def code_rows(destination, core, per_peer, width):
    positions = jnp.arange(destination.shape[0], dtype=jnp.int32)
    same = (destination[:, None] == destination[None, :]) & (
        positions[:, None] < positions[None, :]
    )
    earlier = jnp.sum(same.astype(jnp.int32), axis=0)
    codes = jnp.stack([destination, core * per_peer + earlier]).astype(jnp.bfloat16)
    return jnp.pad(codes, ((0, CODE_ROWS - 2), (0, width - destination.shape[0])))


def vmem(count):
    return [pl.BlockSpec(memory_space=pltpu.VMEM)] * count


def hbm(count):
    return [pl.BlockSpec(memory_space=pltpu.HBM)] * count


SCALAR = pl.BlockSpec(memory_space=pltpu.SMEM)
PARAMS = pltpu.CompilerParams(vmem_limit_bytes=VMEM_LIMIT)


COST = pl.CostEstimate(flops=1024, bytes_accessed=1024, transcendentals=0)
TRANSFER_COST = pl.CostEstimate(flops=1024, bytes_accessed=28 << 20, transcendentals=0)


def per_device_paired(tokens, key_cot, routes, counts, widths, key_weight):
    rows, width_model = tokens.shape
    cols = key_cot.shape[1]
    half_cols = cols // 2
    size = lax.axis_size("dp")
    chips = size // 2
    levels = size // PLANE
    per_peer = 2 * rows // size
    receive = size * per_peer
    wide = width_model // levels
    me = lax.axis_index("dp")
    core = me % 2
    me_scalar = me.astype(jnp.int32).reshape(1)

    def mine(value):
        return lax.dynamic_slice_in_dim(value, core * half_cols, half_cols, 1)

    def theirs(value):
        return lax.dynamic_slice_in_dim(value, (1 - core) * half_cols, half_cols, 1)

    mate_shard = swap(key_weight, CORE)
    piece = jnp.where(
        core == 0,
        jnp.concatenate([key_weight[:, :half_cols], mate_shard[:, :half_cols]], axis=0),
        jnp.concatenate([mate_shard[:, half_cols:], key_weight[:, half_cols:]], axis=0),
    )
    near, far, both = PLANE, 2 * PLANE, 3 * PLANE
    column = {0: piece, far: swap(piece, far), near: swap(piece, near)}
    column[both] = swap(column[far], near)
    half = piece.shape[0] // 2
    sets, masks = [], []
    for n, (mask, own) in enumerate(sorted(column.items())):
        by_x, by_y = swap(own, X), swap(own, Y)
        if mask == both:
            across = [swap(by_y[:half], X), swap(by_x[half:], Y)]
        else:
            across = [swap(by_x, Y) if mask == near else swap(by_y, X)]
        places = [(0, 0), (1, 0), (2, 0), (3, 0), (3, half)]
        sets.append(([own, by_x, by_y, *across], places[: 3 + len(across)]))
        masks += [mask, mask | X, mask | Y, mask | X | Y]
    order = jnp.stack([lax.shift_right_logical(me ^ mask, 1) for mask in masks])

    mate_tokens = swap(after(tokens, column[near]), CORE)
    late_tokens = after(tokens, column[both])
    columns = [[p + PLANE * z for z in range(levels)] for p in range(PLANE)]
    own_features = lax.all_to_all(
        jnp.stack([late_tokens[:, z * wide : (z + 1) * wide] for z in range(levels)]),
        "dp",
        split_axis=0,
        concat_axis=0,
        axis_index_groups=columns,
        tiled=True,
    )
    mate_features = swap(own_features, CORE)

    key_cot, counts, routes = lax.optimization_barrier((key_cot, counts, routes, column[near]))[:3]
    bounds = jnp.cumsum(counts[0])
    positions = jnp.arange(rows, dtype=jnp.int32)
    subnet = jnp.sum((positions[:, None] >= bounds[None, : NSUB - 1]).astype(jnp.int32), axis=1)
    subnet_match = subnet[:, None] == jnp.arange(NSUB, dtype=jnp.int32)[None, :]
    row_width = jnp.sum(jnp.where(subnet_match, widths[None, :], 0), axis=1)
    head_of_col = jnp.arange(cols, dtype=jnp.int32) // HEAD_DIM
    upstream = jnp.where(
        head_of_col[None, :] < row_width[:, None], key_cot, jnp.zeros_like(key_cot)
    )
    codes = code_rows(routes[:, 0], core, per_peer, half_cols)
    own_cot = jnp.concatenate([mine(upstream), codes], axis=0)
    mate_cot = swap(jnp.concatenate([theirs(upstream), codes], axis=0), CORE)

    kept = jax.ShapeDtypeStruct((width_model // levels, half_cols), jnp.bfloat16)
    sums = jax.ShapeDtypeStruct((2, rows, half_cols), jnp.float32)
    deltas = jax.ShapeDtypeStruct((2 * rows + CODE_ROWS, half_cols), jnp.bfloat16)
    kept_weights, begun = [], []
    for n, (pieces, places) in enumerate(sets):
        last = n == levels - 1
        extra = [own_cot, mate_cot] if last else []
        weight, result = pl.pallas_call(
            functools.partial(project_kernel, places, n * len(sets), last),
            out_shape=(kept, deltas if last else sums),
            in_specs=[SCALAR] * 2
            + hbm(2)
            + vmem(len(extra) + len(begun))
            + hbm(len(pieces)),
            out_specs=(hbm(1)[0], vmem(1)[0]),
            scratch_shapes=[
                pltpu.VMEM((2, rows, width_model), jnp.bfloat16),
                pltpu.VMEM(kept.shape, jnp.bfloat16),
                pltpu.SemaphoreType.DMA((2 + 2 * len(pieces),)),
            ]
            + ([pltpu.VMEM(sums.shape, sums.dtype)] if last else []),
            compiler_params=PARAMS,
            cost_estimate=COST if last else TRANSFER_COST,
            name="delta" if last else f"project_{n}",
        )(order, me_scalar, tokens, mate_tokens, *extra, *begun, *pieces)
        kept_weights += [weight, swap(weight, CORE)]
        begun = [result]
    delta = begun[0]

    delta_far, delta_near = swap(delta, far), swap(delta, near)
    delta_both = swap(delta_far, near)
    planes = [[z * PLANE + p for p in range(PLANE)] for z in range(levels)]

    def to_plane(value):
        got = lax.all_to_all(
            value, "dp", split_axis=0, concat_axis=0, axis_index_groups=planes, tiled=True
        )
        return got.reshape(PLANE // 2, 2, *value.shape[1:])

    per_chip = 2 * per_peer
    near_deltas = [delta, delta_near, delta_far]
    selected = pl.pallas_call(
        select_kernel,
        out_shape=jax.ShapeDtypeStruct((PLANE * 3 * per_chip, half_cols), jnp.bfloat16),
        in_specs=[SCALAR] + hbm(3),
        out_specs=vmem(1)[0],
        scratch_shapes=[
            pltpu.VMEM((3, *delta.shape), jnp.bfloat16),
            pltpu.SemaphoreType.DMA((3,)),
        ],
        compiler_params=PARAMS,
        cost_estimate=COST,
        name="select",
    )(me_scalar, *near_deltas)
    got_near = to_plane(selected.reshape(PLANE, 3 * per_chip, half_cols))

    shard = width_model // size
    terms = pl.pallas_call(
        weight_grad_kernel,
        out_shape=jax.ShapeDtypeStruct((PLANE, shard + per_chip, half_cols), jnp.bfloat16),
        in_specs=[SCALAR] + hbm(2 + levels),
        out_specs=hbm(1)[0],
        scratch_shapes=[
            pltpu.VMEM((levels, 2, rows, wide), jnp.bfloat16),
            pltpu.VMEM((levels, *delta.shape), jnp.bfloat16),
            pltpu.VMEM((wide, half_cols), jnp.float32),
            pltpu.VMEM((PLANE, shard + per_chip, half_cols), jnp.bfloat16),
            pltpu.SemaphoreType.DMA((3 * levels + PLANE,)),
        ],
        compiler_params=PARAMS,
        cost_estimate=COST,
        name="weight_grad",
    )(me_scalar, own_features, mate_features, *near_deltas, delta_both)
    got = to_plane(terms)

    depth = width_model // chips
    weight_specs = [pl.BlockSpec((depth, half_cols), lambda i, *_: (i, 0))] * len(kept_weights)
    row_shape = jax.ShapeDtypeStruct((receive, width_model), jnp.bfloat16)
    row_grads = pl.pallas_call(
        row_grad_kernel,
        out_shape=row_shape,
        grid_spec=pltpu.PrefetchScalarGridSpec(
            num_scalar_prefetch=2,
            grid=(chips // levels,),
            in_specs=[pl.BlockSpec(got_near.shape, lambda i, *_: (0, 0, 0, 0))] + weight_specs,
            out_specs=pl.BlockSpec((receive, width_model), lambda i, *_: (0, 0)),
            scratch_shapes=[
                pltpu.VMEM((2, half_cols, receive), jnp.bfloat16),
                pltpu.VMEM((receive, half_cols), jnp.float32),
            ],
        ),
        compiler_params=PARAMS,
        cost_estimate=COST,
        name="row_grad",
    )(order, me_scalar, got_near, *kept_weights)
    count = receive // levels
    row_grads = pl.pallas_call(
        far_row_grad_kernel,
        out_shape=row_shape,
        grid_spec=pltpu.PrefetchScalarGridSpec(
            num_scalar_prefetch=2,
            grid=(chips // levels,),
            in_specs=hbm(1)
            + [pl.BlockSpec(got.shape, lambda i, *_: (0, 0, 0, 0))]
            + weight_specs,
            out_specs=pl.BlockSpec(
                (count, width_model),
                lambda i, order, me: (lax.shift_right_logical(me[0], 3) ^ (levels - 1), 0),
            ),
            scratch_shapes=[
                pltpu.VMEM((2, half_cols, 128), jnp.bfloat16),
                pltpu.VMEM((128, half_cols), jnp.float32),
            ],
        ),
        input_output_aliases={2: 0},
        compiler_params=PARAMS,
        cost_estimate=COST,
        name="far_row_grad",
    )(order, me_scalar, row_grads, got, *kept_weights)

    key_grad = pl.pallas_call(
        functools.partial(sum_kernel, math.sqrt(rows * size)),
        out_shape=jax.ShapeDtypeStruct((shard, cols), jnp.float32),
        in_specs=vmem(1),
        out_specs=vmem(1)[0],
        compiler_params=PARAMS,
        cost_estimate=COST,
        name="sum",
    )(got)
    return (row_grads, key_grad)


def solution(mesh):
    size, split = mesh.shape["dp"], mesh.shape["mp"]
    paired = split == 1 and size == 32
    return jax.shard_map(
        per_device_paired if paired else per_device_general,
        mesh=mesh,
        in_specs=(P("dp", None), P("dp", "mp"), P("dp", None), P("dp", None), P(), P("dp", "mp")),
        out_specs=(P("dp", "mp"), P("dp", "mp")),
        check_vma=False,
    )
```

```python
import functools
import math

import jax
import jax.numpy as jnp
from jax import lax
from jax.experimental import pallas as pl
from jax.experimental.pallas import tpu as pltpu
from jax.sharding import PartitionSpec as P

HEAD_DIM = 128
NSUB = 4
VMEM_LIMIT = 48 * 1024 * 1024
CODE_ROWS = 16
epsilon = 1e-06


def per_device_general(tokens, key_cot, routes, counts, widths, key_weight):
    row_count = tokens.shape[0]
    width_model = tokens.shape[1]
    local_cols = key_cot.shape[1]
    local_heads = local_cols // HEAD_DIM
    dp_size = lax.axis_size("dp")
    per_peer = 2 * row_count // dp_size
    receive = dp_size * per_peer
    destination = routes[:, 0]
    one_hot = (destination[:, None] == jnp.arange(dp_size, dtype=jnp.int32)[None, :]).astype(
        jnp.int32
    )
    earlier = jnp.sum(jnp.cumsum(one_hot, axis=0) * one_hot, axis=1) - 1
    send_slot = destination * per_peer + earlier
    bounds = jnp.cumsum(counts[0])
    positions = jnp.arange(row_count, dtype=jnp.int32)
    subnet = jnp.sum((positions[:, None] >= bounds[None, : NSUB - 1]).astype(jnp.int32), axis=1)
    send_subnet = (
        jnp.full((receive,), -1, jnp.int32).at[send_slot].set(subnet).reshape(dp_size, per_peer)
    )
    send_cot = jnp.zeros((receive, local_cols), jnp.bfloat16).at[send_slot].set(key_cot)
    send_cot = send_cot.reshape(dp_size, per_peer, local_cols)
    send_tokens = jnp.zeros((receive, width_model), jnp.bfloat16).at[send_slot].set(tokens)
    send_tokens = send_tokens.reshape(dp_size, per_peer, width_model)
    got_tokens, got_cot, got_subnet = (
        lax.all_to_all(send_tokens, "dp", split_axis=0, concat_axis=0, tiled=True),
        lax.all_to_all(send_cot, "dp", split_axis=0, concat_axis=0, tiled=True),
        lax.all_to_all(send_subnet, "dp", split_axis=0, concat_axis=0, tiled=True),
    )
    hidden = got_tokens.reshape(receive, width_model)
    got_cot = got_cot.reshape(receive, local_cols)
    got_subnet = got_subnet.reshape(receive)
    full_weight = lax.all_gather(key_weight, "dp", axis=0, tiled=True)
    key_proj = jnp.dot(hidden, full_weight, preferred_element_type=jnp.float32)
    per_head = key_proj.reshape(receive, local_heads, HEAD_DIM)
    head_scale = jnp.sqrt(jnp.mean(per_head * per_head, axis=2, keepdims=True) + epsilon)
    outputs = per_head / head_scale
    subnet_match = got_subnet[:, None] == jnp.arange(NSUB, dtype=jnp.int32)[None, :]
    row_width = jnp.sum(jnp.where(subnet_match, widths[None, :], 0), axis=1)
    head_index = lax.axis_index("mp") * local_heads + jnp.arange(local_heads, dtype=jnp.int32)
    head_mask = (head_index[None, :] < row_width[:, None]).astype(jnp.float32)
    upstream = (
        got_cot.astype(jnp.float32).reshape(receive, local_heads, HEAD_DIM) * head_mask[:, :, None]
    )
    key_delta = (
        upstream - outputs * jnp.mean(upstream * outputs, axis=2, keepdims=True)
    ) / head_scale
    delta_low = key_delta.reshape(receive, local_cols).astype(jnp.bfloat16)
    part_delta = lax.dot_general(
        delta_low, full_weight, (((1,), (1,)), ((), ())), preferred_element_type=jnp.float32
    )
    rounded = lax.optimization_barrier(part_delta.astype(jnp.bfloat16)).astype(jnp.float32)
    feature_delta = lax.psum_scatter(
        rounded.astype(jnp.bfloat16), "mp", scatter_dimension=1, tiled=True
    )
    weight_sum = lax.psum_scatter(
        lax.dot_general(
            hidden, delta_low, (((0,), (0,)), ((), ())), preferred_element_type=jnp.float32
        ),
        "dp",
        scatter_dimension=0,
        tiled=True,
    )
    key_grad = weight_sum / math.sqrt(row_count * dp_size)
    return (feature_delta, key_grad)


CORE, X, Y = 1, 2, 4
PLANE = 8


def swap(value, mask):
    size = lax.axis_size("dp")
    return lax.ppermute(value, "dp", [(i, i ^ mask) for i in range(size)])


def after(value, *others):
    return lax.optimization_barrier((value, *others))[0]


def dot(a, b, dims):
    return lax.dot_general(a, b, (dims, ((), ())), preferred_element_type=jnp.float32)


def delta_kernel(places, chips_ref, me_ref, own_ref, mate_ref, own_cot_ref, mate_cot_ref, *refs):
    *pieces, delta_ref, weight_ref, acc = refs
    core = me_ref[0] & 1
    rows = own_ref.shape[0]
    chip_rows = pieces[0].shape[0]
    for n, ((chip, first), piece_ref) in enumerate(zip(places, pieces)):
        piece = piece_ref[...]
        depth = piece.shape[0]
        weight_ref[chip * chip_rows + first : chip * chip_rows + first + depth, :] = piece
        at = pl.multiple_of(chips_ref[chip] * chip_rows + first, 128)
        for side, ref in enumerate((own_ref, mate_ref)):
            part = dot(ref[:, pl.ds(at, depth)], piece, ((1,), (0,)))
            if n == 0:
                acc[side] = part
            else:
                acc[side] += part
    delta_ref[2 * rows :, :] = jnp.zeros_like(delta_ref[2 * rows :, :])
    for side, cot_ref in enumerate((own_cot_ref, mate_cot_ref)):
        at = pl.multiple_of((core ^ side) * rows, rows)
        for head in range(own_cot_ref.shape[1] // HEAD_DIM):
            cols = slice(head * HEAD_DIM, (head + 1) * HEAD_DIM)
            proj = acc[side, :, cols]
            scale = jnp.sqrt(jnp.mean(proj * proj, axis=1, keepdims=True) + epsilon)
            normed = proj / scale
            upstream = cot_ref[:rows, cols].astype(jnp.float32)
            delta = (upstream - normed * jnp.mean(upstream * normed, axis=1, keepdims=True)) / scale
            delta_ref[pl.ds(at, rows), cols] = delta.astype(jnp.bfloat16)
        delta_ref[2 * rows :, pl.ds(at, rows)] = cot_ref[rows:, :rows]


def selected_rows(plane, deltas, slot_count):
    rows = (deltas[0].shape[0] - CODE_ROWS) // 2
    per_chip = slot_count // (PLANE * len(deltas))
    iota = lax.broadcasted_iota(jnp.int32, (slot_count, 2 * rows), 0)
    destination, slot = iota // (per_chip * len(deltas)), iota % (per_chip * len(deltas))
    destination = destination + plane * PLANE
    total = None
    for n, delta in enumerate(deltas):
        code = delta[2 * rows :, : 2 * rows].astype(jnp.float32).astype(jnp.int32)
        hot = (destination == code[0:1, :]) & (slot == code[1:2, :] + n * per_chip)
        part = dot(hot.astype(jnp.bfloat16), delta[: 2 * rows, :], ((1,), (0,)))
        total = part if total is None else total + part
    return total.astype(jnp.bfloat16)


def select_kernel(me_ref, *refs):
    *deltas, sent_ref = refs
    plane = lax.shift_right_logical(me_ref[0], 3)
    values = [ref[...] for ref in deltas]
    sent_ref[...] = selected_rows(plane, values, sent_ref.shape[0])


def weight_grad_kernel(me_ref, own_ref, mate_ref, *refs):
    *deltas, part_ref, acc = refs
    plane = lax.shift_right_logical(me_ref[0], 3)
    core = me_ref[0] & 1
    rows = own_ref.shape[1]
    for n, delta_ref in enumerate(deltas):
        for side, ref in enumerate((own_ref, mate_ref)):
            at = pl.multiple_of((core ^ side) * rows, rows)
            part = dot(ref[plane ^ n], delta_ref[pl.ds(at, rows), :], ((0,), (0,)))
            if n + side == 0:
                acc[...] = part
            else:
                acc[...] += part
    part_ref[...] = acc[...].astype(jnp.bfloat16)


def sum_kernel(norm, parts_ref, grad_ref):
    half = parts_ref.shape[3]
    for side in range(2):
        total = parts_ref[0, side].astype(jnp.float32)
        for chip in range(1, parts_ref.shape[0]):
            total += parts_ref[chip, side].astype(jnp.float32)
        grad_ref[:, side * half : (side + 1) * half] = total / norm


def row_grad_kernel(chips_ref, me_ref, got_ref, *refs):
    *weights, out_ref, rows_ref, held = refs
    step = pl.program_id(0)
    chips, _, count, half = got_ref.shape
    block = held.shape[0] // (chips * 4)
    level = lax.shift_right_logical(me_ref[0], 3)

    @pl.when(step == 0)
    def _():
        for side in range(2):
            for n in range(count // block):
                for chip in range(chips):
                    at = pl.multiple_of(((level ^ n) * chips + chip) * block, block)
                    rows = got_ref[chip, side, n * block : (n + 1) * block, :]
                    held[pl.ds(at, block), :] = rows.astype(jnp.float32)
            rows_ref[side] = held[...].T.astype(jnp.bfloat16)

    core = me_ref[0] & 1
    own, mate = rows_ref[core], rows_ref[1 - core]
    depth = half // 2
    for n in range(weights[0].shape[0] // depth):
        total = dot(weights[0][n * depth : (n + 1) * depth, :], own, ((1,), (0,)))
        total += dot(weights[1][n * depth : (n + 1) * depth, :], mate, ((1,), (0,)))
        at = chips_ref[weights[0].shape[0] // depth * step + n] * depth
        out_ref[:, pl.ds(pl.multiple_of(at, depth), depth)] = total.T.astype(jnp.bfloat16)


def code_rows(destination, core, per_peer, width):
    positions = jnp.arange(destination.shape[0], dtype=jnp.int32)
    same = (destination[:, None] == destination[None, :]) & (
        positions[:, None] < positions[None, :]
    )
    earlier = jnp.sum(same.astype(jnp.int32), axis=0)
    codes = jnp.stack([destination, core * per_peer + earlier]).astype(jnp.bfloat16)
    return jnp.pad(codes, ((0, CODE_ROWS - 2), (0, width - destination.shape[0])))


def vmem(count):
    return [pl.BlockSpec(memory_space=pltpu.VMEM)] * count


def anywhere(count):
    return [pl.BlockSpec(memory_space=pl.ANY)] * count


SCALAR = pl.BlockSpec(memory_space=pltpu.SMEM)
PARAMS = pltpu.CompilerParams(vmem_limit_bytes=VMEM_LIMIT)


def per_device_paired(tokens, key_cot, routes, counts, widths, key_weight):
    rows, width_model = tokens.shape
    cols = key_cot.shape[1]
    half_cols = cols // 2
    size = lax.axis_size("dp")
    chips = size // 2
    levels = size // PLANE
    per_peer = 2 * rows // size
    receive = size * per_peer
    wide = width_model // levels
    me = lax.axis_index("dp")
    core = me % 2
    me_scalar = me.astype(jnp.int32).reshape(1)

    def mine(value):
        return lax.dynamic_slice_in_dim(value, core * half_cols, half_cols, 1)

    def theirs(value):
        return lax.dynamic_slice_in_dim(value, (1 - core) * half_cols, half_cols, 1)

    mate_shard = swap(key_weight, CORE)
    piece = jnp.where(
        core == 0,
        jnp.concatenate([key_weight[:, :half_cols], mate_shard[:, :half_cols]], axis=0),
        jnp.concatenate([mate_shard[:, half_cols:], key_weight[:, half_cols:]], axis=0),
    )
    near, far, both = PLANE, 2 * PLANE, 3 * PLANE
    column = {0: piece, far: swap(piece, far), near: swap(piece, near)}
    column[both] = swap(column[far], near)
    half = piece.shape[0] // 2
    pieces, places, masks = [], [], []
    for n, (mask, own) in enumerate(sorted(column.items())):
        by_x, by_y = swap(own, X), swap(own, Y)
        masks += [mask, mask | X, mask | Y, mask | X | Y]
        pieces += [own, by_x, by_y, swap(by_y[:half], X), swap(by_x[half:], Y)]
        places += [(4 * n, 0), (4 * n + 1, 0), (4 * n + 2, 0), (4 * n + 3, 0), (4 * n + 3, half)]
    order = jnp.stack([lax.shift_right_logical(me ^ mask, 1) for mask in masks])

    mate_tokens = swap(after(tokens, column[near]), CORE)
    columns = [[p + PLANE * z for z in range(levels)] for p in range(PLANE)]
    own_features = lax.all_to_all(
        jnp.stack([tokens[:, z * wide : (z + 1) * wide] for z in range(levels)]),
        "dp",
        split_axis=0,
        concat_axis=0,
        axis_index_groups=columns,
        tiled=True,
    )
    mate_features = swap(own_features, CORE)

    key_cot, counts, routes = lax.optimization_barrier((key_cot, counts, routes, column[near]))[:3]
    bounds = jnp.cumsum(counts[0])
    positions = jnp.arange(rows, dtype=jnp.int32)
    subnet = jnp.sum((positions[:, None] >= bounds[None, : NSUB - 1]).astype(jnp.int32), axis=1)
    subnet_match = subnet[:, None] == jnp.arange(NSUB, dtype=jnp.int32)[None, :]
    row_width = jnp.sum(jnp.where(subnet_match, widths[None, :], 0), axis=1)
    head_of_col = jnp.arange(cols, dtype=jnp.int32) // HEAD_DIM
    upstream = jnp.where(
        head_of_col[None, :] < row_width[:, None], key_cot, jnp.zeros_like(key_cot)
    )
    codes = code_rows(routes[:, 0], core, per_peer, half_cols)
    own_cot = jnp.concatenate([mine(upstream), codes], axis=0)
    mate_cot = swap(jnp.concatenate([theirs(upstream), codes], axis=0), CORE)

    kept = jax.ShapeDtypeStruct((width_model, half_cols), jnp.bfloat16)
    delta, own_half = pl.pallas_call(
        functools.partial(delta_kernel, places),
        out_shape=(jax.ShapeDtypeStruct((2 * rows + CODE_ROWS, half_cols), jnp.bfloat16), kept),
        in_specs=[SCALAR] * 2 + vmem(4 + len(pieces)),
        out_specs=tuple(vmem(2)),
        scratch_shapes=[pltpu.VMEM((2, rows, half_cols), jnp.float32)],
        compiler_params=PARAMS,
        name="delta",
    )(order, me_scalar, tokens, mate_tokens, own_cot, mate_cot, *pieces)

    deltas = [delta, *(swap(delta, mask) for mask in (near, far, both))]
    planes = [[z * PLANE + p for p in range(PLANE)] for z in range(levels)]

    def to_plane(value):
        got = lax.all_to_all(
            value, "dp", split_axis=0, concat_axis=0, axis_index_groups=planes, tiled=True
        )
        return got.reshape(PLANE // 2, 2, *value.shape[1:])

    selected = pl.pallas_call(
        select_kernel,
        out_shape=jax.ShapeDtypeStruct((PLANE * 2 * levels * per_peer, half_cols), jnp.bfloat16),
        in_specs=[SCALAR] + vmem(levels),
        out_specs=vmem(1)[0],
        compiler_params=PARAMS,
        name="select",
    )(me_scalar, *deltas)
    got = to_plane(selected.reshape(PLANE, 2 * levels * per_peer, half_cols))

    shard = width_model // size
    terms = pl.pallas_call(
        weight_grad_kernel,
        out_shape=jax.ShapeDtypeStruct((wide, half_cols), jnp.bfloat16),
        in_specs=[SCALAR] + vmem(2 + levels),
        out_specs=vmem(1)[0],
        scratch_shapes=[pltpu.VMEM((wide, half_cols), jnp.float32)],
        compiler_params=PARAMS,
        name="weight_grad",
    )(me_scalar, own_features, mate_features, after(delta, selected), *deltas[1:])
    parts = to_plane(terms.reshape(PLANE, shard, half_cols))

    depth = width_model // 4
    row_grads = pl.pallas_call(
        row_grad_kernel,
        out_shape=jax.ShapeDtypeStruct((receive, width_model), jnp.bfloat16),
        grid_spec=pltpu.PrefetchScalarGridSpec(
            num_scalar_prefetch=2,
            grid=(width_model // depth,),
            in_specs=[pl.BlockSpec(got.shape, lambda i, *_: (0, 0, 0, 0))]
            + [pl.BlockSpec((depth, half_cols), lambda i, *_: (i, 0))] * 2,
            out_specs=pl.BlockSpec((receive, width_model), lambda i, *_: (0, 0)),
            scratch_shapes=[
                pltpu.VMEM((2, half_cols, receive), jnp.bfloat16),
                pltpu.VMEM((receive, half_cols), jnp.float32),
            ],
        ),
        compiler_params=PARAMS,
        name="row_grad",
    )(order, me_scalar, got, own_half, swap(own_half, CORE))

    key_grad = pl.pallas_call(
        functools.partial(sum_kernel, math.sqrt(rows * size)),
        out_shape=jax.ShapeDtypeStruct((shard, cols), jnp.float32),
        in_specs=vmem(1),
        out_specs=vmem(1)[0],
        compiler_params=PARAMS,
        name="sum",
    )(after(parts, row_grads))
    return (row_grads, key_grad)


def solution(mesh):
    size, split = mesh.shape["dp"], mesh.shape["mp"]
    paired = split == 1 and size == 32
    return jax.shard_map(
        per_device_paired if paired else per_device_general,
        mesh=mesh,
        in_specs=(P("dp", None), P("dp", "mp"), P("dp", None), P("dp", None), P(), P("dp", "mp")),
        out_specs=(P("dp", "mp"), P("dp", "mp")),
        check_vma=False,
    )
```

```python
import functools
import math

import jax
import jax.numpy as jnp
from jax import lax
from jax.experimental import pallas as pl
from jax.experimental.pallas import tpu as pltpu
from jax.sharding import PartitionSpec as P

HEAD_DIM = 128
NSUB = 4
VMEM_LIMIT = 60 * 1024 * 1024
CODE_ROWS = 16
epsilon = 1e-06


def per_device_general(tokens, key_cot, routes, counts, widths, key_weight):
    row_count = tokens.shape[0]
    width_model = tokens.shape[1]
    local_cols = key_cot.shape[1]
    local_heads = local_cols // HEAD_DIM
    dp_size = lax.axis_size("dp")
    per_peer = 2 * row_count // dp_size
    receive = dp_size * per_peer
    destination = routes[:, 0]
    one_hot = (destination[:, None] == jnp.arange(dp_size, dtype=jnp.int32)[None, :]).astype(
        jnp.int32
    )
    earlier = jnp.sum(jnp.cumsum(one_hot, axis=0) * one_hot, axis=1) - 1
    send_slot = destination * per_peer + earlier
    bounds = jnp.cumsum(counts[0])
    positions = jnp.arange(row_count, dtype=jnp.int32)
    subnet = jnp.sum((positions[:, None] >= bounds[None, : NSUB - 1]).astype(jnp.int32), axis=1)
    send_subnet = (
        jnp.full((receive,), -1, jnp.int32).at[send_slot].set(subnet).reshape(dp_size, per_peer)
    )
    send_cot = jnp.zeros((receive, local_cols), jnp.bfloat16).at[send_slot].set(key_cot)
    send_cot = send_cot.reshape(dp_size, per_peer, local_cols)
    send_tokens = jnp.zeros((receive, width_model), jnp.bfloat16).at[send_slot].set(tokens)
    send_tokens = send_tokens.reshape(dp_size, per_peer, width_model)
    got_tokens, got_cot, got_subnet = (
        lax.all_to_all(send_tokens, "dp", split_axis=0, concat_axis=0, tiled=True),
        lax.all_to_all(send_cot, "dp", split_axis=0, concat_axis=0, tiled=True),
        lax.all_to_all(send_subnet, "dp", split_axis=0, concat_axis=0, tiled=True),
    )
    hidden = got_tokens.reshape(receive, width_model)
    got_cot = got_cot.reshape(receive, local_cols)
    got_subnet = got_subnet.reshape(receive)
    full_weight = lax.all_gather(key_weight, "dp", axis=0, tiled=True)
    key_proj = jnp.dot(hidden, full_weight, preferred_element_type=jnp.float32)
    per_head = key_proj.reshape(receive, local_heads, HEAD_DIM)
    head_scale = jnp.sqrt(jnp.mean(per_head * per_head, axis=2, keepdims=True) + epsilon)
    outputs = per_head / head_scale
    subnet_match = got_subnet[:, None] == jnp.arange(NSUB, dtype=jnp.int32)[None, :]
    row_width = jnp.sum(jnp.where(subnet_match, widths[None, :], 0), axis=1)
    head_index = lax.axis_index("mp") * local_heads + jnp.arange(local_heads, dtype=jnp.int32)
    head_mask = (head_index[None, :] < row_width[:, None]).astype(jnp.float32)
    upstream = (
        got_cot.astype(jnp.float32).reshape(receive, local_heads, HEAD_DIM) * head_mask[:, :, None]
    )
    key_delta = (
        upstream - outputs * jnp.mean(upstream * outputs, axis=2, keepdims=True)
    ) / head_scale
    delta_low = key_delta.reshape(receive, local_cols).astype(jnp.bfloat16)
    part_delta = lax.dot_general(
        delta_low, full_weight, (((1,), (1,)), ((), ())), preferred_element_type=jnp.float32
    )
    rounded = lax.optimization_barrier(part_delta.astype(jnp.bfloat16)).astype(jnp.float32)
    feature_delta = lax.psum_scatter(
        rounded.astype(jnp.bfloat16), "mp", scatter_dimension=1, tiled=True
    )
    weight_sum = lax.psum_scatter(
        lax.dot_general(
            hidden, delta_low, (((0,), (0,)), ((), ())), preferred_element_type=jnp.float32
        ),
        "dp",
        scatter_dimension=0,
        tiled=True,
    )
    key_grad = weight_sum / math.sqrt(row_count * dp_size)
    return (feature_delta, key_grad)


CORE, X, Y = 1, 2, 4
PLANE = 8
PLANE_MASKS = (0, X, Y, X | Y)


def swap(value, mask):
    size = lax.axis_size("dp")
    return lax.ppermute(value, "dp", [(i, i ^ mask) for i in range(size)])


def after(value, *others):
    return lax.optimization_barrier((value, *others))[0]


def dot(a, b, dims):
    return lax.dot_general(a, b, (dims, ((), ())), preferred_element_type=jnp.float32)


def fetch(pairs, sems):
    copies = [
        pltpu.make_async_copy(source, target, sems.at[n])
        for n, (source, target) in enumerate(pairs)
    ]
    for copy in copies:
        copy.start()
    return copies


def delta_kernel(chips_ref, me_ref, own_cot_ref, mate_cot_ref, own_ref, mate_ref, *refs):
    *pieces, delta_ref, weight_ref, held, weights, acc, sems = refs
    core = me_ref[0] & 1
    rows = own_ref.shape[0]
    depth = pieces[0].shape[0]
    count = len(pieces)

    def rows_of(ref, n):
        return ref.at[n * depth : (n + 1) * depth, :]

    pairs = [(own_ref, held.at[0]), (mate_ref, held.at[1])]
    pairs += [(ref, rows_of(weights, n)) for n, ref in enumerate(pieces)]
    copies = fetch(pairs, sems)
    for copy in copies[:2]:
        copy.wait()
    kept = []
    for n in range(count):
        copies[2 + n].wait()
        out = pltpu.make_async_copy(
            rows_of(weights, n), rows_of(weight_ref, n), sems.at[2 + count + n]
        )
        out.start()
        kept.append(out)
        piece = rows_of(weights, n)[...]
        at = pl.multiple_of(chips_ref[n] * depth, depth)
        for side in range(2):
            part = dot(held[side, :, pl.ds(at, depth)], piece, ((1,), (0,)))
            if n == 0:
                acc[side] = part
            else:
                acc[side] += part
    delta_ref[2 * rows :, :] = jnp.zeros_like(delta_ref[2 * rows :, :])
    for side, cot_ref in enumerate((own_cot_ref, mate_cot_ref)):
        at = pl.multiple_of((core ^ side) * rows, rows)
        for head in range(own_cot_ref.shape[1] // HEAD_DIM):
            cols = slice(head * HEAD_DIM, (head + 1) * HEAD_DIM)
            proj = acc[side, :, cols]
            scale = jnp.sqrt(jnp.mean(proj * proj, axis=1, keepdims=True) + epsilon)
            normed = proj / scale
            upstream = cot_ref[:rows, cols].astype(jnp.float32)
            delta = (upstream - normed * jnp.mean(upstream * normed, axis=1, keepdims=True)) / scale
            delta_ref[pl.ds(at, rows), cols] = delta.astype(jnp.bfloat16)
        delta_ref[2 * rows :, pl.ds(at, rows)] = cot_ref[rows:, :rows]
    for copy in kept:
        copy.wait()


def select_kernel(me_ref, *refs):
    deltas, sent, (held, sems) = refs[:4], refs[4:8], refs[8:]
    copies = fetch([(ref, held.at[n]) for n, ref in enumerate(deltas)], sems)
    for copy in copies:
        copy.wait()
    rows = (held.shape[1] - CODE_ROWS) // 2
    per_core = sent[0].shape[0] // 2
    per_chip = per_core // len(deltas)
    iota = lax.broadcasted_iota(jnp.int32, (2 * per_core, 2 * rows), 0)
    core = (iota >= per_core).astype(jnp.int32)
    slot = iota - core * per_core
    for out_ref, mask in zip(sent, PLANE_MASKS):
        total = None
        for n in range(len(deltas)):
            code = held[n, 2 * rows :, : 2 * rows].astype(jnp.float32).astype(jnp.int32)
            want = code[0:1, :] - ((me_ref[0] ^ mask) & -2)
            hot = (core == want) & (slot == code[1:2, :] + n * per_chip)
            part = dot(hot.astype(jnp.bfloat16), held[n, : 2 * rows, :], ((1,), (0,)))
            total = part if total is None else total + part
        out_ref[...] = total.astype(jnp.bfloat16)


def share_kernel(me_ref, *refs):
    got, (keep_ref, give_ref) = refs[:4], refs[4:]
    count = keep_ref.shape[1]
    core = me_ref[0] & 1
    for n, ref in enumerate(got):
        keep_ref[n] = ref[pl.ds(pl.multiple_of(core * count, count), count), :]
        give_ref[n] = ref[pl.ds(pl.multiple_of((1 - core) * count, count), count), :]


def weight_grad_kernel(me_ref, own_ref, mate_ref, *refs):
    *deltas, part_ref, hidden, held, acc, sems = refs
    plane = lax.shift_right_logical(me_ref[0], 3)
    core = me_ref[0] & 1
    rows = own_ref.shape[1]
    pairs = []
    for n, ref in enumerate(deltas):
        pairs += [
            (own_ref.at[plane ^ n], hidden.at[n, 0]),
            (mate_ref.at[plane ^ n], hidden.at[n, 1]),
            (ref, held.at[n]),
        ]
    copies = fetch(pairs, sems)
    for n in range(len(deltas)):
        for copy in copies[3 * n : 3 * n + 3]:
            copy.wait()
        for side in range(2):
            at = pl.multiple_of((core ^ side) * rows, rows)
            part = dot(hidden[n, side], held[n, pl.ds(at, rows), :], ((0,), (0,)))
            if n + side == 0:
                acc[...] = part
            else:
                acc[...] += part
    part_ref[...] = acc[...].astype(jnp.bfloat16)


def sum_kernel(norm, parts_ref, grad_ref):
    half = parts_ref.shape[3]
    for side in range(2):
        total = parts_ref[0, side].astype(jnp.float32)
        for chip in range(1, parts_ref.shape[0]):
            total += parts_ref[chip, side].astype(jnp.float32)
        grad_ref[:, side * half : (side + 1) * half] = total / norm


def row_grad_kernel(chips_ref, me_ref, own_got_ref, mate_got_ref, *refs):
    own_weight_ref, mate_weight_ref, out_ref, rows_ref, held = refs
    step = pl.program_id(0)
    chips, count, half = own_got_ref.shape
    block = count // 4
    level = lax.shift_right_logical(me_ref[0], 3)

    @pl.when(step == 0)
    def _():
        for side, got_ref in enumerate((own_got_ref, mate_got_ref)):
            for chip, mask in enumerate(PLANE_MASKS):
                place = lax.shift_right_logical((me_ref[0] ^ mask) & 6, 1)
                for n in range(4):
                    at = pl.multiple_of(((level ^ n) * chips + place) * block, block)
                    rows = got_ref[chip, n * block : (n + 1) * block, :]
                    held[pl.ds(at, block), :] = rows.astype(jnp.float32)
            rows_ref[side] = held[...].T.astype(jnp.bfloat16)

    depth = half // 2
    for n in range(own_weight_ref.shape[0] // depth):
        part = slice(n * depth, (n + 1) * depth)
        total = dot(own_weight_ref[part, :], rows_ref[0], ((1,), (0,)))
        total += dot(mate_weight_ref[part, :], rows_ref[1], ((1,), (0,)))
        at = chips_ref[own_weight_ref.shape[0] // depth * step + n] * depth
        out_ref[:, pl.ds(pl.multiple_of(at, depth), depth)] = total.T.astype(jnp.bfloat16)


def code_rows(destination, core, per_peer, width):
    positions = jnp.arange(destination.shape[0], dtype=jnp.int32)
    same = (destination[:, None] == destination[None, :]) & (
        positions[:, None] < positions[None, :]
    )
    earlier = jnp.sum(same.astype(jnp.int32), axis=0)
    codes = jnp.stack([destination, core * per_peer + earlier]).astype(jnp.bfloat16)
    return jnp.pad(codes, ((0, CODE_ROWS - 2), (0, width - destination.shape[0])))


def anywhere(count):
    return [pl.BlockSpec(memory_space=pl.ANY)] * count


def vmem(count):
    return [pl.BlockSpec(memory_space=pltpu.VMEM)] * count


def anywhere(count):
    return [pl.BlockSpec(memory_space=pl.ANY)] * count


SCALAR = pl.BlockSpec(memory_space=pltpu.SMEM)
PARAMS = pltpu.CompilerParams(vmem_limit_bytes=VMEM_LIMIT)


def per_device_paired(tokens, key_cot, routes, counts, widths, key_weight):
    rows, width_model = tokens.shape
    cols = key_cot.shape[1]
    half_cols = cols // 2
    size = lax.axis_size("dp")
    chips = size // 2
    levels = size // PLANE
    per_peer = 2 * rows // size
    receive = size * per_peer
    wide = width_model // levels
    me = lax.axis_index("dp")
    core = me % 2
    me_scalar = me.astype(jnp.int32).reshape(1)

    def mine(value):
        return lax.dynamic_slice_in_dim(value, core * half_cols, half_cols, 1)

    def theirs(value):
        return lax.dynamic_slice_in_dim(value, (1 - core) * half_cols, half_cols, 1)

    mate_shard = swap(key_weight, CORE)
    piece = jnp.where(
        core == 0,
        jnp.concatenate([key_weight[:, :half_cols], mate_shard[:, :half_cols]], axis=0),
        jnp.concatenate([mate_shard[:, half_cols:], key_weight[:, half_cols:]], axis=0),
    )
    near, far, both = PLANE, 2 * PLANE, 3 * PLANE
    have = {0: piece}

    def after_round(**beside):
        names, masks = list(beside), list(have)
        values = lax.optimization_barrier([*beside.values(), *have.values()])
        have.update(zip(masks, values[len(names) :]))
        return values[: len(names)]

    mate_tokens = swap(tokens, CORE)
    have.update(
        {
            far: swap(piece, far),
            near: swap(piece, near),
            X: swap(piece, X),
            Y: swap(piece, Y),
        }
    )
    mate_tokens, key_cot, counts, routes = after_round(
        mate_tokens=mate_tokens, key_cot=key_cot, counts=counts, routes=routes
    )
    have.update(
        {
            near | X: swap(have[near], X),
            near | Y: swap(have[near], Y),
            far | X: swap(have[far], X),
            far | Y: swap(have[far], Y),
            both: swap(have[far], near),
        }
    )
    bounds = jnp.cumsum(counts[0])
    positions = jnp.arange(rows, dtype=jnp.int32)
    subnet = jnp.sum((positions[:, None] >= bounds[None, : NSUB - 1]).astype(jnp.int32), axis=1)
    subnet_match = subnet[:, None] == jnp.arange(NSUB, dtype=jnp.int32)[None, :]
    row_width = jnp.sum(jnp.where(subnet_match, widths[None, :], 0), axis=1)
    head_of_col = jnp.arange(cols, dtype=jnp.int32) // HEAD_DIM
    upstream = jnp.where(
        head_of_col[None, :] < row_width[:, None], key_cot, jnp.zeros_like(key_cot)
    )
    codes = code_rows(routes[:, 0], core, per_peer, half_cols)
    own_cot = jnp.concatenate([mine(upstream), codes], axis=0)

    late_tokens, own_cot, give_cot = after_round(
        tokens=tokens,
        own_cot=own_cot,
        give_cot=jnp.concatenate([theirs(upstream), codes], axis=0),
    )
    columns = [[p + PLANE * z for z in range(levels)] for p in range(PLANE)]
    own_features = lax.all_to_all(
        jnp.stack([late_tokens[:, z * wide : (z + 1) * wide] for z in range(levels)]),
        "dp",
        split_axis=0,
        concat_axis=0,
        axis_index_groups=columns,
        tiled=True,
    )
    have.update(
        {
            both | X: swap(have[both], X),
            both | Y: swap(have[both], Y),
            X | Y: swap(have[Y], X),
            far | X | Y: swap(have[far | X], Y),
        }
    )
    mate_cot = swap(give_cot, CORE)
    mate_cot, own_cot = after_round(mate_cot=mate_cot, own_cot=own_cot)
    have.update(
        {
            near | X | Y: swap(have[near | Y], X),
            both | X | Y: swap(have[both | X], Y),
        }
    )
    mate_cot, own_cot, own_features = after_round(
        mate_cot=mate_cot, own_cot=own_cot, own_features=own_features
    )
    mate_features = swap(own_features, CORE)

    masks = sorted(have)
    order = jnp.stack([lax.shift_right_logical(me ^ mask, 1) for mask in masks])
    kept = jax.ShapeDtypeStruct((width_model, half_cols), jnp.bfloat16)
    delta, own_half = pl.pallas_call(
        delta_kernel,
        out_shape=(jax.ShapeDtypeStruct((2 * rows + CODE_ROWS, half_cols), jnp.bfloat16), kept),
        in_specs=[SCALAR] * 2 + vmem(2) + anywhere(2 + len(masks)),
        out_specs=(vmem(1)[0], anywhere(1)[0]),
        scratch_shapes=[
            pltpu.VMEM((2, rows, width_model), jnp.bfloat16),
            pltpu.VMEM(kept.shape, jnp.bfloat16),
            pltpu.VMEM((2, rows, half_cols), jnp.float32),
            pltpu.SemaphoreType.DMA((2 + 2 * len(masks),)),
        ],
        compiler_params=PARAMS,
        name="delta",
    )(
        order,
        me_scalar,
        own_cot,
        mate_cot,
        tokens,
        mate_tokens,
        *[have[mask] for mask in masks],
    )

    deltas = [delta, *(swap(delta, mask) for mask in (near, far, both))]
    mate_half = swap(after(own_half, *deltas[1:]), CORE)
    count = levels * 2 * per_peer
    delta_room = pltpu.VMEM((levels, *delta.shape), jnp.bfloat16)
    selected = pl.pallas_call(
        select_kernel,
        out_shape=[jax.ShapeDtypeStruct((2 * count, half_cols), jnp.bfloat16)] * 4,
        in_specs=[SCALAR] + anywhere(levels),
        out_specs=vmem(4),
        scratch_shapes=[delta_room, pltpu.SemaphoreType.DMA((levels,))],
        compiler_params=PARAMS,
        name="select",
    )(me_scalar, *deltas)
    got = [
        swap(value, mask) if mask else value for value, mask in zip(selected, PLANE_MASKS)
    ]
    shard = width_model // size
    terms = pl.pallas_call(
        weight_grad_kernel,
        out_shape=jax.ShapeDtypeStruct((wide, half_cols), jnp.bfloat16),
        in_specs=[SCALAR] + anywhere(2 + levels),
        out_specs=vmem(1)[0],
        scratch_shapes=[
            pltpu.VMEM((levels, 2, rows, wide), jnp.bfloat16),
            delta_room,
            pltpu.VMEM((wide, half_cols), jnp.float32),
            pltpu.SemaphoreType.DMA((3 * levels,)),
        ],
        compiler_params=PARAMS,
        name="weight_grad",
    )(me_scalar, own_features, mate_features, after(delta, *selected), *deltas[1:])
    parts = lax.all_to_all(
        terms.reshape(PLANE, shard, half_cols),
        "dp",
        split_axis=0,
        concat_axis=0,
        axis_index_groups=[[z * PLANE + p for p in range(PLANE)] for z in range(levels)],
        tiled=True,
    ).reshape(PLANE // 2, 2, shard, half_cols)

    own_got, give_got = pl.pallas_call(
        share_kernel,
        out_shape=[jax.ShapeDtypeStruct((4, count, half_cols), jnp.bfloat16)] * 2,
        in_specs=[SCALAR] + vmem(4),
        out_specs=vmem(2),
        compiler_params=PARAMS,
        name="share",
    )(me_scalar, after(got[0], terms), *got[1:])
    mate_got = swap(give_got, CORE)

    depth = width_model // 4
    row_grads = pl.pallas_call(
        row_grad_kernel,
        out_shape=jax.ShapeDtypeStruct((receive, width_model), jnp.bfloat16),
        grid_spec=pltpu.PrefetchScalarGridSpec(
            num_scalar_prefetch=2,
            grid=(width_model // depth,),
            in_specs=[pl.BlockSpec(own_got.shape, lambda i, *_: (0, 0, 0))] * 2
            + [pl.BlockSpec((depth, half_cols), lambda i, *_: (i, 0))] * 2,
            out_specs=pl.BlockSpec((receive, width_model), lambda i, *_: (0, 0)),
            scratch_shapes=[
                pltpu.VMEM((2, half_cols, receive), jnp.bfloat16),
                pltpu.VMEM((receive, half_cols), jnp.float32),
            ],
        ),
        compiler_params=PARAMS,
        name="row_grad",
    )(order, me_scalar, own_got, mate_got, own_half, mate_half)

    key_grad = pl.pallas_call(
        functools.partial(sum_kernel, math.sqrt(rows * size)),
        out_shape=jax.ShapeDtypeStruct((shard, cols), jnp.float32),
        in_specs=vmem(1),
        out_specs=vmem(1)[0],
        compiler_params=PARAMS,
        name="sum",
    )(after(parts, row_grads))
    return (row_grads, key_grad)


def solution(mesh):
    size, split = mesh.shape["dp"], mesh.shape["mp"]
    paired = split == 1 and size == 32
    return jax.shard_map(
        per_device_paired if paired else per_device_general,
        mesh=mesh,
        in_specs=(P("dp", None), P("dp", "mp"), P("dp", None), P("dp", None), P(), P("dp", "mp")),
        out_specs=(P("dp", "mp"), P("dp", "mp")),
        check_vma=False,
    )
```

```python
import functools
import math

import jax
import jax.numpy as jnp
from jax import lax
from jax.experimental import pallas as pl
from jax.experimental.pallas import tpu as pltpu
from jax.sharding import PartitionSpec as P

HEAD_DIM = 128
NSUB = 4
VMEM_LIMIT = 60 * 1024 * 1024
CODE_ROWS = 16
epsilon = 1e-06


def per_device_general(tokens, key_cot, routes, counts, widths, key_weight):
    row_count = tokens.shape[0]
    width_model = tokens.shape[1]
    local_cols = key_cot.shape[1]
    local_heads = local_cols // HEAD_DIM
    dp_size = lax.axis_size("dp")
    per_peer = 2 * row_count // dp_size
    receive = dp_size * per_peer
    destination = routes[:, 0]
    one_hot = (destination[:, None] == jnp.arange(dp_size, dtype=jnp.int32)[None, :]).astype(
        jnp.int32
    )
    earlier = jnp.sum(jnp.cumsum(one_hot, axis=0) * one_hot, axis=1) - 1
    send_slot = destination * per_peer + earlier
    bounds = jnp.cumsum(counts[0])
    positions = jnp.arange(row_count, dtype=jnp.int32)
    subnet = jnp.sum((positions[:, None] >= bounds[None, : NSUB - 1]).astype(jnp.int32), axis=1)
    send_subnet = (
        jnp.full((receive,), -1, jnp.int32).at[send_slot].set(subnet).reshape(dp_size, per_peer)
    )
    send_cot = jnp.zeros((receive, local_cols), jnp.bfloat16).at[send_slot].set(key_cot)
    send_cot = send_cot.reshape(dp_size, per_peer, local_cols)
    send_tokens = jnp.zeros((receive, width_model), jnp.bfloat16).at[send_slot].set(tokens)
    send_tokens = send_tokens.reshape(dp_size, per_peer, width_model)
    got_tokens, got_cot, got_subnet = (
        lax.all_to_all(send_tokens, "dp", split_axis=0, concat_axis=0, tiled=True),
        lax.all_to_all(send_cot, "dp", split_axis=0, concat_axis=0, tiled=True),
        lax.all_to_all(send_subnet, "dp", split_axis=0, concat_axis=0, tiled=True),
    )
    hidden = got_tokens.reshape(receive, width_model)
    got_cot = got_cot.reshape(receive, local_cols)
    got_subnet = got_subnet.reshape(receive)
    full_weight = lax.all_gather(key_weight, "dp", axis=0, tiled=True)
    key_proj = jnp.dot(hidden, full_weight, preferred_element_type=jnp.float32)
    per_head = key_proj.reshape(receive, local_heads, HEAD_DIM)
    head_scale = jnp.sqrt(jnp.mean(per_head * per_head, axis=2, keepdims=True) + epsilon)
    outputs = per_head / head_scale
    subnet_match = got_subnet[:, None] == jnp.arange(NSUB, dtype=jnp.int32)[None, :]
    row_width = jnp.sum(jnp.where(subnet_match, widths[None, :], 0), axis=1)
    head_index = lax.axis_index("mp") * local_heads + jnp.arange(local_heads, dtype=jnp.int32)
    head_mask = (head_index[None, :] < row_width[:, None]).astype(jnp.float32)
    upstream = (
        got_cot.astype(jnp.float32).reshape(receive, local_heads, HEAD_DIM) * head_mask[:, :, None]
    )
    key_delta = (
        upstream - outputs * jnp.mean(upstream * outputs, axis=2, keepdims=True)
    ) / head_scale
    delta_low = key_delta.reshape(receive, local_cols).astype(jnp.bfloat16)
    part_delta = lax.dot_general(
        delta_low, full_weight, (((1,), (1,)), ((), ())), preferred_element_type=jnp.float32
    )
    rounded = lax.optimization_barrier(part_delta.astype(jnp.bfloat16)).astype(jnp.float32)
    feature_delta = lax.psum_scatter(
        rounded.astype(jnp.bfloat16), "mp", scatter_dimension=1, tiled=True
    )
    weight_sum = lax.psum_scatter(
        lax.dot_general(
            hidden, delta_low, (((0,), (0,)), ((), ())), preferred_element_type=jnp.float32
        ),
        "dp",
        scatter_dimension=0,
        tiled=True,
    )
    key_grad = weight_sum / math.sqrt(row_count * dp_size)
    return (feature_delta, key_grad)


CORE, X, Y = 1, 2, 4
PLANE = 8
PLANE_MASKS = (0, X, Y, X | Y)


def swap(value, mask):
    size = lax.axis_size("dp")
    return lax.ppermute(value, "dp", [(i, i ^ mask) for i in range(size)])


def after(value, *others):
    return lax.optimization_barrier((value, *others))[0]


def dot(a, b, dims):
    return lax.dot_general(a, b, (dims, ((), ())), preferred_element_type=jnp.float32)


def fetch(pairs, sems):
    copies = [
        pltpu.make_async_copy(source, target, sems.at[n])
        for n, (source, target) in enumerate(pairs)
    ]
    for copy in copies:
        copy.start()
    return copies


def project_kernel(begin, chips_ref, own_ref, mate_ref, *refs):
    begun = None
    if begin:
        begun, *refs = refs
    *pieces, weight_ref, acc, held, weights, sems = refs
    depth = pieces[0].shape[0]
    count = len(pieces)

    def rows_of(ref, n):
        return ref.at[n * depth : (n + 1) * depth, :]

    pairs = []
    for n, ref in enumerate(pieces):
        at = pl.multiple_of(chips_ref[begin + n] * depth, depth)
        pairs += [
            (ref, rows_of(weights, n)),
            (own_ref.at[:, pl.ds(at, depth)], held.at[n, 0]),
            (mate_ref.at[:, pl.ds(at, depth)], held.at[n, 1]),
        ]
    copies = fetch(pairs, sems)
    if begin:
        acc[...] = begun[...]
    kept = []
    for n in range(count):
        for copy in copies[3 * n : 3 * n + 3]:
            copy.wait()
        out = pltpu.make_async_copy(
            rows_of(weights, n), rows_of(weight_ref, n), sems.at[3 * count + n]
        )
        out.start()
        kept.append(out)
        piece = rows_of(weights, n)[...]
        for side in range(2):
            part = dot(held[n, side], piece, ((1,), (0,)))
            if begin + n == 0:
                acc[side] = part
            else:
                acc[side] += part
    return kept


def first_project_kernel(*refs):
    for copy in project_kernel(0, *refs):
        copy.wait()


def delta_kernel(begin, chips_ref, me_ref, own_cot_ref, mate_cot_ref, *refs):
    *refs, delta_ref, weight_ref, acc, held, weights, sems = refs
    kept = project_kernel(begin, chips_ref, *refs, weight_ref, acc, held, weights, sems)
    core = me_ref[0] & 1
    rows = acc.shape[1]
    delta_ref[2 * rows :, :] = jnp.zeros_like(delta_ref[2 * rows :, :])
    for side, cot_ref in enumerate((own_cot_ref, mate_cot_ref)):
        at = pl.multiple_of((core ^ side) * rows, rows)
        for head in range(own_cot_ref.shape[1] // HEAD_DIM):
            cols = slice(head * HEAD_DIM, (head + 1) * HEAD_DIM)
            proj = acc[side, :, cols]
            scale = jnp.sqrt(jnp.mean(proj * proj, axis=1, keepdims=True) + epsilon)
            normed = proj / scale
            upstream = cot_ref[:rows, cols].astype(jnp.float32)
            delta = (upstream - normed * jnp.mean(upstream * normed, axis=1, keepdims=True)) / scale
            delta_ref[pl.ds(at, rows), cols] = delta.astype(jnp.bfloat16)
        delta_ref[2 * rows :, pl.ds(at, rows)] = cot_ref[rows:, :rows]
    for copy in kept:
        copy.wait()


def select_kernel(me_ref, *refs):
    deltas, sent, (held, sems) = refs[:4], refs[4:8], refs[8:]
    copies = fetch([(ref, held.at[n]) for n, ref in enumerate(deltas)], sems)
    for copy in copies:
        copy.wait()
    rows = (held.shape[1] - CODE_ROWS) // 2
    per_core = sent[0].shape[0] // 2
    per_chip = per_core // len(deltas)
    iota = lax.broadcasted_iota(jnp.int32, (2 * per_core, 2 * rows), 0)
    core = (iota >= per_core).astype(jnp.int32)
    slot = iota - core * per_core
    for out_ref, mask in zip(sent, PLANE_MASKS):
        total = None
        for n in range(len(deltas)):
            code = held[n, 2 * rows :, : 2 * rows].astype(jnp.float32).astype(jnp.int32)
            want = code[0:1, :] - ((me_ref[0] ^ mask) & -2)
            hot = (core == want) & (slot == code[1:2, :] + n * per_chip)
            part = dot(hot.astype(jnp.bfloat16), held[n, : 2 * rows, :], ((1,), (0,)))
            total = part if total is None else total + part
        out_ref[...] = total.astype(jnp.bfloat16)


def share_kernel(me_ref, *refs):
    got, (keep_ref, give_ref) = refs[:4], refs[4:]
    count = keep_ref.shape[1]
    core = me_ref[0] & 1
    for n, ref in enumerate(got):
        keep_ref[n] = ref[pl.ds(pl.multiple_of(core * count, count), count), :]
        give_ref[n] = ref[pl.ds(pl.multiple_of((1 - core) * count, count), count), :]


def weight_grad_kernel(me_ref, own_ref, mate_ref, *refs):
    *deltas, part_ref, hidden, held, acc, sems = refs
    plane = lax.shift_right_logical(me_ref[0], 3)
    core = me_ref[0] & 1
    rows = own_ref.shape[1]
    pairs = []
    for n, ref in enumerate(deltas):
        own = pl.multiple_of((2 * n + core) * rows, rows)
        mate = pl.multiple_of((2 * n + 1 - core) * rows, rows)
        pairs += [
            (own_ref.at[plane ^ n], hidden.at[pl.ds(own, rows), :]),
            (mate_ref.at[plane ^ n], hidden.at[pl.ds(mate, rows), :]),
            (ref.at[: 2 * rows, :], held.at[2 * n * rows : 2 * (n + 1) * rows, :]),
        ]
    copies = fetch(pairs, sems)
    for first in (0, 2):
        for copy in copies[3 * first : 3 * first + 6]:
            copy.wait()
        part = slice(2 * first * rows, 2 * (first + 2) * rows)
        terms = dot(hidden[part, :], held[part, :], ((0,), (0,)))
        if first == 0:
            acc[...] = terms
        else:
            part_ref[...] = (acc[...] + terms).astype(jnp.bfloat16)


def sum_kernel(norm, parts_ref, grad_ref, held, sems):
    chips, _, _, half = parts_ref.shape
    copies = fetch(
        [(parts_ref.at[n // 2, n % 2], held.at[n]) for n in range(2 * chips)], sems
    )
    for copy in copies:
        copy.wait()
    for side in range(2):
        total = held[side].astype(jnp.float32)
        for chip in range(1, chips):
            total += held[2 * chip + side].astype(jnp.float32)
        grad_ref[:, side * half : (side + 1) * half] = total / norm


def row_grad_kernel(chips_ref, me_ref, own_got_ref, mate_got_ref, *refs):
    *weights, out_ref, rows_ref, held = refs
    step = pl.program_id(0)
    chips, count, half = own_got_ref.shape
    block = count // 4
    level = lax.shift_right_logical(me_ref[0], 3)

    @pl.when(step == 0)
    def _():
        for side, got_ref in enumerate((own_got_ref, mate_got_ref)):
            for chip, mask in enumerate(PLANE_MASKS):
                place = lax.shift_right_logical((me_ref[0] ^ mask) & 6, 1)
                for n in range(4):
                    at = pl.multiple_of(((level ^ n) * chips + place) * block, block)
                    rows = got_ref[chip, n * block : (n + 1) * block, :]
                    held[pl.ds(at, block), :] = rows.astype(jnp.float32)
            rows_ref[side] = held[...].T.astype(jnp.bfloat16)

    depth = half // 2

    def add(own_ref, mate_ref, begin):
        for n in range(own_ref.shape[0] // depth):
            part = slice(n * depth, (n + 1) * depth)
            total = dot(own_ref[part, :], rows_ref[0], ((1,), (0,)))
            total += dot(mate_ref[part, :], rows_ref[1], ((1,), (0,)))
            at = pl.multiple_of(chips_ref[begin + n] * depth, depth)
            out_ref[:, pl.ds(at, depth)] = total.T.astype(jnp.bfloat16)

    per_step = weights[0].shape[0] // depth
    add(*weights[:2], step * per_step)

    @pl.when(step == pl.num_programs(0) - 1)
    def _():
        add(*weights[2:], pl.num_programs(0) * per_step)


def code_rows(destination, core, per_peer, width):
    positions = jnp.arange(destination.shape[0], dtype=jnp.int32)
    same = (destination[:, None] == destination[None, :]) & (
        positions[:, None] < positions[None, :]
    )
    earlier = jnp.sum(same.astype(jnp.int32), axis=0)
    codes = jnp.stack([destination, core * per_peer + earlier]).astype(jnp.bfloat16)
    return jnp.pad(codes, ((0, CODE_ROWS - 2), (0, width - destination.shape[0])))


def anywhere(count):
    return [pl.BlockSpec(memory_space=pl.ANY)] * count


def vmem(count):
    return [pl.BlockSpec(memory_space=pltpu.VMEM)] * count


def anywhere(count):
    return [pl.BlockSpec(memory_space=pl.ANY)] * count


SCALAR = pl.BlockSpec(memory_space=pltpu.SMEM)
PARAMS = pltpu.CompilerParams(vmem_limit_bytes=VMEM_LIMIT)


def per_device_paired(tokens, key_cot, routes, counts, widths, key_weight):
    rows, width_model = tokens.shape
    cols = key_cot.shape[1]
    half_cols = cols // 2
    size = lax.axis_size("dp")
    chips = size // 2
    levels = size // PLANE
    per_peer = 2 * rows // size
    receive = size * per_peer
    wide = width_model // levels
    me = lax.axis_index("dp")
    core = me % 2
    me_scalar = me.astype(jnp.int32).reshape(1)

    def mine(value):
        return lax.dynamic_slice_in_dim(value, core * half_cols, half_cols, 1)

    def theirs(value):
        return lax.dynamic_slice_in_dim(value, (1 - core) * half_cols, half_cols, 1)

    mate_shard = swap(key_weight, CORE)
    piece = jnp.where(
        core == 0,
        jnp.concatenate([key_weight[:, :half_cols], mate_shard[:, :half_cols]], axis=0),
        jnp.concatenate([mate_shard[:, half_cols:], key_weight[:, half_cols:]], axis=0),
    )
    near, far, both = PLANE, 2 * PLANE, 3 * PLANE
    have = {0: piece}

    def after_round(**beside):
        names, masks = list(beside), list(have)
        values = lax.optimization_barrier([*beside.values(), *have.values()])
        have.update(zip(masks, values[len(names) :]))
        return values[: len(names)]

    mate_tokens = swap(after(tokens, mate_shard), CORE)
    have.update(
        {
            Y: swap(piece, Y),
            X: swap(piece, X),
            near: swap(piece, near),
            far: swap(piece, far),
        }
    )
    mate_tokens, key_cot, counts, routes = after_round(
        mate_tokens=mate_tokens, key_cot=key_cot, counts=counts, routes=routes
    )
    have.update(
        {
            near | X: swap(have[near], X),
            near | Y: swap(have[near], Y),
            far | X: swap(have[far], X),
            far | Y: swap(have[far], Y),
            both: swap(have[far], near),
        }
    )
    bounds = jnp.cumsum(counts[0])
    positions = jnp.arange(rows, dtype=jnp.int32)
    subnet = jnp.sum((positions[:, None] >= bounds[None, : NSUB - 1]).astype(jnp.int32), axis=1)
    subnet_match = subnet[:, None] == jnp.arange(NSUB, dtype=jnp.int32)[None, :]
    row_width = jnp.sum(jnp.where(subnet_match, widths[None, :], 0), axis=1)
    head_of_col = jnp.arange(cols, dtype=jnp.int32) // HEAD_DIM
    upstream = jnp.where(
        head_of_col[None, :] < row_width[:, None], key_cot, jnp.zeros_like(key_cot)
    )
    codes = code_rows(routes[:, 0], core, per_peer, half_cols)
    own_cot = jnp.concatenate([mine(upstream), codes], axis=0)

    late_tokens, own_cot, give_cot = after_round(
        tokens=tokens,
        own_cot=own_cot,
        give_cot=jnp.concatenate([theirs(upstream), codes], axis=0),
    )
    columns = [[p + PLANE * z for z in range(levels)] for p in range(PLANE)]
    own_features = lax.all_to_all(
        jnp.stack([late_tokens[:, z * wide : (z + 1) * wide] for z in range(levels)]),
        "dp",
        split_axis=0,
        concat_axis=0,
        axis_index_groups=columns,
        tiled=True,
    )
    have.update(
        {
            both | X: swap(have[both], X),
            both | Y: swap(have[both], Y),
            X | Y: swap(have[Y], X),
            far | X | Y: swap(have[far | X], Y),
        }
    )
    mate_cot = swap(give_cot, CORE)
    mate_cot, own_cot = after_round(mate_cot=mate_cot, own_cot=own_cot)
    first_masks = list(have)
    last_masks = [near | X | Y, both | X | Y]
    order = jnp.stack([lax.shift_right_logical(me ^ mask, 1) for mask in first_masks + last_masks])
    depth = width_model // chips
    sums = jax.ShapeDtypeStruct((2, rows, half_cols), jnp.float32)

    def project(kernel, count, results, inputs, specs, name):
        return pl.pallas_call(
            kernel,
            out_shape=(*results, jax.ShapeDtypeStruct((count * depth, half_cols), jnp.bfloat16))
            + ((sums,) if name == "project" else ()),
            in_specs=specs + anywhere(count),
            out_specs=(*vmem(len(results)), anywhere(1)[0])
            + (tuple(vmem(1)) if name == "project" else ()),
            scratch_shapes=([] if name == "project" else [pltpu.VMEM(sums.shape, sums.dtype)])
            + [
                pltpu.VMEM((count, 2, rows, depth), jnp.bfloat16),
                pltpu.VMEM((count * depth, half_cols), jnp.bfloat16),
                pltpu.SemaphoreType.DMA((4 * count,)),
            ],
            compiler_params=PARAMS,
            name=name,
        )(*inputs)

    first_weight, begun = project(
        first_project_kernel,
        len(first_masks),
        (),
        (order, tokens, mate_tokens, *[have[mask] for mask in first_masks]),
        [SCALAR] + anywhere(2),
        "project",
    )
    have.update(
        {
            near | X | Y: swap(have[near | Y], X),
            both | X | Y: swap(have[both | X], Y),
        }
    )
    mate_cot, own_cot, own_features, begun, first_weight = after_round(
        mate_cot=mate_cot,
        own_cot=own_cot,
        own_features=own_features,
        begun=begun,
        first_weight=first_weight,
    )
    mate_features = swap(own_features, CORE)
    delta, last_weight = project(
        functools.partial(delta_kernel, len(first_masks)),
        len(last_masks),
        (jax.ShapeDtypeStruct((2 * rows + CODE_ROWS, half_cols), jnp.bfloat16),),
        (
            order,
            me_scalar,
            own_cot,
            mate_cot,
            tokens,
            mate_tokens,
            begun,
            *[have[mask] for mask in last_masks],
        ),
        [SCALAR] * 2 + vmem(2) + anywhere(2) + vmem(1),
        "delta",
    )

    deltas = [delta, *(swap(delta, mask) for mask in (near, far, both))]
    mate_features, first_weight, last_weight, *deltas[1:] = lax.optimization_barrier(
        (mate_features, first_weight, last_weight, *deltas[1:])
    )
    mate_first, mate_last = swap(first_weight, CORE), swap(last_weight, CORE)
    count = levels * 2 * per_peer
    delta_room = pltpu.VMEM((levels, *delta.shape), jnp.bfloat16)
    selected = pl.pallas_call(
        select_kernel,
        out_shape=[jax.ShapeDtypeStruct((2 * count, half_cols), jnp.bfloat16)] * 4,
        in_specs=[SCALAR] + anywhere(levels),
        out_specs=vmem(4),
        scratch_shapes=[delta_room, pltpu.SemaphoreType.DMA((levels,))],
        compiler_params=PARAMS,
        name="select",
    )(me_scalar, *deltas)
    got = [
        swap(value, mask) if mask else value for value, mask in zip(selected, PLANE_MASKS)
    ]
    shard = width_model // size
    terms = pl.pallas_call(
        weight_grad_kernel,
        out_shape=jax.ShapeDtypeStruct((wide, half_cols), jnp.bfloat16),
        in_specs=[SCALAR] + anywhere(2 + levels),
        out_specs=vmem(1)[0],
        scratch_shapes=[
            pltpu.VMEM((levels * 2 * rows, wide), jnp.bfloat16),
            pltpu.VMEM((levels * 2 * rows, half_cols), jnp.bfloat16),
            pltpu.VMEM((wide, half_cols), jnp.float32),
            pltpu.SemaphoreType.DMA((3 * levels,)),
        ],
        compiler_params=PARAMS,
        name="weight_grad",
    )(me_scalar, own_features, mate_features, after(delta, *selected), *deltas[1:])
    parts = lax.all_to_all(
        after(terms, *got).reshape(PLANE, shard, half_cols),
        "dp",
        split_axis=0,
        concat_axis=0,
        axis_index_groups=[[z * PLANE + p for p in range(PLANE)] for z in range(levels)],
        tiled=True,
    ).reshape(PLANE // 2, 2, shard, half_cols)

    own_got, give_got = pl.pallas_call(
        share_kernel,
        out_shape=[jax.ShapeDtypeStruct((4, count, half_cols), jnp.bfloat16)] * 2,
        in_specs=[SCALAR] + vmem(4),
        out_specs=vmem(2),
        compiler_params=PARAMS,
        name="share",
    )(me_scalar, *got)
    mate_got = swap(give_got, CORE)

    block, last_rows = (2 * depth, half_cols), (len(last_masks) * depth, half_cols)
    row_grads = pl.pallas_call(
        row_grad_kernel,
        out_shape=jax.ShapeDtypeStruct((receive, width_model), jnp.bfloat16),
        grid_spec=pltpu.PrefetchScalarGridSpec(
            num_scalar_prefetch=2,
            grid=(len(first_masks) // 2,),
            in_specs=[pl.BlockSpec(own_got.shape, lambda i, *_: (0, 0, 0))] * 2
            + [pl.BlockSpec(block, lambda i, *_: (i, 0))] * 2
            + [pl.BlockSpec(last_rows, lambda i, *_: (0, 0))] * 2,
            out_specs=pl.BlockSpec((receive, width_model), lambda i, *_: (0, 0)),
            scratch_shapes=[
                pltpu.VMEM((2, half_cols, receive), jnp.bfloat16),
                pltpu.VMEM((receive, half_cols), jnp.float32),
            ],
        ),
        compiler_params=PARAMS,
        name="row_grad",
    )(order, me_scalar, own_got, mate_got, first_weight, mate_first, last_weight, mate_last)

    key_grad = pl.pallas_call(
        functools.partial(sum_kernel, math.sqrt(rows * size)),
        out_shape=jax.ShapeDtypeStruct((shard, cols), jnp.float32),
        in_specs=anywhere(1),
        out_specs=vmem(1)[0],
        scratch_shapes=[
            pltpu.VMEM((PLANE, shard, half_cols), jnp.bfloat16),
            pltpu.SemaphoreType.DMA((PLANE,)),
        ],
        compiler_params=PARAMS,
        name="sum",
    )(after(parts, row_grads))
    return (row_grads, key_grad)


def solution(mesh):
    size, split = mesh.shape["dp"], mesh.shape["mp"]
    paired = split == 1 and size == 32
    return jax.shard_map(
        per_device_paired if paired else per_device_general,
        mesh=mesh,
        in_specs=(P("dp", None), P("dp", "mp"), P("dp", None), P("dp", None), P(), P("dp", "mp")),
        out_specs=(P("dp", "mp"), P("dp", "mp")),
        check_vma=False,
    )
```

```python
import functools
import math

import jax
import jax.numpy as jnp
from jax import lax
from jax.experimental import pallas as pl
from jax.experimental.pallas import tpu as pltpu
from jax.sharding import PartitionSpec as P

HEAD_DIM = 128
NSUB = 4
VMEM_LIMIT = 60 * 1024 * 1024
CODE_ROWS = 16
epsilon = 1e-06


def per_device_general(tokens, key_cot, routes, counts, widths, key_weight):
    row_count = tokens.shape[0]
    width_model = tokens.shape[1]
    local_cols = key_cot.shape[1]
    local_heads = local_cols // HEAD_DIM
    dp_size = lax.axis_size("dp")
    per_peer = 2 * row_count // dp_size
    receive = dp_size * per_peer
    destination = routes[:, 0]
    one_hot = (destination[:, None] == jnp.arange(dp_size, dtype=jnp.int32)[None, :]).astype(
        jnp.int32
    )
    earlier = jnp.sum(jnp.cumsum(one_hot, axis=0) * one_hot, axis=1) - 1
    send_slot = destination * per_peer + earlier
    bounds = jnp.cumsum(counts[0])
    positions = jnp.arange(row_count, dtype=jnp.int32)
    subnet = jnp.sum((positions[:, None] >= bounds[None, : NSUB - 1]).astype(jnp.int32), axis=1)
    send_subnet = (
        jnp.full((receive,), -1, jnp.int32).at[send_slot].set(subnet).reshape(dp_size, per_peer)
    )
    send_cot = jnp.zeros((receive, local_cols), jnp.bfloat16).at[send_slot].set(key_cot)
    send_cot = send_cot.reshape(dp_size, per_peer, local_cols)
    send_tokens = jnp.zeros((receive, width_model), jnp.bfloat16).at[send_slot].set(tokens)
    send_tokens = send_tokens.reshape(dp_size, per_peer, width_model)
    got_tokens, got_cot, got_subnet = (
        lax.all_to_all(send_tokens, "dp", split_axis=0, concat_axis=0, tiled=True),
        lax.all_to_all(send_cot, "dp", split_axis=0, concat_axis=0, tiled=True),
        lax.all_to_all(send_subnet, "dp", split_axis=0, concat_axis=0, tiled=True),
    )
    hidden = got_tokens.reshape(receive, width_model)
    got_cot = got_cot.reshape(receive, local_cols)
    got_subnet = got_subnet.reshape(receive)
    full_weight = lax.all_gather(key_weight, "dp", axis=0, tiled=True)
    key_proj = jnp.dot(hidden, full_weight, preferred_element_type=jnp.float32)
    per_head = key_proj.reshape(receive, local_heads, HEAD_DIM)
    head_scale = jnp.sqrt(jnp.mean(per_head * per_head, axis=2, keepdims=True) + epsilon)
    outputs = per_head / head_scale
    subnet_match = got_subnet[:, None] == jnp.arange(NSUB, dtype=jnp.int32)[None, :]
    row_width = jnp.sum(jnp.where(subnet_match, widths[None, :], 0), axis=1)
    head_index = lax.axis_index("mp") * local_heads + jnp.arange(local_heads, dtype=jnp.int32)
    head_mask = (head_index[None, :] < row_width[:, None]).astype(jnp.float32)
    upstream = (
        got_cot.astype(jnp.float32).reshape(receive, local_heads, HEAD_DIM) * head_mask[:, :, None]
    )
    key_delta = (
        upstream - outputs * jnp.mean(upstream * outputs, axis=2, keepdims=True)
    ) / head_scale
    delta_low = key_delta.reshape(receive, local_cols).astype(jnp.bfloat16)
    part_delta = lax.dot_general(
        delta_low, full_weight, (((1,), (1,)), ((), ())), preferred_element_type=jnp.float32
    )
    rounded = lax.optimization_barrier(part_delta.astype(jnp.bfloat16)).astype(jnp.float32)
    feature_delta = lax.psum_scatter(
        rounded.astype(jnp.bfloat16), "mp", scatter_dimension=1, tiled=True
    )
    weight_sum = lax.psum_scatter(
        lax.dot_general(
            hidden, delta_low, (((0,), (0,)), ((), ())), preferred_element_type=jnp.float32
        ),
        "dp",
        scatter_dimension=0,
        tiled=True,
    )
    key_grad = weight_sum / math.sqrt(row_count * dp_size)
    return (feature_delta, key_grad)


CORE, X, Y = 1, 2, 4
PLANE = 8
PLANE_MASKS = (0, X, Y, X | Y)


def swap(value, mask):
    size = lax.axis_size("dp")
    return lax.ppermute(value, "dp", [(i, i ^ mask) for i in range(size)])


def after(value, *others):
    return lax.optimization_barrier((value, *others))[0]


def dot(a, b, dims):
    return lax.dot_general(a, b, (dims, ((), ())), preferred_element_type=jnp.float32)


def fetch(pairs, sems):
    copies = [
        pltpu.make_async_copy(source, target, sems.at[n])
        for n, (source, target) in enumerate(pairs)
    ]
    for copy in copies:
        copy.start()
    return copies


def project_kernel(begin, chips_ref, own_ref, mate_ref, *refs):
    begun = None
    if begin:
        begun, *refs = refs
    *pieces, weight_ref, acc, held, weights, sems = refs
    depth = pieces[0].shape[0]
    count = len(pieces)

    def rows_of(ref, n):
        return ref.at[n * depth : (n + 1) * depth, :]

    pairs = []
    for n, ref in enumerate(pieces):
        at = pl.multiple_of(chips_ref[begin + n] * depth, depth)
        pairs += [
            (ref, rows_of(weights, n)),
            (own_ref.at[:, pl.ds(at, depth)], held.at[n, 0]),
            (mate_ref.at[:, pl.ds(at, depth)], held.at[n, 1]),
        ]
    copies = fetch(pairs, sems)
    if begin:
        acc[...] = begun[...]
    kept = []
    for n in range(count):
        for copy in copies[3 * n : 3 * n + 3]:
            copy.wait()
        out = pltpu.make_async_copy(
            rows_of(weights, n), rows_of(weight_ref, n), sems.at[3 * count + n]
        )
        out.start()
        kept.append(out)
        piece = rows_of(weights, n)[...]
        for side in range(2):
            part = dot(held[n, side], piece, ((1,), (0,)))
            if begin + n == 0:
                acc[side] = part
            else:
                acc[side] += part
    return kept


def first_project_kernel(*refs):
    for copy in project_kernel(0, *refs):
        copy.wait()


def delta_kernel(begin, chips_ref, me_ref, own_cot_ref, mate_cot_ref, *refs):
    *refs, delta_ref, weight_ref, acc, held, weights, sems = refs
    kept = project_kernel(begin, chips_ref, *refs, weight_ref, acc, held, weights, sems)
    core = me_ref[0] & 1
    rows = acc.shape[1]
    delta_ref[2 * rows :, :] = jnp.zeros_like(delta_ref[2 * rows :, :])
    for side, cot_ref in enumerate((own_cot_ref, mate_cot_ref)):
        at = pl.multiple_of((core ^ side) * rows, rows)
        for head in range(own_cot_ref.shape[1] // HEAD_DIM):
            cols = slice(head * HEAD_DIM, (head + 1) * HEAD_DIM)
            proj = acc[side, :, cols]
            scale = jnp.sqrt(jnp.mean(proj * proj, axis=1, keepdims=True) + epsilon)
            normed = proj / scale
            upstream = cot_ref[:rows, cols].astype(jnp.float32)
            delta = (upstream - normed * jnp.mean(upstream * normed, axis=1, keepdims=True)) / scale
            delta_ref[pl.ds(at, rows), cols] = delta.astype(jnp.bfloat16)
        delta_ref[2 * rows :, pl.ds(at, rows)] = cot_ref[rows:, :rows]
    for copy in kept:
        copy.wait()


def select_kernel(me_ref, *refs):
    deltas, sent, (held, sems) = refs[:4], refs[4:8], refs[8:]
    copies = fetch([(ref, held.at[n]) for n, ref in enumerate(deltas)], sems)
    for copy in copies:
        copy.wait()
    rows = (held.shape[1] - CODE_ROWS) // 2
    per_core = sent[0].shape[0] // 2
    per_chip = per_core // len(deltas)
    iota = lax.broadcasted_iota(jnp.int32, (2 * per_core, 2 * rows), 0)
    core = (iota >= per_core).astype(jnp.int32)
    slot = iota - core * per_core
    for out_ref, mask in zip(sent, PLANE_MASKS):
        total = None
        for n in range(len(deltas)):
            code = held[n, 2 * rows :, : 2 * rows].astype(jnp.float32).astype(jnp.int32)
            want = code[0:1, :] - ((me_ref[0] ^ mask) & -2)
            hot = (core == want) & (slot == code[1:2, :] + n * per_chip)
            part = dot(hot.astype(jnp.bfloat16), held[n, : 2 * rows, :], ((1,), (0,)))
            total = part if total is None else total + part
        out_ref[...] = total.astype(jnp.bfloat16)


def share_kernel(me_ref, *refs):
    got, (keep_ref, give_ref) = refs[:4], refs[4:]
    count = keep_ref.shape[1]
    core = me_ref[0] & 1
    for n, ref in enumerate(got):
        keep_ref[n] = ref[pl.ds(pl.multiple_of(core * count, count), count), :]
        give_ref[n] = ref[pl.ds(pl.multiple_of((1 - core) * count, count), count), :]


def weight_grad_kernel(me_ref, own_ref, mate_ref, *refs):
    *deltas, part_ref, hidden, held, acc, sems = refs
    plane = lax.shift_right_logical(me_ref[0], 3)
    core = me_ref[0] & 1
    rows = own_ref.shape[1]
    pairs = []
    for n, ref in enumerate(deltas):
        own = pl.multiple_of((2 * n + core) * rows, rows)
        mate = pl.multiple_of((2 * n + 1 - core) * rows, rows)
        pairs += [
            (own_ref.at[plane ^ n], hidden.at[pl.ds(own, rows), :]),
            (mate_ref.at[plane ^ n], hidden.at[pl.ds(mate, rows), :]),
            (ref.at[: 2 * rows, :], held.at[2 * n * rows : 2 * (n + 1) * rows, :]),
        ]
    copies = fetch(pairs, sems)
    for first in (0, 2):
        for copy in copies[3 * first : 3 * first + 6]:
            copy.wait()
        part = slice(2 * first * rows, 2 * (first + 2) * rows)
        terms = dot(hidden[part, :], held[part, :], ((0,), (0,)))
        if first == 0:
            acc[...] = terms
        else:
            part_ref[...] = (acc[...] + terms).astype(jnp.bfloat16)


def sum_kernel(norm, parts_ref, grad_ref):
    half = parts_ref.shape[3]
    for side in range(2):
        total = parts_ref[0, side].astype(jnp.float32)
        for chip in range(1, parts_ref.shape[0]):
            total += parts_ref[chip, side].astype(jnp.float32)
        grad_ref[:, side * half : (side + 1) * half] = total / norm


def row_grad_kernel(chips_ref, me_ref, own_got_ref, mate_got_ref, *refs):
    weight_refs, (out_ref, weights, out, rows_ref, held, sems) = refs[:4], refs[4:]
    chips, count, half = own_got_ref.shape
    block = count // 4
    depth = half // 2
    pieces = weights.shape[1] // depth
    level = lax.shift_right_logical(me_ref[0], 3)

    def rows_of(ref, n):
        return ref.at[n * depth : (n + 1) * depth, :]

    pairs = []
    for n in range(pieces):
        first = weight_refs[0].shape[0] // depth
        for side in range(2):
            ref = weight_refs[side] if n < first else weight_refs[2 + side]
            pairs.append((rows_of(ref, n % first), rows_of(weights.at[side], n)))
    copies = fetch(pairs, sems)
    for side, got_ref in enumerate((own_got_ref, mate_got_ref)):
        for chip, mask in enumerate(PLANE_MASKS):
            place = lax.shift_right_logical((me_ref[0] ^ mask) & 6, 1)
            for n in range(4):
                at = pl.multiple_of(((level ^ n) * chips + place) * block, block)
                rows = got_ref[chip, n * block : (n + 1) * block, :]
                held[pl.ds(at, block), :] = rows.astype(jnp.float32)
        rows_ref[side] = held[...].T.astype(jnp.bfloat16)
    written = []
    for n in range(pieces):
        for copy in copies[2 * n : 2 * n + 2]:
            copy.wait()
        total = dot(rows_of(weights.at[0], n)[...], rows_ref[0], ((1,), (0,)))
        total += dot(rows_of(weights.at[1], n)[...], rows_ref[1], ((1,), (0,)))
        out[n] = total.T.astype(jnp.bfloat16)
        at = pl.multiple_of(chips_ref[n] * depth, depth)
        copy = pltpu.make_async_copy(
            out.at[n], out_ref.at[:, pl.ds(at, depth)], sems.at[2 * pieces + n]
        )
        copy.start()
        written.append(copy)
    for copy in written:
        copy.wait()


def code_rows(destination, core, per_peer, width):
    positions = jnp.arange(destination.shape[0], dtype=jnp.int32)
    same = (destination[:, None] == destination[None, :]) & (
        positions[:, None] < positions[None, :]
    )
    earlier = jnp.sum(same.astype(jnp.int32), axis=0)
    codes = jnp.stack([destination, core * per_peer + earlier]).astype(jnp.bfloat16)
    return jnp.pad(codes, ((0, CODE_ROWS - 2), (0, width - destination.shape[0])))


def anywhere(count):
    return [pl.BlockSpec(memory_space=pl.ANY)] * count


def vmem(count):
    return [pl.BlockSpec(memory_space=pltpu.VMEM)] * count


def anywhere(count):
    return [pl.BlockSpec(memory_space=pl.ANY)] * count


SCALAR = pl.BlockSpec(memory_space=pltpu.SMEM)
PARAMS = pltpu.CompilerParams(vmem_limit_bytes=VMEM_LIMIT)


def per_device_paired(tokens, key_cot, routes, counts, widths, key_weight):
    rows, width_model = tokens.shape
    cols = key_cot.shape[1]
    half_cols = cols // 2
    size = lax.axis_size("dp")
    chips = size // 2
    levels = size // PLANE
    per_peer = 2 * rows // size
    receive = size * per_peer
    wide = width_model // levels
    me = lax.axis_index("dp")
    core = me % 2
    me_scalar = me.astype(jnp.int32).reshape(1)

    def mine(value):
        return lax.dynamic_slice_in_dim(value, core * half_cols, half_cols, 1)

    def theirs(value):
        return lax.dynamic_slice_in_dim(value, (1 - core) * half_cols, half_cols, 1)

    mate_shard = swap(key_weight, CORE)
    piece = jnp.where(
        core == 0,
        jnp.concatenate([key_weight[:, :half_cols], mate_shard[:, :half_cols]], axis=0),
        jnp.concatenate([mate_shard[:, half_cols:], key_weight[:, half_cols:]], axis=0),
    )
    near, far, both = PLANE, 2 * PLANE, 3 * PLANE
    have = {0: piece}

    def after_round(**beside):
        names, masks = list(beside), list(have)
        values = lax.optimization_barrier([*beside.values(), *have.values()])
        have.update(zip(masks, values[len(names) :]))
        return values[: len(names)]

    mate_tokens = swap(after(tokens, mate_shard), CORE)
    have.update(
        {
            Y: swap(piece, Y),
            X: swap(piece, X),
            near: swap(piece, near),
            far: swap(piece, far),
        }
    )
    mate_tokens, key_cot, counts, routes = after_round(
        mate_tokens=mate_tokens, key_cot=key_cot, counts=counts, routes=routes
    )
    have.update(
        {
            near | X: swap(have[near], X),
            near | Y: swap(have[near], Y),
            far | X: swap(have[far], X),
            far | Y: swap(have[far], Y),
            both: swap(have[far], near),
        }
    )
    bounds = jnp.cumsum(counts[0])
    positions = jnp.arange(rows, dtype=jnp.int32)
    subnet = jnp.sum((positions[:, None] >= bounds[None, : NSUB - 1]).astype(jnp.int32), axis=1)
    subnet_match = subnet[:, None] == jnp.arange(NSUB, dtype=jnp.int32)[None, :]
    row_width = jnp.sum(jnp.where(subnet_match, widths[None, :], 0), axis=1)
    head_of_col = jnp.arange(cols, dtype=jnp.int32) // HEAD_DIM
    upstream = jnp.where(
        head_of_col[None, :] < row_width[:, None], key_cot, jnp.zeros_like(key_cot)
    )
    codes = code_rows(routes[:, 0], core, per_peer, half_cols)
    own_cot = jnp.concatenate([mine(upstream), codes], axis=0)

    by_level = jnp.stack([tokens[:, z * wide : (z + 1) * wide] for z in range(levels)])
    by_level, own_cot, give_cot = after_round(
        by_level=by_level,
        own_cot=own_cot,
        give_cot=jnp.concatenate([theirs(upstream), codes], axis=0),
    )
    columns = [[p + PLANE * z for z in range(levels)] for p in range(PLANE)]
    own_features = lax.all_to_all(
        by_level,
        "dp",
        split_axis=0,
        concat_axis=0,
        axis_index_groups=columns,
        tiled=True,
    )
    have.update(
        {
            both | X: swap(have[both], X),
            both | Y: swap(have[both], Y),
            X | Y: swap(have[Y], X),
            far | X | Y: swap(have[far | X], Y),
        }
    )
    mate_cot = swap(give_cot, CORE)
    mate_cot, own_cot = after_round(mate_cot=mate_cot, own_cot=own_cot)
    first_masks = list(have)
    last_masks = [near | X | Y, both | X | Y]
    order = jnp.stack([lax.shift_right_logical(me ^ mask, 1) for mask in first_masks + last_masks])
    depth = width_model // chips
    sums = jax.ShapeDtypeStruct((2, rows, half_cols), jnp.float32)

    def project(kernel, count, results, inputs, specs, name):
        return pl.pallas_call(
            kernel,
            out_shape=(*results, jax.ShapeDtypeStruct((count * depth, half_cols), jnp.bfloat16))
            + ((sums,) if name == "project" else ()),
            in_specs=specs + anywhere(count),
            out_specs=(*vmem(len(results)), anywhere(1)[0])
            + (tuple(vmem(1)) if name == "project" else ()),
            scratch_shapes=([] if name == "project" else [pltpu.VMEM(sums.shape, sums.dtype)])
            + [
                pltpu.VMEM((count, 2, rows, depth), jnp.bfloat16),
                pltpu.VMEM((count * depth, half_cols), jnp.bfloat16),
                pltpu.SemaphoreType.DMA((4 * count,)),
            ],
            compiler_params=PARAMS,
            name=name,
        )(*inputs)

    first_weight, begun = project(
        first_project_kernel,
        len(first_masks),
        (),
        (order, tokens, mate_tokens, *[have[mask] for mask in first_masks]),
        [SCALAR] + anywhere(2),
        "project",
    )
    have.update(
        {
            near | X | Y: swap(have[near | Y], X),
            both | X | Y: swap(have[both | X], Y),
        }
    )
    mate_cot, own_cot, own_features, begun, first_weight = after_round(
        mate_cot=mate_cot,
        own_cot=own_cot,
        own_features=own_features,
        begun=begun,
        first_weight=first_weight,
    )
    mate_features = swap(own_features, CORE)
    delta, last_weight = project(
        functools.partial(delta_kernel, len(first_masks)),
        len(last_masks),
        (jax.ShapeDtypeStruct((2 * rows + CODE_ROWS, half_cols), jnp.bfloat16),),
        (
            order,
            me_scalar,
            own_cot,
            mate_cot,
            tokens,
            mate_tokens,
            begun,
            *[have[mask] for mask in last_masks],
        ),
        [SCALAR] * 2 + vmem(2) + anywhere(2) + vmem(1),
        "delta",
    )

    delta_near, delta_far, mate_features = lax.optimization_barrier(
        (swap(delta, near), swap(delta, far), mate_features)
    )
    deltas = [delta, delta_near, delta_far, swap(delta_far, near)]
    first_weight, last_weight, *deltas[1:] = lax.optimization_barrier(
        (first_weight, last_weight, *deltas[1:])
    )
    mate_first, mate_last = swap(first_weight, CORE), swap(last_weight, CORE)
    count = levels * 2 * per_peer
    delta_room = pltpu.VMEM((levels, *delta.shape), jnp.bfloat16)
    selected = pl.pallas_call(
        select_kernel,
        out_shape=[jax.ShapeDtypeStruct((2 * count, half_cols), jnp.bfloat16)] * 4,
        in_specs=[SCALAR] + anywhere(levels),
        out_specs=vmem(4),
        scratch_shapes=[delta_room, pltpu.SemaphoreType.DMA((levels,))],
        compiler_params=PARAMS,
        name="select",
    )(me_scalar, *deltas)
    got = [
        swap(value, mask) if mask else value for value, mask in zip(selected, PLANE_MASKS)
    ]
    shard = width_model // size
    terms = pl.pallas_call(
        weight_grad_kernel,
        out_shape=jax.ShapeDtypeStruct((wide, half_cols), jnp.bfloat16),
        in_specs=[SCALAR] + anywhere(2 + levels),
        out_specs=vmem(1)[0],
        scratch_shapes=[
            pltpu.VMEM((levels * 2 * rows, wide), jnp.bfloat16),
            pltpu.VMEM((levels * 2 * rows, half_cols), jnp.bfloat16),
            pltpu.VMEM((wide, half_cols), jnp.float32),
            pltpu.SemaphoreType.DMA((3 * levels,)),
        ],
        compiler_params=PARAMS,
        name="weight_grad",
    )(me_scalar, own_features, mate_features, after(delta, *selected), *deltas[1:])
    parts = lax.all_to_all(
        after(terms, *got).reshape(PLANE, shard, half_cols),
        "dp",
        split_axis=0,
        concat_axis=0,
        axis_index_groups=[[z * PLANE + p for p in range(PLANE)] for z in range(levels)],
        tiled=True,
    ).reshape(PLANE // 2, 2, shard, half_cols)

    own_got, give_got = pl.pallas_call(
        share_kernel,
        out_shape=[jax.ShapeDtypeStruct((4, count, half_cols), jnp.bfloat16)] * 2,
        in_specs=[SCALAR] + vmem(4),
        out_specs=vmem(2),
        compiler_params=PARAMS,
        name="share",
    )(me_scalar, *got)
    mate_got = swap(give_got, CORE)

    row_grads = pl.pallas_call(
        row_grad_kernel,
        out_shape=jax.ShapeDtypeStruct((receive, width_model), jnp.bfloat16),
        in_specs=[SCALAR] * 2 + vmem(2) + anywhere(4),
        out_specs=anywhere(1)[0],
        scratch_shapes=[
            pltpu.VMEM((2, width_model, half_cols), jnp.bfloat16),
            pltpu.VMEM((chips, receive, depth), jnp.bfloat16),
            pltpu.VMEM((2, half_cols, receive), jnp.bfloat16),
            pltpu.VMEM((receive, half_cols), jnp.float32),
            pltpu.SemaphoreType.DMA((3 * chips,)),
        ],
        compiler_params=PARAMS,
        name="row_grad",
    )(order, me_scalar, own_got, mate_got, first_weight, mate_first, last_weight, mate_last)

    key_grad = pl.pallas_call(
        functools.partial(sum_kernel, math.sqrt(rows * size)),
        out_shape=jax.ShapeDtypeStruct((shard, cols), jnp.float32),
        in_specs=vmem(1),
        out_specs=vmem(1)[0],
        compiler_params=PARAMS,
        name="sum",
    )(after(parts, row_grads))
    return (row_grads, key_grad)


def solution(mesh):
    size, split = mesh.shape["dp"], mesh.shape["mp"]
    paired = split == 1 and size == 32
    return jax.shard_map(
        per_device_paired if paired else per_device_general,
        mesh=mesh,
        in_specs=(P("dp", None), P("dp", "mp"), P("dp", None), P("dp", None), P(), P("dp", "mp")),
        out_specs=(P("dp", "mp"), P("dp", "mp")),
        check_vma=False,
    )
```

```python
import functools
import math

import jax
import jax.numpy as jnp
from jax import lax
from jax.experimental import pallas as pl
from jax.experimental.pallas import tpu as pltpu
from jax.sharding import PartitionSpec as P

HEAD_DIM = 128
NSUB = 4
VMEM_LIMIT = 60 * 1024 * 1024
CODE_ROWS = 16
epsilon = 1e-06


def per_device_general(tokens, key_cot, routes, counts, widths, key_weight):
    row_count = tokens.shape[0]
    width_model = tokens.shape[1]
    local_cols = key_cot.shape[1]
    local_heads = local_cols // HEAD_DIM
    dp_size = lax.axis_size("dp")
    per_peer = 2 * row_count // dp_size
    receive = dp_size * per_peer
    destination = routes[:, 0]
    one_hot = (destination[:, None] == jnp.arange(dp_size, dtype=jnp.int32)[None, :]).astype(
        jnp.int32
    )
    earlier = jnp.sum(jnp.cumsum(one_hot, axis=0) * one_hot, axis=1) - 1
    send_slot = destination * per_peer + earlier
    bounds = jnp.cumsum(counts[0])
    positions = jnp.arange(row_count, dtype=jnp.int32)
    subnet = jnp.sum((positions[:, None] >= bounds[None, : NSUB - 1]).astype(jnp.int32), axis=1)
    send_subnet = (
        jnp.full((receive,), -1, jnp.int32).at[send_slot].set(subnet).reshape(dp_size, per_peer)
    )
    send_cot = jnp.zeros((receive, local_cols), jnp.bfloat16).at[send_slot].set(key_cot)
    send_cot = send_cot.reshape(dp_size, per_peer, local_cols)
    send_tokens = jnp.zeros((receive, width_model), jnp.bfloat16).at[send_slot].set(tokens)
    send_tokens = send_tokens.reshape(dp_size, per_peer, width_model)
    got_tokens, got_cot, got_subnet = (
        lax.all_to_all(send_tokens, "dp", split_axis=0, concat_axis=0, tiled=True),
        lax.all_to_all(send_cot, "dp", split_axis=0, concat_axis=0, tiled=True),
        lax.all_to_all(send_subnet, "dp", split_axis=0, concat_axis=0, tiled=True),
    )
    hidden = got_tokens.reshape(receive, width_model)
    got_cot = got_cot.reshape(receive, local_cols)
    got_subnet = got_subnet.reshape(receive)
    full_weight = lax.all_gather(key_weight, "dp", axis=0, tiled=True)
    key_proj = jnp.dot(hidden, full_weight, preferred_element_type=jnp.float32)
    per_head = key_proj.reshape(receive, local_heads, HEAD_DIM)
    head_scale = jnp.sqrt(jnp.mean(per_head * per_head, axis=2, keepdims=True) + epsilon)
    outputs = per_head / head_scale
    subnet_match = got_subnet[:, None] == jnp.arange(NSUB, dtype=jnp.int32)[None, :]
    row_width = jnp.sum(jnp.where(subnet_match, widths[None, :], 0), axis=1)
    head_index = lax.axis_index("mp") * local_heads + jnp.arange(local_heads, dtype=jnp.int32)
    head_mask = (head_index[None, :] < row_width[:, None]).astype(jnp.float32)
    upstream = (
        got_cot.astype(jnp.float32).reshape(receive, local_heads, HEAD_DIM) * head_mask[:, :, None]
    )
    key_delta = (
        upstream - outputs * jnp.mean(upstream * outputs, axis=2, keepdims=True)
    ) / head_scale
    delta_low = key_delta.reshape(receive, local_cols).astype(jnp.bfloat16)
    part_delta = lax.dot_general(
        delta_low, full_weight, (((1,), (1,)), ((), ())), preferred_element_type=jnp.float32
    )
    rounded = lax.optimization_barrier(part_delta.astype(jnp.bfloat16)).astype(jnp.float32)
    feature_delta = lax.psum_scatter(
        rounded.astype(jnp.bfloat16), "mp", scatter_dimension=1, tiled=True
    )
    weight_sum = lax.psum_scatter(
        lax.dot_general(
            hidden, delta_low, (((0,), (0,)), ((), ())), preferred_element_type=jnp.float32
        ),
        "dp",
        scatter_dimension=0,
        tiled=True,
    )
    key_grad = weight_sum / math.sqrt(row_count * dp_size)
    return (feature_delta, key_grad)


CORE, X, Y = 1, 2, 4
PLANE = 8
PLANE_MASKS = (0, X, Y, X | Y)


def swap(value, mask):
    size = lax.axis_size("dp")
    return lax.ppermute(value, "dp", [(i, i ^ mask) for i in range(size)])


def after(value, *others):
    return lax.optimization_barrier((value, *others))[0]


def dot(a, b, dims):
    return lax.dot_general(a, b, (dims, ((), ())), preferred_element_type=jnp.float32)


def fetch(pairs, sems):
    copies = [
        pltpu.make_async_copy(source, target, sems.at[n])
        for n, (source, target) in enumerate(pairs)
    ]
    for copy in copies:
        copy.start()
    return copies


def project_kernel(begin, chips_ref, own_ref, mate_ref, *refs):
    begun = None
    if begin:
        begun, *refs = refs
    *pieces, weight_ref, acc, held, weights, sems = refs
    depth = pieces[0].shape[0]
    count = len(pieces)

    def rows_of(ref, n):
        return ref.at[n * depth : (n + 1) * depth, :]

    pairs = []
    for n, ref in enumerate(pieces):
        at = pl.multiple_of(chips_ref[begin + n] * depth, depth)
        pairs += [
            (ref, rows_of(weights, n)),
            (own_ref.at[:, pl.ds(at, depth)], held.at[n, 0]),
            (mate_ref.at[:, pl.ds(at, depth)], held.at[n, 1]),
        ]
    copies = fetch(pairs, sems)
    if begin:
        acc[...] = begun[...]
    kept = []
    for n in range(count):
        for copy in copies[3 * n : 3 * n + 3]:
            copy.wait()
        out = pltpu.make_async_copy(
            rows_of(weights, n), rows_of(weight_ref, n), sems.at[3 * count + n]
        )
        out.start()
        kept.append(out)
        piece = rows_of(weights, n)[...]
        for side in range(2):
            part = dot(held[n, side], piece, ((1,), (0,)))
            if begin + n == 0:
                acc[side] = part
            else:
                acc[side] += part
    return kept


def first_project_kernel(*refs):
    for copy in project_kernel(0, *refs):
        copy.wait()


def delta_kernel(begin, chips_ref, me_ref, own_cot_ref, mate_cot_ref, *refs):
    *refs, delta_ref, weight_ref, acc, held, weights, sems = refs
    kept = project_kernel(begin, chips_ref, *refs, weight_ref, acc, held, weights, sems)
    core = me_ref[0] & 1
    rows = acc.shape[1]
    delta_ref[2 * rows :, :] = jnp.zeros_like(delta_ref[2 * rows :, :])
    for side, cot_ref in enumerate((own_cot_ref, mate_cot_ref)):
        at = pl.multiple_of((core ^ side) * rows, rows)
        for head in range(own_cot_ref.shape[1] // HEAD_DIM):
            cols = slice(head * HEAD_DIM, (head + 1) * HEAD_DIM)
            proj = acc[side, :, cols]
            scale = jnp.sqrt(jnp.mean(proj * proj, axis=1, keepdims=True) + epsilon)
            normed = proj / scale
            upstream = cot_ref[:rows, cols].astype(jnp.float32)
            delta = (upstream - normed * jnp.mean(upstream * normed, axis=1, keepdims=True)) / scale
            delta_ref[pl.ds(at, rows), cols] = delta.astype(jnp.bfloat16)
        delta_ref[2 * rows :, pl.ds(at, rows)] = cot_ref[rows:, :rows]
    for copy in kept:
        copy.wait()


def select_kernel(me_ref, *refs):
    deltas, sent, (held, sems) = refs[:4], refs[4:8], refs[8:]
    copies = fetch([(ref, held.at[n]) for n, ref in enumerate(deltas)], sems)
    rows = (held.shape[1] - CODE_ROWS) // 2
    per_core = sent[0].shape[0] // 2
    per_chip = per_core // len(deltas)
    iota = lax.broadcasted_iota(jnp.int32, (8 * per_chip, 2 * rows), 0)
    block = lax.shift_right_logical(iota, per_chip.bit_length() - 1)
    slot = iota & (per_chip - 1)
    wanted = ((me_ref[0] & -2) ^ (block & -2)) | (block & 1)
    for n in range(len(deltas)):
        copies[n].wait()
        code = held[n, 2 * rows :, : 2 * rows].astype(jnp.float32).astype(jnp.int32)
        hot = (wanted == code[0:1, :]) & (slot == code[1:2, :])
        found = dot(hot.astype(jnp.bfloat16), held[n, : 2 * rows, :], ((1,), (0,)))
        found = found.astype(jnp.bfloat16)
        for place in range(8):
            at = place % 2 * per_core + n * per_chip
            sent[place // 2][at : at + per_chip, :] = found[
                place * per_chip : (place + 1) * per_chip, :
            ]


def share_kernel(me_ref, *refs):
    got, (keep_ref, give_ref) = refs[:4], refs[4:]
    count = keep_ref.shape[1]
    core = me_ref[0] & 1
    for n, ref in enumerate(got):
        keep_ref[n] = ref[pl.ds(pl.multiple_of(core * count, count), count), :]
        give_ref[n] = ref[pl.ds(pl.multiple_of((1 - core) * count, count), count), :]


def weight_grad_kernel(me_ref, own_ref, mate_ref, *refs):
    *deltas, part_ref, hidden, held, acc, sems = refs
    plane = lax.shift_right_logical(me_ref[0], 3)
    core = me_ref[0] & 1
    rows = own_ref.shape[1]
    pairs = []
    for n, ref in enumerate(deltas):
        own = pl.multiple_of((2 * n + core) * rows, rows)
        mate = pl.multiple_of((2 * n + 1 - core) * rows, rows)
        pairs += [
            (own_ref.at[plane ^ n], hidden.at[pl.ds(own, rows), :]),
            (mate_ref.at[plane ^ n], hidden.at[pl.ds(mate, rows), :]),
            (ref.at[: 2 * rows, :], held.at[2 * n * rows : 2 * (n + 1) * rows, :]),
        ]
    copies = fetch(pairs, sems)
    for first in (0, 2):
        for copy in copies[3 * first : 3 * first + 6]:
            copy.wait()
        part = slice(2 * first * rows, 2 * (first + 2) * rows)
        terms = dot(hidden[part, :], held[part, :], ((0,), (0,)))
        if first == 0:
            acc[...] = terms
        else:
            part_ref[...] = (acc[...] + terms).astype(jnp.bfloat16)


def sum_kernel(norm, parts_ref, grad_ref):
    half = parts_ref.shape[3]
    for side in range(2):
        total = parts_ref[0, side].astype(jnp.float32)
        for chip in range(1, parts_ref.shape[0]):
            total += parts_ref[chip, side].astype(jnp.float32)
        grad_ref[:, side * half : (side + 1) * half] = total / norm


def row_grad_kernel(chips_ref, me_ref, own_got_ref, mate_got_ref, *refs):
    weight_refs, (out_ref, weights, out, rows_ref, sems) = refs[:4], refs[4:]
    chips, count, half = own_got_ref.shape
    block = count // 4
    depth = half // 2
    pieces = weights.shape[1] // depth
    level = lax.shift_right_logical(me_ref[0], 3)

    def rows_of(ref, n):
        return ref.at[n * depth : (n + 1) * depth, :]

    pairs = []
    for n in range(pieces):
        first = weight_refs[0].shape[0] // depth
        for side in range(2):
            ref = weight_refs[side] if n < first else weight_refs[2 + side]
            pairs.append((rows_of(ref, n % first), rows_of(weights.at[side], n)))
    copies = fetch(pairs, sems)
    for side, got_ref in enumerate((own_got_ref, mate_got_ref)):
        for chip, mask in enumerate(PLANE_MASKS):
            place = lax.shift_right_logical((me_ref[0] ^ mask) & 6, 1)
            for n in range(4):
                at = pl.multiple_of(((level ^ n) * chips + place) * block, block)
                rows_ref[side, pl.ds(at, block), :] = got_ref[chip, n * block : (n + 1) * block, :]
    written = []
    for n in range(pieces):
        for copy in copies[2 * n : 2 * n + 2]:
            copy.wait()
        total = dot(rows_ref[0], rows_of(weights.at[0], n)[...], ((1,), (1,)))
        total += dot(rows_ref[1], rows_of(weights.at[1], n)[...], ((1,), (1,)))
        out[n] = total.astype(jnp.bfloat16)
        at = pl.multiple_of(chips_ref[n] * depth, depth)
        copy = pltpu.make_async_copy(
            out.at[n], out_ref.at[:, pl.ds(at, depth)], sems.at[2 * pieces + n]
        )
        copy.start()
        written.append(copy)
    for copy in written:
        copy.wait()


def code_rows(destination, core, per_peer, width):
    positions = jnp.arange(destination.shape[0], dtype=jnp.int32)
    same = (destination[:, None] == destination[None, :]) & (
        positions[:, None] < positions[None, :]
    )
    earlier = jnp.sum(same.astype(jnp.int32), axis=0)
    codes = jnp.stack([destination, core * per_peer + earlier]).astype(jnp.bfloat16)
    return jnp.pad(codes, ((0, CODE_ROWS - 2), (0, width - destination.shape[0])))


def anywhere(count):
    return [pl.BlockSpec(memory_space=pl.ANY)] * count


def vmem(count):
    return [pl.BlockSpec(memory_space=pltpu.VMEM)] * count


def anywhere(count):
    return [pl.BlockSpec(memory_space=pl.ANY)] * count


SCALAR = pl.BlockSpec(memory_space=pltpu.SMEM)
PARAMS = pltpu.CompilerParams(vmem_limit_bytes=VMEM_LIMIT)
COST = pl.CostEstimate(flops=1024, bytes_accessed=1024, transcendentals=0)


def grant(mebibytes):
    return pltpu.CompilerParams(vmem_limit_bytes=mebibytes << 20)


def per_device_paired(tokens, key_cot, routes, counts, widths, key_weight):
    rows, width_model = tokens.shape
    cols = key_cot.shape[1]
    half_cols = cols // 2
    size = lax.axis_size("dp")
    chips = size // 2
    levels = size // PLANE
    per_peer = 2 * rows // size
    receive = size * per_peer
    wide = width_model // levels
    me = lax.axis_index("dp")
    core = me % 2
    me_scalar = me.astype(jnp.int32).reshape(1)

    def mine(value):
        return lax.dynamic_slice_in_dim(value, core * half_cols, half_cols, 1)

    def theirs(value):
        return lax.dynamic_slice_in_dim(value, (1 - core) * half_cols, half_cols, 1)

    mate_shard = swap(key_weight, CORE)
    piece = jnp.where(
        core == 0,
        jnp.concatenate([key_weight[:, :half_cols], mate_shard[:, :half_cols]], axis=0),
        jnp.concatenate([mate_shard[:, half_cols:], key_weight[:, half_cols:]], axis=0),
    )
    near, far, both = PLANE, 2 * PLANE, 3 * PLANE
    have = {0: piece}

    def after_round(**beside):
        names, masks = list(beside), list(have)
        values = lax.optimization_barrier([*beside.values(), *have.values()])
        have.update(zip(masks, values[len(names) :]))
        return values[: len(names)]

    mate_tokens = swap(after(tokens, mate_shard), CORE)
    have.update(
        {
            Y: swap(piece, Y),
            X: swap(piece, X),
            near: swap(piece, near),
            far: swap(piece, far),
        }
    )
    mate_tokens, key_cot, counts, routes = after_round(
        mate_tokens=mate_tokens, key_cot=key_cot, counts=counts, routes=routes
    )
    have.update(
        {
            near | X: swap(have[near], X),
            near | Y: swap(have[near], Y),
            far | X: swap(have[far], X),
            far | Y: swap(have[far], Y),
            both: swap(have[far], near),
        }
    )
    bounds = jnp.cumsum(counts[0])
    positions = jnp.arange(rows, dtype=jnp.int32)
    subnet = jnp.sum((positions[:, None] >= bounds[None, : NSUB - 1]).astype(jnp.int32), axis=1)
    subnet_match = subnet[:, None] == jnp.arange(NSUB, dtype=jnp.int32)[None, :]
    row_width = jnp.sum(jnp.where(subnet_match, widths[None, :], 0), axis=1)
    head_of_col = jnp.arange(cols, dtype=jnp.int32) // HEAD_DIM
    upstream = jnp.where(
        head_of_col[None, :] < row_width[:, None], key_cot, jnp.zeros_like(key_cot)
    )
    codes = code_rows(routes[:, 0], core, per_peer, half_cols)
    own_cot = jnp.concatenate([mine(upstream), codes], axis=0)

    by_level = jnp.stack([tokens[:, z * wide : (z + 1) * wide] for z in range(levels)])
    by_level, own_cot, give_cot = after_round(
        by_level=by_level,
        own_cot=own_cot,
        give_cot=jnp.concatenate([theirs(upstream), codes], axis=0),
    )
    columns = [[p + PLANE * z for z in range(levels)] for p in range(PLANE)]
    own_features = lax.all_to_all(
        by_level,
        "dp",
        split_axis=0,
        concat_axis=0,
        axis_index_groups=columns,
        tiled=True,
    )
    have.update(
        {
            both | X: swap(have[both], X),
            both | Y: swap(have[both], Y),
            X | Y: swap(have[Y], X),
            far | X | Y: swap(have[far | X], Y),
        }
    )
    mate_cot = swap(give_cot, CORE)
    mate_cot, own_cot = after_round(mate_cot=mate_cot, own_cot=own_cot)
    first_masks = list(have)
    last_masks = [near | X | Y, both | X | Y]
    order = jnp.stack([lax.shift_right_logical(me ^ mask, 1) for mask in first_masks + last_masks])
    depth = width_model // chips
    sums = jax.ShapeDtypeStruct((2, rows, half_cols), jnp.float32)

    def project(kernel, count, results, inputs, specs, name):
        return pl.pallas_call(
            kernel,
            out_shape=(*results, jax.ShapeDtypeStruct((count * depth, half_cols), jnp.bfloat16))
            + ((sums,) if name == "project" else ()),
            in_specs=specs + anywhere(count),
            out_specs=(*vmem(len(results)), anywhere(1)[0])
            + (tuple(vmem(1)) if name == "project" else ()),
            scratch_shapes=([] if name == "project" else [pltpu.VMEM(sums.shape, sums.dtype)])
            + [
                pltpu.VMEM((count, 2, rows, depth), jnp.bfloat16),
                pltpu.VMEM((count * depth, half_cols), jnp.bfloat16),
                pltpu.SemaphoreType.DMA((4 * count,)),
            ],
            compiler_params=PARAMS,
            cost_estimate=COST,
            name=name,
        )(*inputs)

    first_weight, begun = project(
        first_project_kernel,
        len(first_masks),
        (),
        (order, tokens, mate_tokens, *[have[mask] for mask in first_masks]),
        [SCALAR] + anywhere(2),
        "project",
    )
    have.update(
        {
            near | X | Y: swap(have[near | Y], X),
            both | X | Y: swap(have[both | X], Y),
        }
    )
    mate_cot, own_cot, begun, first_weight = after_round(
        mate_cot=mate_cot,
        own_cot=own_cot,
        begun=begun,
        first_weight=first_weight,
    )
    mate_features = swap(own_features, CORE)
    delta, last_weight = project(
        functools.partial(delta_kernel, len(first_masks)),
        len(last_masks),
        (jax.ShapeDtypeStruct((2 * rows + CODE_ROWS, half_cols), jnp.bfloat16),),
        (
            order,
            me_scalar,
            own_cot,
            mate_cot,
            tokens,
            mate_tokens,
            begun,
            *[have[mask] for mask in last_masks],
        ),
        [SCALAR] * 2 + vmem(2) + anywhere(2) + vmem(1),
        "delta",
    )

    delta_near, delta_far, mate_features = lax.optimization_barrier(
        (swap(delta, near), swap(delta, far), mate_features)
    )
    deltas = [delta, delta_near, delta_far, swap(delta_far, near)]
    first_weight, last_weight, *deltas[1:] = lax.optimization_barrier(
        (first_weight, last_weight, *deltas[1:])
    )
    mate_first, mate_last = swap(first_weight, CORE), swap(last_weight, CORE)
    count = levels * 2 * per_peer
    delta_room = pltpu.VMEM((levels, *delta.shape), jnp.bfloat16)
    selected = pl.pallas_call(
        select_kernel,
        out_shape=[jax.ShapeDtypeStruct((2 * count, half_cols), jnp.bfloat16)] * 4,
        in_specs=[SCALAR] + anywhere(levels),
        out_specs=vmem(4),
        scratch_shapes=[delta_room, pltpu.SemaphoreType.DMA((levels,))],
        compiler_params=PARAMS,
        name="select",
    )(me_scalar, *deltas)
    got = [
        swap(value, mask) if mask else value for value, mask in zip(selected, PLANE_MASKS)
    ]
    shard = width_model // size
    terms = pl.pallas_call(
        weight_grad_kernel,
        out_shape=jax.ShapeDtypeStruct((wide, half_cols), jnp.bfloat16),
        in_specs=[SCALAR] + anywhere(2 + levels),
        out_specs=vmem(1)[0],
        scratch_shapes=[
            pltpu.VMEM((levels * 2 * rows, wide), jnp.bfloat16),
            pltpu.VMEM((levels * 2 * rows, half_cols), jnp.bfloat16),
            pltpu.VMEM((wide, half_cols), jnp.float32),
            pltpu.SemaphoreType.DMA((3 * levels,)),
        ],
        compiler_params=PARAMS,
        name="weight_grad",
    )(me_scalar, own_features, mate_features, after(delta, *selected), *deltas[1:])
    parts = lax.all_to_all(
        after(terms, *got).reshape(PLANE, shard, half_cols),
        "dp",
        split_axis=0,
        concat_axis=0,
        axis_index_groups=[[z * PLANE + p for p in range(PLANE)] for z in range(levels)],
        tiled=True,
    ).reshape(PLANE // 2, 2, shard, half_cols)

    own_got, give_got = pl.pallas_call(
        share_kernel,
        out_shape=[jax.ShapeDtypeStruct((4, count, half_cols), jnp.bfloat16)] * 2,
        in_specs=[SCALAR] + vmem(4),
        out_specs=vmem(2),
        compiler_params=PARAMS,
        name="share",
    )(me_scalar, *got)
    mate_got = swap(give_got, CORE)

    row_grads = pl.pallas_call(
        row_grad_kernel,
        out_shape=jax.ShapeDtypeStruct((receive, width_model), jnp.bfloat16),
        in_specs=[SCALAR] * 2 + vmem(2) + anywhere(4),
        out_specs=anywhere(1)[0],
        scratch_shapes=[
            pltpu.VMEM((2, width_model, half_cols), jnp.bfloat16),
            pltpu.VMEM((chips, receive, depth), jnp.bfloat16),
            pltpu.VMEM((2, receive, half_cols), jnp.bfloat16),
            pltpu.SemaphoreType.DMA((3 * chips,)),
        ],
        compiler_params=grant(56),
        name="row_grad",
    )(order, me_scalar, own_got, mate_got, first_weight, mate_first, last_weight, mate_last)

    key_grad = pl.pallas_call(
        functools.partial(sum_kernel, math.sqrt(rows * size)),
        out_shape=jax.ShapeDtypeStruct((shard, cols), jnp.float32),
        in_specs=vmem(1),
        out_specs=vmem(1)[0],
        compiler_params=grant(16),
        name="sum",
    )(after(parts, row_grads))
    return (row_grads, key_grad)


def solution(mesh):
    size, split = mesh.shape["dp"], mesh.shape["mp"]
    paired = split == 1 and size == 32
    return jax.shard_map(
        per_device_paired if paired else per_device_general,
        mesh=mesh,
        in_specs=(P("dp", None), P("dp", "mp"), P("dp", None), P("dp", None), P(), P("dp", "mp")),
        out_specs=(P("dp", "mp"), P("dp", "mp")),
        check_vma=False,
    )
```

```python
import functools
import math

import jax
import jax.numpy as jnp
from jax import lax
from jax.experimental import pallas as pl
from jax.experimental.pallas import tpu as pltpu
from jax.sharding import PartitionSpec as P

HEAD_DIM = 128
NSUB = 4
VMEM_LIMIT = 60 * 1024 * 1024
CODE_ROWS = 16
epsilon = 1e-06


def per_device_general(tokens, key_cot, routes, counts, widths, key_weight):
    row_count = tokens.shape[0]
    width_model = tokens.shape[1]
    local_cols = key_cot.shape[1]
    local_heads = local_cols // HEAD_DIM
    dp_size = lax.axis_size("dp")
    per_peer = 2 * row_count // dp_size
    receive = dp_size * per_peer
    destination = routes[:, 0]
    one_hot = (destination[:, None] == jnp.arange(dp_size, dtype=jnp.int32)[None, :]).astype(
        jnp.int32
    )
    earlier = jnp.sum(jnp.cumsum(one_hot, axis=0) * one_hot, axis=1) - 1
    send_slot = destination * per_peer + earlier
    bounds = jnp.cumsum(counts[0])
    positions = jnp.arange(row_count, dtype=jnp.int32)
    subnet = jnp.sum((positions[:, None] >= bounds[None, : NSUB - 1]).astype(jnp.int32), axis=1)
    send_subnet = (
        jnp.full((receive,), -1, jnp.int32).at[send_slot].set(subnet).reshape(dp_size, per_peer)
    )
    send_cot = jnp.zeros((receive, local_cols), jnp.bfloat16).at[send_slot].set(key_cot)
    send_cot = send_cot.reshape(dp_size, per_peer, local_cols)
    send_tokens = jnp.zeros((receive, width_model), jnp.bfloat16).at[send_slot].set(tokens)
    send_tokens = send_tokens.reshape(dp_size, per_peer, width_model)
    got_tokens, got_cot, got_subnet = (
        lax.all_to_all(send_tokens, "dp", split_axis=0, concat_axis=0, tiled=True),
        lax.all_to_all(send_cot, "dp", split_axis=0, concat_axis=0, tiled=True),
        lax.all_to_all(send_subnet, "dp", split_axis=0, concat_axis=0, tiled=True),
    )
    hidden = got_tokens.reshape(receive, width_model)
    got_cot = got_cot.reshape(receive, local_cols)
    got_subnet = got_subnet.reshape(receive)
    full_weight = lax.all_gather(key_weight, "dp", axis=0, tiled=True)
    key_proj = jnp.dot(hidden, full_weight, preferred_element_type=jnp.float32)
    per_head = key_proj.reshape(receive, local_heads, HEAD_DIM)
    head_scale = jnp.sqrt(jnp.mean(per_head * per_head, axis=2, keepdims=True) + epsilon)
    outputs = per_head / head_scale
    subnet_match = got_subnet[:, None] == jnp.arange(NSUB, dtype=jnp.int32)[None, :]
    row_width = jnp.sum(jnp.where(subnet_match, widths[None, :], 0), axis=1)
    head_index = lax.axis_index("mp") * local_heads + jnp.arange(local_heads, dtype=jnp.int32)
    head_mask = (head_index[None, :] < row_width[:, None]).astype(jnp.float32)
    upstream = (
        got_cot.astype(jnp.float32).reshape(receive, local_heads, HEAD_DIM) * head_mask[:, :, None]
    )
    key_delta = (
        upstream - outputs * jnp.mean(upstream * outputs, axis=2, keepdims=True)
    ) / head_scale
    delta_low = key_delta.reshape(receive, local_cols).astype(jnp.bfloat16)
    part_delta = lax.dot_general(
        delta_low, full_weight, (((1,), (1,)), ((), ())), preferred_element_type=jnp.float32
    )
    rounded = lax.optimization_barrier(part_delta.astype(jnp.bfloat16)).astype(jnp.float32)
    feature_delta = lax.psum_scatter(
        rounded.astype(jnp.bfloat16), "mp", scatter_dimension=1, tiled=True
    )
    weight_sum = lax.psum_scatter(
        lax.dot_general(
            hidden, delta_low, (((0,), (0,)), ((), ())), preferred_element_type=jnp.float32
        ),
        "dp",
        scatter_dimension=0,
        tiled=True,
    )
    key_grad = weight_sum / math.sqrt(row_count * dp_size)
    return (feature_delta, key_grad)


CORE, X, Y = 1, 2, 4
PLANE = 8
PLANE_MASKS = (0, X, Y, X | Y)


def swap(value, mask):
    size = lax.axis_size("dp")
    return lax.ppermute(value, "dp", [(i, i ^ mask) for i in range(size)])


def after(value, *others):
    return lax.optimization_barrier((value, *others))[0]


def dot(a, b, dims):
    return lax.dot_general(a, b, (dims, ((), ())), preferred_element_type=jnp.float32)


def fetch(pairs, sems):
    copies = [
        pltpu.make_async_copy(source, target, sems.at[n])
        for n, (source, target) in enumerate(pairs)
    ]
    for copy in copies:
        copy.start()
    return copies


def project_kernel(begin, chips_ref, own_ref, mate_ref, *refs):
    begun = None
    if begin:
        begun, *refs = refs
    *pieces, weight_ref, acc, held, weights, sems = refs
    depth = pieces[0].shape[0]
    count = len(pieces)

    def rows_of(ref, n):
        return ref.at[n * depth : (n + 1) * depth, :]

    pairs = []
    for n, ref in enumerate(pieces):
        at = pl.multiple_of(chips_ref[begin + n] * depth, depth)
        pairs += [
            (ref, rows_of(weights, n)),
            (own_ref.at[:, pl.ds(at, depth)], held.at[n, 0]),
            (mate_ref.at[:, pl.ds(at, depth)], held.at[n, 1]),
        ]
    copies = fetch(pairs, sems)
    if begin:
        acc[...] = begun[...]
    kept = []
    for n in range(count):
        for copy in copies[3 * n : 3 * n + 3]:
            copy.wait()
        out = pltpu.make_async_copy(
            rows_of(weights, n), rows_of(weight_ref, n), sems.at[3 * count + n]
        )
        out.start()
        kept.append(out)
        piece = rows_of(weights, n)[...]
        for side in range(2):
            part = dot(held[n, side], piece, ((1,), (0,)))
            if begin + n == 0:
                acc[side] = part
            else:
                acc[side] += part
    return kept


def first_project_kernel(*refs):
    for copy in project_kernel(0, *refs):
        copy.wait()


def delta_kernel(begin, chips_ref, me_ref, own_cot_ref, mate_cot_ref, *refs):
    *refs, delta_ref, weight_ref, acc, held, weights, sems = refs
    kept = project_kernel(begin, chips_ref, *refs, weight_ref, acc, held, weights, sems)
    core = me_ref[0] & 1
    rows = acc.shape[1]
    delta_ref[2 * rows :, :] = jnp.zeros_like(delta_ref[2 * rows :, :])
    for side, cot_ref in enumerate((own_cot_ref, mate_cot_ref)):
        at = pl.multiple_of((core ^ side) * rows, rows)
        for head in range(own_cot_ref.shape[1] // HEAD_DIM):
            cols = slice(head * HEAD_DIM, (head + 1) * HEAD_DIM)
            proj = acc[side, :, cols]
            scale = jnp.sqrt(jnp.mean(proj * proj, axis=1, keepdims=True) + epsilon)
            normed = proj / scale
            upstream = cot_ref[:rows, cols].astype(jnp.float32)
            delta = (upstream - normed * jnp.mean(upstream * normed, axis=1, keepdims=True)) / scale
            delta_ref[pl.ds(at, rows), cols] = delta.astype(jnp.bfloat16)
        delta_ref[2 * rows :, pl.ds(at, rows)] = cot_ref[rows:, :rows]
    for copy in kept:
        copy.wait()


def select_kernel(me_ref, *refs):
    deltas, sent, (held, sems) = refs[:4], refs[4:8], refs[8:]
    copies = fetch([(ref, held.at[n]) for n, ref in enumerate(deltas)], sems)
    rows = (held.shape[1] - CODE_ROWS) // 2
    per_core = sent[0].shape[0] // 2
    per_chip = per_core // len(deltas)
    iota = lax.broadcasted_iota(jnp.int32, (8 * per_chip, 2 * rows), 0)
    block = lax.shift_right_logical(iota, per_chip.bit_length() - 1)
    slot = iota & (per_chip - 1)
    wanted = ((me_ref[0] & -2) ^ (block & -2)) | (block & 1)
    for n in range(len(deltas)):
        copies[n].wait()
        code = held[n, 2 * rows :, : 2 * rows].astype(jnp.float32).astype(jnp.int32)
        hot = (wanted == code[0:1, :]) & (slot == code[1:2, :])
        found = dot(hot.astype(jnp.bfloat16), held[n, : 2 * rows, :], ((1,), (0,)))
        found = found.astype(jnp.bfloat16)
        for place in range(8):
            at = place % 2 * per_core + n * per_chip
            sent[place // 2][at : at + per_chip, :] = found[
                place * per_chip : (place + 1) * per_chip, :
            ]


def share_kernel(me_ref, *refs):
    got, (keep_ref, give_ref) = refs[:4], refs[4:]
    count = keep_ref.shape[1]
    core = me_ref[0] & 1
    for n, ref in enumerate(got):
        keep_ref[n] = ref[pl.ds(pl.multiple_of(core * count, count), count), :]
        give_ref[n] = ref[pl.ds(pl.multiple_of((1 - core) * count, count), count), :]


def weight_grad_kernel(me_ref, own_ref, mate_ref, *refs):
    *deltas, part_ref, hidden, held, acc, sems = refs
    plane = lax.shift_right_logical(me_ref[0], 3)
    core = me_ref[0] & 1
    rows = own_ref.shape[1]
    pairs = []
    for n, ref in enumerate(deltas):
        own = pl.multiple_of((2 * n + core) * rows, rows)
        mate = pl.multiple_of((2 * n + 1 - core) * rows, rows)
        pairs += [
            (own_ref.at[plane ^ n], hidden.at[pl.ds(own, rows), :]),
            (mate_ref.at[plane ^ n], hidden.at[pl.ds(mate, rows), :]),
            (ref.at[: 2 * rows, :], held.at[2 * n * rows : 2 * (n + 1) * rows, :]),
        ]
    copies = fetch(pairs, sems)
    for first in (0, 2):
        for copy in copies[3 * first : 3 * first + 6]:
            copy.wait()
        part = slice(2 * first * rows, 2 * (first + 2) * rows)
        terms = dot(hidden[part, :], held[part, :], ((0,), (0,)))
        if first == 0:
            acc[...] = terms
        else:
            part_ref[...] = (acc[...] + terms).astype(jnp.bfloat16)


def sum_kernel(norm, parts_ref, grad_ref):
    half = parts_ref.shape[3]
    for side in range(2):
        total = parts_ref[0, side].astype(jnp.float32)
        for chip in range(1, parts_ref.shape[0]):
            total += parts_ref[chip, side].astype(jnp.float32)
        grad_ref[:, side * half : (side + 1) * half] = total / norm


def row_grad_kernel(chips_ref, me_ref, own_got_ref, mate_got_ref, *refs):
    weight_refs, (out_ref, weights, out, rows_ref, sems) = refs[:4], refs[4:]
    chips, count, half = own_got_ref.shape
    block = count // 4
    depth = half // 2
    pieces = weights.shape[1] // depth
    level = lax.shift_right_logical(me_ref[0], 3)

    def rows_of(ref, n):
        return ref.at[n * depth : (n + 1) * depth, :]

    pairs = []
    for n in range(pieces):
        first = weight_refs[0].shape[0] // depth
        for side in range(2):
            ref = weight_refs[side] if n < first else weight_refs[2 + side]
            pairs.append((rows_of(ref, n % first), rows_of(weights.at[side], n)))
    copies = fetch(pairs, sems)
    for side, got_ref in enumerate((own_got_ref, mate_got_ref)):
        for chip, mask in enumerate(PLANE_MASKS):
            place = lax.shift_right_logical((me_ref[0] ^ mask) & 6, 1)
            for n in range(4):
                at = pl.multiple_of(((level ^ n) * chips + place) * block, block)
                rows_ref[side, pl.ds(at, block), :] = got_ref[chip, n * block : (n + 1) * block, :]
    written = []
    for n in range(pieces):
        for copy in copies[2 * n : 2 * n + 2]:
            copy.wait()
        total = dot(rows_ref[0], rows_of(weights.at[0], n)[...], ((1,), (1,)))
        total += dot(rows_ref[1], rows_of(weights.at[1], n)[...], ((1,), (1,)))
        out[n] = total.astype(jnp.bfloat16)
        at = pl.multiple_of(chips_ref[n] * depth, depth)
        copy = pltpu.make_async_copy(
            out.at[n], out_ref.at[:, pl.ds(at, depth)], sems.at[2 * pieces + n]
        )
        copy.start()
        written.append(copy)
    for copy in written:
        copy.wait()


def code_rows(destination, core, per_peer, width):
    positions = jnp.arange(destination.shape[0], dtype=jnp.int32)
    same = (destination[:, None] == destination[None, :]) & (
        positions[:, None] < positions[None, :]
    )
    earlier = jnp.sum(same.astype(jnp.int32), axis=0)
    codes = jnp.stack([destination, core * per_peer + earlier]).astype(jnp.bfloat16)
    return jnp.pad(codes, ((0, CODE_ROWS - 2), (0, width - destination.shape[0])))


def anywhere(count):
    return [pl.BlockSpec(memory_space=pl.ANY)] * count


def vmem(count):
    return [pl.BlockSpec(memory_space=pltpu.VMEM)] * count


def anywhere(count):
    return [pl.BlockSpec(memory_space=pl.ANY)] * count


SCALAR = pl.BlockSpec(memory_space=pltpu.SMEM)
PARAMS = pltpu.CompilerParams(vmem_limit_bytes=VMEM_LIMIT)
def grant(mebibytes):
    return pltpu.CompilerParams(vmem_limit_bytes=mebibytes << 20)


def per_device_paired(tokens, key_cot, routes, counts, widths, key_weight):
    rows, width_model = tokens.shape
    cols = key_cot.shape[1]
    half_cols = cols // 2
    size = lax.axis_size("dp")
    chips = size // 2
    levels = size // PLANE
    per_peer = 2 * rows // size
    receive = size * per_peer
    wide = width_model // levels
    me = lax.axis_index("dp")
    core = me % 2
    me_scalar = me.astype(jnp.int32).reshape(1)

    def mine(value):
        return lax.dynamic_slice_in_dim(value, core * half_cols, half_cols, 1)

    def theirs(value):
        return lax.dynamic_slice_in_dim(value, (1 - core) * half_cols, half_cols, 1)

    mate_shard = swap(key_weight, CORE)
    piece = jnp.where(
        core == 0,
        jnp.concatenate([key_weight[:, :half_cols], mate_shard[:, :half_cols]], axis=0),
        jnp.concatenate([mate_shard[:, half_cols:], key_weight[:, half_cols:]], axis=0),
    )
    near, far, both = PLANE, 2 * PLANE, 3 * PLANE
    have = {0: piece}

    def after_round(**beside):
        names, masks = list(beside), list(have)
        values = lax.optimization_barrier([*beside.values(), *have.values()])
        have.update(zip(masks, values[len(names) :]))
        return values[: len(names)]

    have.update(
        {
            Y: swap(piece, Y),
            X: swap(piece, X),
            near: swap(piece, near),
            far: swap(piece, far),
        }
    )
    from_both = swap(piece, both)
    by_level = jnp.stack([tokens[:, z * wide : (z + 1) * wide] for z in range(levels)])
    by_level, key_cot, counts, routes = after_round(
        by_level=by_level, key_cot=key_cot, counts=counts, routes=routes
    )
    columns = [[p + PLANE * z for z in range(levels)] for p in range(PLANE)]
    own_features = lax.all_to_all(
        by_level, "dp", split_axis=0, concat_axis=0, axis_index_groups=columns, tiled=True
    )
    have.update(
        {
            near | X: swap(have[near], X),
            near | Y: swap(have[near], Y),
            far | X: swap(have[far], X),
            far | Y: swap(have[far], Y),
        }
    )
    have[both] = from_both
    bounds = jnp.cumsum(counts[0])
    positions = jnp.arange(rows, dtype=jnp.int32)
    subnet = jnp.sum((positions[:, None] >= bounds[None, : NSUB - 1]).astype(jnp.int32), axis=1)
    subnet_match = subnet[:, None] == jnp.arange(NSUB, dtype=jnp.int32)[None, :]
    row_width = jnp.sum(jnp.where(subnet_match, widths[None, :], 0), axis=1)
    head_of_col = jnp.arange(cols, dtype=jnp.int32) // HEAD_DIM
    upstream = jnp.where(
        head_of_col[None, :] < row_width[:, None], key_cot, jnp.zeros_like(key_cot)
    )
    codes = code_rows(routes[:, 0], core, per_peer, half_cols)
    own_cot = jnp.concatenate([mine(upstream), codes], axis=0)

    own_cot, give_cot, tokens = after_round(
        own_cot=own_cot,
        give_cot=jnp.concatenate([theirs(upstream), codes], axis=0),
        tokens=tokens,
    )
    mate_tokens = swap(tokens, CORE)
    have.update(
        {
            both | X: swap(have[both], X),
            both | Y: swap(have[both], Y),
            X | Y: swap(have[Y], X),
            far | X | Y: swap(have[far | X], Y),
        }
    )
    mate_tokens, give_cot, own_cot = after_round(
        mate_tokens=mate_tokens, give_cot=give_cot, own_cot=own_cot
    )
    mate_cot = swap(give_cot, CORE)

    first_masks = list(have)
    last_masks = [near | X | Y, both | X | Y]
    order = jnp.stack([lax.shift_right_logical(me ^ mask, 1) for mask in first_masks + last_masks])
    depth = width_model // chips
    sums = jax.ShapeDtypeStruct((2, rows, half_cols), jnp.float32)

    def project(kernel, count, results, inputs, specs, name):
        return pl.pallas_call(
            kernel,
            out_shape=(*results, jax.ShapeDtypeStruct((count * depth, half_cols), jnp.bfloat16))
            + ((sums,) if name == "project" else ()),
            in_specs=specs + anywhere(count),
            out_specs=(*vmem(len(results)), anywhere(1)[0])
            + (tuple(vmem(1)) if name == "project" else ()),
            scratch_shapes=([] if name == "project" else [pltpu.VMEM(sums.shape, sums.dtype)])
            + [
                pltpu.VMEM((count, 2, rows, depth), jnp.bfloat16),
                pltpu.VMEM((count * depth, half_cols), jnp.bfloat16),
                pltpu.SemaphoreType.DMA((4 * count,)),
            ],
            compiler_params=PARAMS,
            name=name,
        )(*inputs)

    first_weight, begun = project(
        first_project_kernel,
        len(first_masks),
        (),
        (order, tokens, mate_tokens, *[have[mask] for mask in first_masks]),
        [SCALAR] + anywhere(2),
        "project",
    )
    have.update(
        {
            near | X | Y: swap(have[near | Y], X),
            both | X | Y: swap(have[both | X], Y),
        }
    )
    mate_cot, own_cot, own_features, begun, first_weight = after_round(
        mate_cot=mate_cot,
        own_cot=own_cot,
        own_features=own_features,
        begun=begun,
        first_weight=first_weight,
    )
    mate_features = swap(own_features, CORE)
    delta, last_weight = project(
        functools.partial(delta_kernel, len(first_masks)),
        len(last_masks),
        (jax.ShapeDtypeStruct((2 * rows + CODE_ROWS, half_cols), jnp.bfloat16),),
        (
            order,
            me_scalar,
            own_cot,
            mate_cot,
            tokens,
            mate_tokens,
            begun,
            *[have[mask] for mask in last_masks],
        ),
        [SCALAR] * 2 + vmem(2) + anywhere(2) + vmem(1),
        "delta",
    )

    delta_near, delta_far, mate_features = lax.optimization_barrier(
        (swap(delta, near), swap(delta, far), mate_features)
    )
    deltas = [delta, delta_near, delta_far, swap(delta_far, near)]
    first_weight, last_weight, *deltas[1:] = lax.optimization_barrier(
        (first_weight, last_weight, *deltas[1:])
    )
    mate_first, mate_last = swap(first_weight, CORE), swap(last_weight, CORE)
    count = levels * 2 * per_peer
    delta_room = pltpu.VMEM((levels, *delta.shape), jnp.bfloat16)
    selected = pl.pallas_call(
        select_kernel,
        out_shape=[jax.ShapeDtypeStruct((2 * count, half_cols), jnp.bfloat16)] * 4,
        in_specs=[SCALAR] + anywhere(levels),
        out_specs=vmem(4),
        scratch_shapes=[delta_room, pltpu.SemaphoreType.DMA((levels,))],
        compiler_params=grant(16),
        name="select",
    )(me_scalar, *deltas)
    got = [
        swap(value, mask) if mask else value for value, mask in zip(selected, PLANE_MASKS)
    ]
    shard = width_model // size
    terms = pl.pallas_call(
        weight_grad_kernel,
        out_shape=jax.ShapeDtypeStruct((wide, half_cols), jnp.bfloat16),
        in_specs=[SCALAR] + anywhere(2 + levels),
        out_specs=vmem(1)[0],
        scratch_shapes=[
            pltpu.VMEM((levels * 2 * rows, wide), jnp.bfloat16),
            pltpu.VMEM((levels * 2 * rows, half_cols), jnp.bfloat16),
            pltpu.VMEM((wide, half_cols), jnp.float32),
            pltpu.SemaphoreType.DMA((3 * levels,)),
        ],
        compiler_params=grant(16),
        name="weight_grad",
    )(me_scalar, own_features, mate_features, after(delta, *selected), *deltas[1:])
    parts = lax.all_to_all(
        after(terms, *got).reshape(PLANE, shard, half_cols),
        "dp",
        split_axis=0,
        concat_axis=0,
        axis_index_groups=[[z * PLANE + p for p in range(PLANE)] for z in range(levels)],
        tiled=True,
    ).reshape(PLANE // 2, 2, shard, half_cols)

    own_got, give_got = pl.pallas_call(
        share_kernel,
        out_shape=[jax.ShapeDtypeStruct((4, count, half_cols), jnp.bfloat16)] * 2,
        in_specs=[SCALAR] + vmem(4),
        out_specs=vmem(2),
        compiler_params=grant(16),
        name="share",
    )(me_scalar, *got)
    mate_got = swap(give_got, CORE)

    row_grads = pl.pallas_call(
        row_grad_kernel,
        out_shape=jax.ShapeDtypeStruct((receive, width_model), jnp.bfloat16),
        in_specs=[SCALAR] * 2 + vmem(2) + anywhere(4),
        out_specs=anywhere(1)[0],
        scratch_shapes=[
            pltpu.VMEM((2, width_model, half_cols), jnp.bfloat16),
            pltpu.VMEM((chips, receive, depth), jnp.bfloat16),
            pltpu.VMEM((2, receive, half_cols), jnp.bfloat16),
            pltpu.SemaphoreType.DMA((3 * chips,)),
        ],
        compiler_params=grant(32),
        name="row_grad",
    )(order, me_scalar, own_got, mate_got, first_weight, mate_first, last_weight, mate_last)

    key_grad = pl.pallas_call(
        functools.partial(sum_kernel, math.sqrt(rows * size)),
        out_shape=jax.ShapeDtypeStruct((shard, cols), jnp.float32),
        in_specs=vmem(1),
        out_specs=vmem(1)[0],
        compiler_params=grant(16),
        name="sum",
    )(after(parts, row_grads))
    return (row_grads, key_grad)


def solution(mesh):
    size, split = mesh.shape["dp"], mesh.shape["mp"]
    paired = split == 1 and size == 32
    return jax.shard_map(
        per_device_paired if paired else per_device_general,
        mesh=mesh,
        in_specs=(P("dp", None), P("dp", "mp"), P("dp", None), P("dp", None), P(), P("dp", "mp")),
        out_specs=(P("dp", "mp"), P("dp", "mp")),
        check_vma=False,
    )
```

```python
import functools
import math

import jax
import jax.numpy as jnp
from jax import lax
from jax.experimental import pallas as pl
from jax.experimental.pallas import tpu as pltpu
from jax.sharding import PartitionSpec as P

HEAD_DIM = 128
NSUB = 4
VMEM_LIMIT = 60 * 1024 * 1024
CODE_ROWS = 16
epsilon = 1e-06


def per_device_general(tokens, key_cot, routes, counts, widths, key_weight):
    row_count = tokens.shape[0]
    width_model = tokens.shape[1]
    local_cols = key_cot.shape[1]
    local_heads = local_cols // HEAD_DIM
    dp_size = lax.axis_size("dp")
    per_peer = 2 * row_count // dp_size
    receive = dp_size * per_peer
    destination = routes[:, 0]
    one_hot = (destination[:, None] == jnp.arange(dp_size, dtype=jnp.int32)[None, :]).astype(
        jnp.int32
    )
    earlier = jnp.sum(jnp.cumsum(one_hot, axis=0) * one_hot, axis=1) - 1
    send_slot = destination * per_peer + earlier
    bounds = jnp.cumsum(counts[0])
    positions = jnp.arange(row_count, dtype=jnp.int32)
    subnet = jnp.sum((positions[:, None] >= bounds[None, : NSUB - 1]).astype(jnp.int32), axis=1)
    send_subnet = (
        jnp.full((receive,), -1, jnp.int32).at[send_slot].set(subnet).reshape(dp_size, per_peer)
    )
    send_cot = jnp.zeros((receive, local_cols), jnp.bfloat16).at[send_slot].set(key_cot)
    send_cot = send_cot.reshape(dp_size, per_peer, local_cols)
    send_tokens = jnp.zeros((receive, width_model), jnp.bfloat16).at[send_slot].set(tokens)
    send_tokens = send_tokens.reshape(dp_size, per_peer, width_model)
    got_tokens, got_cot, got_subnet = (
        lax.all_to_all(send_tokens, "dp", split_axis=0, concat_axis=0, tiled=True),
        lax.all_to_all(send_cot, "dp", split_axis=0, concat_axis=0, tiled=True),
        lax.all_to_all(send_subnet, "dp", split_axis=0, concat_axis=0, tiled=True),
    )
    hidden = got_tokens.reshape(receive, width_model)
    got_cot = got_cot.reshape(receive, local_cols)
    got_subnet = got_subnet.reshape(receive)
    full_weight = lax.all_gather(key_weight, "dp", axis=0, tiled=True)
    key_proj = jnp.dot(hidden, full_weight, preferred_element_type=jnp.float32)
    per_head = key_proj.reshape(receive, local_heads, HEAD_DIM)
    head_scale = jnp.sqrt(jnp.mean(per_head * per_head, axis=2, keepdims=True) + epsilon)
    outputs = per_head / head_scale
    subnet_match = got_subnet[:, None] == jnp.arange(NSUB, dtype=jnp.int32)[None, :]
    row_width = jnp.sum(jnp.where(subnet_match, widths[None, :], 0), axis=1)
    head_index = lax.axis_index("mp") * local_heads + jnp.arange(local_heads, dtype=jnp.int32)
    head_mask = (head_index[None, :] < row_width[:, None]).astype(jnp.float32)
    upstream = (
        got_cot.astype(jnp.float32).reshape(receive, local_heads, HEAD_DIM) * head_mask[:, :, None]
    )
    key_delta = (
        upstream - outputs * jnp.mean(upstream * outputs, axis=2, keepdims=True)
    ) / head_scale
    delta_low = key_delta.reshape(receive, local_cols).astype(jnp.bfloat16)
    part_delta = lax.dot_general(
        delta_low, full_weight, (((1,), (1,)), ((), ())), preferred_element_type=jnp.float32
    )
    rounded = lax.optimization_barrier(part_delta.astype(jnp.bfloat16)).astype(jnp.float32)
    feature_delta = lax.psum_scatter(
        rounded.astype(jnp.bfloat16), "mp", scatter_dimension=1, tiled=True
    )
    weight_sum = lax.psum_scatter(
        lax.dot_general(
            hidden, delta_low, (((0,), (0,)), ((), ())), preferred_element_type=jnp.float32
        ),
        "dp",
        scatter_dimension=0,
        tiled=True,
    )
    key_grad = weight_sum / math.sqrt(row_count * dp_size)
    return (feature_delta, key_grad)


CORE, X, Y = 1, 2, 4
PLANE = 8
PLANE_MASKS = (0, X, Y, X | Y)


def swap(value, mask):
    size = lax.axis_size("dp")
    return lax.ppermute(value, "dp", [(i, i ^ mask) for i in range(size)])


def after(value, *others):
    return lax.optimization_barrier((value, *others))[0]


def dot(a, b, dims):
    return lax.dot_general(a, b, (dims, ((), ())), preferred_element_type=jnp.float32)


def fetch(pairs, sems):
    copies = [
        pltpu.make_async_copy(source, target, sems.at[n])
        for n, (source, target) in enumerate(pairs)
    ]
    for copy in copies:
        copy.start()
    return copies


def project_kernel(begin, chips_ref, own_ref, mate_ref, *refs):
    begun = None
    if begin:
        begun, *refs = refs
    *pieces, weight_ref, acc, held, weights, sems = refs
    depth = pieces[0].shape[0]
    count = len(pieces)

    def rows_of(ref, n):
        return ref.at[n * depth : (n + 1) * depth, :]

    pairs = []
    for n, ref in enumerate(pieces):
        at = pl.multiple_of(chips_ref[begin + n] * depth, depth)
        pairs += [
            (ref, rows_of(weights, n)),
            (own_ref.at[:, pl.ds(at, depth)], held.at[n, 0]),
            (mate_ref.at[:, pl.ds(at, depth)], held.at[n, 1]),
        ]
    copies = fetch(pairs, sems)
    if begin:
        acc[...] = begun[...]
    kept = []
    for n in range(count):
        for copy in copies[3 * n : 3 * n + 3]:
            copy.wait()
        out = pltpu.make_async_copy(
            rows_of(weights, n), rows_of(weight_ref, n), sems.at[3 * count + n]
        )
        out.start()
        kept.append(out)
        piece = rows_of(weights, n)[...]
        for side in range(2):
            part = dot(held[n, side], piece, ((1,), (0,)))
            if begin + n == 0:
                acc[side] = part
            else:
                acc[side] += part
    return kept


def first_project_kernel(*refs):
    for copy in project_kernel(0, *refs):
        copy.wait()


def delta_kernel(begin, chips_ref, me_ref, own_cot_ref, mate_cot_ref, *refs):
    *refs, delta_ref, weight_ref, acc, held, weights, sems = refs
    kept = project_kernel(begin, chips_ref, *refs, weight_ref, acc, held, weights, sems)
    core = me_ref[0] & 1
    rows = acc.shape[1]
    delta_ref[2 * rows :, :] = jnp.zeros_like(delta_ref[2 * rows :, :])
    for side, cot_ref in enumerate((own_cot_ref, mate_cot_ref)):
        at = pl.multiple_of((core ^ side) * rows, rows)
        for head in range(own_cot_ref.shape[1] // HEAD_DIM):
            cols = slice(head * HEAD_DIM, (head + 1) * HEAD_DIM)
            proj = acc[side, :, cols]
            scale = jnp.sqrt(jnp.mean(proj * proj, axis=1, keepdims=True) + epsilon)
            normed = proj / scale
            upstream = cot_ref[:rows, cols].astype(jnp.float32)
            delta = (upstream - normed * jnp.mean(upstream * normed, axis=1, keepdims=True)) / scale
            delta_ref[pl.ds(at, rows), cols] = delta.astype(jnp.bfloat16)
        delta_ref[2 * rows :, pl.ds(at, rows)] = cot_ref[rows:, :rows]
    for copy in kept:
        copy.wait()


def select_kernel(me_ref, *refs):
    *deltas, sent_ref, held, sems = refs
    copies = fetch([(ref, held.at[n]) for n, ref in enumerate(deltas)], sems)
    rows = (held.shape[1] - CODE_ROWS) // 2
    per_chip = sent_ref.shape[1] // len(deltas)
    iota = lax.broadcasted_iota(jnp.int32, (PLANE * per_chip, 2 * rows), 0)
    wanted = (me_ref[0] & -PLANE) + lax.shift_right_logical(iota, per_chip.bit_length() - 1)
    slot = iota & (per_chip - 1)
    for n in range(len(deltas)):
        copies[n].wait()
        code = held[n, 2 * rows :, : 2 * rows].astype(jnp.float32).astype(jnp.int32)
        hot = (wanted == code[0:1, :]) & (slot == code[1:2, :])
        found = dot(hot.astype(jnp.bfloat16), held[n, : 2 * rows, :], ((1,), (0,)))
        found = found.astype(jnp.bfloat16)
        for place in range(PLANE):
            sent_ref[place, n * per_chip : (n + 1) * per_chip, :] = found[
                place * per_chip : (place + 1) * per_chip, :
            ]


def weight_grad_kernel(me_ref, own_ref, mate_ref, *refs):
    *deltas, own_part_ref, part_x, part_y, part_both, hidden, held, acc, sems = refs
    part_refs = (part_x, part_y, part_both)
    plane = lax.shift_right_logical(me_ref[0], 3)
    core = me_ref[0] & 1
    rows = own_ref.shape[1]
    pairs = []
    for n, ref in enumerate(deltas):
        own = pl.multiple_of((2 * n + core) * rows, rows)
        mate = pl.multiple_of((2 * n + 1 - core) * rows, rows)
        pairs += [
            (own_ref.at[plane ^ n], hidden.at[pl.ds(own, rows), :]),
            (mate_ref.at[plane ^ n], hidden.at[pl.ds(mate, rows), :]),
            (ref.at[: 2 * rows, :], held.at[2 * n * rows : 2 * (n + 1) * rows, :]),
        ]
    copies = fetch(pairs, sems)
    for first in (0, 2):
        for copy in copies[3 * first : 3 * first + 6]:
            copy.wait()
        part = slice(2 * first * rows, 2 * (first + 2) * rows)
        terms = dot(hidden[part, :], held[part, :], ((0,), (0,)))
        if first == 0:
            acc[...] = terms
        else:
            acc[...] += terms
    count = own_part_ref.shape[0]
    for ref, mask in zip((own_part_ref, *part_refs), PLANE_MASKS):
        place = lax.shift_right_logical((me_ref[0] ^ mask) & 6, 1)
        at = pl.multiple_of(place * count, count)
        ref[...] = acc[pl.ds(at, count), :].astype(ref.dtype)


def sum_kernel(me_ref, own_ref, *refs):
    *part_refs, keep_ref, give_ref = refs
    count = keep_ref.shape[0]
    for ref, core in ((keep_ref, me_ref[0] & 1), (give_ref, 1 - (me_ref[0] & 1))):
        here = pl.ds(pl.multiple_of(core * count, count), count)
        total = own_ref[here, :]
        for part_ref in part_refs:
            total += part_ref[here, :].astype(jnp.float32)
        ref[...] = total


def join_kernel(norm, me_ref, own_ref, mate_ref, grad_ref):
    half = own_ref.shape[1]
    for ref, core in ((own_ref, me_ref[0] & 1), (mate_ref, 1 - (me_ref[0] & 1))):
        grad_ref[:, pl.ds(pl.multiple_of(core * half, half), half)] = ref[...] / norm


def row_grad_kernel(chips_ref, me_ref, got_ref, *refs):
    weight_refs, (out_ref, weights, out, rows_ref, sems) = refs[:4], refs[4:]
    chips, _, count, half = got_ref.shape
    block = count // 4
    depth = half // 2
    pieces = weights.shape[1] // depth
    level = lax.shift_right_logical(me_ref[0], 3)

    def rows_of(ref, n):
        return ref.at[n * depth : (n + 1) * depth, :]

    pairs = []
    for n in range(pieces):
        first = weight_refs[0].shape[0] // depth
        for side in range(2):
            ref = weight_refs[side] if n < first else weight_refs[2 + side]
            pairs.append((rows_of(ref, n % first), rows_of(weights.at[side], n)))
    copies = fetch(pairs, sems)
    core = me_ref[0] & 1
    for chip in range(chips):
        for n in range(4):
            at = pl.multiple_of(((level ^ n) * chips + chip) * block, block)
            for side in range(2):
                rows = got_ref[chip, pl.ds(core ^ side, 1), n * block : (n + 1) * block, :]
                rows_ref[side, pl.ds(at, block), :] = rows[0]
    written = []
    for n in range(pieces):
        for copy in copies[2 * n : 2 * n + 2]:
            copy.wait()
        total = dot(rows_ref[0], rows_of(weights.at[0], n)[...], ((1,), (1,)))
        total += dot(rows_ref[1], rows_of(weights.at[1], n)[...], ((1,), (1,)))
        out[n] = total.astype(jnp.bfloat16)
        at = pl.multiple_of(chips_ref[n] * depth, depth)
        copy = pltpu.make_async_copy(
            out.at[n], out_ref.at[:, pl.ds(at, depth)], sems.at[2 * pieces + n]
        )
        copy.start()
        written.append(copy)
    for copy in written:
        copy.wait()


def code_rows(destination, core, per_peer, width):
    positions = jnp.arange(destination.shape[0], dtype=jnp.int32)
    same = (destination[:, None] == destination[None, :]) & (
        positions[:, None] < positions[None, :]
    )
    earlier = jnp.sum(same.astype(jnp.int32), axis=0)
    codes = jnp.stack([destination, core * per_peer + earlier]).astype(jnp.bfloat16)
    return jnp.pad(codes, ((0, CODE_ROWS - 2), (0, width - destination.shape[0])))


def anywhere(count):
    return [pl.BlockSpec(memory_space=pl.ANY)] * count


def vmem(count):
    return [pl.BlockSpec(memory_space=pltpu.VMEM)] * count


def anywhere(count):
    return [pl.BlockSpec(memory_space=pl.ANY)] * count


SCALAR = pl.BlockSpec(memory_space=pltpu.SMEM)
PARAMS = pltpu.CompilerParams(vmem_limit_bytes=VMEM_LIMIT)
def grant(mebibytes):
    return pltpu.CompilerParams(vmem_limit_bytes=mebibytes << 20)


def per_device_paired(tokens, key_cot, routes, counts, widths, key_weight):
    rows, width_model = tokens.shape
    cols = key_cot.shape[1]
    half_cols = cols // 2
    size = lax.axis_size("dp")
    chips = size // 2
    levels = size // PLANE
    per_peer = 2 * rows // size
    receive = size * per_peer
    wide = width_model // levels
    me = lax.axis_index("dp")
    core = me % 2
    me_scalar = me.astype(jnp.int32).reshape(1)

    def mine(value):
        return lax.dynamic_slice_in_dim(value, core * half_cols, half_cols, 1)

    def theirs(value):
        return lax.dynamic_slice_in_dim(value, (1 - core) * half_cols, half_cols, 1)

    mate_shard = swap(key_weight, CORE)
    piece = jnp.where(
        core == 0,
        jnp.concatenate([key_weight[:, :half_cols], mate_shard[:, :half_cols]], axis=0),
        jnp.concatenate([mate_shard[:, half_cols:], key_weight[:, half_cols:]], axis=0),
    )
    near, far, both = PLANE, 2 * PLANE, 3 * PLANE
    have = {0: piece}

    def after_round(**beside):
        names, masks = list(beside), list(have)
        values = lax.optimization_barrier([*beside.values(), *have.values()])
        have.update(zip(masks, values[len(names) :]))
        return values[: len(names)]

    have.update(
        {
            Y: swap(piece, Y),
            X: swap(piece, X),
            near: swap(piece, near),
            far: swap(piece, far),
        }
    )
    from_both = swap(piece, both)
    by_level = jnp.stack([tokens[:, z * wide : (z + 1) * wide] for z in range(levels)])
    by_level, key_cot, counts, routes = after_round(
        by_level=by_level, key_cot=key_cot, counts=counts, routes=routes
    )
    columns = [[p + PLANE * z for z in range(levels)] for p in range(PLANE)]
    own_features = lax.all_to_all(
        by_level, "dp", split_axis=0, concat_axis=0, axis_index_groups=columns, tiled=True
    )
    have.update(
        {
            near | X: swap(have[near], X),
            near | Y: swap(have[near], Y),
            far | X: swap(have[far], X),
            far | Y: swap(have[far], Y),
        }
    )
    have[both] = from_both
    bounds = jnp.cumsum(counts[0])
    positions = jnp.arange(rows, dtype=jnp.int32)
    subnet = jnp.sum((positions[:, None] >= bounds[None, : NSUB - 1]).astype(jnp.int32), axis=1)
    subnet_match = subnet[:, None] == jnp.arange(NSUB, dtype=jnp.int32)[None, :]
    row_width = jnp.sum(jnp.where(subnet_match, widths[None, :], 0), axis=1)
    head_of_col = jnp.arange(cols, dtype=jnp.int32) // HEAD_DIM
    upstream = jnp.where(
        head_of_col[None, :] < row_width[:, None], key_cot, jnp.zeros_like(key_cot)
    )
    codes = code_rows(routes[:, 0], core, per_peer, half_cols)
    own_cot = jnp.concatenate([mine(upstream), codes], axis=0)

    own_cot, give_cot, tokens = after_round(
        own_cot=own_cot,
        give_cot=jnp.concatenate([theirs(upstream), codes], axis=0),
        tokens=tokens,
    )
    mate_tokens = swap(tokens, CORE)
    have.update(
        {
            both | X: swap(have[both], X),
            both | Y: swap(have[both], Y),
            X | Y: swap(have[Y], X),
            far | X | Y: swap(have[far | X], Y),
        }
    )
    mate_tokens, give_cot, own_cot = after_round(
        mate_tokens=mate_tokens, give_cot=give_cot, own_cot=own_cot
    )
    mate_cot = swap(give_cot, CORE)

    first_masks = list(have)
    last_masks = [near | X | Y, both | X | Y]
    order = jnp.stack([lax.shift_right_logical(me ^ mask, 1) for mask in first_masks + last_masks])
    depth = width_model // chips
    sums = jax.ShapeDtypeStruct((2, rows, half_cols), jnp.float32)

    def project(kernel, count, results, inputs, specs, name):
        return pl.pallas_call(
            kernel,
            out_shape=(*results, jax.ShapeDtypeStruct((count * depth, half_cols), jnp.bfloat16))
            + ((sums,) if name == "project" else ()),
            in_specs=specs + anywhere(count),
            out_specs=(*vmem(len(results)), anywhere(1)[0])
            + (tuple(vmem(1)) if name == "project" else ()),
            scratch_shapes=([] if name == "project" else [pltpu.VMEM(sums.shape, sums.dtype)])
            + [
                pltpu.VMEM((count, 2, rows, depth), jnp.bfloat16),
                pltpu.VMEM((count * depth, half_cols), jnp.bfloat16),
                pltpu.SemaphoreType.DMA((4 * count,)),
            ],
            compiler_params=PARAMS,
            name=name,
        )(*inputs)

    first_weight, begun = project(
        first_project_kernel,
        len(first_masks),
        (),
        (order, tokens, mate_tokens, *[have[mask] for mask in first_masks]),
        [SCALAR] + anywhere(2),
        "project",
    )
    have.update(
        {
            near | X | Y: swap(have[near | Y], X),
            both | X | Y: swap(have[both | X], Y),
        }
    )
    mate_cot, own_cot, own_features, begun, first_weight = after_round(
        mate_cot=mate_cot,
        own_cot=own_cot,
        own_features=own_features,
        begun=begun,
        first_weight=first_weight,
    )
    mate_features = swap(own_features, CORE)
    delta, last_weight = project(
        functools.partial(delta_kernel, len(first_masks)),
        len(last_masks),
        (jax.ShapeDtypeStruct((2 * rows + CODE_ROWS, half_cols), jnp.bfloat16),),
        (
            order,
            me_scalar,
            own_cot,
            mate_cot,
            tokens,
            mate_tokens,
            begun,
            *[have[mask] for mask in last_masks],
        ),
        [SCALAR] * 2 + vmem(2) + anywhere(2) + vmem(1),
        "delta",
    )

    delta_near, delta_far, mate_features = lax.optimization_barrier(
        (swap(delta, near), swap(delta, far), mate_features)
    )
    deltas = [delta, delta_near, delta_far, swap(delta_far, near)]
    first_weight, last_weight, *deltas[1:] = lax.optimization_barrier(
        (first_weight, last_weight, *deltas[1:])
    )
    mate_first, mate_last = swap(first_weight, CORE), swap(last_weight, CORE)
    count = levels * 2 * per_peer
    delta_room = pltpu.VMEM((levels, *delta.shape), jnp.bfloat16)
    selected = pl.pallas_call(
        select_kernel,
        out_shape=jax.ShapeDtypeStruct((PLANE, count, half_cols), jnp.bfloat16),
        in_specs=[SCALAR] + anywhere(levels),
        out_specs=vmem(1)[0],
        scratch_shapes=[delta_room, pltpu.SemaphoreType.DMA((levels,))],
        compiler_params=grant(16),
        name="select",
    )(me_scalar, *deltas)
    got = lax.all_to_all(
        selected,
        "dp",
        split_axis=0,
        concat_axis=0,
        axis_index_groups=[[z * PLANE + p for p in range(PLANE)] for z in range(levels)],
        tiled=True,
    ).reshape(PLANE // 2, 2, count, half_cols)

    shard = width_model // size
    mine_terms = jax.ShapeDtypeStruct((wide // 4, half_cols), jnp.float32)
    sent_terms = jax.ShapeDtypeStruct(mine_terms.shape, jnp.bfloat16)
    own_part, *parts = pl.pallas_call(
        weight_grad_kernel,
        out_shape=(mine_terms, *[sent_terms] * 3),
        in_specs=[SCALAR] + anywhere(2 + levels),
        out_specs=tuple(vmem(4)),
        scratch_shapes=[
            pltpu.VMEM((levels * 2 * rows, wide), jnp.bfloat16),
            pltpu.VMEM((levels * 2 * rows, half_cols), jnp.bfloat16),
            pltpu.VMEM((wide, half_cols), jnp.float32),
            pltpu.SemaphoreType.DMA((3 * levels,)),
        ],
        compiler_params=grant(16),
        name="weight_grad",
    )(me_scalar, own_features, mate_features, after(delta, selected), *deltas[1:])
    parts = [swap(part, mask) for part, mask in zip(parts, PLANE_MASKS[1:])]

    row_grads = pl.pallas_call(
        row_grad_kernel,
        out_shape=jax.ShapeDtypeStruct((receive, width_model), jnp.bfloat16),
        in_specs=[SCALAR] * 2 + vmem(1) + anywhere(4),
        out_specs=anywhere(1)[0],
        scratch_shapes=[
            pltpu.VMEM((2, width_model, half_cols), jnp.bfloat16),
            pltpu.VMEM((chips, receive, depth), jnp.bfloat16),
            pltpu.VMEM((2, receive, half_cols), jnp.bfloat16),
            pltpu.SemaphoreType.DMA((3 * chips,)),
        ],
        compiler_params=grant(32),
        name="row_grad",
    )(order, me_scalar, got, first_weight, mate_first, last_weight, mate_last)

    half_grad = jax.ShapeDtypeStruct((shard, half_cols), jnp.float32)
    keep_grad, give_grad = pl.pallas_call(
        sum_kernel,
        out_shape=(half_grad, half_grad),
        in_specs=[SCALAR] + vmem(4),
        out_specs=tuple(vmem(2)),
        compiler_params=grant(16),
        name="sum",
    )(me_scalar, after(own_part, row_grads), *parts)
    key_grad = pl.pallas_call(
        functools.partial(join_kernel, math.sqrt(rows * size)),
        out_shape=jax.ShapeDtypeStruct((shard, cols), jnp.float32),
        in_specs=[SCALAR] + vmem(2),
        out_specs=vmem(1)[0],
        compiler_params=grant(16),
        name="join",
    )(me_scalar, keep_grad, swap(give_grad, CORE))
    return (row_grads, key_grad)


def solution(mesh):
    size, split = mesh.shape["dp"], mesh.shape["mp"]
    paired = split == 1 and size == 32
    return jax.shard_map(
        per_device_paired if paired else per_device_general,
        mesh=mesh,
        in_specs=(P("dp", None), P("dp", "mp"), P("dp", None), P("dp", None), P(), P("dp", "mp")),
        out_specs=(P("dp", "mp"), P("dp", "mp")),
        check_vma=False,
    )
```

```python
import functools
import math

import jax
import jax.numpy as jnp
from jax import lax
from jax.experimental import pallas as pl
from jax.experimental.pallas import tpu as pltpu
from jax.sharding import PartitionSpec as P

HEAD_DIM = 128
NSUB = 4
VMEM_LIMIT = 60 * 1024 * 1024
CODE_ROWS = 16
epsilon = 1e-06


def per_device_general(tokens, key_cot, routes, counts, widths, key_weight):
    row_count = tokens.shape[0]
    width_model = tokens.shape[1]
    local_cols = key_cot.shape[1]
    local_heads = local_cols // HEAD_DIM
    dp_size = lax.axis_size("dp")
    per_peer = 2 * row_count // dp_size
    receive = dp_size * per_peer
    destination = routes[:, 0]
    one_hot = (destination[:, None] == jnp.arange(dp_size, dtype=jnp.int32)[None, :]).astype(
        jnp.int32
    )
    earlier = jnp.sum(jnp.cumsum(one_hot, axis=0) * one_hot, axis=1) - 1
    send_slot = destination * per_peer + earlier
    bounds = jnp.cumsum(counts[0])
    positions = jnp.arange(row_count, dtype=jnp.int32)
    subnet = jnp.sum((positions[:, None] >= bounds[None, : NSUB - 1]).astype(jnp.int32), axis=1)
    send_subnet = (
        jnp.full((receive,), -1, jnp.int32).at[send_slot].set(subnet).reshape(dp_size, per_peer)
    )
    send_cot = jnp.zeros((receive, local_cols), jnp.bfloat16).at[send_slot].set(key_cot)
    send_cot = send_cot.reshape(dp_size, per_peer, local_cols)
    send_tokens = jnp.zeros((receive, width_model), jnp.bfloat16).at[send_slot].set(tokens)
    send_tokens = send_tokens.reshape(dp_size, per_peer, width_model)
    got_tokens, got_cot, got_subnet = (
        lax.all_to_all(send_tokens, "dp", split_axis=0, concat_axis=0, tiled=True),
        lax.all_to_all(send_cot, "dp", split_axis=0, concat_axis=0, tiled=True),
        lax.all_to_all(send_subnet, "dp", split_axis=0, concat_axis=0, tiled=True),
    )
    hidden = got_tokens.reshape(receive, width_model)
    got_cot = got_cot.reshape(receive, local_cols)
    got_subnet = got_subnet.reshape(receive)
    full_weight = lax.all_gather(key_weight, "dp", axis=0, tiled=True)
    key_proj = jnp.dot(hidden, full_weight, preferred_element_type=jnp.float32)
    per_head = key_proj.reshape(receive, local_heads, HEAD_DIM)
    head_scale = jnp.sqrt(jnp.mean(per_head * per_head, axis=2, keepdims=True) + epsilon)
    outputs = per_head / head_scale
    subnet_match = got_subnet[:, None] == jnp.arange(NSUB, dtype=jnp.int32)[None, :]
    row_width = jnp.sum(jnp.where(subnet_match, widths[None, :], 0), axis=1)
    head_index = lax.axis_index("mp") * local_heads + jnp.arange(local_heads, dtype=jnp.int32)
    head_mask = (head_index[None, :] < row_width[:, None]).astype(jnp.float32)
    upstream = (
        got_cot.astype(jnp.float32).reshape(receive, local_heads, HEAD_DIM) * head_mask[:, :, None]
    )
    key_delta = (
        upstream - outputs * jnp.mean(upstream * outputs, axis=2, keepdims=True)
    ) / head_scale
    delta_low = key_delta.reshape(receive, local_cols).astype(jnp.bfloat16)
    part_delta = lax.dot_general(
        delta_low, full_weight, (((1,), (1,)), ((), ())), preferred_element_type=jnp.float32
    )
    rounded = lax.optimization_barrier(part_delta.astype(jnp.bfloat16)).astype(jnp.float32)
    feature_delta = lax.psum_scatter(
        rounded.astype(jnp.bfloat16), "mp", scatter_dimension=1, tiled=True
    )
    weight_sum = lax.psum_scatter(
        lax.dot_general(
            hidden, delta_low, (((0,), (0,)), ((), ())), preferred_element_type=jnp.float32
        ),
        "dp",
        scatter_dimension=0,
        tiled=True,
    )
    key_grad = weight_sum / math.sqrt(row_count * dp_size)
    return (feature_delta, key_grad)


CORE, X, Y = 1, 2, 4
PLANE = 8
PLANE_MASKS = (0, X, Y, X | Y)


def swap(value, mask):
    size = lax.axis_size("dp")
    return lax.ppermute(value, "dp", [(i, i ^ mask) for i in range(size)])


def after(value, *others):
    return lax.optimization_barrier((value, *others))[0]


def dot(a, b, dims):
    return lax.dot_general(a, b, (dims, ((), ())), preferred_element_type=jnp.float32)


def fetch(pairs, sems):
    copies = [
        pltpu.make_async_copy(source, target, sems.at[n])
        for n, (source, target) in enumerate(pairs)
    ]
    for copy in copies:
        copy.start()
    return copies


def project_kernel(begin, chips_ref, own_ref, mate_ref, *refs):
    begun = None
    if begin:
        begun, *refs = refs
    *pieces, weight_ref, acc, held, weights, sems = refs
    depth = pieces[0].shape[0]
    count = len(pieces)

    def rows_of(ref, n):
        return ref.at[n * depth : (n + 1) * depth, :]

    pairs = []
    for n, ref in enumerate(pieces):
        at = pl.multiple_of(chips_ref[begin + n] * depth, depth)
        pairs += [
            (ref, rows_of(weights, n)),
            (own_ref.at[:, pl.ds(at, depth)], held.at[n, 0]),
            (mate_ref.at[:, pl.ds(at, depth)], held.at[n, 1]),
        ]
    copies = fetch(pairs, sems)
    if begin:
        acc[...] = begun[...]
    kept = []
    for n in range(count):
        for copy in copies[3 * n : 3 * n + 3]:
            copy.wait()
        out = pltpu.make_async_copy(
            rows_of(weights, n), rows_of(weight_ref, n), sems.at[3 * count + n]
        )
        out.start()
        kept.append(out)
        piece = rows_of(weights, n)[...]
        for side in range(2):
            part = dot(held[n, side], piece, ((1,), (0,)))
            if begin + n == 0:
                acc[side] = part
            else:
                acc[side] += part
    return kept


def first_project_kernel(*refs):
    for copy in project_kernel(0, *refs):
        copy.wait()


def delta_kernel(begin, chips_ref, me_ref, own_cot_ref, mate_cot_ref, *refs):
    *refs, delta_ref, weight_ref, acc, held, weights, sems = refs
    kept = project_kernel(begin, chips_ref, *refs, weight_ref, acc, held, weights, sems)
    core = me_ref[0] & 1
    rows = acc.shape[1]
    delta_ref[2 * rows :, :] = jnp.zeros_like(delta_ref[2 * rows :, :])
    for side, cot_ref in enumerate((own_cot_ref, mate_cot_ref)):
        at = pl.multiple_of((core ^ side) * rows, rows)
        for head in range(own_cot_ref.shape[1] // HEAD_DIM):
            cols = slice(head * HEAD_DIM, (head + 1) * HEAD_DIM)
            proj = acc[side, :, cols]
            scale = jnp.sqrt(jnp.mean(proj * proj, axis=1, keepdims=True) + epsilon)
            normed = proj / scale
            upstream = cot_ref[:rows, cols].astype(jnp.float32)
            delta = (upstream - normed * jnp.mean(upstream * normed, axis=1, keepdims=True)) / scale
            delta_ref[pl.ds(at, rows), cols] = delta.astype(jnp.bfloat16)
        delta_ref[2 * rows :, pl.ds(at, rows)] = cot_ref[rows:, :rows]
    for copy in kept:
        copy.wait()


def select_kernel(me_ref, *refs):
    *deltas, sent_ref, held, sems = refs
    copies = fetch([(ref, held.at[n]) for n, ref in enumerate(deltas)], sems)
    rows = (held.shape[1] - CODE_ROWS) // 2
    per_chip = sent_ref.shape[1] // len(deltas)
    iota = lax.broadcasted_iota(jnp.int32, (PLANE * per_chip, 2 * rows), 0)
    wanted = (me_ref[0] & -PLANE) + lax.shift_right_logical(iota, per_chip.bit_length() - 1)
    slot = iota & (per_chip - 1)
    for n in range(len(deltas)):
        copies[n].wait()
        code = held[n, 2 * rows :, : 2 * rows].astype(jnp.float32).astype(jnp.int32)
        hot = (wanted == code[0:1, :]) & (slot == code[1:2, :])
        found = dot(hot.astype(jnp.bfloat16), held[n, : 2 * rows, :], ((1,), (0,)))
        found = found.astype(jnp.bfloat16)
        for place in range(PLANE):
            sent_ref[place, n * per_chip : (n + 1) * per_chip, :] = found[
                place * per_chip : (place + 1) * per_chip, :
            ]


def weight_grad_kernel(me_ref, own_ref, mate_ref, *refs):
    *deltas, own_part_ref, part_x, part_y, part_both, hidden, held, acc, sems = refs
    part_refs = (part_x, part_y, part_both)
    plane = lax.shift_right_logical(me_ref[0], 3)
    core = me_ref[0] & 1
    rows = own_ref.shape[1]
    pairs = []
    for n, ref in enumerate(deltas):
        own = pl.multiple_of((2 * n + core) * rows, rows)
        mate = pl.multiple_of((2 * n + 1 - core) * rows, rows)
        pairs += [
            (own_ref.at[plane ^ n], hidden.at[pl.ds(own, rows), :]),
            (mate_ref.at[plane ^ n], hidden.at[pl.ds(mate, rows), :]),
            (ref.at[: 2 * rows, :], held.at[2 * n * rows : 2 * (n + 1) * rows, :]),
        ]
    copies = fetch(pairs, sems)
    for first in (0, 2):
        for copy in copies[3 * first : 3 * first + 6]:
            copy.wait()
        part = slice(2 * first * rows, 2 * (first + 2) * rows)
        terms = dot(hidden[part, :], held[part, :], ((0,), (0,)))
        if first == 0:
            acc[...] = terms
        else:
            acc[...] += terms
    count = own_part_ref.shape[0]

    def block(mask):
        place = lax.shift_right_logical((me_ref[0] ^ mask) & 6, 1)
        return acc.at[pl.ds(pl.multiple_of(place * count, count), count), :]

    own = pltpu.make_async_copy(block(0), own_part_ref, sems.at[3 * len(deltas)])
    own.start()
    for ref, mask in zip(part_refs, PLANE_MASKS[1:]):
        ref[...] = block(mask)[...].astype(ref.dtype)
    own.wait()


def sum_kernel(me_ref, own_ref, *refs):
    *part_refs, keep_ref, give_ref = refs
    count = keep_ref.shape[0]
    for ref, core in ((keep_ref, me_ref[0] & 1), (give_ref, 1 - (me_ref[0] & 1))):
        here = pl.ds(pl.multiple_of(core * count, count), count)
        total = own_ref[here, :]
        for part_ref in part_refs:
            total += part_ref[here, :].astype(jnp.float32)
        ref[...] = total


def join_kernel(norm, me_ref, own_ref, mate_ref, grad_ref):
    half = own_ref.shape[1]
    for ref, core in ((own_ref, me_ref[0] & 1), (mate_ref, 1 - (me_ref[0] & 1))):
        grad_ref[:, pl.ds(pl.multiple_of(core * half, half), half)] = ref[...] / norm


def row_grad_kernel(chips_ref, me_ref, got_ref, *refs):
    weight_refs, (out_ref, weights, out, rows_ref, sems) = refs[:4], refs[4:]
    chips, _, count, half = got_ref.shape
    block = count // 4
    depth = half // 2
    pieces = weights.shape[0] // depth
    level = lax.shift_right_logical(me_ref[0], 3)

    def rows_of(ref, n):
        return ref.at[n * depth : (n + 1) * depth, :]

    pairs = []
    for n in range(pieces):
        first = weight_refs[0].shape[0] // depth
        for side in range(2):
            ref = weight_refs[side] if n < first else weight_refs[2 + side]
            target = weights.at[n * depth : (n + 1) * depth, side * half : (side + 1) * half]
            pairs.append((rows_of(ref, n % first), target))
    copies = fetch(pairs, sems)
    core = me_ref[0] & 1
    for chip in range(chips):
        for n in range(4):
            at = pl.multiple_of(((level ^ n) * chips + chip) * block, block)
            for side in range(2):
                rows = got_ref[chip, pl.ds(core ^ side, 1), n * block : (n + 1) * block, :]
                rows_ref[pl.ds(at, block), side * half : (side + 1) * half] = rows[0]
    written = []
    for first in range(0, pieces, 2):
        for copy in copies[2 * first : 2 * first + 4]:
            copy.wait()
        total = dot(rows_ref[...], weights[first * depth : (first + 2) * depth, :], ((1,), (1,)))
        for n in (first, first + 1):
            out[n] = total[:, (n - first) * depth : (n - first + 1) * depth].astype(jnp.bfloat16)
            at = pl.multiple_of(chips_ref[n] * depth, depth)
            copy = pltpu.make_async_copy(
                out.at[n], out_ref.at[:, pl.ds(at, depth)], sems.at[2 * pieces + n]
            )
            copy.start()
            written.append(copy)
    for copy in written:
        copy.wait()


def code_rows(destination, core, per_peer, width):
    positions = jnp.arange(destination.shape[0], dtype=jnp.int32)
    same = (destination[:, None] == destination[None, :]) & (
        positions[:, None] < positions[None, :]
    )
    earlier = jnp.sum(same.astype(jnp.int32), axis=0)
    codes = jnp.stack([destination, core * per_peer + earlier]).astype(jnp.bfloat16)
    return jnp.pad(codes, ((0, CODE_ROWS - 2), (0, width - destination.shape[0])))


def anywhere(count):
    return [pl.BlockSpec(memory_space=pl.ANY)] * count


def hbm(count):
    return [pl.BlockSpec(memory_space=pltpu.HBM)] * count


def vmem(count):
    return [pl.BlockSpec(memory_space=pltpu.VMEM)] * count


def anywhere(count):
    return [pl.BlockSpec(memory_space=pl.ANY)] * count


SCALAR = pl.BlockSpec(memory_space=pltpu.SMEM)
PARAMS = pltpu.CompilerParams(vmem_limit_bytes=VMEM_LIMIT)
def grant(mebibytes):
    return pltpu.CompilerParams(vmem_limit_bytes=mebibytes << 20)


def per_device_paired(tokens, key_cot, routes, counts, widths, key_weight):
    rows, width_model = tokens.shape
    cols = key_cot.shape[1]
    half_cols = cols // 2
    size = lax.axis_size("dp")
    chips = size // 2
    levels = size // PLANE
    per_peer = 2 * rows // size
    receive = size * per_peer
    wide = width_model // levels
    me = lax.axis_index("dp")
    core = me % 2
    me_scalar = me.astype(jnp.int32).reshape(1)

    def mine(value):
        return lax.dynamic_slice_in_dim(value, core * half_cols, half_cols, 1)

    def theirs(value):
        return lax.dynamic_slice_in_dim(value, (1 - core) * half_cols, half_cols, 1)

    mate_shard = swap(key_weight, CORE)
    piece = jnp.where(
        core == 0,
        jnp.concatenate([key_weight[:, :half_cols], mate_shard[:, :half_cols]], axis=0),
        jnp.concatenate([mate_shard[:, half_cols:], key_weight[:, half_cols:]], axis=0),
    )
    near, far, both = PLANE, 2 * PLANE, 3 * PLANE
    have = {0: piece}

    def after_round(**beside):
        names, masks = list(beside), list(have)
        values = lax.optimization_barrier([*beside.values(), *have.values()])
        have.update(zip(masks, values[len(names) :]))
        return values[: len(names)]

    have.update(
        {
            Y: swap(piece, Y),
            X: swap(piece, X),
            near: swap(piece, near),
            far: swap(piece, far),
        }
    )
    from_both = swap(piece, both)
    by_level = jnp.stack([tokens[:, z * wide : (z + 1) * wide] for z in range(levels)])
    by_level, key_cot, counts, routes = after_round(
        by_level=by_level, key_cot=key_cot, counts=counts, routes=routes
    )
    columns = [[p + PLANE * z for z in range(levels)] for p in range(PLANE)]
    own_features = lax.all_to_all(
        by_level, "dp", split_axis=0, concat_axis=0, axis_index_groups=columns, tiled=True
    )
    have.update(
        {
            near | X: swap(have[near], X),
            near | Y: swap(have[near], Y),
            far | X: swap(have[far], X),
            far | Y: swap(have[far], Y),
        }
    )
    have[both] = from_both
    bounds = jnp.cumsum(counts[0])
    positions = jnp.arange(rows, dtype=jnp.int32)
    subnet = jnp.sum((positions[:, None] >= bounds[None, : NSUB - 1]).astype(jnp.int32), axis=1)
    subnet_match = subnet[:, None] == jnp.arange(NSUB, dtype=jnp.int32)[None, :]
    row_width = jnp.sum(jnp.where(subnet_match, widths[None, :], 0), axis=1)
    head_of_col = jnp.arange(cols, dtype=jnp.int32) // HEAD_DIM
    upstream = jnp.where(
        head_of_col[None, :] < row_width[:, None], key_cot, jnp.zeros_like(key_cot)
    )
    codes = code_rows(routes[:, 0], core, per_peer, half_cols)
    own_cot = jnp.concatenate([mine(upstream), codes], axis=0)

    own_cot, give_cot, tokens = after_round(
        own_cot=own_cot,
        give_cot=jnp.concatenate([theirs(upstream), codes], axis=0),
        tokens=tokens,
    )
    mate_tokens = swap(tokens, CORE)
    have.update(
        {
            both | X: swap(have[both], X),
            both | Y: swap(have[both], Y),
            X | Y: swap(have[Y], X),
            far | X | Y: swap(have[far | X], Y),
        }
    )
    mate_tokens, give_cot, own_cot = after_round(
        mate_tokens=mate_tokens, give_cot=give_cot, own_cot=own_cot
    )
    mate_cot = swap(give_cot, CORE)

    first_masks = list(have)
    last_masks = [near | X | Y, both | X | Y]
    order = jnp.stack([lax.shift_right_logical(me ^ mask, 1) for mask in first_masks + last_masks])
    depth = width_model // chips
    sums = jax.ShapeDtypeStruct((2, rows, half_cols), jnp.float32)

    def project(kernel, count, results, inputs, specs, name):
        return pl.pallas_call(
            kernel,
            out_shape=(*results, jax.ShapeDtypeStruct((count * depth, half_cols), jnp.bfloat16))
            + ((sums,) if name == "project" else ()),
            in_specs=specs + anywhere(count),
            out_specs=(*vmem(len(results)), anywhere(1)[0])
            + (tuple(vmem(1)) if name == "project" else ()),
            scratch_shapes=([] if name == "project" else [pltpu.VMEM(sums.shape, sums.dtype)])
            + [
                pltpu.VMEM((count, 2, rows, depth), jnp.bfloat16),
                pltpu.VMEM((count * depth, half_cols), jnp.bfloat16),
                pltpu.SemaphoreType.DMA((4 * count,)),
            ],
            compiler_params=PARAMS if name == "project" else grant(24),
            name=name,
        )(*inputs)

    first_weight, begun = project(
        first_project_kernel,
        len(first_masks),
        (),
        (order, tokens, mate_tokens, *[have[mask] for mask in first_masks]),
        [SCALAR] + anywhere(2),
        "project",
    )
    have.update(
        {
            near | X | Y: swap(have[near | Y], X),
            both | X | Y: swap(have[both | X], Y),
        }
    )
    mate_cot, own_cot, own_features, begun, first_weight = after_round(
        mate_cot=mate_cot,
        own_cot=own_cot,
        own_features=own_features,
        begun=begun,
        first_weight=first_weight,
    )
    mate_features = swap(own_features, CORE)
    delta, last_weight = project(
        functools.partial(delta_kernel, len(first_masks)),
        len(last_masks),
        (jax.ShapeDtypeStruct((2 * rows + CODE_ROWS, half_cols), jnp.bfloat16),),
        (
            order,
            me_scalar,
            own_cot,
            mate_cot,
            tokens,
            mate_tokens,
            begun,
            *[have[mask] for mask in last_masks],
        ),
        [SCALAR] * 2 + vmem(2) + hbm(2) + vmem(1),
        "delta",
    )

    delta_near, delta_far, mate_features = lax.optimization_barrier(
        (swap(delta, near), swap(delta, far), mate_features)
    )
    deltas = [delta, delta_near, delta_far, swap(delta_far, near)]
    first_weight, last_weight, *deltas[1:] = lax.optimization_barrier(
        (first_weight, last_weight, *deltas[1:])
    )
    mate_first, mate_last = swap(first_weight, CORE), swap(last_weight, CORE)
    count = levels * 2 * per_peer
    delta_room = pltpu.VMEM((levels, *delta.shape), jnp.bfloat16)
    selected = pl.pallas_call(
        select_kernel,
        out_shape=jax.ShapeDtypeStruct((PLANE, count, half_cols), jnp.bfloat16),
        in_specs=[SCALAR] + hbm(1) + anywhere(levels - 1),
        out_specs=vmem(1)[0],
        scratch_shapes=[delta_room, pltpu.SemaphoreType.DMA((levels,))],
        compiler_params=grant(16),
        name="select",
    )(me_scalar, *deltas)
    got = lax.all_to_all(
        selected,
        "dp",
        split_axis=0,
        concat_axis=0,
        axis_index_groups=[[z * PLANE + p for p in range(PLANE)] for z in range(levels)],
        tiled=True,
    ).reshape(PLANE // 2, 2, count, half_cols)

    shard = width_model // size
    mine_terms = jax.ShapeDtypeStruct((wide // 4, half_cols), jnp.float32)
    sent_terms = jax.ShapeDtypeStruct(mine_terms.shape, jnp.bfloat16)
    own_part, *parts = pl.pallas_call(
        weight_grad_kernel,
        out_shape=(mine_terms, *[sent_terms] * 3),
        in_specs=[SCALAR] + anywhere(2) + hbm(1) + anywhere(levels - 1),
        out_specs=tuple(hbm(1) + vmem(3)),
        scratch_shapes=[
            pltpu.VMEM((levels * 2 * rows, wide), jnp.bfloat16),
            pltpu.VMEM((levels * 2 * rows, half_cols), jnp.bfloat16),
            pltpu.VMEM((wide, half_cols), jnp.float32),
            pltpu.SemaphoreType.DMA((3 * levels + 1,)),
        ],
        compiler_params=grant(16),
        name="weight_grad",
    )(me_scalar, own_features, mate_features, after(delta, selected), *deltas[1:])
    parts = [swap(part, mask) for part, mask in zip(parts, PLANE_MASKS[1:])]

    row_grads = pl.pallas_call(
        row_grad_kernel,
        out_shape=jax.ShapeDtypeStruct((receive, width_model), jnp.bfloat16),
        in_specs=[SCALAR] * 2 + vmem(1) + hbm(4),
        out_specs=anywhere(1)[0],
        scratch_shapes=[
            pltpu.VMEM((width_model, cols), jnp.bfloat16),
            pltpu.VMEM((chips, receive, depth), jnp.bfloat16),
            pltpu.VMEM((receive, cols), jnp.bfloat16),
            pltpu.SemaphoreType.DMA((3 * chips,)),
        ],
        compiler_params=grant(32),
        name="row_grad",
    )(order, me_scalar, got, first_weight, mate_first, last_weight, mate_last)

    half_grad = jax.ShapeDtypeStruct((shard, half_cols), jnp.float32)
    keep_grad, give_grad = pl.pallas_call(
        sum_kernel,
        out_shape=(half_grad, half_grad),
        in_specs=[SCALAR] + vmem(4),
        out_specs=tuple(vmem(2)),
        compiler_params=grant(16),
        name="sum",
    )(me_scalar, after(own_part, row_grads), *parts)
    key_grad = pl.pallas_call(
        functools.partial(join_kernel, math.sqrt(rows * size)),
        out_shape=jax.ShapeDtypeStruct((shard, cols), jnp.float32),
        in_specs=[SCALAR] + vmem(2),
        out_specs=vmem(1)[0],
        compiler_params=grant(16),
        name="join",
    )(me_scalar, keep_grad, swap(give_grad, CORE))
    return (row_grads, key_grad)


def solution(mesh):
    size, split = mesh.shape["dp"], mesh.shape["mp"]
    paired = split == 1 and size == 32
    return jax.shard_map(
        per_device_paired if paired else per_device_general,
        mesh=mesh,
        in_specs=(P("dp", None), P("dp", "mp"), P("dp", None), P("dp", None), P(), P("dp", "mp")),
        out_specs=(P("dp", "mp"), P("dp", "mp")),
        check_vma=False,
    )
```

```python
import functools
import math

import jax
import jax.numpy as jnp
from jax import lax
from jax.experimental import pallas as pl
from jax.experimental.pallas import tpu as pltpu
from jax.sharding import PartitionSpec as P

HEAD_DIM = 128
NSUB = 4
VMEM_LIMIT = 60 * 1024 * 1024
CODE_ROWS = 16
epsilon = 1e-06


def per_device_general(tokens, key_cot, routes, counts, widths, key_weight):
    row_count = tokens.shape[0]
    width_model = tokens.shape[1]
    local_cols = key_cot.shape[1]
    local_heads = local_cols // HEAD_DIM
    dp_size = lax.axis_size("dp")
    per_peer = 2 * row_count // dp_size
    receive = dp_size * per_peer
    destination = routes[:, 0]
    one_hot = (destination[:, None] == jnp.arange(dp_size, dtype=jnp.int32)[None, :]).astype(
        jnp.int32
    )
    earlier = jnp.sum(jnp.cumsum(one_hot, axis=0) * one_hot, axis=1) - 1
    send_slot = destination * per_peer + earlier
    bounds = jnp.cumsum(counts[0])
    positions = jnp.arange(row_count, dtype=jnp.int32)
    subnet = jnp.sum((positions[:, None] >= bounds[None, : NSUB - 1]).astype(jnp.int32), axis=1)
    send_subnet = (
        jnp.full((receive,), -1, jnp.int32).at[send_slot].set(subnet).reshape(dp_size, per_peer)
    )
    send_cot = jnp.zeros((receive, local_cols), jnp.bfloat16).at[send_slot].set(key_cot)
    send_cot = send_cot.reshape(dp_size, per_peer, local_cols)
    send_tokens = jnp.zeros((receive, width_model), jnp.bfloat16).at[send_slot].set(tokens)
    send_tokens = send_tokens.reshape(dp_size, per_peer, width_model)
    got_tokens, got_cot, got_subnet = (
        lax.all_to_all(send_tokens, "dp", split_axis=0, concat_axis=0, tiled=True),
        lax.all_to_all(send_cot, "dp", split_axis=0, concat_axis=0, tiled=True),
        lax.all_to_all(send_subnet, "dp", split_axis=0, concat_axis=0, tiled=True),
    )
    hidden = got_tokens.reshape(receive, width_model)
    got_cot = got_cot.reshape(receive, local_cols)
    got_subnet = got_subnet.reshape(receive)
    full_weight = lax.all_gather(key_weight, "dp", axis=0, tiled=True)
    key_proj = jnp.dot(hidden, full_weight, preferred_element_type=jnp.float32)
    per_head = key_proj.reshape(receive, local_heads, HEAD_DIM)
    head_scale = jnp.sqrt(jnp.mean(per_head * per_head, axis=2, keepdims=True) + epsilon)
    outputs = per_head / head_scale
    subnet_match = got_subnet[:, None] == jnp.arange(NSUB, dtype=jnp.int32)[None, :]
    row_width = jnp.sum(jnp.where(subnet_match, widths[None, :], 0), axis=1)
    head_index = lax.axis_index("mp") * local_heads + jnp.arange(local_heads, dtype=jnp.int32)
    head_mask = (head_index[None, :] < row_width[:, None]).astype(jnp.float32)
    upstream = (
        got_cot.astype(jnp.float32).reshape(receive, local_heads, HEAD_DIM) * head_mask[:, :, None]
    )
    key_delta = (
        upstream - outputs * jnp.mean(upstream * outputs, axis=2, keepdims=True)
    ) / head_scale
    delta_low = key_delta.reshape(receive, local_cols).astype(jnp.bfloat16)
    part_delta = lax.dot_general(
        delta_low, full_weight, (((1,), (1,)), ((), ())), preferred_element_type=jnp.float32
    )
    rounded = lax.optimization_barrier(part_delta.astype(jnp.bfloat16)).astype(jnp.float32)
    feature_delta = lax.psum_scatter(
        rounded.astype(jnp.bfloat16), "mp", scatter_dimension=1, tiled=True
    )
    weight_sum = lax.psum_scatter(
        lax.dot_general(
            hidden, delta_low, (((0,), (0,)), ((), ())), preferred_element_type=jnp.float32
        ),
        "dp",
        scatter_dimension=0,
        tiled=True,
    )
    key_grad = weight_sum / math.sqrt(row_count * dp_size)
    return (feature_delta, key_grad)


CORE, X, Y = 1, 2, 4
PLANE = 8
PLANE_MASKS = (0, X, Y, X | Y)


def swap(value, mask):
    size = lax.axis_size("dp")
    return lax.ppermute(value, "dp", [(i, i ^ mask) for i in range(size)])


def after(value, *others):
    return lax.optimization_barrier((value, *others))[0]


def dot(a, b, dims):
    return lax.dot_general(a, b, (dims, ((), ())), preferred_element_type=jnp.float32)


def fetch(pairs, sems):
    copies = [
        pltpu.make_async_copy(source, target, sems.at[n])
        for n, (source, target) in enumerate(pairs)
    ]
    for copy in copies:
        copy.start()
    return copies


def project_kernel(begin, chips_ref, own_ref, mate_ref, *refs):
    begun = None
    if begin:
        begun, *refs = refs
    *pieces, weight_ref, acc, held, weights, sems = refs
    depth = pieces[0].shape[0]
    count = len(pieces)

    def rows_of(ref, n):
        return ref.at[n * depth : (n + 1) * depth, :]

    pairs = []
    for n, ref in enumerate(pieces):
        at = pl.multiple_of(chips_ref[begin + n] * depth, depth)
        pairs += [
            (ref, rows_of(weights, n)),
            (own_ref.at[:, pl.ds(at, depth)], held.at[n, 0]),
            (mate_ref.at[:, pl.ds(at, depth)], held.at[n, 1]),
        ]
    copies = fetch(pairs, sems)
    if begin:
        acc[...] = begun[...]
    kept = []
    for n in range(count):
        for copy in copies[3 * n : 3 * n + 3]:
            copy.wait()
        out = pltpu.make_async_copy(
            rows_of(weights, n), rows_of(weight_ref, n), sems.at[3 * count + n]
        )
        out.start()
        kept.append(out)
        piece = rows_of(weights, n)[...]
        for side in range(2):
            part = dot(held[n, side], piece, ((1,), (0,)))
            if begin + n == 0:
                acc[side] = part
            else:
                acc[side] += part
    return kept


def first_project_kernel(*refs):
    for copy in project_kernel(0, *refs):
        copy.wait()


def delta_kernel(begin, chips_ref, me_ref, own_cot_ref, mate_cot_ref, *refs):
    *refs, delta_ref, weight_ref, acc, held, weights, sems = refs
    kept = project_kernel(begin, chips_ref, *refs, weight_ref, acc, held, weights, sems)
    core = me_ref[0] & 1
    rows = acc.shape[1]
    delta_ref[2 * rows :, :] = jnp.zeros_like(delta_ref[2 * rows :, :])
    for side, cot_ref in enumerate((own_cot_ref, mate_cot_ref)):
        at = pl.multiple_of((core ^ side) * rows, rows)
        for head in range(own_cot_ref.shape[1] // HEAD_DIM):
            cols = slice(head * HEAD_DIM, (head + 1) * HEAD_DIM)
            proj = acc[side, :, cols]
            scale = jnp.sqrt(jnp.mean(proj * proj, axis=1, keepdims=True) + epsilon)
            normed = proj / scale
            upstream = cot_ref[:rows, cols].astype(jnp.float32)
            delta = (upstream - normed * jnp.mean(upstream * normed, axis=1, keepdims=True)) / scale
            delta_ref[pl.ds(at, rows), cols] = delta.astype(jnp.bfloat16)
        delta_ref[2 * rows :, pl.ds(at, rows)] = cot_ref[rows:, :rows]
    for copy in kept:
        copy.wait()


def select_kernel(me_ref, *refs):
    *deltas, sent_ref, held, sems = refs
    copies = fetch([(ref, held.at[n]) for n, ref in enumerate(deltas)], sems)
    rows = (held.shape[1] - CODE_ROWS) // 2
    per_chip = sent_ref.shape[1] // len(deltas)
    iota = lax.broadcasted_iota(jnp.int32, (PLANE * per_chip, 2 * rows), 0)
    wanted = (me_ref[0] & -PLANE) + lax.shift_right_logical(iota, per_chip.bit_length() - 1)
    slot = iota & (per_chip - 1)
    for n in range(len(deltas)):
        copies[n].wait()
        code = held[n, 2 * rows :, : 2 * rows].astype(jnp.float32).astype(jnp.int32)
        hot = (wanted == code[0:1, :]) & (slot == code[1:2, :])
        found = dot(hot.astype(jnp.bfloat16), held[n, : 2 * rows, :], ((1,), (0,)))
        found = found.astype(jnp.bfloat16)
        for place in range(PLANE):
            sent_ref[place, n * per_chip : (n + 1) * per_chip, :] = found[
                place * per_chip : (place + 1) * per_chip, :
            ]


def weight_grad_kernel(me_ref, own_ref, mate_ref, *refs):
    *deltas, own_part_ref, part_x, part_y, part_both, hidden, held, acc, sems = refs
    part_refs = (part_x, part_y, part_both)
    plane = lax.shift_right_logical(me_ref[0], 3)
    core = me_ref[0] & 1
    rows = own_ref.shape[1]
    pairs = []
    for n, ref in enumerate(deltas):
        own = pl.multiple_of((2 * n + core) * rows, rows)
        mate = pl.multiple_of((2 * n + 1 - core) * rows, rows)
        pairs += [
            (own_ref.at[plane ^ n], hidden.at[pl.ds(own, rows), :]),
            (mate_ref.at[plane ^ n], hidden.at[pl.ds(mate, rows), :]),
            (ref.at[: 2 * rows, :], held.at[2 * n * rows : 2 * (n + 1) * rows, :]),
        ]
    copies = fetch(pairs, sems)
    for first in (0, 2):
        for copy in copies[3 * first : 3 * first + 6]:
            copy.wait()
        part = slice(2 * first * rows, 2 * (first + 2) * rows)
        terms = dot(hidden[part, :], held[part, :], ((0,), (0,)))
        if first == 0:
            acc[...] = terms
        else:
            acc[...] += terms
    count = own_part_ref.shape[0]

    def block(mask):
        place = lax.shift_right_logical((me_ref[0] ^ mask) & 6, 1)
        return acc.at[pl.ds(pl.multiple_of(place * count, count), count), :]

    own = pltpu.make_async_copy(block(0), own_part_ref, sems.at[3 * len(deltas)])
    own.start()
    for ref, mask in zip(part_refs, PLANE_MASKS[1:]):
        ref[...] = block(mask)[...].astype(ref.dtype)
    own.wait()


def sum_kernel(me_ref, own_ref, *refs):
    *part_refs, keep_ref, give_ref = refs
    count = keep_ref.shape[0]
    for ref, core in ((keep_ref, me_ref[0] & 1), (give_ref, 1 - (me_ref[0] & 1))):
        here = pl.ds(pl.multiple_of(core * count, count), count)
        total = own_ref[here, :]
        for part_ref in part_refs:
            total += part_ref[here, :].astype(jnp.float32)
        ref[...] = total


def join_kernel(norm, me_ref, own_ref, mate_ref, grad_ref):
    half = own_ref.shape[1]
    for ref, core in ((own_ref, me_ref[0] & 1), (mate_ref, 1 - (me_ref[0] & 1))):
        grad_ref[:, pl.ds(pl.multiple_of(core * half, half), half)] = ref[...] / norm


def row_grad_kernel(chips_ref, me_ref, got_ref, *refs):
    weight_refs, (out_ref, weights, out, rows_ref, sems) = refs[:4], refs[4:]
    chips, _, count, half = got_ref.shape
    block = count // 4
    depth = half // 2
    pieces = weights.shape[0] // depth
    level = lax.shift_right_logical(me_ref[0], 3)

    def rows_of(ref, n):
        return ref.at[n * depth : (n + 1) * depth, :]

    pairs = []
    for n in range(pieces):
        first = weight_refs[0].shape[0] // depth
        for side in range(2):
            ref = weight_refs[side] if n < first else weight_refs[2 + side]
            target = weights.at[n * depth : (n + 1) * depth, side * half : (side + 1) * half]
            pairs.append((rows_of(ref, n % first), target))
    copies = fetch(pairs, sems)
    core = me_ref[0] & 1
    for chip in range(chips):
        for n in range(4):
            at = pl.multiple_of(((level ^ n) * chips + chip) * block, block)
            for side in range(2):
                rows = got_ref[chip, pl.ds(core ^ side, 1), n * block : (n + 1) * block, :]
                rows_ref[pl.ds(at, block), side * half : (side + 1) * half] = rows[0]
    written = []
    for first in range(0, pieces, 2):
        for copy in copies[2 * first : 2 * first + 4]:
            copy.wait()
        total = dot(rows_ref[...], weights[first * depth : (first + 2) * depth, :], ((1,), (1,)))
        for n in (first, first + 1):
            out[n] = total[:, (n - first) * depth : (n - first + 1) * depth].astype(jnp.bfloat16)
            at = pl.multiple_of(chips_ref[n] * depth, depth)
            copy = pltpu.make_async_copy(
                out.at[n], out_ref.at[:, pl.ds(at, depth)], sems.at[2 * pieces + n]
            )
            copy.start()
            written.append(copy)
    for copy in written:
        copy.wait()


def code_rows(destination, core, per_peer, width):
    positions = jnp.arange(destination.shape[0], dtype=jnp.int32)
    same = (destination[:, None] == destination[None, :]) & (
        positions[:, None] < positions[None, :]
    )
    earlier = jnp.sum(same.astype(jnp.int32), axis=0)
    codes = jnp.stack([destination, core * per_peer + earlier]).astype(jnp.bfloat16)
    return jnp.pad(codes, ((0, CODE_ROWS - 2), (0, width - destination.shape[0])))


def anywhere(count):
    return [pl.BlockSpec(memory_space=pl.ANY)] * count


def hbm(count):
    return [pl.BlockSpec(memory_space=pltpu.HBM)] * count


def vmem(count):
    return [pl.BlockSpec(memory_space=pltpu.VMEM)] * count


def anywhere(count):
    return [pl.BlockSpec(memory_space=pl.ANY)] * count


SCALAR = pl.BlockSpec(memory_space=pltpu.SMEM)
PARAMS = pltpu.CompilerParams(vmem_limit_bytes=VMEM_LIMIT)
def grant(mebibytes):
    return pltpu.CompilerParams(vmem_limit_bytes=mebibytes << 20)


def per_device_paired(tokens, key_cot, routes, counts, widths, key_weight):
    rows, width_model = tokens.shape
    cols = key_cot.shape[1]
    half_cols = cols // 2
    size = lax.axis_size("dp")
    chips = size // 2
    levels = size // PLANE
    per_peer = 2 * rows // size
    receive = size * per_peer
    wide = width_model // levels
    me = lax.axis_index("dp")
    core = me % 2
    me_scalar = me.astype(jnp.int32).reshape(1)

    def mine(value):
        return lax.dynamic_slice_in_dim(value, core * half_cols, half_cols, 1)

    def theirs(value):
        return lax.dynamic_slice_in_dim(value, (1 - core) * half_cols, half_cols, 1)

    mate_shard = swap(key_weight, CORE)
    piece = jnp.where(
        core == 0,
        jnp.concatenate([key_weight[:, :half_cols], mate_shard[:, :half_cols]], axis=0),
        jnp.concatenate([mate_shard[:, half_cols:], key_weight[:, half_cols:]], axis=0),
    )
    near, far, both = PLANE, 2 * PLANE, 3 * PLANE
    have = {0: piece}

    def after_round(**beside):
        names, masks = list(beside), list(have)
        values = lax.optimization_barrier([*beside.values(), *have.values()])
        have.update(zip(masks, values[len(names) :]))
        return values[: len(names)]

    have.update(
        {
            Y: swap(piece, Y),
            X: swap(piece, X),
            near: swap(piece, near),
            far: swap(piece, far),
        }
    )
    from_both = swap(piece, both)
    by_level = jnp.stack([tokens[:, z * wide : (z + 1) * wide] for z in range(levels)])
    by_level, key_cot, counts, routes = after_round(
        by_level=by_level, key_cot=key_cot, counts=counts, routes=routes
    )
    columns = [[p + PLANE * z for z in range(levels)] for p in range(PLANE)]
    own_features = lax.all_to_all(
        by_level, "dp", split_axis=0, concat_axis=0, axis_index_groups=columns, tiled=True
    )
    have.update(
        {
            near | X: swap(have[near], X),
            near | Y: swap(have[near], Y),
            far | X: swap(have[far], X),
            far | Y: swap(have[far], Y),
        }
    )
    have[both] = from_both
    bounds = jnp.cumsum(counts[0])
    positions = jnp.arange(rows, dtype=jnp.int32)
    subnet = jnp.sum((positions[:, None] >= bounds[None, : NSUB - 1]).astype(jnp.int32), axis=1)
    subnet_match = subnet[:, None] == jnp.arange(NSUB, dtype=jnp.int32)[None, :]
    row_width = jnp.sum(jnp.where(subnet_match, widths[None, :], 0), axis=1)
    head_of_col = jnp.arange(cols, dtype=jnp.int32) // HEAD_DIM
    upstream = jnp.where(
        head_of_col[None, :] < row_width[:, None], key_cot, jnp.zeros_like(key_cot)
    )
    codes = code_rows(routes[:, 0], core, per_peer, half_cols)
    own_cot = jnp.concatenate([mine(upstream), codes], axis=0)

    own_cot, give_cot, tokens = after_round(
        own_cot=own_cot,
        give_cot=jnp.concatenate([theirs(upstream), codes], axis=0),
        tokens=tokens,
    )
    mate_tokens = swap(tokens, CORE)
    have.update(
        {
            both | X: swap(have[both], X),
            both | Y: swap(have[both], Y),
            X | Y: swap(have[Y], X),
            far | X | Y: swap(have[far | X], Y),
        }
    )
    mate_tokens, give_cot, own_cot = after_round(
        mate_tokens=mate_tokens, give_cot=give_cot, own_cot=own_cot
    )
    mate_cot = swap(give_cot, CORE)

    first_masks = list(have)
    last_masks = [near | X | Y, both | X | Y]
    order = jnp.stack([lax.shift_right_logical(me ^ mask, 1) for mask in first_masks + last_masks])
    depth = width_model // chips
    sums = jax.ShapeDtypeStruct((2, rows, half_cols), jnp.float32)

    def project(kernel, count, results, inputs, specs, name):
        return pl.pallas_call(
            kernel,
            out_shape=(*results, jax.ShapeDtypeStruct((count * depth, half_cols), jnp.bfloat16))
            + ((sums,) if name == "project" else ()),
            in_specs=specs + anywhere(count),
            out_specs=(*vmem(len(results)), anywhere(1)[0])
            + (tuple(vmem(1)) if name == "project" else ()),
            scratch_shapes=([] if name == "project" else [pltpu.VMEM(sums.shape, sums.dtype)])
            + [
                pltpu.VMEM((count, 2, rows, depth), jnp.bfloat16),
                pltpu.VMEM((count * depth, half_cols), jnp.bfloat16),
                pltpu.SemaphoreType.DMA((4 * count,)),
            ],
            compiler_params=PARAMS,
            name=name,
        )(*inputs)

    first_weight, begun = project(
        first_project_kernel,
        len(first_masks),
        (),
        (order, tokens, mate_tokens, *[have[mask] for mask in first_masks]),
        [SCALAR] + anywhere(2),
        "project",
    )
    have.update(
        {
            near | X | Y: swap(have[near | Y], X),
            both | X | Y: swap(have[both | X], Y),
        }
    )
    mate_cot, own_cot, own_features, begun, first_weight = after_round(
        mate_cot=mate_cot,
        own_cot=own_cot,
        own_features=own_features,
        begun=begun,
        first_weight=first_weight,
    )
    mate_features = swap(own_features, CORE)
    delta, last_weight = project(
        functools.partial(delta_kernel, len(first_masks)),
        len(last_masks),
        (jax.ShapeDtypeStruct((2 * rows + CODE_ROWS, half_cols), jnp.bfloat16),),
        (
            order,
            me_scalar,
            own_cot,
            mate_cot,
            tokens,
            mate_tokens,
            begun,
            *[have[mask] for mask in last_masks],
        ),
        [SCALAR] * 2 + vmem(2) + anywhere(2) + vmem(1),
        "delta",
    )

    delta_near, delta_far, mate_features = lax.optimization_barrier(
        (swap(delta, near), swap(delta, far), mate_features)
    )
    deltas = [delta, delta_near, delta_far, swap(delta_far, near)]
    first_weight, last_weight, *deltas[1:] = lax.optimization_barrier(
        (first_weight, last_weight, *deltas[1:])
    )
    mate_first, mate_last = swap(first_weight, CORE), swap(last_weight, CORE)
    count = levels * 2 * per_peer
    delta_room = pltpu.VMEM((levels, *delta.shape), jnp.bfloat16)
    selected = pl.pallas_call(
        select_kernel,
        out_shape=jax.ShapeDtypeStruct((PLANE, count, half_cols), jnp.bfloat16),
        in_specs=[SCALAR] + anywhere(levels),
        out_specs=vmem(1)[0],
        scratch_shapes=[delta_room, pltpu.SemaphoreType.DMA((levels,))],
        compiler_params=grant(16),
        name="select",
    )(me_scalar, *deltas)
    got = lax.all_to_all(
        selected,
        "dp",
        split_axis=0,
        concat_axis=0,
        axis_index_groups=[[z * PLANE + p for p in range(PLANE)] for z in range(levels)],
        tiled=True,
    ).reshape(PLANE // 2, 2, count, half_cols)

    shard = width_model // size
    mine_terms = jax.ShapeDtypeStruct((wide // 4, half_cols), jnp.float32)
    sent_terms = jax.ShapeDtypeStruct(mine_terms.shape, jnp.bfloat16)
    own_part, *parts = pl.pallas_call(
        weight_grad_kernel,
        out_shape=(mine_terms, *[sent_terms] * 3),
        in_specs=[SCALAR] + anywhere(2 + levels),
        out_specs=tuple(hbm(1) + vmem(3)),
        scratch_shapes=[
            pltpu.VMEM((levels * 2 * rows, wide), jnp.bfloat16),
            pltpu.VMEM((levels * 2 * rows, half_cols), jnp.bfloat16),
            pltpu.VMEM((wide, half_cols), jnp.float32),
            pltpu.SemaphoreType.DMA((3 * levels + 1,)),
        ],
        compiler_params=grant(16),
        name="weight_grad",
    )(me_scalar, own_features, mate_features, after(delta, selected), *deltas[1:])
    parts = [swap(part, mask) for part, mask in zip(parts, PLANE_MASKS[1:])]

    row_grads = pl.pallas_call(
        row_grad_kernel,
        out_shape=jax.ShapeDtypeStruct((receive, width_model), jnp.bfloat16),
        in_specs=[SCALAR] * 2 + vmem(1) + anywhere(4),
        out_specs=anywhere(1)[0],
        scratch_shapes=[
            pltpu.VMEM((width_model, cols), jnp.bfloat16),
            pltpu.VMEM((chips, receive, depth), jnp.bfloat16),
            pltpu.VMEM((receive, cols), jnp.bfloat16),
            pltpu.SemaphoreType.DMA((3 * chips,)),
        ],
        compiler_params=grant(62),
        name="row_grad",
    )(order, me_scalar, got, first_weight, mate_first, last_weight, mate_last)

    half_grad = jax.ShapeDtypeStruct((shard, half_cols), jnp.float32)
    keep_grad, give_grad = pl.pallas_call(
        sum_kernel,
        out_shape=(half_grad, half_grad),
        in_specs=[SCALAR] + vmem(4),
        out_specs=tuple(vmem(2)),
        compiler_params=grant(16),
        name="sum",
    )(me_scalar, after(own_part, row_grads), *parts)
    key_grad = pl.pallas_call(
        functools.partial(join_kernel, math.sqrt(rows * size)),
        out_shape=jax.ShapeDtypeStruct((shard, cols), jnp.float32),
        in_specs=[SCALAR] + vmem(2),
        out_specs=vmem(1)[0],
        compiler_params=grant(16),
        name="join",
    )(me_scalar, keep_grad, swap(give_grad, CORE))
    return (row_grads, key_grad)


def solution(mesh):
    size, split = mesh.shape["dp"], mesh.shape["mp"]
    paired = split == 1 and size == 32
    return jax.shard_map(
        per_device_paired if paired else per_device_general,
        mesh=mesh,
        in_specs=(P("dp", None), P("dp", "mp"), P("dp", None), P("dp", None), P(), P("dp", "mp")),
        out_specs=(P("dp", "mp"), P("dp", "mp")),
        check_vma=False,
    )
```

```python
import functools
import math

import jax
import jax.numpy as jnp
from jax import lax
from jax.experimental import pallas as pl
from jax.experimental.pallas import tpu as pltpu
from jax.sharding import PartitionSpec as P

HEAD_DIM = 128
NSUB = 4
VMEM_LIMIT = 60 * 1024 * 1024
CODE_ROWS = 16
epsilon = 1e-06


def per_device_general(tokens, key_cot, routes, counts, widths, key_weight):
    row_count = tokens.shape[0]
    width_model = tokens.shape[1]
    local_cols = key_cot.shape[1]
    local_heads = local_cols // HEAD_DIM
    dp_size = lax.axis_size("dp")
    per_peer = 2 * row_count // dp_size
    receive = dp_size * per_peer
    destination = routes[:, 0]
    one_hot = (destination[:, None] == jnp.arange(dp_size, dtype=jnp.int32)[None, :]).astype(
        jnp.int32
    )
    earlier = jnp.sum(jnp.cumsum(one_hot, axis=0) * one_hot, axis=1) - 1
    send_slot = destination * per_peer + earlier
    bounds = jnp.cumsum(counts[0])
    positions = jnp.arange(row_count, dtype=jnp.int32)
    subnet = jnp.sum((positions[:, None] >= bounds[None, : NSUB - 1]).astype(jnp.int32), axis=1)
    send_subnet = (
        jnp.full((receive,), -1, jnp.int32).at[send_slot].set(subnet).reshape(dp_size, per_peer)
    )
    send_cot = jnp.zeros((receive, local_cols), jnp.bfloat16).at[send_slot].set(key_cot)
    send_cot = send_cot.reshape(dp_size, per_peer, local_cols)
    send_tokens = jnp.zeros((receive, width_model), jnp.bfloat16).at[send_slot].set(tokens)
    send_tokens = send_tokens.reshape(dp_size, per_peer, width_model)
    got_tokens, got_cot, got_subnet = (
        lax.all_to_all(send_tokens, "dp", split_axis=0, concat_axis=0, tiled=True),
        lax.all_to_all(send_cot, "dp", split_axis=0, concat_axis=0, tiled=True),
        lax.all_to_all(send_subnet, "dp", split_axis=0, concat_axis=0, tiled=True),
    )
    hidden = got_tokens.reshape(receive, width_model)
    got_cot = got_cot.reshape(receive, local_cols)
    got_subnet = got_subnet.reshape(receive)
    full_weight = lax.all_gather(key_weight, "dp", axis=0, tiled=True)
    key_proj = jnp.dot(hidden, full_weight, preferred_element_type=jnp.float32)
    per_head = key_proj.reshape(receive, local_heads, HEAD_DIM)
    head_scale = jnp.sqrt(jnp.mean(per_head * per_head, axis=2, keepdims=True) + epsilon)
    outputs = per_head / head_scale
    subnet_match = got_subnet[:, None] == jnp.arange(NSUB, dtype=jnp.int32)[None, :]
    row_width = jnp.sum(jnp.where(subnet_match, widths[None, :], 0), axis=1)
    head_index = lax.axis_index("mp") * local_heads + jnp.arange(local_heads, dtype=jnp.int32)
    head_mask = (head_index[None, :] < row_width[:, None]).astype(jnp.float32)
    upstream = (
        got_cot.astype(jnp.float32).reshape(receive, local_heads, HEAD_DIM) * head_mask[:, :, None]
    )
    key_delta = (
        upstream - outputs * jnp.mean(upstream * outputs, axis=2, keepdims=True)
    ) / head_scale
    delta_low = key_delta.reshape(receive, local_cols).astype(jnp.bfloat16)
    part_delta = lax.dot_general(
        delta_low, full_weight, (((1,), (1,)), ((), ())), preferred_element_type=jnp.float32
    )
    rounded = lax.optimization_barrier(part_delta.astype(jnp.bfloat16)).astype(jnp.float32)
    feature_delta = lax.psum_scatter(
        rounded.astype(jnp.bfloat16), "mp", scatter_dimension=1, tiled=True
    )
    weight_sum = lax.psum_scatter(
        lax.dot_general(
            hidden, delta_low, (((0,), (0,)), ((), ())), preferred_element_type=jnp.float32
        ),
        "dp",
        scatter_dimension=0,
        tiled=True,
    )
    key_grad = weight_sum / math.sqrt(row_count * dp_size)
    return (feature_delta, key_grad)


CORE, X, Y = 1, 2, 4
PLANE = 8
PLANE_MASKS = (0, X, Y, X | Y)


def swap(value, mask):
    size = lax.axis_size("dp")
    return lax.ppermute(value, "dp", [(i, i ^ mask) for i in range(size)])


def after(value, *others):
    return lax.optimization_barrier((value, *others))[0]


def dot(a, b, dims):
    return lax.dot_general(a, b, (dims, ((), ())), preferred_element_type=jnp.float32)


def fetch(pairs, sems):
    copies = [
        pltpu.make_async_copy(source, target, sems.at[n])
        for n, (source, target) in enumerate(pairs)
    ]
    for copy in copies:
        copy.start()
    return copies


def project_kernel(begin, chips_ref, own_ref, mate_ref, *refs):
    begun = None
    if begin:
        begun, *refs = refs
    *pieces, weight_ref, acc, held, weights, sems = refs
    depth = pieces[0].shape[0]
    count = len(pieces)

    def rows_of(ref, n):
        return ref.at[n * depth : (n + 1) * depth, :]

    pairs = []
    for n, ref in enumerate(pieces):
        at = pl.multiple_of(chips_ref[begin + n] * depth, depth)
        pairs += [
            (ref, rows_of(weights, n)),
            (own_ref.at[:, pl.ds(at, depth)], held.at[n, 0]),
            (mate_ref.at[:, pl.ds(at, depth)], held.at[n, 1]),
        ]
    copies = fetch(pairs, sems)
    if begin:
        acc[...] = begun[...]
    kept = []
    for n in range(count):
        for copy in copies[3 * n : 3 * n + 3]:
            copy.wait()
        out = pltpu.make_async_copy(
            rows_of(weights, n), rows_of(weight_ref, n), sems.at[3 * count + n]
        )
        out.start()
        kept.append(out)
        piece = rows_of(weights, n)[...]
        for side in range(2):
            part = dot(held[n, side], piece, ((1,), (0,)))
            if begin + n == 0:
                acc[side] = part
            else:
                acc[side] += part
    return kept


def first_project_kernel(*refs):
    for copy in project_kernel(0, *refs):
        copy.wait()


def delta_kernel(begin, chips_ref, me_ref, own_cot_ref, mate_cot_ref, *refs):
    *refs, delta_ref, weight_ref, acc, held, weights, sems = refs
    kept = project_kernel(begin, chips_ref, *refs, weight_ref, acc, held, weights, sems)
    core = me_ref[0] & 1
    rows = acc.shape[1]
    delta_ref[2 * rows :, :] = jnp.zeros_like(delta_ref[2 * rows :, :])
    for side, cot_ref in enumerate((own_cot_ref, mate_cot_ref)):
        at = pl.multiple_of((core ^ side) * rows, rows)
        for head in range(own_cot_ref.shape[1] // HEAD_DIM):
            cols = slice(head * HEAD_DIM, (head + 1) * HEAD_DIM)
            proj = acc[side, :, cols]
            scale = jnp.sqrt(jnp.mean(proj * proj, axis=1, keepdims=True) + epsilon)
            normed = proj / scale
            upstream = cot_ref[:rows, cols].astype(jnp.float32)
            delta = (upstream - normed * jnp.mean(upstream * normed, axis=1, keepdims=True)) / scale
            delta_ref[pl.ds(at, rows), cols] = delta.astype(jnp.bfloat16)
        delta_ref[2 * rows :, pl.ds(at, rows)] = cot_ref[rows:, :rows]
    for copy in kept:
        copy.wait()


def select_kernel(begin, me_ref, *refs):
    *deltas, sent_ref, held, sems = refs
    copies = fetch([(ref, held.at[n]) for n, ref in enumerate(deltas[-held.shape[0] :])], sems)
    rows = (held.shape[1] - CODE_ROWS) // 2
    per_chip = sent_ref.shape[1] // (begin + held.shape[0])
    if begin:
        sent_ref[:, : begin * per_chip, :] = deltas[0][...]
    iota = lax.broadcasted_iota(jnp.int32, (PLANE * per_chip, 2 * rows), 0)
    wanted = (me_ref[0] & -PLANE) + lax.shift_right_logical(iota, per_chip.bit_length() - 1)
    slot = iota & (per_chip - 1)
    for n in range(held.shape[0]):
        copies[n].wait()
        code = held[n, 2 * rows :, : 2 * rows].astype(jnp.float32).astype(jnp.int32)
        hot = (wanted == code[0:1, :]) & (slot == code[1:2, :])
        found = dot(hot.astype(jnp.bfloat16), held[n, : 2 * rows, :], ((1,), (0,)))
        found = found.astype(jnp.bfloat16)
        at = (begin + n) * per_chip
        for place in range(PLANE):
            sent_ref[place, at : at + per_chip, :] = found[
                place * per_chip : (place + 1) * per_chip, :
            ]


def plane_terms(begin, me_ref, own_ref, mate_ref, deltas, hidden, held, sems):
    plane = lax.shift_right_logical(me_ref[0], 3)
    core = me_ref[0] & 1
    rows = own_ref.shape[1]
    pairs = []
    for n, ref in enumerate(deltas):
        own = pl.multiple_of((2 * n + core) * rows, rows)
        mate = pl.multiple_of((2 * n + 1 - core) * rows, rows)
        pairs += [
            (own_ref.at[plane ^ (begin + n)], hidden.at[pl.ds(own, rows), :]),
            (mate_ref.at[plane ^ (begin + n)], hidden.at[pl.ds(mate, rows), :]),
            (ref.at[: 2 * rows, :], held.at[2 * n * rows : 2 * (n + 1) * rows, :]),
        ]
    for copy in fetch(pairs, sems):
        copy.wait()
    return dot(hidden[...], held[...], ((0,), (0,)))


def first_terms_kernel(me_ref, own_ref, mate_ref, *refs):
    *deltas, terms_ref, hidden, held, sems = refs
    terms_ref[...] = plane_terms(0, me_ref, own_ref, mate_ref, deltas, hidden, held, sems)


def weight_grad_kernel(begin, me_ref, own_ref, mate_ref, begun_ref, *refs):
    *deltas, own_part_ref, part_x, part_y, part_both, hidden, held, acc, sems = refs
    part_refs = (part_x, part_y, part_both)
    acc[...] = begun_ref[...] + plane_terms(
        begin, me_ref, own_ref, mate_ref, deltas, hidden, held, sems
    )
    count = own_part_ref.shape[0]

    def block(mask):
        place = lax.shift_right_logical((me_ref[0] ^ mask) & 6, 1)
        return acc.at[pl.ds(pl.multiple_of(place * count, count), count), :]

    own = pltpu.make_async_copy(block(0), own_part_ref, sems.at[3 * len(deltas)])
    own.start()
    for ref, mask in zip(part_refs, PLANE_MASKS[1:]):
        ref[...] = block(mask)[...].astype(ref.dtype)
    own.wait()


def sum_kernel(me_ref, own_ref, *refs):
    *part_refs, keep_ref, give_ref = refs
    count = keep_ref.shape[0]
    for ref, core in ((keep_ref, me_ref[0] & 1), (give_ref, 1 - (me_ref[0] & 1))):
        here = pl.ds(pl.multiple_of(core * count, count), count)
        total = own_ref[here, :]
        for part_ref in part_refs:
            total += part_ref[here, :].astype(jnp.float32)
        ref[...] = total


def join_kernel(norm, me_ref, own_ref, mate_ref, grad_ref):
    half = own_ref.shape[1]
    for ref, core in ((own_ref, me_ref[0] & 1), (mate_ref, 1 - (me_ref[0] & 1))):
        grad_ref[:, pl.ds(pl.multiple_of(core * half, half), half)] = ref[...] / norm


def row_grad_kernel(chips_ref, me_ref, got_ref, *refs):
    weight_refs, (out_ref, weights, out, rows_ref, sems) = refs[:4], refs[4:]
    chips, _, count, half = got_ref.shape
    block = count // 4
    depth = half // 2
    pieces = weights.shape[0] // depth
    level = lax.shift_right_logical(me_ref[0], 3)

    def rows_of(ref, n):
        return ref.at[n * depth : (n + 1) * depth, :]

    pairs = []
    for n in range(pieces):
        first = weight_refs[0].shape[0] // depth
        for side in range(2):
            ref = weight_refs[side] if n < first else weight_refs[2 + side]
            target = weights.at[n * depth : (n + 1) * depth, side * half : (side + 1) * half]
            pairs.append((rows_of(ref, n % first), target))
    copies = fetch(pairs, sems)
    core = me_ref[0] & 1
    for chip in range(chips):
        for n in range(4):
            at = pl.multiple_of(((level ^ n) * chips + chip) * block, block)
            for side in range(2):
                rows = got_ref[chip, pl.ds(core ^ side, 1), n * block : (n + 1) * block, :]
                rows_ref[pl.ds(at, block), side * half : (side + 1) * half] = rows[0]
    written = []
    for first in range(0, pieces, 2):
        for copy in copies[2 * first : 2 * first + 4]:
            copy.wait()
        total = dot(rows_ref[...], weights[first * depth : (first + 2) * depth, :], ((1,), (1,)))
        for n in (first, first + 1):
            out[n] = total[:, (n - first) * depth : (n - first + 1) * depth].astype(jnp.bfloat16)
            at = pl.multiple_of(chips_ref[n] * depth, depth)
            copy = pltpu.make_async_copy(
                out.at[n], out_ref.at[:, pl.ds(at, depth)], sems.at[2 * pieces + n]
            )
            copy.start()
            written.append(copy)
    for copy in written:
        copy.wait()


def code_rows(destination, core, per_peer, width):
    positions = jnp.arange(destination.shape[0], dtype=jnp.int32)
    same = (destination[:, None] == destination[None, :]) & (
        positions[:, None] < positions[None, :]
    )
    earlier = jnp.sum(same.astype(jnp.int32), axis=0)
    codes = jnp.stack([destination, core * per_peer + earlier]).astype(jnp.bfloat16)
    return jnp.pad(codes, ((0, CODE_ROWS - 2), (0, width - destination.shape[0])))


def anywhere(count):
    return [pl.BlockSpec(memory_space=pl.ANY)] * count


def hbm(count):
    return [pl.BlockSpec(memory_space=pltpu.HBM)] * count


def vmem(count):
    return [pl.BlockSpec(memory_space=pltpu.VMEM)] * count


def anywhere(count):
    return [pl.BlockSpec(memory_space=pl.ANY)] * count


SCALAR = pl.BlockSpec(memory_space=pltpu.SMEM)
PARAMS = pltpu.CompilerParams(vmem_limit_bytes=VMEM_LIMIT)
def grant(mebibytes):
    return pltpu.CompilerParams(vmem_limit_bytes=mebibytes << 20)


def per_device_paired(tokens, key_cot, routes, counts, widths, key_weight):
    rows, width_model = tokens.shape
    cols = key_cot.shape[1]
    half_cols = cols // 2
    size = lax.axis_size("dp")
    chips = size // 2
    levels = size // PLANE
    per_peer = 2 * rows // size
    receive = size * per_peer
    wide = width_model // levels
    me = lax.axis_index("dp")
    core = me % 2
    me_scalar = me.astype(jnp.int32).reshape(1)

    def mine(value):
        return lax.dynamic_slice_in_dim(value, core * half_cols, half_cols, 1)

    def theirs(value):
        return lax.dynamic_slice_in_dim(value, (1 - core) * half_cols, half_cols, 1)

    mate_shard = swap(key_weight, CORE)
    piece = jnp.where(
        core == 0,
        jnp.concatenate([key_weight[:, :half_cols], mate_shard[:, :half_cols]], axis=0),
        jnp.concatenate([mate_shard[:, half_cols:], key_weight[:, half_cols:]], axis=0),
    )
    near, far, both = PLANE, 2 * PLANE, 3 * PLANE
    have = {0: piece}

    def after_round(**beside):
        names, masks = list(beside), list(have)
        values = lax.optimization_barrier([*beside.values(), *have.values()])
        have.update(zip(masks, values[len(names) :]))
        return values[: len(names)]

    have.update(
        {
            Y: swap(piece, Y),
            X: swap(piece, X),
            near: swap(piece, near),
            far: swap(piece, far),
        }
    )
    from_both = swap(piece, both)
    by_level = jnp.stack([tokens[:, z * wide : (z + 1) * wide] for z in range(levels)])
    by_level, key_cot, counts, routes = after_round(
        by_level=by_level, key_cot=key_cot, counts=counts, routes=routes
    )
    columns = [[p + PLANE * z for z in range(levels)] for p in range(PLANE)]
    own_features = lax.all_to_all(
        by_level, "dp", split_axis=0, concat_axis=0, axis_index_groups=columns, tiled=True
    )
    have.update(
        {
            near | X: swap(have[near], X),
            near | Y: swap(have[near], Y),
            far | X: swap(have[far], X),
            far | Y: swap(have[far], Y),
        }
    )
    have[both] = from_both
    bounds = jnp.cumsum(counts[0])
    positions = jnp.arange(rows, dtype=jnp.int32)
    subnet = jnp.sum((positions[:, None] >= bounds[None, : NSUB - 1]).astype(jnp.int32), axis=1)
    subnet_match = subnet[:, None] == jnp.arange(NSUB, dtype=jnp.int32)[None, :]
    row_width = jnp.sum(jnp.where(subnet_match, widths[None, :], 0), axis=1)
    head_of_col = jnp.arange(cols, dtype=jnp.int32) // HEAD_DIM
    upstream = jnp.where(
        head_of_col[None, :] < row_width[:, None], key_cot, jnp.zeros_like(key_cot)
    )
    codes = code_rows(routes[:, 0], core, per_peer, half_cols)
    own_cot = jnp.concatenate([mine(upstream), codes], axis=0)

    own_cot, give_cot, tokens = after_round(
        own_cot=own_cot,
        give_cot=jnp.concatenate([theirs(upstream), codes], axis=0),
        tokens=tokens,
    )
    mate_tokens = swap(tokens, CORE)
    have.update(
        {
            both | X: swap(have[both], X),
            both | Y: swap(have[both], Y),
            X | Y: swap(have[Y], X),
            far | X | Y: swap(have[far | X], Y),
        }
    )
    mate_tokens, give_cot, own_cot = after_round(
        mate_tokens=mate_tokens, give_cot=give_cot, own_cot=own_cot
    )
    mate_cot = swap(give_cot, CORE)

    first_masks = list(have)
    last_masks = [near | X | Y, both | X | Y]
    order = jnp.stack([lax.shift_right_logical(me ^ mask, 1) for mask in first_masks + last_masks])
    depth = width_model // chips
    sums = jax.ShapeDtypeStruct((2, rows, half_cols), jnp.float32)

    def project(kernel, count, results, inputs, specs, name):
        return pl.pallas_call(
            kernel,
            out_shape=(*results, jax.ShapeDtypeStruct((count * depth, half_cols), jnp.bfloat16))
            + ((sums,) if name == "project" else ()),
            in_specs=specs + anywhere(count),
            out_specs=(*vmem(len(results)), anywhere(1)[0])
            + (tuple(vmem(1)) if name == "project" else ()),
            scratch_shapes=([] if name == "project" else [pltpu.VMEM(sums.shape, sums.dtype)])
            + [
                pltpu.VMEM((count, 2, rows, depth), jnp.bfloat16),
                pltpu.VMEM((count * depth, half_cols), jnp.bfloat16),
                pltpu.SemaphoreType.DMA((4 * count,)),
            ],
            compiler_params=PARAMS,
            name=name,
        )(*inputs)

    first_weight, begun = project(
        first_project_kernel,
        len(first_masks),
        (),
        (order, tokens, mate_tokens, *[have[mask] for mask in first_masks]),
        [SCALAR] + anywhere(2),
        "project",
    )
    have.update(
        {
            near | X | Y: swap(have[near | Y], X),
            both | X | Y: swap(have[both | X], Y),
        }
    )
    mate_cot, own_cot, own_features, begun, first_weight = after_round(
        mate_cot=mate_cot,
        own_cot=own_cot,
        own_features=own_features,
        begun=begun,
        first_weight=first_weight,
    )
    mate_features = swap(own_features, CORE)
    delta, last_weight = project(
        functools.partial(delta_kernel, len(first_masks)),
        len(last_masks),
        (jax.ShapeDtypeStruct((2 * rows + CODE_ROWS, half_cols), jnp.bfloat16),),
        (
            order,
            me_scalar,
            own_cot,
            mate_cot,
            tokens,
            mate_tokens,
            begun,
            *[have[mask] for mask in last_masks],
        ),
        [SCALAR] * 2 + vmem(2) + anywhere(2) + vmem(1),
        "delta",
    )

    delta_near, delta_far, mate_features = lax.optimization_barrier(
        (swap(delta, near), swap(delta, far), mate_features)
    )
    deltas = [delta, delta_near, delta_far, swap(delta_far, near)]
    first_weight, last_weight, *deltas[1:] = lax.optimization_barrier(
        (first_weight, last_weight, *deltas[1:])
    )
    mate_first, mate_last = swap(first_weight, CORE), swap(last_weight, CORE)
    count = levels * 2 * per_peer
    def select(begin, before, deltas, name):
        return pl.pallas_call(
            functools.partial(select_kernel, begin),
            out_shape=jax.ShapeDtypeStruct(
                (PLANE, count // levels * (begin + len(deltas)), half_cols), jnp.bfloat16
            ),
            in_specs=[SCALAR] + vmem(len(before)) + anywhere(len(deltas)),
            out_specs=vmem(1)[0],
            scratch_shapes=[
                pltpu.VMEM((len(deltas), *delta.shape), jnp.bfloat16),
                pltpu.SemaphoreType.DMA((len(deltas),)),
            ],
            compiler_params=grant(16),
            name=name,
        )(me_scalar, *before, *deltas)

    there = [delta, delta_near, delta_far]
    selected = select(0, [], there, "first_select")
    selected = select(3, [selected], deltas[3:], "select")
    got = lax.all_to_all(
        selected,
        "dp",
        split_axis=0,
        concat_axis=0,
        axis_index_groups=[[z * PLANE + p for p in range(PLANE)] for z in range(levels)],
        tiled=True,
    ).reshape(PLANE // 2, 2, count, half_cols)

    shard = width_model // size
    mine_terms = jax.ShapeDtypeStruct((wide // 4, half_cols), jnp.float32)
    sent_terms = jax.ShapeDtypeStruct(mine_terms.shape, jnp.bfloat16)
    all_terms = jax.ShapeDtypeStruct((wide, half_cols), jnp.float32)

    def room(chips):
        return [
            pltpu.VMEM((chips * 2 * rows, wide), jnp.bfloat16),
            pltpu.VMEM((chips * 2 * rows, half_cols), jnp.bfloat16),
        ]

    begun_terms = pl.pallas_call(
        first_terms_kernel,
        out_shape=all_terms,
        in_specs=[SCALAR] + anywhere(5),
        out_specs=vmem(1)[0],
        scratch_shapes=room(3) + [pltpu.SemaphoreType.DMA((9,))],
        compiler_params=grant(16),
        name="first_terms",
    )(me_scalar, own_features, mate_features, *there)
    own_part, *parts = pl.pallas_call(
        functools.partial(weight_grad_kernel, 3),
        out_shape=(mine_terms, *[sent_terms] * 3),
        in_specs=[SCALAR] + anywhere(2) + vmem(1) + anywhere(1),
        out_specs=tuple(hbm(1) + vmem(3)),
        scratch_shapes=room(1)
        + [pltpu.VMEM(all_terms.shape, all_terms.dtype), pltpu.SemaphoreType.DMA((4,))],
        compiler_params=grant(16),
        name="weight_grad",
    )(me_scalar, own_features, mate_features, begun_terms, after(deltas[3], selected))
    parts = [swap(part, mask) for part, mask in zip(parts, PLANE_MASKS[1:])]

    row_grads = pl.pallas_call(
        row_grad_kernel,
        out_shape=jax.ShapeDtypeStruct((receive, width_model), jnp.bfloat16),
        in_specs=[SCALAR] * 2 + vmem(1) + anywhere(4),
        out_specs=anywhere(1)[0],
        scratch_shapes=[
            pltpu.VMEM((width_model, cols), jnp.bfloat16),
            pltpu.VMEM((chips, receive, depth), jnp.bfloat16),
            pltpu.VMEM((receive, cols), jnp.bfloat16),
            pltpu.SemaphoreType.DMA((3 * chips,)),
        ],
        compiler_params=grant(62),
        name="row_grad",
    )(order, me_scalar, got, first_weight, mate_first, last_weight, mate_last)

    half_grad = jax.ShapeDtypeStruct((shard, half_cols), jnp.float32)
    keep_grad, give_grad = pl.pallas_call(
        sum_kernel,
        out_shape=(half_grad, half_grad),
        in_specs=[SCALAR] + vmem(4),
        out_specs=tuple(vmem(2)),
        compiler_params=grant(16),
        name="sum",
    )(me_scalar, after(own_part, row_grads), *parts)
    key_grad = pl.pallas_call(
        functools.partial(join_kernel, math.sqrt(rows * size)),
        out_shape=jax.ShapeDtypeStruct((shard, cols), jnp.float32),
        in_specs=[SCALAR] + vmem(2),
        out_specs=vmem(1)[0],
        compiler_params=grant(16),
        name="join",
    )(me_scalar, keep_grad, swap(give_grad, CORE))
    return (row_grads, key_grad)


def solution(mesh):
    size, split = mesh.shape["dp"], mesh.shape["mp"]
    paired = split == 1 and size == 32
    return jax.shard_map(
        per_device_paired if paired else per_device_general,
        mesh=mesh,
        in_specs=(P("dp", None), P("dp", "mp"), P("dp", None), P("dp", None), P(), P("dp", "mp")),
        out_specs=(P("dp", "mp"), P("dp", "mp")),
        check_vma=False,
    )
```

```python
import functools
import math

import jax
import jax.numpy as jnp
from jax import lax
from jax.experimental import pallas as pl
from jax.experimental.pallas import tpu as pltpu
from jax.sharding import PartitionSpec as P

HEAD_DIM = 128
NSUB = 4
VMEM_LIMIT = 60 * 1024 * 1024
CODE_ROWS = 16
epsilon = 1e-06


def per_device_general(tokens, key_cot, routes, counts, widths, key_weight):
    row_count = tokens.shape[0]
    width_model = tokens.shape[1]
    local_cols = key_cot.shape[1]
    local_heads = local_cols // HEAD_DIM
    dp_size = lax.axis_size("dp")
    per_peer = 2 * row_count // dp_size
    receive = dp_size * per_peer
    destination = routes[:, 0]
    one_hot = (destination[:, None] == jnp.arange(dp_size, dtype=jnp.int32)[None, :]).astype(
        jnp.int32
    )
    earlier = jnp.sum(jnp.cumsum(one_hot, axis=0) * one_hot, axis=1) - 1
    send_slot = destination * per_peer + earlier
    bounds = jnp.cumsum(counts[0])
    positions = jnp.arange(row_count, dtype=jnp.int32)
    subnet = jnp.sum((positions[:, None] >= bounds[None, : NSUB - 1]).astype(jnp.int32), axis=1)
    send_subnet = (
        jnp.full((receive,), -1, jnp.int32).at[send_slot].set(subnet).reshape(dp_size, per_peer)
    )
    send_cot = jnp.zeros((receive, local_cols), jnp.bfloat16).at[send_slot].set(key_cot)
    send_cot = send_cot.reshape(dp_size, per_peer, local_cols)
    send_tokens = jnp.zeros((receive, width_model), jnp.bfloat16).at[send_slot].set(tokens)
    send_tokens = send_tokens.reshape(dp_size, per_peer, width_model)
    got_tokens, got_cot, got_subnet = (
        lax.all_to_all(send_tokens, "dp", split_axis=0, concat_axis=0, tiled=True),
        lax.all_to_all(send_cot, "dp", split_axis=0, concat_axis=0, tiled=True),
        lax.all_to_all(send_subnet, "dp", split_axis=0, concat_axis=0, tiled=True),
    )
    hidden = got_tokens.reshape(receive, width_model)
    got_cot = got_cot.reshape(receive, local_cols)
    got_subnet = got_subnet.reshape(receive)
    full_weight = lax.all_gather(key_weight, "dp", axis=0, tiled=True)
    key_proj = jnp.dot(hidden, full_weight, preferred_element_type=jnp.float32)
    per_head = key_proj.reshape(receive, local_heads, HEAD_DIM)
    head_scale = jnp.sqrt(jnp.mean(per_head * per_head, axis=2, keepdims=True) + epsilon)
    outputs = per_head / head_scale
    subnet_match = got_subnet[:, None] == jnp.arange(NSUB, dtype=jnp.int32)[None, :]
    row_width = jnp.sum(jnp.where(subnet_match, widths[None, :], 0), axis=1)
    head_index = lax.axis_index("mp") * local_heads + jnp.arange(local_heads, dtype=jnp.int32)
    head_mask = (head_index[None, :] < row_width[:, None]).astype(jnp.float32)
    upstream = (
        got_cot.astype(jnp.float32).reshape(receive, local_heads, HEAD_DIM) * head_mask[:, :, None]
    )
    key_delta = (
        upstream - outputs * jnp.mean(upstream * outputs, axis=2, keepdims=True)
    ) / head_scale
    delta_low = key_delta.reshape(receive, local_cols).astype(jnp.bfloat16)
    part_delta = lax.dot_general(
        delta_low, full_weight, (((1,), (1,)), ((), ())), preferred_element_type=jnp.float32
    )
    rounded = lax.optimization_barrier(part_delta.astype(jnp.bfloat16)).astype(jnp.float32)
    feature_delta = lax.psum_scatter(
        rounded.astype(jnp.bfloat16), "mp", scatter_dimension=1, tiled=True
    )
    weight_sum = lax.psum_scatter(
        lax.dot_general(
            hidden, delta_low, (((0,), (0,)), ((), ())), preferred_element_type=jnp.float32
        ),
        "dp",
        scatter_dimension=0,
        tiled=True,
    )
    key_grad = weight_sum / math.sqrt(row_count * dp_size)
    return (feature_delta, key_grad)


CORE, X, Y = 1, 2, 4
PLANE = 8
PLANE_MASKS = (0, X, Y, X | Y)


def swap(value, mask):
    size = lax.axis_size("dp")
    return lax.ppermute(value, "dp", [(i, i ^ mask) for i in range(size)])


def after(value, *others):
    return lax.optimization_barrier((value, *others))[0]


def dot(a, b, dims):
    return lax.dot_general(a, b, (dims, ((), ())), preferred_element_type=jnp.float32)


def fetch(pairs, sems):
    copies = [
        pltpu.make_async_copy(source, target, sems.at[n])
        for n, (source, target) in enumerate(pairs)
    ]
    for copy in copies:
        copy.start()
    return copies


def project_kernel(begin, chips_ref, own_ref, mate_ref, *refs):
    begun = None
    if begin:
        begun, *refs = refs
    *pieces, weight_ref, acc, held, weights, sems = refs
    depth = pieces[0].shape[0]
    count = len(pieces)

    def rows_of(ref, n):
        return ref.at[n * depth : (n + 1) * depth, :]

    pairs = []
    for n, ref in enumerate(pieces):
        at = pl.multiple_of(chips_ref[begin + n] * depth, depth)
        pairs += [
            (ref, rows_of(weights, n)),
            (own_ref.at[:, pl.ds(at, depth)], held.at[n, 0]),
            (mate_ref.at[:, pl.ds(at, depth)], held.at[n, 1]),
        ]
    copies = fetch(pairs, sems)
    if begin:
        acc[...] = begun[...]
    kept = []
    for n in range(count):
        for copy in copies[3 * n : 3 * n + 3]:
            copy.wait()
        out = pltpu.make_async_copy(
            rows_of(weights, n), rows_of(weight_ref, n), sems.at[3 * count + n]
        )
        out.start()
        kept.append(out)
        piece = rows_of(weights, n)[...]
        for side in range(2):
            part = dot(held[n, side], piece, ((1,), (0,)))
            if begin + n == 0:
                acc[side] = part
            else:
                acc[side] += part
    return kept


def first_project_kernel(*refs):
    for copy in project_kernel(0, *refs):
        copy.wait()


def delta_kernel(begin, chips_ref, me_ref, own_cot_ref, mate_cot_ref, *refs):
    *refs, delta_ref, weight_ref, acc, held, weights, sems = refs
    kept = project_kernel(begin, chips_ref, *refs, weight_ref, acc, held, weights, sems)
    core = me_ref[0] & 1
    rows = acc.shape[1]
    delta_ref[2 * rows :, :] = jnp.zeros_like(delta_ref[2 * rows :, :])
    for side, cot_ref in enumerate((own_cot_ref, mate_cot_ref)):
        at = pl.multiple_of((core ^ side) * rows, rows)
        for head in range(own_cot_ref.shape[1] // HEAD_DIM):
            cols = slice(head * HEAD_DIM, (head + 1) * HEAD_DIM)
            proj = acc[side, :, cols]
            scale = jnp.sqrt(jnp.mean(proj * proj, axis=1, keepdims=True) + epsilon)
            normed = proj / scale
            upstream = cot_ref[:rows, cols].astype(jnp.float32)
            delta = (upstream - normed * jnp.mean(upstream * normed, axis=1, keepdims=True)) / scale
            delta_ref[pl.ds(at, rows), cols] = delta.astype(jnp.bfloat16)
        delta_ref[2 * rows :, pl.ds(at, rows)] = cot_ref[rows:, :rows]
    for copy in kept:
        copy.wait()


def select_kernel(begin, me_ref, *refs):
    *deltas, sent_ref, held, sems = refs
    copies = fetch([(ref, held.at[n]) for n, ref in enumerate(deltas[-held.shape[0] :])], sems)
    rows = (held.shape[1] - CODE_ROWS) // 2
    per_chip = sent_ref.shape[1] // (begin + held.shape[0])
    if begin:
        sent_ref[:, : begin * per_chip, :] = deltas[0][...]
    iota = lax.broadcasted_iota(jnp.int32, (PLANE * per_chip, 2 * rows), 0)
    wanted = (me_ref[0] & -PLANE) + lax.shift_right_logical(iota, per_chip.bit_length() - 1)
    slot = iota & (per_chip - 1)
    for n in range(held.shape[0]):
        copies[n].wait()
        code = held[n, 2 * rows :, : 2 * rows].astype(jnp.float32).astype(jnp.int32)
        hot = (wanted == code[0:1, :]) & (slot == code[1:2, :])
        found = dot(hot.astype(jnp.bfloat16), held[n, : 2 * rows, :], ((1,), (0,)))
        found = found.astype(jnp.bfloat16)
        at = (begin + n) * per_chip
        for place in range(PLANE):
            sent_ref[place, at : at + per_chip, :] = found[
                place * per_chip : (place + 1) * per_chip, :
            ]


def plane_terms(begin, me_ref, own_ref, mate_ref, deltas, hidden, held, sems):
    plane = lax.shift_right_logical(me_ref[0], 3)
    core = me_ref[0] & 1
    rows = own_ref.shape[1]
    pairs = []
    for n, ref in enumerate(deltas):
        own = pl.multiple_of((2 * n + core) * rows, rows)
        mate = pl.multiple_of((2 * n + 1 - core) * rows, rows)
        pairs += [
            (own_ref.at[plane ^ (begin + n)], hidden.at[pl.ds(own, rows), :]),
            (mate_ref.at[plane ^ (begin + n)], hidden.at[pl.ds(mate, rows), :]),
            (ref.at[: 2 * rows, :], held.at[2 * n * rows : 2 * (n + 1) * rows, :]),
        ]
    for copy in fetch(pairs, sems):
        copy.wait()
    return dot(hidden[...], held[...], ((0,), (0,)))


def first_terms_kernel(me_ref, own_ref, mate_ref, *refs):
    *deltas, terms_ref, hidden, held, sems = refs
    terms_ref[...] = plane_terms(0, me_ref, own_ref, mate_ref, deltas, hidden, held, sems)


def weight_grad_kernel(begin, me_ref, own_ref, mate_ref, begun_ref, *refs):
    *deltas, own_part_ref, part_x, part_y, part_both, hidden, held, acc, sems = refs
    part_refs = (part_x, part_y, part_both)
    acc[...] = begun_ref[...] + plane_terms(
        begin, me_ref, own_ref, mate_ref, deltas, hidden, held, sems
    )
    count = own_part_ref.shape[0]

    def block(mask):
        place = lax.shift_right_logical((me_ref[0] ^ mask) & 6, 1)
        return acc.at[pl.ds(pl.multiple_of(place * count, count), count), :]

    own = pltpu.make_async_copy(block(0), own_part_ref, sems.at[3 * len(deltas)])
    own.start()
    for ref, mask in zip(part_refs, PLANE_MASKS[1:]):
        ref[...] = block(mask)[...].astype(ref.dtype)
    own.wait()


def sum_kernel(me_ref, own_ref, *refs):
    *part_refs, keep_ref, give_ref = refs
    count = keep_ref.shape[0]
    for ref, core in ((keep_ref, me_ref[0] & 1), (give_ref, 1 - (me_ref[0] & 1))):
        here = pl.ds(pl.multiple_of(core * count, count), count)
        total = own_ref[here, :]
        for part_ref in part_refs:
            total += part_ref[here, :].astype(jnp.float32)
        ref[...] = total


def join_kernel(norm, me_ref, own_ref, mate_ref, grad_ref):
    half = own_ref.shape[1]
    for ref, core in ((own_ref, me_ref[0] & 1), (mate_ref, 1 - (me_ref[0] & 1))):
        grad_ref[:, pl.ds(pl.multiple_of(core * half, half), half)] = ref[...] / norm


def row_grad_kernel(chips_ref, me_ref, got_ref, *refs):
    weight_refs, (out_ref, weights, out, rows_ref, sems) = refs[:4], refs[4:]
    chips, _, count, half = got_ref.shape
    block = count // 4
    depth = half // 2
    pieces = weights.shape[0] // depth
    level = lax.shift_right_logical(me_ref[0], 3)

    def rows_of(ref, n):
        return ref.at[n * depth : (n + 1) * depth, :]

    pairs = []
    for n in range(pieces):
        first = weight_refs[0].shape[0] // depth
        for side in range(2):
            ref = weight_refs[side] if n < first else weight_refs[2 + side]
            target = weights.at[n * depth : (n + 1) * depth, side * half : (side + 1) * half]
            pairs.append((rows_of(ref, n % first), target))
    copies = fetch(pairs, sems)
    core = me_ref[0] & 1
    for chip in range(chips):
        for n in range(4):
            at = pl.multiple_of(((level ^ n) * chips + chip) * block, block)
            for side in range(2):
                rows = got_ref[chip, pl.ds(core ^ side, 1), n * block : (n + 1) * block, :]
                rows_ref[pl.ds(at, block), side * half : (side + 1) * half] = rows[0]
    written = []
    for first in range(0, pieces, 2):
        for copy in copies[2 * first : 2 * first + 4]:
            copy.wait()
        total = dot(rows_ref[...], weights[first * depth : (first + 2) * depth, :], ((1,), (1,)))
        for n in (first, first + 1):
            out[n] = total[:, (n - first) * depth : (n - first + 1) * depth].astype(jnp.bfloat16)
            at = pl.multiple_of(chips_ref[n] * depth, depth)
            copy = pltpu.make_async_copy(
                out.at[n], out_ref.at[:, pl.ds(at, depth)], sems.at[2 * pieces + n]
            )
            copy.start()
            written.append(copy)
    for copy in written:
        copy.wait()


def code_rows(destination, core, per_peer, width):
    positions = jnp.arange(destination.shape[0], dtype=jnp.int32)
    same = (destination[:, None] == destination[None, :]) & (
        positions[:, None] < positions[None, :]
    )
    earlier = jnp.sum(same.astype(jnp.int32), axis=0)
    codes = jnp.stack([destination, core * per_peer + earlier]).astype(jnp.bfloat16)
    return jnp.pad(codes, ((0, CODE_ROWS - 2), (0, width - destination.shape[0])))


def anywhere(count):
    return [pl.BlockSpec(memory_space=pl.ANY)] * count


def hbm(count):
    return [pl.BlockSpec(memory_space=pltpu.HBM)] * count


def vmem(count):
    return [pl.BlockSpec(memory_space=pltpu.VMEM)] * count


def anywhere(count):
    return [pl.BlockSpec(memory_space=pl.ANY)] * count


SCALAR = pl.BlockSpec(memory_space=pltpu.SMEM)
PARAMS = pltpu.CompilerParams(vmem_limit_bytes=VMEM_LIMIT)
def grant(mebibytes):
    return pltpu.CompilerParams(vmem_limit_bytes=mebibytes << 20)


def per_device_paired(tokens, key_cot, routes, counts, widths, key_weight):
    rows, width_model = tokens.shape
    cols = key_cot.shape[1]
    half_cols = cols // 2
    size = lax.axis_size("dp")
    chips = size // 2
    levels = size // PLANE
    per_peer = 2 * rows // size
    receive = size * per_peer
    wide = width_model // levels
    me = lax.axis_index("dp")
    core = me % 2
    me_scalar = me.astype(jnp.int32).reshape(1)

    def mine(value):
        return lax.dynamic_slice_in_dim(value, core * half_cols, half_cols, 1)

    def theirs(value):
        return lax.dynamic_slice_in_dim(value, (1 - core) * half_cols, half_cols, 1)

    mate_shard = swap(key_weight, CORE)
    piece = jnp.where(
        core == 0,
        jnp.concatenate([key_weight[:, :half_cols], mate_shard[:, :half_cols]], axis=0),
        jnp.concatenate([mate_shard[:, half_cols:], key_weight[:, half_cols:]], axis=0),
    )
    near, far, both = PLANE, 2 * PLANE, 3 * PLANE
    have = {0: piece}

    def after_round(**beside):
        names, masks = list(beside), list(have)
        values = lax.optimization_barrier([*beside.values(), *have.values()])
        have.update(zip(masks, values[len(names) :]))
        return values[: len(names)]

    have.update(
        {
            Y: swap(piece, Y),
            X: swap(piece, X),
            near: swap(piece, near),
            far: swap(piece, far),
        }
    )
    from_both = swap(piece, both)
    by_level = jnp.stack([tokens[:, z * wide : (z + 1) * wide] for z in range(levels)])
    by_level, key_cot, counts, routes = after_round(
        by_level=by_level, key_cot=key_cot, counts=counts, routes=routes
    )
    columns = [[p + PLANE * z for z in range(levels)] for p in range(PLANE)]
    own_features = lax.all_to_all(
        by_level, "dp", split_axis=0, concat_axis=0, axis_index_groups=columns, tiled=True
    )
    have.update(
        {
            near | X: swap(have[near], X),
            near | Y: swap(have[near], Y),
            far | X: swap(have[far], X),
            far | Y: swap(have[far], Y),
        }
    )
    have[both] = from_both
    bounds = jnp.cumsum(counts[0])
    positions = jnp.arange(rows, dtype=jnp.int32)
    subnet = jnp.sum((positions[:, None] >= bounds[None, : NSUB - 1]).astype(jnp.int32), axis=1)
    subnet_match = subnet[:, None] == jnp.arange(NSUB, dtype=jnp.int32)[None, :]
    row_width = jnp.sum(jnp.where(subnet_match, widths[None, :], 0), axis=1)
    head_of_col = jnp.arange(cols, dtype=jnp.int32) // HEAD_DIM
    upstream = jnp.where(
        head_of_col[None, :] < row_width[:, None], key_cot, jnp.zeros_like(key_cot)
    )
    codes = code_rows(routes[:, 0], core, per_peer, half_cols)
    own_cot = jnp.concatenate([mine(upstream), codes], axis=0)

    own_cot, give_cot, tokens = after_round(
        own_cot=own_cot,
        give_cot=jnp.concatenate([theirs(upstream), codes], axis=0),
        tokens=tokens,
    )
    mate_tokens = swap(tokens, CORE)
    have.update(
        {
            both | X: swap(have[both], X),
            both | Y: swap(have[both], Y),
            X | Y: swap(have[Y], X),
            far | X | Y: swap(have[far | X], Y),
        }
    )
    mate_tokens, give_cot, own_cot = after_round(
        mate_tokens=mate_tokens, give_cot=give_cot, own_cot=own_cot
    )
    mate_cot = swap(give_cot, CORE)

    first_masks = list(have)
    last_masks = [near | X | Y, both | X | Y]
    order = jnp.stack([lax.shift_right_logical(me ^ mask, 1) for mask in first_masks + last_masks])
    depth = width_model // chips
    sums = jax.ShapeDtypeStruct((2, rows, half_cols), jnp.float32)

    def project(kernel, count, results, inputs, specs, name):
        return pl.pallas_call(
            kernel,
            out_shape=(*results, jax.ShapeDtypeStruct((count * depth, half_cols), jnp.bfloat16))
            + ((sums,) if name == "project" else ()),
            in_specs=specs + anywhere(count),
            out_specs=(*vmem(len(results)), anywhere(1)[0])
            + (tuple(vmem(1)) if name == "project" else ()),
            scratch_shapes=([] if name == "project" else [pltpu.VMEM(sums.shape, sums.dtype)])
            + [
                pltpu.VMEM((count, 2, rows, depth), jnp.bfloat16),
                pltpu.VMEM((count * depth, half_cols), jnp.bfloat16),
                pltpu.SemaphoreType.DMA((4 * count,)),
            ],
            compiler_params=PARAMS,
            name=name,
        )(*inputs)

    first_weight, begun = project(
        first_project_kernel,
        len(first_masks),
        (),
        (order, tokens, mate_tokens, *[have[mask] for mask in first_masks]),
        [SCALAR] + anywhere(2),
        "project",
    )
    have.update(
        {
            near | X | Y: swap(have[near | Y], X),
            both | X | Y: swap(have[both | X], Y),
        }
    )
    mate_cot, own_cot, own_features, begun, first_weight = after_round(
        mate_cot=mate_cot,
        own_cot=own_cot,
        own_features=own_features,
        begun=begun,
        first_weight=first_weight,
    )
    mate_features = swap(own_features, CORE)
    delta, last_weight = project(
        functools.partial(delta_kernel, len(first_masks)),
        len(last_masks),
        (jax.ShapeDtypeStruct((2 * rows + CODE_ROWS, half_cols), jnp.bfloat16),),
        (
            order,
            me_scalar,
            own_cot,
            mate_cot,
            tokens,
            mate_tokens,
            begun,
            *[have[mask] for mask in last_masks],
        ),
        [SCALAR] * 2 + vmem(2) + anywhere(2) + vmem(1),
        "delta",
    )

    delta_near, delta_far, mate_features = lax.optimization_barrier(
        (swap(delta, near), swap(delta, far), mate_features)
    )
    deltas = [delta, delta_near, delta_far, swap(delta_far, near)]
    count = levels * 2 * per_peer
    def select(begin, before, deltas, name):
        return pl.pallas_call(
            functools.partial(select_kernel, begin),
            out_shape=jax.ShapeDtypeStruct(
                (PLANE, count // levels * (begin + len(deltas)), half_cols), jnp.bfloat16
            ),
            in_specs=[SCALAR] + vmem(len(before)) + anywhere(len(deltas)),
            out_specs=vmem(1)[0],
            scratch_shapes=[
                pltpu.VMEM((len(deltas), *delta.shape), jnp.bfloat16),
                pltpu.SemaphoreType.DMA((len(deltas),)),
            ],
            compiler_params=grant(16),
            name=name,
        )(me_scalar, *before, *deltas)

    there = [delta, delta_near, delta_far]
    selected = select(0, [], there, "first_select")
    shard = width_model // size
    mine_terms = jax.ShapeDtypeStruct((wide // 4, half_cols), jnp.float32)
    sent_terms = jax.ShapeDtypeStruct(mine_terms.shape, jnp.bfloat16)
    all_terms = jax.ShapeDtypeStruct((wide, half_cols), jnp.float32)

    def room(chips):
        return [
            pltpu.VMEM((chips * 2 * rows, wide), jnp.bfloat16),
            pltpu.VMEM((chips * 2 * rows, half_cols), jnp.bfloat16),
        ]

    begun_terms = pl.pallas_call(
        first_terms_kernel,
        out_shape=all_terms,
        in_specs=[SCALAR] + anywhere(5),
        out_specs=vmem(1)[0],
        scratch_shapes=room(3) + [pltpu.SemaphoreType.DMA((9,))],
        compiler_params=grant(16),
        name="first_terms",
    )(me_scalar, own_features, mate_features, *there)
    first_weight, last_weight, selected, begun_terms, *deltas[1:] = lax.optimization_barrier(
        (first_weight, last_weight, selected, begun_terms, *deltas[1:])
    )
    mate_first, mate_last = swap(first_weight, CORE), swap(last_weight, CORE)
    selected = select(3, [selected], deltas[3:], "select")
    got = lax.all_to_all(
        selected,
        "dp",
        split_axis=0,
        concat_axis=0,
        axis_index_groups=[[z * PLANE + p for p in range(PLANE)] for z in range(levels)],
        tiled=True,
    ).reshape(PLANE // 2, 2, count, half_cols)
    own_part, *parts = pl.pallas_call(
        functools.partial(weight_grad_kernel, 3),
        out_shape=(mine_terms, *[sent_terms] * 3),
        in_specs=[SCALAR] + anywhere(2) + vmem(1) + anywhere(1),
        out_specs=tuple(hbm(1) + vmem(3)),
        scratch_shapes=room(1)
        + [pltpu.VMEM(all_terms.shape, all_terms.dtype), pltpu.SemaphoreType.DMA((4,))],
        compiler_params=grant(16),
        name="weight_grad",
    )(me_scalar, own_features, mate_features, begun_terms, after(deltas[3], selected))
    parts = [swap(part, mask) for part, mask in zip(parts, PLANE_MASKS[1:])]

    row_grads = pl.pallas_call(
        row_grad_kernel,
        out_shape=jax.ShapeDtypeStruct((receive, width_model), jnp.bfloat16),
        in_specs=[SCALAR] * 2 + vmem(1) + anywhere(4),
        out_specs=anywhere(1)[0],
        scratch_shapes=[
            pltpu.VMEM((width_model, cols), jnp.bfloat16),
            pltpu.VMEM((chips, receive, depth), jnp.bfloat16),
            pltpu.VMEM((receive, cols), jnp.bfloat16),
            pltpu.SemaphoreType.DMA((3 * chips,)),
        ],
        compiler_params=grant(62),
        name="row_grad",
    )(order, me_scalar, got, first_weight, mate_first, last_weight, mate_last)

    half_grad = jax.ShapeDtypeStruct((shard, half_cols), jnp.float32)
    keep_grad, give_grad = pl.pallas_call(
        sum_kernel,
        out_shape=(half_grad, half_grad),
        in_specs=[SCALAR] + vmem(4),
        out_specs=tuple(vmem(2)),
        compiler_params=grant(16),
        name="sum",
    )(me_scalar, after(own_part, row_grads), *parts)
    key_grad = pl.pallas_call(
        functools.partial(join_kernel, math.sqrt(rows * size)),
        out_shape=jax.ShapeDtypeStruct((shard, cols), jnp.float32),
        in_specs=[SCALAR] + vmem(2),
        out_specs=vmem(1)[0],
        compiler_params=grant(16),
        name="join",
    )(me_scalar, keep_grad, swap(give_grad, CORE))
    return (row_grads, key_grad)


def solution(mesh):
    size, split = mesh.shape["dp"], mesh.shape["mp"]
    paired = split == 1 and size == 32
    return jax.shard_map(
        per_device_paired if paired else per_device_general,
        mesh=mesh,
        in_specs=(P("dp", None), P("dp", "mp"), P("dp", None), P("dp", None), P(), P("dp", "mp")),
        out_specs=(P("dp", "mp"), P("dp", "mp")),
        check_vma=False,
    )
```

```python
import functools
import math

import jax
import jax.numpy as jnp
from jax import lax
from jax.experimental import pallas as pl
from jax.experimental.pallas import tpu as pltpu
from jax.sharding import PartitionSpec as P

HEAD_DIM = 128
NSUB = 4
VMEM_LIMIT = 60 * 1024 * 1024
CODE_ROWS = 16
epsilon = 1e-06


def per_device_general(tokens, key_cot, routes, counts, widths, key_weight):
    row_count = tokens.shape[0]
    width_model = tokens.shape[1]
    local_cols = key_cot.shape[1]
    local_heads = local_cols // HEAD_DIM
    dp_size = lax.axis_size("dp")
    per_peer = 2 * row_count // dp_size
    receive = dp_size * per_peer
    destination = routes[:, 0]
    one_hot = (destination[:, None] == jnp.arange(dp_size, dtype=jnp.int32)[None, :]).astype(
        jnp.int32
    )
    earlier = jnp.sum(jnp.cumsum(one_hot, axis=0) * one_hot, axis=1) - 1
    send_slot = destination * per_peer + earlier
    bounds = jnp.cumsum(counts[0])
    positions = jnp.arange(row_count, dtype=jnp.int32)
    subnet = jnp.sum((positions[:, None] >= bounds[None, : NSUB - 1]).astype(jnp.int32), axis=1)
    send_subnet = (
        jnp.full((receive,), -1, jnp.int32).at[send_slot].set(subnet).reshape(dp_size, per_peer)
    )
    send_cot = jnp.zeros((receive, local_cols), jnp.bfloat16).at[send_slot].set(key_cot)
    send_cot = send_cot.reshape(dp_size, per_peer, local_cols)
    send_tokens = jnp.zeros((receive, width_model), jnp.bfloat16).at[send_slot].set(tokens)
    send_tokens = send_tokens.reshape(dp_size, per_peer, width_model)
    got_tokens, got_cot, got_subnet = (
        lax.all_to_all(send_tokens, "dp", split_axis=0, concat_axis=0, tiled=True),
        lax.all_to_all(send_cot, "dp", split_axis=0, concat_axis=0, tiled=True),
        lax.all_to_all(send_subnet, "dp", split_axis=0, concat_axis=0, tiled=True),
    )
    hidden = got_tokens.reshape(receive, width_model)
    got_cot = got_cot.reshape(receive, local_cols)
    got_subnet = got_subnet.reshape(receive)
    full_weight = lax.all_gather(key_weight, "dp", axis=0, tiled=True)
    key_proj = jnp.dot(hidden, full_weight, preferred_element_type=jnp.float32)
    per_head = key_proj.reshape(receive, local_heads, HEAD_DIM)
    head_scale = jnp.sqrt(jnp.mean(per_head * per_head, axis=2, keepdims=True) + epsilon)
    outputs = per_head / head_scale
    subnet_match = got_subnet[:, None] == jnp.arange(NSUB, dtype=jnp.int32)[None, :]
    row_width = jnp.sum(jnp.where(subnet_match, widths[None, :], 0), axis=1)
    head_index = lax.axis_index("mp") * local_heads + jnp.arange(local_heads, dtype=jnp.int32)
    head_mask = (head_index[None, :] < row_width[:, None]).astype(jnp.float32)
    upstream = (
        got_cot.astype(jnp.float32).reshape(receive, local_heads, HEAD_DIM) * head_mask[:, :, None]
    )
    key_delta = (
        upstream - outputs * jnp.mean(upstream * outputs, axis=2, keepdims=True)
    ) / head_scale
    delta_low = key_delta.reshape(receive, local_cols).astype(jnp.bfloat16)
    part_delta = lax.dot_general(
        delta_low, full_weight, (((1,), (1,)), ((), ())), preferred_element_type=jnp.float32
    )
    rounded = lax.optimization_barrier(part_delta.astype(jnp.bfloat16)).astype(jnp.float32)
    feature_delta = lax.psum_scatter(
        rounded.astype(jnp.bfloat16), "mp", scatter_dimension=1, tiled=True
    )
    weight_sum = lax.psum_scatter(
        lax.dot_general(
            hidden, delta_low, (((0,), (0,)), ((), ())), preferred_element_type=jnp.float32
        ),
        "dp",
        scatter_dimension=0,
        tiled=True,
    )
    key_grad = weight_sum / math.sqrt(row_count * dp_size)
    return (feature_delta, key_grad)


CORE, X, Y = 1, 2, 4
PLANE = 8
PLANE_MASKS = (0, X, Y, X | Y)


def swap(value, mask):
    size = lax.axis_size("dp")
    return lax.ppermute(value, "dp", [(i, i ^ mask) for i in range(size)])


def after(value, *others):
    return lax.optimization_barrier((value, *others))[0]


def dot(a, b, dims):
    return lax.dot_general(a, b, (dims, ((), ())), preferred_element_type=jnp.float32)


def fetch(pairs, sems):
    copies = [
        pltpu.make_async_copy(source, target, sems.at[n])
        for n, (source, target) in enumerate(pairs)
    ]
    for copy in copies:
        copy.start()
    return copies


def project_kernel(begin, chips_ref, own_ref, mate_ref, *refs):
    begun = None
    if begin:
        begun, *refs = refs
    *pieces, weight_ref, acc, held, weights, sems = refs
    depth = pieces[0].shape[0]
    count = len(pieces)

    def rows_of(ref, n):
        return ref.at[n * depth : (n + 1) * depth, :]

    pairs = []
    for n, ref in enumerate(pieces):
        at = pl.multiple_of(chips_ref[begin + n] * depth, depth)
        pairs += [
            (ref, rows_of(weights, n)),
            (own_ref.at[:, pl.ds(at, depth)], held.at[n, 0]),
            (mate_ref.at[:, pl.ds(at, depth)], held.at[n, 1]),
        ]
    copies = fetch(pairs, sems)
    if begin:
        acc[...] = begun[...]
    kept = []
    for n in range(count):
        for copy in copies[3 * n : 3 * n + 3]:
            copy.wait()
        out = pltpu.make_async_copy(
            rows_of(weights, n), rows_of(weight_ref, n), sems.at[3 * count + n]
        )
        out.start()
        kept.append(out)
        piece = rows_of(weights, n)[...]
        for side in range(2):
            part = dot(held[n, side], piece, ((1,), (0,)))
            if begin + n == 0:
                acc[side] = part
            else:
                acc[side] += part
    return kept


def first_project_kernel(*refs):
    for copy in project_kernel(0, *refs):
        copy.wait()


def delta_kernel(begin, chips_ref, me_ref, own_cot_ref, mate_cot_ref, *refs):
    *refs, delta_ref, weight_ref, acc, held, weights, sems = refs
    kept = project_kernel(begin, chips_ref, *refs, weight_ref, acc, held, weights, sems)
    core = me_ref[0] & 1
    rows = acc.shape[1]
    delta_ref[2 * rows :, :] = jnp.zeros_like(delta_ref[2 * rows :, :])
    for side, cot_ref in enumerate((own_cot_ref, mate_cot_ref)):
        at = pl.multiple_of((core ^ side) * rows, rows)
        for head in range(own_cot_ref.shape[1] // HEAD_DIM):
            cols = slice(head * HEAD_DIM, (head + 1) * HEAD_DIM)
            proj = acc[side, :, cols]
            scale = jnp.sqrt(jnp.mean(proj * proj, axis=1, keepdims=True) + epsilon)
            normed = proj / scale
            upstream = cot_ref[:rows, cols].astype(jnp.float32)
            delta = (upstream - normed * jnp.mean(upstream * normed, axis=1, keepdims=True)) / scale
            delta_ref[pl.ds(at, rows), cols] = delta.astype(jnp.bfloat16)
        delta_ref[2 * rows :, pl.ds(at, rows)] = cot_ref[rows:, :rows]
    for copy in kept:
        copy.wait()


def select_kernel(begin, me_ref, *refs):
    *deltas, sent_ref, held, sems = refs
    copies = fetch([(ref, held.at[n]) for n, ref in enumerate(deltas[-held.shape[0] :])], sems)
    rows = (held.shape[1] - CODE_ROWS) // 2
    per_chip = sent_ref.shape[1] // (begin + held.shape[0])
    if begin:
        sent_ref[:, : begin * per_chip, :] = deltas[0][...]
    iota = lax.broadcasted_iota(jnp.int32, (PLANE * per_chip, 2 * rows), 0)
    wanted = (me_ref[0] & -PLANE) + lax.shift_right_logical(iota, per_chip.bit_length() - 1)
    slot = iota & (per_chip - 1)
    for n in range(held.shape[0]):
        copies[n].wait()
        code = held[n, 2 * rows :, : 2 * rows].astype(jnp.float32).astype(jnp.int32)
        hot = (wanted == code[0:1, :]) & (slot == code[1:2, :])
        found = dot(hot.astype(jnp.bfloat16), held[n, : 2 * rows, :], ((1,), (0,)))
        found = found.astype(jnp.bfloat16)
        at = (begin + n) * per_chip
        for place in range(PLANE):
            sent_ref[place, at : at + per_chip, :] = found[
                place * per_chip : (place + 1) * per_chip, :
            ]


def plane_terms(begin, me_ref, own_ref, mate_ref, deltas, hidden, held, sems):
    plane = lax.shift_right_logical(me_ref[0], 3)
    core = me_ref[0] & 1
    rows = own_ref.shape[1]
    pairs = []
    for n, ref in enumerate(deltas):
        own = pl.multiple_of((2 * n + core) * rows, rows)
        mate = pl.multiple_of((2 * n + 1 - core) * rows, rows)
        pairs += [
            (own_ref.at[plane ^ (begin + n)], hidden.at[pl.ds(own, rows), :]),
            (mate_ref.at[plane ^ (begin + n)], hidden.at[pl.ds(mate, rows), :]),
            (ref.at[: 2 * rows, :], held.at[2 * n * rows : 2 * (n + 1) * rows, :]),
        ]
    for copy in fetch(pairs, sems):
        copy.wait()
    return dot(hidden[...], held[...], ((0,), (0,)))


def first_terms_kernel(me_ref, own_ref, mate_ref, *refs):
    *deltas, terms_ref, hidden, held, sems = refs
    terms_ref[...] = plane_terms(0, me_ref, own_ref, mate_ref, deltas, hidden, held, sems)


def weight_grad_kernel(begin, me_ref, own_ref, mate_ref, begun_ref, *refs):
    *deltas, own_part_ref, part_x, part_y, part_both, hidden, held, acc, sems = refs
    part_refs = (part_x, part_y, part_both)
    acc[...] = begun_ref[...] + plane_terms(
        begin, me_ref, own_ref, mate_ref, deltas, hidden, held, sems
    )
    count = own_part_ref.shape[0]

    def block(mask):
        place = lax.shift_right_logical((me_ref[0] ^ mask) & 6, 1)
        return acc.at[pl.ds(pl.multiple_of(place * count, count), count), :]

    own = pltpu.make_async_copy(block(0), own_part_ref, sems.at[3 * len(deltas)])
    own.start()
    for ref, mask in zip(part_refs, PLANE_MASKS[1:]):
        ref[...] = block(mask)[...].astype(ref.dtype)
    own.wait()


def sum_kernel(me_ref, own_ref, *refs):
    *part_refs, keep_ref, give_ref = refs
    count = keep_ref.shape[0]
    for ref, core in ((keep_ref, me_ref[0] & 1), (give_ref, 1 - (me_ref[0] & 1))):
        here = pl.ds(pl.multiple_of(core * count, count), count)
        total = own_ref[here, :]
        for part_ref in part_refs:
            total += part_ref[here, :].astype(jnp.float32)
        ref[...] = total


def join_kernel(norm, me_ref, own_ref, mate_ref, grad_ref):
    half = own_ref.shape[1]
    for ref, core in ((own_ref, me_ref[0] & 1), (mate_ref, 1 - (me_ref[0] & 1))):
        grad_ref[:, pl.ds(pl.multiple_of(core * half, half), half)] = ref[...] / norm


def row_grad_kernel(chips_ref, me_ref, got_ref, *refs):
    weight_refs, (out_ref, weights, out, rows_ref, sems) = refs[:4], refs[4:]
    chips, _, count, half = got_ref.shape
    block = count // 4
    depth = half // 2
    pieces = weights.shape[0] // depth
    level = lax.shift_right_logical(me_ref[0], 3)

    def rows_of(ref, n):
        return ref.at[n * depth : (n + 1) * depth, :]

    pairs = []
    for n in range(pieces):
        first = weight_refs[0].shape[0] // depth
        for side in range(2):
            ref = weight_refs[side] if n < first else weight_refs[2 + side]
            target = weights.at[n * depth : (n + 1) * depth, side * half : (side + 1) * half]
            pairs.append((rows_of(ref, n % first), target))
    copies = fetch(pairs, sems)
    core = me_ref[0] & 1
    for chip in range(chips):
        for n in range(4):
            at = pl.multiple_of(((level ^ n) * chips + chip) * block, block)
            for side in range(2):
                rows = got_ref[chip, pl.ds(core ^ side, 1), n * block : (n + 1) * block, :]
                rows_ref[pl.ds(at, block), side * half : (side + 1) * half] = rows[0]
    written = []
    for first in range(0, pieces, 2):
        for copy in copies[2 * first : 2 * first + 4]:
            copy.wait()
        total = dot(rows_ref[...], weights[first * depth : (first + 2) * depth, :], ((1,), (1,)))
        for n in (first, first + 1):
            out[n] = total[:, (n - first) * depth : (n - first + 1) * depth].astype(jnp.bfloat16)
            at = pl.multiple_of(chips_ref[n] * depth, depth)
            copy = pltpu.make_async_copy(
                out.at[n], out_ref.at[:, pl.ds(at, depth)], sems.at[2 * pieces + n]
            )
            copy.start()
            written.append(copy)
    for copy in written:
        copy.wait()


def code_rows(destination, core, per_peer, width):
    positions = jnp.arange(destination.shape[0], dtype=jnp.int32)
    same = (destination[:, None] == destination[None, :]) & (
        positions[:, None] < positions[None, :]
    )
    earlier = jnp.sum(same.astype(jnp.int32), axis=0)
    codes = jnp.stack([destination, core * per_peer + earlier]).astype(jnp.bfloat16)
    return jnp.pad(codes, ((0, CODE_ROWS - 2), (0, width - destination.shape[0])))


def anywhere(count):
    return [pl.BlockSpec(memory_space=pl.ANY)] * count


def hbm(count):
    return [pl.BlockSpec(memory_space=pltpu.HBM)] * count


def vmem(count):
    return [pl.BlockSpec(memory_space=pltpu.VMEM)] * count


def anywhere(count):
    return [pl.BlockSpec(memory_space=pl.ANY)] * count


SCALAR = pl.BlockSpec(memory_space=pltpu.SMEM)
PARAMS = pltpu.CompilerParams(vmem_limit_bytes=VMEM_LIMIT)
def grant(mebibytes):
    return pltpu.CompilerParams(vmem_limit_bytes=mebibytes << 20)


def per_device_paired(tokens, key_cot, routes, counts, widths, key_weight):
    rows, width_model = tokens.shape
    cols = key_cot.shape[1]
    half_cols = cols // 2
    size = lax.axis_size("dp")
    chips = size // 2
    levels = size // PLANE
    per_peer = 2 * rows // size
    receive = size * per_peer
    wide = width_model // levels
    me = lax.axis_index("dp")
    core = me % 2
    me_scalar = me.astype(jnp.int32).reshape(1)

    def mine(value):
        return lax.dynamic_slice_in_dim(value, core * half_cols, half_cols, 1)

    def theirs(value):
        return lax.dynamic_slice_in_dim(value, (1 - core) * half_cols, half_cols, 1)

    mate_shard = swap(key_weight, CORE)
    piece = jnp.where(
        core == 0,
        jnp.concatenate([key_weight[:, :half_cols], mate_shard[:, :half_cols]], axis=0),
        jnp.concatenate([mate_shard[:, half_cols:], key_weight[:, half_cols:]], axis=0),
    )
    near, far, both = PLANE, 2 * PLANE, 3 * PLANE
    have = {0: piece}

    def after_round(**beside):
        names, masks = list(beside), list(have)
        values = lax.optimization_barrier([*beside.values(), *have.values()])
        have.update(zip(masks, values[len(names) :]))
        return values[: len(names)]

    have.update(
        {
            Y: swap(piece, Y),
            X: swap(piece, X),
            near: swap(piece, near),
            far: swap(piece, far),
        }
    )
    from_both = swap(piece, both)
    by_level = jnp.stack([tokens[:, z * wide : (z + 1) * wide] for z in range(levels)])
    by_level, key_cot, counts, routes = after_round(
        by_level=by_level, key_cot=key_cot, counts=counts, routes=routes
    )
    columns = [[p + PLANE * z for z in range(levels)] for p in range(PLANE)]
    own_features = lax.all_to_all(
        by_level, "dp", split_axis=0, concat_axis=0, axis_index_groups=columns, tiled=True
    )
    have.update(
        {
            near | X: swap(have[near], X),
            near | Y: swap(have[near], Y),
            far | X: swap(have[far], X),
            far | Y: swap(have[far], Y),
        }
    )
    have[both] = from_both
    bounds = jnp.cumsum(counts[0])
    positions = jnp.arange(rows, dtype=jnp.int32)
    subnet = jnp.sum((positions[:, None] >= bounds[None, : NSUB - 1]).astype(jnp.int32), axis=1)
    subnet_match = subnet[:, None] == jnp.arange(NSUB, dtype=jnp.int32)[None, :]
    row_width = jnp.sum(jnp.where(subnet_match, widths[None, :], 0), axis=1)
    head_of_col = jnp.arange(cols, dtype=jnp.int32) // HEAD_DIM
    upstream = jnp.where(
        head_of_col[None, :] < row_width[:, None], key_cot, jnp.zeros_like(key_cot)
    )
    codes = code_rows(routes[:, 0], core, per_peer, half_cols)
    own_cot = jnp.concatenate([mine(upstream), codes], axis=0)

    own_cot, give_cot, tokens = after_round(
        own_cot=own_cot,
        give_cot=jnp.concatenate([theirs(upstream), codes], axis=0),
        tokens=tokens,
    )
    mate_tokens = swap(tokens, CORE)
    have.update(
        {
            both | X: swap(have[both], X),
            both | Y: swap(have[both], Y),
            X | Y: swap(have[Y], X),
            far | X | Y: swap(have[far | X], Y),
        }
    )
    mate_tokens, give_cot, own_cot = after_round(
        mate_tokens=mate_tokens, give_cot=give_cot, own_cot=own_cot
    )
    mate_cot = swap(give_cot, CORE)

    first_masks = list(have)
    last_masks = [near | X | Y, both | X | Y]
    order = jnp.stack([lax.shift_right_logical(me ^ mask, 1) for mask in first_masks + last_masks])
    depth = width_model // chips
    sums = jax.ShapeDtypeStruct((2, rows, half_cols), jnp.float32)

    def project(kernel, count, results, inputs, specs, name):
        return pl.pallas_call(
            kernel,
            out_shape=(*results, jax.ShapeDtypeStruct((count * depth, half_cols), jnp.bfloat16))
            + ((sums,) if name == "project" else ()),
            in_specs=specs + anywhere(count),
            out_specs=(*vmem(len(results)), anywhere(1)[0])
            + (tuple(vmem(1)) if name == "project" else ()),
            scratch_shapes=([] if name == "project" else [pltpu.VMEM(sums.shape, sums.dtype)])
            + [
                pltpu.VMEM((count, 2, rows, depth), jnp.bfloat16),
                pltpu.VMEM((count * depth, half_cols), jnp.bfloat16),
                pltpu.SemaphoreType.DMA((4 * count,)),
            ],
            compiler_params=PARAMS,
            name=name,
        )(*inputs)

    first_weight, begun = project(
        first_project_kernel,
        len(first_masks),
        (),
        (order, tokens, mate_tokens, *[have[mask] for mask in first_masks]),
        [SCALAR] + anywhere(2),
        "project",
    )
    have.update(
        {
            near | X | Y: swap(have[near | Y], X),
            both | X | Y: swap(have[both | X], Y),
        }
    )
    mate_cot, own_cot, own_features, begun, first_weight = after_round(
        mate_cot=mate_cot,
        own_cot=own_cot,
        own_features=own_features,
        begun=begun,
        first_weight=first_weight,
    )
    mate_features = swap(own_features, CORE)
    delta, last_weight = project(
        functools.partial(delta_kernel, len(first_masks)),
        len(last_masks),
        (jax.ShapeDtypeStruct((2 * rows + CODE_ROWS, half_cols), jnp.bfloat16),),
        (
            order,
            me_scalar,
            own_cot,
            mate_cot,
            tokens,
            mate_tokens,
            begun,
            *[have[mask] for mask in last_masks],
        ),
        [SCALAR] * 2 + vmem(2) + anywhere(2) + vmem(1),
        "delta",
    )

    delta_near, delta_far, mate_features = lax.optimization_barrier(
        (swap(delta, near), swap(delta, far), mate_features)
    )
    deltas = [delta, delta_near, delta_far, swap(delta_far, near)]
    count = levels * 2 * per_peer
    def select(begin, before, deltas, name):
        return pl.pallas_call(
            functools.partial(select_kernel, begin),
            out_shape=jax.ShapeDtypeStruct(
                (PLANE, count // levels * (begin + len(deltas)), half_cols), jnp.bfloat16
            ),
            in_specs=[SCALAR] + vmem(len(before)) + anywhere(len(deltas)),
            out_specs=vmem(1)[0],
            scratch_shapes=[
                pltpu.VMEM((len(deltas), *delta.shape), jnp.bfloat16),
                pltpu.SemaphoreType.DMA((len(deltas),)),
            ],
            compiler_params=grant(62),
            name=name,
        )(me_scalar, *before, *deltas)

    there = [delta, delta_near, delta_far]
    selected = select(0, [], there, "first_select")
    shard = width_model // size
    mine_terms = jax.ShapeDtypeStruct((wide // 4, half_cols), jnp.float32)
    sent_terms = jax.ShapeDtypeStruct(mine_terms.shape, jnp.bfloat16)
    all_terms = jax.ShapeDtypeStruct((wide, half_cols), jnp.float32)

    def room(chips):
        return [
            pltpu.VMEM((chips * 2 * rows, wide), jnp.bfloat16),
            pltpu.VMEM((chips * 2 * rows, half_cols), jnp.bfloat16),
        ]

    begun_terms = pl.pallas_call(
        first_terms_kernel,
        out_shape=all_terms,
        in_specs=[SCALAR] + anywhere(5),
        out_specs=vmem(1)[0],
        scratch_shapes=room(3) + [pltpu.SemaphoreType.DMA((9,))],
        compiler_params=grant(62),
        name="first_terms",
    )(me_scalar, own_features, mate_features, *there)
    first_weight, last_weight, selected, begun_terms, *deltas[1:] = lax.optimization_barrier(
        (first_weight, last_weight, selected, begun_terms, *deltas[1:])
    )
    mate_first, mate_last = swap(first_weight, CORE), swap(last_weight, CORE)
    selected = select(3, [selected], deltas[3:], "select")
    got = lax.all_to_all(
        selected,
        "dp",
        split_axis=0,
        concat_axis=0,
        axis_index_groups=[[z * PLANE + p for p in range(PLANE)] for z in range(levels)],
        tiled=True,
    ).reshape(PLANE // 2, 2, count, half_cols)
    own_part, *parts = pl.pallas_call(
        functools.partial(weight_grad_kernel, 3),
        out_shape=(mine_terms, *[sent_terms] * 3),
        in_specs=[SCALAR] + anywhere(2) + vmem(1) + anywhere(1),
        out_specs=tuple(hbm(1) + vmem(3)),
        scratch_shapes=room(1)
        + [pltpu.VMEM(all_terms.shape, all_terms.dtype), pltpu.SemaphoreType.DMA((4,))],
        compiler_params=grant(62),
        name="weight_grad",
    )(me_scalar, own_features, mate_features, begun_terms, after(deltas[3], selected))
    parts = [swap(part, mask) for part, mask in zip(parts, PLANE_MASKS[1:])]

    row_grads = pl.pallas_call(
        row_grad_kernel,
        out_shape=jax.ShapeDtypeStruct((receive, width_model), jnp.bfloat16),
        in_specs=[SCALAR] * 2 + vmem(1) + anywhere(4),
        out_specs=anywhere(1)[0],
        scratch_shapes=[
            pltpu.VMEM((width_model, cols), jnp.bfloat16),
            pltpu.VMEM((chips, receive, depth), jnp.bfloat16),
            pltpu.VMEM((receive, cols), jnp.bfloat16),
            pltpu.SemaphoreType.DMA((3 * chips,)),
        ],
        compiler_params=grant(62),
        name="row_grad",
    )(order, me_scalar, got, first_weight, mate_first, last_weight, mate_last)

    half_grad = jax.ShapeDtypeStruct((shard, half_cols), jnp.float32)
    keep_grad, give_grad = pl.pallas_call(
        sum_kernel,
        out_shape=(half_grad, half_grad),
        in_specs=[SCALAR] + vmem(4),
        out_specs=tuple(vmem(2)),
        compiler_params=grant(16),
        name="sum",
    )(me_scalar, after(own_part, row_grads), *parts)
    key_grad = pl.pallas_call(
        functools.partial(join_kernel, math.sqrt(rows * size)),
        out_shape=jax.ShapeDtypeStruct((shard, cols), jnp.float32),
        in_specs=[SCALAR] + vmem(2),
        out_specs=vmem(1)[0],
        compiler_params=grant(16),
        name="join",
    )(me_scalar, keep_grad, swap(give_grad, CORE))
    return (row_grads, key_grad)


def solution(mesh):
    size, split = mesh.shape["dp"], mesh.shape["mp"]
    paired = split == 1 and size == 32
    return jax.shard_map(
        per_device_paired if paired else per_device_general,
        mesh=mesh,
        in_specs=(P("dp", None), P("dp", "mp"), P("dp", None), P("dp", None), P(), P("dp", "mp")),
        out_specs=(P("dp", "mp"), P("dp", "mp")),
        check_vma=False,
    )
```
